32 devices in a mesh: groups: 2 (over x), req: 4 (over y, core), tp: 4 (over z).
Axes of the slice: x: 2, y: 2, z: 4, core: 2. Of those that a mesh axis runs over, the one named last changes fastest.
Arguments:
- attention_rows: bfloat16 [4096, 8192], P(('groups', 'req'), 'tp'), parts along dimension 0, may hold values from -6 to 6
- output_weight_matrix: bfloat16 [8192, 4096], P('tp'), may hold values from -0.0625 to 0.0625
- adapter_down_maps: bfloat16 [1024, 16, 8192], P(('groups', 'req'), None, 'tp'), parts along dimension 0, may hold values from -0.0625 to 0.0625
- adapter_up_maps: bfloat16 [1024, 16, 4096], P(('groups', 'req'), None, 'tp'), parts along dimension 0, may hold values from -1.5 to 1.5
- adapter_pool_slot: int32 [1024], P('groups'), parts along dimension 0, may hold values from 0 to 511, as said below
- segment_adapter_ids: int32 [8, 12], P(('groups', 'req')), parts along dimension 0, may hold values from 0 to 511, as said below
- segment_row_count: int32 [8, 12], P(('groups', 'req')), parts along dimension 0, may hold values from 1 to 128, 512 in all within a row
Outputs:
- mixed: bfloat16 [4096, 4096], P(('groups', 'req'), 'tp'), parts along dimension 0
The draws below stay inside these ranges and needn't reach their ends.
There are 2 independent parts, one for each index of `groups`. The reference program is written for one: setup_inputs(seed, part) draws one part's arguments, and reference() takes and returns one part's arrays. A program takes and returns all parts, laid end to end along the dimension named above; an argument that names none is the same for every part. Nothing has to cross between parts.
Inputs may be any that keep to these rules, and one draw needn't show every extreme that they name: adapter_pool_slot is a permutation of the slots; slots j * 128 to (j + 1) * 128 - 1 form pool share j. `segment_adapter_ids`: in each request group, at most 6 segments name adapters whose slots lie in any one pool share, and exactly 6 for some share. `segment_row_count`: each request group's lengths sum to 512, the longest exactly 128.
All inputs are finite; a program needn't handle non-finite values.
Results may differ from the reference program's by a relative error of at most 0.014.
Values may be sent and summed in bfloat16 or wider, within the bound.
No kernel may reach another device: no remote copies, remote signals or barrier semaphores. Data moves between devices by JAX's collectives and lax.ppermute only.
A program may use at most 192 MiB of HBM per device.

```python
import math
import jax
import jax.numpy as jnp
import numpy as np
from jax import lax

MODEL_WIDTH = 8192
OUTPUT_WIDTH = 4096
ADAPTER_RANK = 16
ADAPTER_COUNT = 512
CAP = 6
ROWS_DEV = 512
REQ_GROUPS = 4
NSEG = 12
MOSTLEN = 128
ROWS = 2048
N_TP = 4


def shared_order(key):
    return jax.random.permutation(jax.random.fold_in(key, 11), ADAPTER_COUNT).astype(jnp.int32)


def draw_adapter_pool_slot(key, part):
    return shared_order(key)


def draw_segment_adapter_ids(key, part):
    order = shared_order(key)
    holder = jnp.argsort(order).astype(jnp.int32)
    key = jax.random.fold_in(key, 5)
    per_owner = ADAPTER_COUNT // REQ_GROUPS

    def one_group(group_key):
        first_key, second_key, third_key, fourth_key = jax.random.split(group_key, 4)
        busiest = jax.random.randint(first_key, (), 0, REQ_GROUPS).astype(jnp.int32)
        others = (busiest + 1 + jnp.arange((REQ_GROUPS - 1) * CAP, dtype=jnp.int32) // CAP) % REQ_GROUPS
        others = jax.random.permutation(second_key, others)[:NSEG - CAP]
        owners = jnp.concatenate([jnp.full((CAP,), busiest, jnp.int32), others.astype(jnp.int32)])
        owners = jax.random.permutation(fourth_key, owners)
        local_ids = jax.random.randint(third_key, (NSEG,), 0, per_owner).astype(jnp.int32)
        return holder[owners * per_owner + local_ids]
    return jax.vmap(one_group)(jax.random.split(key, REQ_GROUPS)).astype(jnp.int32)


def level_of(own_key, shape, cuts, least, largest):
    loudness = 1.0
    for position, blocks in cuts:
        steps = jax.random.uniform(jax.random.fold_in(jax.random.fold_in(own_key, 6), position), (blocks,), jnp.float32, least / len(cuts), largest / len(cuts))
        loudness = loudness * jnp.repeat(jnp.exp(steps), shape[position] // blocks).reshape((-1,) + (1,) * (len(shape) - 1 - position))
    return loudness


def profile(amount, total, bound, skew):
    portions = [(1 << 20) // math.isqrt(standing ** skew) + 1 for standing in range(2, amount + 1)]
    spare, holding = total - bound - (amount - 1), [1] * (amount - 1)
    while spare > 0:
        candidates = [i for i in range(amount - 1) if holding[i] < bound]
        whole, left = sum([portions[i] for i in candidates]), spare
        for i in candidates:
            more = min(bound - holding[i], max(1, left * portions[i] // whole), spare)
            holding[i] = holding[i] + more
            spare = spare - more
    return np.array([bound] + holding)


def uneven(stream_key, number_of, total, bound, skew):
    if number_of == 2:
        one = jax.random.randint(stream_key, (), max(1, total - bound), min(bound, total - 1) + 1)
        return jnp.stack([one, total - one])
    sizes = jnp.asarray(profile(number_of, total, bound, skew), jnp.int32)
    twos = (number_of - 1) // 2
    source_of, sink = sizes[1:1 + 2 * twos:2], sizes[2:2 + 2 * twos:2]
    margin = jnp.minimum(source_of - 1, bound - sink)
    passed = jax.random.randint(jax.random.fold_in(stream_key, 1), (twos,), 0, 1 << 20) % (margin + 1)
    sizes = sizes.at[1:1 + 2 * twos:2].set(source_of - passed).at[2:2 + 2 * twos:2].set(sink + passed)
    return sizes[jax.random.permutation(jax.random.fold_in(stream_key, 2), number_of)]


def noise(stream_key, extent, scale, reach, cuts=(), kind=jnp.bfloat16):
    array = jax.random.normal(stream_key, extent, jnp.float32) * scale
    if len(cuts) > 0:
        array = level_of(stream_key, extent, cuts, -0.22, 0.18) * array
    return jnp.clip(array, min=-reach, max=reach).astype(kind)


def setup_inputs(seed: int = 0, part: int = 0) -> dict:
    splits = jax.random.split(jax.random.key(seed), 8)
    part_splits = jax.random.split(jax.random.fold_in(splits[7], part), 8)
    attention_rows = noise(part_splits[0], (ROWS, MODEL_WIDTH), 1.0, 6.0, ((0, 4), (1, 4)))
    output_weight_matrix = noise(splits[1], (MODEL_WIDTH, OUTPUT_WIDTH), MODEL_WIDTH ** -0.5, 0.0625, ((0, 4),))
    adapter_down_maps = noise(part_splits[2], (ADAPTER_COUNT, ADAPTER_RANK, MODEL_WIDTH), MODEL_WIDTH ** -0.5, 0.0625, ((0, 4), (2, 4)))
    adapter_up_maps = noise(part_splits[3], (ADAPTER_COUNT, ADAPTER_RANK, OUTPUT_WIDTH), ADAPTER_RANK ** -0.5, 1.5, ((0, 4), (2, 4)))
    adapter_pool_slot = draw_adapter_pool_slot(jax.random.fold_in(jax.random.fold_in(splits[7], part), 71), part)
    segment_adapter_ids = draw_segment_adapter_ids(jax.random.fold_in(jax.random.fold_in(splits[7], part), 71), part)
    segment_row_count = jax.vmap(lambda own: uneven(own, NSEG, ROWS_DEV, MOSTLEN, 2))(jax.random.split(part_splits[6], REQ_GROUPS)).reshape((REQ_GROUPS, NSEG)).astype(jnp.int32)
    return dict(attention_rows=attention_rows, output_weight_matrix=output_weight_matrix, adapter_down_maps=adapter_down_maps, adapter_up_maps=adapter_up_maps, adapter_pool_slot=adapter_pool_slot, segment_adapter_ids=segment_adapter_ids, segment_row_count=segment_row_count)


def reference(attention_rows, output_weight_matrix, adapter_down_maps, adapter_up_maps, adapter_pool_slot, segment_adapter_ids, segment_row_count):
    grouped = attention_rows.reshape(REQ_GROUPS, ROWS_DEV, MODEL_WIDTH)
    weights = output_weight_matrix.reshape(N_TP, MODEL_WIDTH // N_TP, OUTPUT_WIDTH).astype(jnp.float32)

    def one_group(packed):
        inputs, adapters, lengths = packed
        seg_ends = jnp.cumsum(lengths)
        row_segment = jnp.sum((seg_ends[None, :] <= jnp.arange(ROWS_DEV)[:, None]).astype(jnp.int32), axis=1).astype(jnp.int32)
        row_pool_slot = adapter_pool_slot[adapters[row_segment]]
        down_projected = adapter_down_maps[row_pool_slot].astype(jnp.float32)
        rank_reduced = jnp.einsum("id,ird->ir", inputs.astype(jnp.float32), down_projected).astype(jnp.bfloat16)
        up_projected = adapter_up_maps[row_pool_slot].astype(jnp.float32)
        adapter_term = jnp.einsum("bw,bwd->bd", rank_reduced.astype(jnp.float32), up_projected)
        shards = inputs.reshape(ROWS_DEV, N_TP, MODEL_WIDTH // N_TP).astype(jnp.float32)
        pieces = jnp.einsum("ikd,kdc->kic", shards, weights).astype(jnp.bfloat16).astype(jnp.float32)
        base_product = jnp.sum(pieces, axis=0)
        return (base_product + adapter_term).astype(jnp.bfloat16)

    mixed = lax.map(one_group, (grouped, segment_adapter_ids, segment_row_count))
    return mixed.reshape(ROWS, OUTPUT_WIDTH)
```

```python
import functools

import jax
import jax.numpy as jnp
from jax import lax
from jax.experimental import pallas as pl
from jax.experimental.pallas import tpu as pltpu
from jax.sharding import PartitionSpec as P

CAP = 6
CHUNKS = 2
VMEM_LIMIT = 48 * 1024 * 1024
F32 = jnp.float32
BF16 = jnp.bfloat16


def product_kernel(tile_ref, rows_ref, weight_ref, out_ref):
    out_ref[...] = jnp.dot(
        rows_ref[...], weight_ref[...], preferred_element_type=F32
    ).astype(out_ref.dtype)


def block_product(rows, weight, first_tile, width, tile):
    row_total, depth = rows.shape
    tiles = width // tile
    return pl.pallas_call(
        product_kernel,
        grid_spec=pltpu.PrefetchScalarGridSpec(
            num_scalar_prefetch=1,
            grid=(tiles,),
            in_specs=[
                pl.BlockSpec((row_total, depth), lambda j, t: (0, 0)),
                pl.BlockSpec((depth, tile), lambda j, t: (0, t[0] + j)),
            ],
            out_specs=pl.BlockSpec((row_total, tile), lambda j, t: (0, j)),
        ),
        out_shape=jax.ShapeDtypeStruct((row_total, width), BF16),
        compiler_params=pltpu.CompilerParams(vmem_limit_bytes=VMEM_LIMIT),
        cost_estimate=pl.CostEstimate(
            flops=2 * row_total * depth * width,
            bytes_accessed=2 * (row_total * depth + depth * width + row_total * width),
            transcendentals=0,
        ),
        name="block_product",
    )(first_tile.reshape(1), rows, weight)


def pick_kernel(me_ref, table_ref, ids_ref, lens_ref, down_ref, up_ref, *rest):
    peers = ids_ref.shape[0]
    segs = ids_ref.shape[1]
    share = down_ref.shape[0]
    downs, ups = rest[:peers], rest[peers : 2 * peers]
    start_ref, end_ref, pick_ref, sem = rest[2 * peers :]
    me = me_ref[0]

    def clear(q, carry):
        pick_ref[q] = 0
        start_ref[q] = 0
        end_ref[q] = 0
        return carry

    lax.fori_loop(0, peers * CAP, clear, 0)

    for k in range(peers):

        def choose(s, count):
            slot = table_ref[ids_ref[k, s]]
            local = slot - me * share
            mine = jnp.logical_and(local >= 0, local < share)

            @pl.when(jnp.logical_and(mine, count < CAP))
            def _():
                pick_ref[k * CAP + count] = local

            return count + mine.astype(jnp.int32)

        lax.fori_loop(0, segs, choose, 0)
        for c in range(CAP):
            source = pick_ref[k * CAP + c]
            pltpu.make_async_copy(down_ref.at[source], downs[k].at[c], sem).start()
            pltpu.make_async_copy(up_ref.at[source], ups[k].at[c], sem).start()

    for k in range(peers):
        owner = lax.rem(me + peers - k, peers)

        def place(s, carry):
            count, first = carry
            local = table_ref[ids_ref[0, s]] - owner * share
            theirs = jnp.logical_and(local >= 0, local < share)
            last = first + lens_ref[0, s]

            @pl.when(jnp.logical_and(theirs, count < CAP))
            def _():
                start_ref[k * CAP + count] = first
                end_ref[k * CAP + count] = last

            return count + theirs.astype(jnp.int32), last

        lax.fori_loop(0, segs, place, (0, 0))

    for k in range(peers):
        for c in range(CAP):
            pltpu.make_async_copy(down_ref.at[0], downs[k].at[c], sem).wait()
            pltpu.make_async_copy(up_ref.at[0], ups[k].at[c], sem).wait()


def pick_adapters(me, table, ids, lens, down, up):
    peers = ids.shape[0]
    _, rank, depth = down.shape
    cols = up.shape[2]
    smem = pl.BlockSpec(memory_space=pltpu.SMEM)
    hbm = pl.BlockSpec(memory_space=pl.ANY)
    out = pl.pallas_call(
        pick_kernel,
        in_specs=[smem, smem, smem, smem, hbm, hbm],
        out_specs=[hbm] * (2 * peers) + [smem, smem],
        out_shape=[jax.ShapeDtypeStruct((CAP, rank, depth), BF16)] * peers
        + [jax.ShapeDtypeStruct((CAP, rank, cols), BF16)] * peers
        + [jax.ShapeDtypeStruct((peers * CAP,), jnp.int32)] * 2,
        scratch_shapes=[pltpu.SMEM((peers * CAP,), jnp.int32), pltpu.SemaphoreType.DMA],
        cost_estimate=pl.CostEstimate(
            flops=0, bytes_accessed=4 * peers * CAP * rank * (depth + cols), transcendentals=0
        ),
        name="pick_adapters",
    )(me.reshape(1), table, ids, lens, down, up)
    return out[:peers], out[peers : 2 * peers], out[2 * peers], out[2 * peers + 1]


def low_kernel(start_ref, end_ref, rows_ref, *rest):
    downs, out_ref = rest[:-1], rest[-1]
    row_total = rows_ref.shape[0]
    rank = out_ref.shape[0]
    place = lax.broadcasted_iota(jnp.int32, (rank, row_total), 1)
    total = jnp.zeros((rank, row_total), F32)
    for k, down_ref in enumerate(downs):
        part = lax.dot_general(
            down_ref[...], rows_ref[...], (((1,), (1,)), ((), ())), preferred_element_type=F32
        )
        for c in range(CAP):
            q = k * CAP + c
            member = jnp.logical_and(place >= start_ref[q], place < end_ref[q])
            total = jnp.where(member, part[c * rank : (c + 1) * rank], total)
    out_ref[...] = total.astype(BF16)


def low_sums(starts, ends, rows, downs, rank):
    row_total, depth = rows.shape
    smem = pl.BlockSpec(memory_space=pltpu.SMEM)
    vmem = pl.BlockSpec(memory_space=pltpu.VMEM)
    return pl.pallas_call(
        low_kernel,
        in_specs=[smem, smem] + [vmem] * (1 + len(downs)),
        out_specs=vmem,
        out_shape=jax.ShapeDtypeStruct((rank, row_total), BF16),
        compiler_params=pltpu.CompilerParams(vmem_limit_bytes=VMEM_LIMIT),
        cost_estimate=pl.CostEstimate(
            flops=2 * row_total * depth * CAP * rank * len(downs),
            bytes_accessed=2 * depth * (row_total + CAP * rank * len(downs)),
            transcendentals=0,
        ),
        name="low_sums",
    )(starts, ends, rows, *[d.reshape(CAP * rank, depth) for d in downs])


def finish_kernel(lows, ups_total, own_total, start_ref, end_ref, *rest):
    low_refs = rest[:lows]
    up_refs = rest[lows : lows + ups_total]
    base_refs = rest[lows + ups_total : -1]
    out_ref = rest[-1]
    rank, row_total = low_refs[0].shape
    low = low_refs[0][...].astype(F32)
    for ref in low_refs[1:]:
        low = low + ref[...].astype(F32)
    low = low.astype(BF16).astype(F32)
    place = lax.broadcasted_iota(jnp.int32, (rank, row_total), 1)
    term = jnp.zeros(out_ref.shape, F32)
    for k, up_ref in enumerate(up_refs):
        spread = []
        for c in range(CAP):
            q = k * CAP + c
            member = jnp.logical_and(place >= start_ref[q], place < end_ref[q])
            spread.append(jnp.where(member, low, 0.0))
        spread = jnp.concatenate(spread, axis=0).astype(BF16)
        term = term + lax.dot_general(
            spread, up_ref[...], (((0,), (0,)), ((), ())), preferred_element_type=F32
        )
    width = base_refs[0].shape[1]
    for c in range(out_ref.shape[1] // width):
        cols = slice(c * width, (c + 1) * width)
        base = base_refs[c * own_total][...].astype(F32)
        for ref in base_refs[c * own_total + 1 : (c + 1) * own_total]:
            base = base + ref[...].astype(F32)
        out_ref[:, cols] = (base + term[:, cols]).astype(out_ref.dtype)


def finish(starts, ends, lows, ups, bases):
    rank, row_total = lows[0].shape
    cols = ups[0].shape[2]
    smem = pl.BlockSpec(memory_space=pltpu.SMEM)
    vmem = pl.BlockSpec(memory_space=pltpu.VMEM)
    flat = [b for chunk in bases for b in chunk]
    return pl.pallas_call(
        functools.partial(finish_kernel, len(lows), len(ups), len(bases[0])),
        in_specs=[smem, smem] + [vmem] * (len(lows) + len(ups) + len(flat)),
        out_specs=vmem,
        out_shape=jax.ShapeDtypeStruct((row_total, cols), BF16),
        compiler_params=pltpu.CompilerParams(vmem_limit_bytes=VMEM_LIMIT),
        cost_estimate=pl.CostEstimate(
            flops=2 * row_total * cols * CAP * rank * len(ups),
            bytes_accessed=2 * row_total * cols * 5,
            transcendentals=0,
        ),
        name="finish",
    )(starts, ends, *lows, *[u.reshape(CAP * rank, cols) for u in ups], *flat)


def add(a, b):
    return (a.astype(F32) + b.astype(F32)).astype(BF16)


def local(req_total, tp_total, rows, weight, down, up, table, ids, lens):
    rank = down.shape[1]
    cols = weight.shape[1] // tp_total
    width = cols // CHUNKS
    tile = min(256, width)
    me_req = lax.axis_index("req").astype(jnp.int32)
    me = lax.axis_index("tp").astype(jnp.int32)
    lower = me < tp_total // 2

    all_ids = [ids]
    for k in range(1, req_total):
        back = [((i + k) % req_total, i) for i in range(req_total)]
        all_ids.append(lax.ppermute(ids, "req", back))
    all_ids = jnp.concatenate(all_ids, axis=0)
    downs, ups, starts, ends = pick_adapters(me_req, table, all_ids, lens, down, up)
    held_down, held_up = [downs[0]], [ups[0]]
    for k in range(1, req_total):
        ahead = [(i, (i + k) % req_total) for i in range(req_total)]
        held_down.append(lax.ppermute(downs[k], "req", ahead))
    for k in range(1, req_total):
        ahead = [(i, (i + k) % req_total) for i in range(req_total)]
        held_up.append(lax.ppermute(ups[k], "req", ahead))

    def partial(block, chunk):
        first = (jnp.clip(block, 0, tp_total - 1) * cols + chunk * width) // tile
        return block_product(rows, weight, first, width, tile)

    arrived = [[] for _ in range(CHUNKS)]
    for step in range(tp_total - 1):
        ahead = tp_total - 1 - step
        for chunk in range(CHUNKS):
            near = partial(jnp.where(lower, me + ahead, me - ahead), chunk)
            far = None
            if 2 * ahead < tp_total:
                far = partial(jnp.where(lower, me - ahead, me + ahead), chunk)
            sent = []
            for k in range(step + 1):
                value = near if k < tp_total // 2 else far
                if k > 0:
                    value = add(value, arrived[chunk][k - 1])
                m = tp_total - 1 - k
                sent.append(lax.ppermute(value, "tp", [(k, k + 1), (m, m - 1)]))
            arrived[chunk] = sent

    low = low_sums(starts, ends, rows, held_down, rank)
    lows = [low]
    for k in range(1, tp_total):
        lows.append(lax.ppermute(low, "tp", [(i, (i + k) % tp_total) for i in range(tp_total)]))
    bases = [[partial(me, chunk)] + arrived[chunk] for chunk in range(CHUNKS)]
    return finish(starts, ends, lows, held_up, bases)


def solution(mesh):
    return jax.shard_map(
        functools.partial(local, mesh.shape["req"], mesh.shape["tp"]),
        mesh=mesh,
        in_specs=(
            P(("groups", "req"), "tp"),
            P("tp", None),
            P(("groups", "req"), None, "tp"),
            P(("groups", "req"), None, "tp"),
            P("groups"),
            P(("groups", "req"), None),
            P(("groups", "req"), None),
        ),
        out_specs=P(("groups", "req"), "tp"),
        check_vma=False,
    )
```

```python
import functools

import jax
import jax.numpy as jnp
from jax import lax
from jax.experimental import pallas as pl
from jax.experimental.pallas import tpu as pltpu
from jax.sharding import PartitionSpec as P

CAP = 6
PIECES = 2
VMEM_LIMIT = 48 * 1024 * 1024
F32 = jnp.float32
BF16 = jnp.bfloat16


def product_kernel(rows_ref, weight_ref, ids_ref, out_ref, ids_out_ref):
    out_ref[0] = jnp.dot(
        rows_ref[...], weight_ref[...], preferred_element_type=F32
    ).astype(out_ref.dtype)

    @pl.when(jnp.logical_and(pl.program_id(0) == 0, pl.program_id(1) == 0))
    def _():
        for s in range(ids_ref.shape[1]):
            ids_out_ref[0, s] = ids_ref[0, s]


def base_piece(rows, weight, ids, blocks, piece, pieces, tile):
    row_total, depth = rows.shape
    cols = weight.shape[1] // blocks
    width = cols // pieces
    tiles = width // tile
    return pl.pallas_call(
        product_kernel,
        grid=(blocks, tiles),
        in_specs=[
            pl.BlockSpec((row_total, depth), lambda d, j: (0, 0)),
            pl.BlockSpec((depth, tile), lambda d, j: (0, (d * pieces + piece) * tiles + j)),
            pl.BlockSpec(memory_space=pltpu.SMEM),
        ],
        out_specs=[
            pl.BlockSpec((1, row_total, tile), lambda d, j: (d, 0, j)),
            pl.BlockSpec(memory_space=pltpu.SMEM),
        ],
        out_shape=[
            jax.ShapeDtypeStruct((blocks, row_total, width), BF16),
            jax.ShapeDtypeStruct(ids.shape, ids.dtype),
        ],
        compiler_params=pltpu.CompilerParams(vmem_limit_bytes=VMEM_LIMIT),
        cost_estimate=pl.CostEstimate(
            flops=2 * row_total * depth * width * blocks,
            bytes_accessed=2 * (row_total * depth + (depth + row_total) * width * blocks),
            transcendentals=0,
        ),
        name="base_piece",
    )(rows, weight, ids)


def pick_kernel(peers, me_ref, table_ref, lens_ref, *rest):
    ids_refs = rest[:peers]
    down_ref, up_ref = rest[peers : peers + 2]
    packs = rest[peers + 2 : 2 * peers + 2]
    start_ref, end_ref, pick_ref, sem = rest[2 * peers + 2 :]
    segs = lens_ref.shape[1]
    share, _, depth = down_ref.shape
    cols = up_ref.shape[2]
    me = me_ref[0]

    def clear(q, carry):
        pick_ref[q] = 0
        start_ref[q] = 0
        end_ref[q] = 0
        return carry

    lax.fori_loop(0, peers * CAP, clear, 0)

    def copies(k, c, source):
        return (
            pltpu.make_async_copy(down_ref.at[source], packs[k].at[c, :, pl.ds(0, depth)], sem),
            pltpu.make_async_copy(up_ref.at[source], packs[k].at[c, :, pl.ds(depth, cols)], sem),
        )

    for k in range(peers):

        def choose(s, count):
            local = table_ref[ids_refs[k][0, s]] - me * share
            mine = jnp.logical_and(local >= 0, local < share)

            @pl.when(jnp.logical_and(mine, count < CAP))
            def _():
                pick_ref[k * CAP + count] = local

            return count + mine.astype(jnp.int32)

        lax.fori_loop(0, segs, choose, 0)
        for c in range(CAP):
            for copy in copies(k, c, pick_ref[k * CAP + c]):
                copy.start()

    for k in range(peers):
        owner = lax.rem(me + peers - k, peers)

        def place(s, carry):
            count, first = carry
            local = table_ref[ids_refs[0][0, s]] - owner * share
            theirs = jnp.logical_and(local >= 0, local < share)
            last = first + lens_ref[0, s]

            @pl.when(jnp.logical_and(theirs, count < CAP))
            def _():
                start_ref[k * CAP + count] = first
                end_ref[k * CAP + count] = last

            return count + theirs.astype(jnp.int32), last

        lax.fori_loop(0, segs, place, (0, 0))

    for k in range(peers):
        for c in range(CAP):
            for copy in copies(k, c, 0):
                copy.wait()


def pick_adapters(me, table, all_ids, lens, down, up):
    peers = len(all_ids)
    _, rank, depth = down.shape
    cols = up.shape[2]
    smem = pl.BlockSpec(memory_space=pltpu.SMEM)
    vmem = pl.BlockSpec(memory_space=pltpu.VMEM)
    hbm = pl.BlockSpec(memory_space=pl.ANY)
    out = pl.pallas_call(
        functools.partial(pick_kernel, peers),
        in_specs=[smem] * (3 + peers) + [hbm, hbm],
        out_specs=[vmem] * peers + [smem, smem],
        out_shape=[jax.ShapeDtypeStruct((CAP, rank, depth + cols), BF16)] * peers
        + [jax.ShapeDtypeStruct((peers * CAP,), jnp.int32)] * 2,
        scratch_shapes=[pltpu.SMEM((peers * CAP,), jnp.int32), pltpu.SemaphoreType.DMA],
        compiler_params=pltpu.CompilerParams(vmem_limit_bytes=VMEM_LIMIT),
        cost_estimate=pl.CostEstimate(
            flops=0, bytes_accessed=4 * peers * CAP * rank * (depth + cols), transcendentals=0
        ),
        name="pick_adapters",
    )(me.reshape(1), table, lens, *all_ids, down, up)
    return out[:peers], out[peers], out[peers + 1]


def low_kernel(start_ref, end_ref, rows_ref, *rest):
    packs, out_ref = rest[:-1], rest[-1]
    row_total, depth = rows_ref.shape
    rank = out_ref.shape[0]
    place = lax.broadcasted_iota(jnp.int32, (rank, row_total), 1)
    total = jnp.zeros((rank, row_total), F32)
    for k, pack_ref in enumerate(packs):
        part = lax.dot_general(
            pack_ref[:, :, :depth].reshape(CAP * rank, depth),
            rows_ref[...],
            (((1,), (1,)), ((), ())),
            preferred_element_type=F32,
        )
        for c in range(CAP):
            q = k * CAP + c
            member = jnp.logical_and(place >= start_ref[q], place < end_ref[q])
            total = jnp.where(member, part[c * rank : (c + 1) * rank], total)
    out_ref[...] = total.astype(BF16)


def low_sums(starts, ends, rows, packs, rank):
    row_total, depth = rows.shape
    smem = pl.BlockSpec(memory_space=pltpu.SMEM)
    vmem = pl.BlockSpec(memory_space=pltpu.VMEM)
    return pl.pallas_call(
        low_kernel,
        in_specs=[smem, smem] + [vmem] * (1 + len(packs)),
        out_specs=vmem,
        out_shape=jax.ShapeDtypeStruct((rank, row_total), BF16),
        compiler_params=pltpu.CompilerParams(vmem_limit_bytes=VMEM_LIMIT),
        cost_estimate=pl.CostEstimate(
            flops=2 * row_total * depth * CAP * rank * len(packs),
            bytes_accessed=2 * depth * (row_total + CAP * rank * len(packs)),
            transcendentals=0,
        ),
        name="low_sums",
    )(starts, ends, rows, *packs)


def term_kernel(lows, start_ref, end_ref, *rest):
    low_refs, pack_refs, out_ref = rest[:lows], rest[lows:-1], rest[-1]
    rank, row_total = low_refs[0].shape
    cols = out_ref.shape[1]
    low = low_refs[0][...].astype(F32)
    for ref in low_refs[1:]:
        low = low + ref[...].astype(F32)
    low = low.astype(BF16).astype(F32)
    place = lax.broadcasted_iota(jnp.int32, (rank, row_total), 1)
    term = jnp.zeros(out_ref.shape, F32)
    for k, pack_ref in enumerate(pack_refs):
        spread = []
        for c in range(CAP):
            q = k * CAP + c
            member = jnp.logical_and(place >= start_ref[q], place < end_ref[q])
            spread.append(jnp.where(member, low, 0.0))
        spread = jnp.concatenate(spread, axis=0).astype(BF16)
        ups = pack_ref[:, :, pack_ref.shape[2] - cols :].reshape(CAP * rank, cols)
        term = term + lax.dot_general(
            spread, ups, (((0,), (0,)), ((), ())), preferred_element_type=F32
        )
    out_ref[...] = term


def adapter_term(starts, ends, lows, packs, cols):
    rank, row_total = lows[0].shape
    smem = pl.BlockSpec(memory_space=pltpu.SMEM)
    vmem = pl.BlockSpec(memory_space=pltpu.VMEM)
    return pl.pallas_call(
        functools.partial(term_kernel, len(lows)),
        in_specs=[smem, smem] + [vmem] * (len(lows) + len(packs)),
        out_specs=vmem,
        out_shape=jax.ShapeDtypeStruct((row_total, cols), F32),
        compiler_params=pltpu.CompilerParams(vmem_limit_bytes=VMEM_LIMIT),
        cost_estimate=pl.CostEstimate(
            flops=2 * row_total * cols * CAP * rank * len(packs),
            bytes_accessed=4 * row_total * cols,
            transcendentals=0,
        ),
        name="adapter_term",
    )(starts, ends, *lows, *packs)


def finish_kernel(term_ref, *rest):
    base_refs, out_ref = rest[:-1], rest[-1]
    width = base_refs[0].shape[1]
    for p, ref in enumerate(base_refs):
        cols = slice(p * width, (p + 1) * width)
        out_ref[:, cols] = (ref[...].astype(F32) + term_ref[:, cols]).astype(out_ref.dtype)


def finish(term, bases):
    row_total, cols = term.shape
    height = min(row_total, 128)
    return pl.pallas_call(
        finish_kernel,
        grid=(row_total // height,),
        in_specs=[pl.BlockSpec((height, cols), lambda i: (i, 0))]
        + [pl.BlockSpec((height, b.shape[1]), lambda i: (i, 0)) for b in bases],
        out_specs=pl.BlockSpec((height, cols), lambda i: (i, 0)),
        out_shape=jax.ShapeDtypeStruct((row_total, cols), BF16),
        compiler_params=pltpu.CompilerParams(vmem_limit_bytes=VMEM_LIMIT),
        cost_estimate=pl.CostEstimate(
            flops=row_total * cols, bytes_accessed=8 * row_total * cols, transcendentals=0
        ),
        name="finish",
    )(term, *bases)


def local(req_total, tp_total, rows, weight, down, up, table, ids, lens):
    rank = down.shape[1]
    cols = up.shape[2]
    tile = min(256, cols // PIECES)
    me_req = lax.axis_index("req").astype(jnp.int32)

    bases = []
    for piece in range(PIECES):
        product, ids = base_piece(rows, weight, ids, tp_total, piece, PIECES, tile)
        if piece == 0:
            first_ids = ids
        bases.append(lax.psum_scatter(product, "tp", scatter_dimension=0, tiled=False))

    all_ids = [first_ids]
    for k in range(1, req_total):
        back = [((i + k) % req_total, i) for i in range(req_total)]
        all_ids.append(lax.ppermute(first_ids, "req", back))
    packs, starts, ends = pick_adapters(me_req, table, all_ids, lens, down, up)
    held = [packs[0]]
    for k in range(1, req_total):
        ahead = [(i, (i + k) % req_total) for i in range(req_total)]
        held.append(lax.ppermute(packs[k], "req", ahead))

    low = low_sums(starts, ends, rows, held, rank)
    lows = [low]
    for k in range(1, tp_total):
        lows.append(lax.ppermute(low, "tp", [(i, (i + k) % tp_total) for i in range(tp_total)]))
    term = adapter_term(starts, ends, lows, held, cols)
    return finish(term, bases)


def solution(mesh):
    return jax.shard_map(
        functools.partial(local, mesh.shape["req"], mesh.shape["tp"]),
        mesh=mesh,
        in_specs=(
            P(("groups", "req"), "tp"),
            P("tp", None),
            P(("groups", "req"), None, "tp"),
            P(("groups", "req"), None, "tp"),
            P("groups"),
            P(("groups", "req"), None),
            P(("groups", "req"), None),
        ),
        out_specs=P(("groups", "req"), "tp"),
        check_vma=False,
    )
```

```python
import functools

import jax
import jax.numpy as jnp
from jax import lax
from jax.experimental import pallas as pl
from jax.experimental.pallas import tpu as pltpu
from jax.sharding import PartitionSpec as P

CAP = 6
PIECES = 2
VMEM_LIMIT = 48 * 1024 * 1024
F32 = jnp.float32
BF16 = jnp.bfloat16
SMALL = pl.CostEstimate(flops=1000, bytes_accessed=1000, transcendentals=0)


def product_kernel(tile_ref, rows_ref, weight_ref, *rest):
    out_ref = rest[-1]
    out_ref[...] = jnp.dot(
        rows_ref[...], weight_ref[...], preferred_element_type=F32
    ).astype(out_ref.dtype)


def block_product(rows, weight, first, width, after=()):
    row_total, depth = rows.shape
    tile = min(256, width)
    return pl.pallas_call(
        product_kernel,
        grid_spec=pltpu.PrefetchScalarGridSpec(
            num_scalar_prefetch=1,
            grid=(width // tile,),
            in_specs=[
                pl.BlockSpec((row_total, depth), lambda j, t: (0, 0)),
                pl.BlockSpec((depth, tile), lambda j, t: (0, t[0] + j)),
            ]
            + [pl.BlockSpec(memory_space=pl.ANY)] * len(after),
            out_specs=pl.BlockSpec((row_total, tile), lambda j, t: (0, j)),
        ),
        out_shape=jax.ShapeDtypeStruct((row_total, width), BF16),
        compiler_params=pltpu.CompilerParams(vmem_limit_bytes=VMEM_LIMIT),
        cost_estimate=SMALL,
        name="block_product",
    )((first // tile).reshape(1), rows, weight, *after)


def pick_kernel(peers, me_ref, table_ref, lens_ref, *rest):
    ids_refs = rest[:peers]
    down_ref, up_ref = rest[peers : peers + 2]
    near_ref, away_ref, start_ref, end_ref, pick_ref, sem = rest[peers + 2 :]
    segs = lens_ref.shape[1]
    share, _, depth = down_ref.shape
    cols = up_ref.shape[2]
    half = near_ref.shape[0]
    me = me_ref[0]

    def clear(q, carry):
        pick_ref[q] = 0
        start_ref[q] = 0
        end_ref[q] = 0
        return carry

    lax.fori_loop(0, peers * CAP, clear, 0)

    def copies(x, c, source):
        pack = near_ref.at[x, c] if x < half else away_ref.at[x - half, c]
        return (
            pltpu.make_async_copy(down_ref.at[source], pack.at[:, pl.ds(0, depth)], sem),
            pltpu.make_async_copy(up_ref.at[source], pack.at[:, pl.ds(depth, cols)], sem),
        )

    for x in reversed(range(peers)):

        def choose(s, count):
            local = table_ref[ids_refs[x][0, s]] - me * share
            mine = jnp.logical_and(local >= 0, local < share)

            @pl.when(jnp.logical_and(mine, count < CAP))
            def _():
                pick_ref[x * CAP + count] = local

            return count + mine.astype(jnp.int32)

        lax.fori_loop(0, segs, choose, 0)
        for c in range(CAP):
            for copy in copies(x, c, pick_ref[x * CAP + c]):
                copy.start()

    for x in range(peers):
        owner = lax.bitwise_xor(me, jnp.int32(x))

        def place(s, carry):
            count, first = carry
            local = table_ref[ids_refs[0][0, s]] - owner * share
            theirs = jnp.logical_and(local >= 0, local < share)
            last = first + lens_ref[0, s]

            @pl.when(jnp.logical_and(theirs, count < CAP))
            def _():
                start_ref[x * CAP + count] = first
                end_ref[x * CAP + count] = last

            return count + theirs.astype(jnp.int32), last

        lax.fori_loop(0, segs, place, (0, 0))

    for x in range(peers):
        for c in range(CAP):
            for copy in copies(x, c, 0):
                copy.wait()


def pick_adapters(me, table, all_ids, lens, down, up):
    peers = len(all_ids)
    _, rank, depth = down.shape
    cols = up.shape[2]
    smem = pl.BlockSpec(memory_space=pltpu.SMEM)
    vmem = pl.BlockSpec(memory_space=pltpu.VMEM)
    hbm = pl.BlockSpec(memory_space=pl.ANY)
    return pl.pallas_call(
        functools.partial(pick_kernel, peers),
        in_specs=[smem] * (3 + peers) + [hbm, hbm],
        out_specs=[vmem] * 2 + [smem, smem],
        out_shape=[jax.ShapeDtypeStruct((peers // 2, CAP, rank, depth + cols), BF16)] * 2
        + [jax.ShapeDtypeStruct((peers * CAP,), jnp.int32)] * 2,
        scratch_shapes=[pltpu.SMEM((peers * CAP,), jnp.int32), pltpu.SemaphoreType.DMA],
        compiler_params=pltpu.CompilerParams(vmem_limit_bytes=VMEM_LIMIT),
        cost_estimate=SMALL,
        name="pick_adapters",
    )(me.reshape(1), table, lens, *all_ids, down, up)


def exchange(near, away, peers):
    half = peers // 2
    held = {x: [(0, near if x < half else away, x % half)] for x in range(peers)}
    bit = half
    while bit:
        leaving = [(x, *entry) for x in sorted(held) if x & bit for entry in held.pop(x)]
        if bit == half:
            packed = away
        else:
            packed = jnp.stack([array[place] for _, _, array, place in leaving])
        came = lax.ppermute(packed, "req", [(i, i ^ bit) for i in range(peers)])
        for place, (x, origin, _, _) in enumerate(leaving):
            held[x ^ bit].append((origin ^ bit, came, place))
        bit //= 2
    return [(array, place) for _, array, place in sorted(held[0], key=lambda e: e[0])]


def pack_spec(pack, first, width):
    array, place = pack
    block = (1,) + array.shape[1:3] + (width,)
    return pl.BlockSpec(block, lambda i: (place, 0, 0, first // width))


def low_kernel(start_ref, end_ref, rows_ref, *rest):
    down_refs, out_ref = rest[:-1], rest[-1]
    row_total, depth = rows_ref.shape
    rank = out_ref.shape[0]
    place = lax.broadcasted_iota(jnp.int32, (rank, row_total), 1)
    total = jnp.zeros((rank, row_total), F32)
    for x, down_ref in enumerate(down_refs):
        part = lax.dot_general(
            down_ref[...].reshape(CAP * rank, depth),
            rows_ref[...],
            (((1,), (1,)), ((), ())),
            preferred_element_type=F32,
        )
        for c in range(CAP):
            q = x * CAP + c
            member = jnp.logical_and(place >= start_ref[q], place < end_ref[q])
            total = jnp.where(member, part[c * rank : (c + 1) * rank], total)
    out_ref[...] = total


def low_sums(starts, ends, rows, packs, rank):
    row_total, depth = rows.shape
    smem = pl.BlockSpec(memory_space=pltpu.SMEM)
    vmem = pl.BlockSpec(memory_space=pltpu.VMEM)
    return pl.pallas_call(
        low_kernel,
        grid=(1,),
        in_specs=[smem, smem, vmem] + [pack_spec(p, 0, depth) for p in packs],
        out_specs=vmem,
        out_shape=jax.ShapeDtypeStruct((rank, row_total), F32),
        compiler_params=pltpu.CompilerParams(vmem_limit_bytes=VMEM_LIMIT),
        cost_estimate=SMALL,
        name="low_sums",
    )(starts, ends, rows, *[array for array, _ in packs])


def term_kernel(start_ref, end_ref, low_ref, came_ref, *rest):
    up_refs, out_ref = rest[:-1], rest[-1]
    rank, row_total = low_ref.shape
    cols = out_ref.shape[1]
    low = (low_ref[...] + came_ref[...]).astype(BF16).astype(F32)
    place = lax.broadcasted_iota(jnp.int32, (rank, row_total), 1)
    term = jnp.zeros(out_ref.shape, F32)
    for x, up_ref in enumerate(up_refs):
        spread = []
        for c in range(CAP):
            q = x * CAP + c
            member = jnp.logical_and(place >= start_ref[q], place < end_ref[q])
            spread.append(jnp.where(member, low, 0.0))
        spread = jnp.concatenate(spread, axis=0).astype(BF16)
        term = term + lax.dot_general(
            spread,
            up_ref[...].reshape(CAP * rank, cols),
            (((0,), (0,)), ((), ())),
            preferred_element_type=F32,
        )
    out_ref[...] = term


def adapter_term(starts, ends, low, came, packs, cols):
    _, row_total = low.shape
    smem = pl.BlockSpec(memory_space=pltpu.SMEM)
    vmem = pl.BlockSpec(memory_space=pltpu.VMEM)
    depth = packs[0][0].shape[3] - cols
    return pl.pallas_call(
        term_kernel,
        grid=(1,),
        in_specs=[smem, smem, vmem, vmem] + [pack_spec(p, depth, cols) for p in packs],
        out_specs=vmem,
        out_shape=jax.ShapeDtypeStruct((row_total, cols), F32),
        compiler_params=pltpu.CompilerParams(vmem_limit_bytes=VMEM_LIMIT),
        cost_estimate=SMALL,
        name="adapter_term",
    )(starts, ends, low, came, *[array for array, _ in packs])


def finish_kernel(pieces, term_ref, *rest):
    base_refs, out_ref = rest[:-1], rest[-1]
    parts = len(base_refs) // pieces
    width = base_refs[0].shape[1]
    for p in range(pieces):
        cols = slice(p * width, (p + 1) * width)
        total = base_refs[p * parts][...].astype(F32)
        for ref in base_refs[p * parts + 1 : (p + 1) * parts]:
            total = total + ref[...].astype(F32)
        out_ref[:, cols] = (total + term_ref[:, cols]).astype(out_ref.dtype)


def finish(term, bases):
    row_total, cols = term.shape
    height = min(row_total, 128)
    flat = [b for piece in bases for b in piece]
    return pl.pallas_call(
        functools.partial(finish_kernel, len(bases)),
        grid=(row_total // height,),
        in_specs=[pl.BlockSpec((height, cols), lambda i: (i, 0))]
        + [pl.BlockSpec((height, b.shape[1]), lambda i: (i, 0)) for b in flat],
        out_specs=pl.BlockSpec((height, cols), lambda i: (i, 0)),
        out_shape=jax.ShapeDtypeStruct((row_total, cols), BF16),
        compiler_params=pltpu.CompilerParams(vmem_limit_bytes=VMEM_LIMIT),
        cost_estimate=SMALL,
        name="finish",
    )(term, *flat)


def chain_steps(total):
    steps = []
    for t in range(total - 1):
        ahead = total - 1 - t
        moves = [(i, i + 1, i + ahead) for i in range(t + 1)]
        moves += [(total - 1 - i, total - 2 - i, total - 1 - i - ahead) for i in range(t + 1)]
        moves.sort(key=lambda m: min(m[0], total - 1 - m[0]))
        permutes = []
        for move in moves:
            for permute in permutes:
                if all(move[0] != m[0] and move[1] != m[1] for m in permute):
                    permute.append(move)
                    break
            else:
                permutes.append([move])
        operands = []
        for permute in permutes:
            sources = {m[0] for m in permute}
            for operand in operands:
                if not any(m[0] in sources for other in operand for m in other):
                    operand.append(permute)
                    break
            else:
                operands.append([permute])
        steps.append(operands)
    return steps


def by_device(me, values, other):
    result = other
    for device, value in values.items():
        result = jnp.where(me == device, value, result)
    return result


def add(a, *others):
    total = a.astype(F32)
    for other in others:
        total = total + other.astype(F32)
    return total.astype(BF16)


def local(req_total, tp_total, rows, weight, down, up, table, ids, lens):
    rank = down.shape[1]
    cols = up.shape[2]
    width = cols // PIECES
    me_req = lax.axis_index("req").astype(jnp.int32)
    me = lax.axis_index("tp").astype(jnp.int32)

    def partial(block, piece, after=()):
        return block_product(rows, weight, block * cols + piece * width, width, after)

    steps = chain_steps(tp_total)
    arrived = [[] for _ in range(PIECES)]
    order = ()
    for t, operands in enumerate(steps):
        moves = [[m for permute in operand for m in permute] for operand in operands]
        products = [
            [
                partial(by_device(me, {m[0]: m[2] for m in operand}, me), piece, order)
                for operand in moves
            ]
            for piece in range(PIECES)
        ]
        before = [permute for operand in steps[t - 1] for permute in operand] if t else []
        for piece in range(PIECES):
            came = []
            for operand, product in enumerate(products[piece]):
                addends = []
                for number, permute in enumerate(before):
                    needed = {
                        m[0]
                        for m in moves[operand]
                        for b in permute
                        if b[1] == m[0] and b[0] - b[1] == m[0] - m[1]
                    }
                    received = {m[0] for m in moves[operand] for b in permute if b[1] == m[0]}
                    if needed:
                        addend = arrived[piece][number]
                        if needed != received:
                            inside = by_device(me, {d: True for d in needed}, False)
                            addend = jnp.where(inside, addend, jnp.zeros_like(addend))
                        addends.append(addend)
                value = add(product, *addends) if addends else product
                for permute in operands[operand]:
                    came.append(lax.ppermute(value, "tp", [(m[0], m[1]) for m in permute]))
                last = value
            arrived[piece] = came
        order = (last,)
    bases = [[partial(me, piece, order)] + arrived[piece] for piece in range(PIECES)]

    all_ids = [ids]
    for x in range(1, req_total):
        all_ids.append(lax.ppermute(ids, "req", [(i, i ^ x) for i in range(req_total)]))
    near, away, starts, ends = pick_adapters(me_req, table, all_ids, lens, down, up)
    packs = exchange(near, away, req_total)

    low = low_sums(starts, ends, rows, packs, rank)
    bit = 1
    while 2 * bit < tp_total:
        low = low + lax.ppermute(low, "tp", [(i, i ^ bit) for i in range(tp_total)])
        bit *= 2
    came = lax.ppermute(low, "tp", [(i, i ^ bit) for i in range(tp_total)])
    term = adapter_term(starts, ends, low, came, packs, cols)
    return finish(term, bases)


def solution(mesh):
    return jax.shard_map(
        functools.partial(local, mesh.shape["req"], mesh.shape["tp"]),
        mesh=mesh,
        in_specs=(
            P(("groups", "req"), "tp"),
            P("tp", None),
            P(("groups", "req"), None, "tp"),
            P(("groups", "req"), None, "tp"),
            P("groups"),
            P(("groups", "req"), None),
            P(("groups", "req"), None),
        ),
        out_specs=P(("groups", "req"), "tp"),
        check_vma=False,
    )
```

```python
import functools

import jax
import jax.numpy as jnp
from jax import lax
from jax.experimental import pallas as pl
from jax.experimental.pallas import tpu as pltpu
from jax.sharding import PartitionSpec as P

CAP = 6
PIECES = 2
VMEM_LIMIT = 48 * 1024 * 1024
F32 = jnp.float32
BF16 = jnp.bfloat16
SMALL = pl.CostEstimate(flops=1000, bytes_accessed=1000, transcendentals=0)


def product_kernel(tile, addends, afters, first_call, first_ref, rows_ref, weight_ref, *rest):
    addend_refs, rest = rest[:addends], rest[addends + afters :]
    if first_call:
        ids_ref, out_ref, ids_out_ref, tiles_ref, tile_sems, held_ref, held_sem = rest
    else:
        out_ref, tiles_ref, tile_sems = rest
    tiles = out_ref.shape[1] // tile
    first = first_ref[0]

    def weight_copy(j):
        columns = pl.ds(pl.multiple_of(first + j * tile, 128), tile)
        return pltpu.make_async_copy(
            weight_ref.at[:, columns], tiles_ref.at[j], tile_sems.at[j]
        )

    if first_call:
        rows_copy = pltpu.make_async_copy(rows_ref, held_ref, held_sem)
        rows_copy.start()
    for j in range(tiles):
        weight_copy(j).start()
    if first_call:
        for s in range(ids_ref.shape[1]):
            ids_out_ref[0, s] = ids_ref[0, s]
        rows_copy.wait()
        rows_ref = held_ref
    for j in range(tiles):
        weight_copy(j).wait()
        columns = slice(j * tile, (j + 1) * tile)
        total = jnp.dot(rows_ref[...], tiles_ref[j], preferred_element_type=F32)
        for ref in addend_refs:
            total = total + ref[:, columns].astype(F32)
        out_ref[:, columns] = total.astype(out_ref.dtype)


def block_product(rows, weight, first, width, addends=(), after=(), ids=None):
    row_total, depth = rows.shape
    tile = min(256, width)
    first_call = ids is not None
    smem = pl.BlockSpec(memory_space=pltpu.SMEM)
    vmem = pl.BlockSpec(memory_space=pltpu.VMEM)
    hbm = pl.BlockSpec(memory_space=pl.ANY)
    out_specs, out_shape = [vmem], [jax.ShapeDtypeStruct((row_total, width), BF16)]
    scratch = [
        pltpu.VMEM((width // tile, depth, tile), BF16),
        pltpu.SemaphoreType.DMA((width // tile,)),
    ]
    if first_call:
        out_specs.append(smem)
        out_shape.append(jax.ShapeDtypeStruct(ids.shape, ids.dtype))
        scratch += [pltpu.VMEM((row_total, depth), BF16), pltpu.SemaphoreType.DMA]
    out = pl.pallas_call(
        functools.partial(product_kernel, tile, len(addends), len(after), first_call),
        in_specs=[smem, hbm if first_call else vmem, hbm]
        + [vmem] * len(addends)
        + [hbm] * len(after)
        + [smem] * first_call,
        out_specs=out_specs,
        out_shape=out_shape,
        scratch_shapes=scratch,
        compiler_params=pltpu.CompilerParams(vmem_limit_bytes=VMEM_LIMIT),
        cost_estimate=SMALL,
        name="block_product",
    )(first.reshape(1), rows, weight, *addends, *after, *([ids] if first_call else []))
    return out if first_call else out[0]


def pick_kernel(peers, afters, me_ref, table_ref, lens_ref, *rest):
    ids_refs = rest[:peers]
    down_ref, up_ref = rest[peers : peers + 2]
    rest = rest[peers + 2 + afters :]
    packs, (start_ref, end_ref, pick_ref, sem) = rest[:peers], rest[peers:]
    segs = lens_ref.shape[1]
    share, _, depth = down_ref.shape
    cols = up_ref.shape[2]
    me = me_ref[0]

    def clear(q, carry):
        pick_ref[q] = 0
        start_ref[q] = 0
        end_ref[q] = 0
        return carry

    lax.fori_loop(0, peers * CAP, clear, 0)

    def copies(x, c, source):
        pack = packs[x].at[c]
        return (
            pltpu.make_async_copy(down_ref.at[source], pack.at[:, pl.ds(0, depth)], sem),
            pltpu.make_async_copy(up_ref.at[source], pack.at[:, pl.ds(depth, cols)], sem),
        )

    for x in reversed(range(peers)):

        def choose(s, count):
            local = table_ref[ids_refs[x][0, s]] - me * share
            mine = jnp.logical_and(local >= 0, local < share)

            @pl.when(jnp.logical_and(mine, count < CAP))
            def _():
                pick_ref[x * CAP + count] = local

            return count + mine.astype(jnp.int32)

        lax.fori_loop(0, segs, choose, 0)
        for c in range(CAP):
            for copy in copies(x, c, pick_ref[x * CAP + c]):
                copy.start()

    for x in range(peers):
        owner = lax.bitwise_xor(me, jnp.int32(x))

        def place(s, carry):
            count, first = carry
            local = table_ref[ids_refs[0][0, s]] - owner * share
            theirs = jnp.logical_and(local >= 0, local < share)
            last = first + lens_ref[0, s]

            @pl.when(jnp.logical_and(theirs, count < CAP))
            def _():
                start_ref[x * CAP + count] = first
                end_ref[x * CAP + count] = last

            return count + theirs.astype(jnp.int32), last

        lax.fori_loop(0, segs, place, (0, 0))

    for x in range(peers):
        for c in range(CAP):
            for copy in copies(x, c, 0):
                copy.wait()


def pick_adapters(me, table, all_ids, lens, down, up, after):
    peers = len(all_ids)
    _, rank, depth = down.shape
    cols = up.shape[2]
    smem = pl.BlockSpec(memory_space=pltpu.SMEM)
    vmem = pl.BlockSpec(memory_space=pltpu.VMEM)
    hbm = pl.BlockSpec(memory_space=pl.ANY)
    out = pl.pallas_call(
        functools.partial(pick_kernel, peers, len(after)),
        in_specs=[smem] * (3 + peers) + [hbm] * (2 + len(after)),
        out_specs=[vmem] * peers + [smem, smem],
        out_shape=[jax.ShapeDtypeStruct((CAP, rank, depth + cols), BF16)] * peers
        + [jax.ShapeDtypeStruct((peers * CAP,), jnp.int32)] * 2,
        scratch_shapes=[pltpu.SMEM((peers * CAP,), jnp.int32), pltpu.SemaphoreType.DMA],
        compiler_params=pltpu.CompilerParams(vmem_limit_bytes=VMEM_LIMIT),
        cost_estimate=SMALL,
        name="pick_adapters",
    )(me.reshape(1), table, lens, *all_ids, down, up, *after)
    return list(out[:-2]), out[-2], out[-1]


def pack_spec(pack, first, width):
    return pl.BlockSpec(pack.shape[:2] + (width,), lambda i: (0, 0, first // width))


def low_kernel(peers, start_ref, end_ref, rows_ref, *rest):
    down_refs, out_ref = rest[:peers], rest[-1]
    row_total, depth = rows_ref.shape
    rank = out_ref.shape[0]
    place = lax.broadcasted_iota(jnp.int32, (rank, row_total), 1)
    total = jnp.zeros((rank, row_total), F32)
    for x, down_ref in enumerate(down_refs):
        part = lax.dot_general(
            down_ref[...].reshape(CAP * rank, depth),
            rows_ref[...],
            (((1,), (1,)), ((), ())),
            preferred_element_type=F32,
        )
        for c in range(CAP):
            q = x * CAP + c
            member = jnp.logical_and(place >= start_ref[q], place < end_ref[q])
            total = jnp.where(member, part[c * rank : (c + 1) * rank], total)
    out_ref[...] = total


def low_sums(starts, ends, rows, packs, rank, after):
    row_total, depth = rows.shape
    smem = pl.BlockSpec(memory_space=pltpu.SMEM)
    vmem = pl.BlockSpec(memory_space=pltpu.VMEM)
    return pl.pallas_call(
        functools.partial(low_kernel, len(packs)),
        grid=(1,),
        in_specs=[smem, smem, vmem]
        + [pack_spec(p, 0, depth) for p in packs]
        + [pl.BlockSpec(memory_space=pl.ANY)] * len(after),
        out_specs=vmem,
        out_shape=jax.ShapeDtypeStruct((rank, row_total), F32),
        compiler_params=pltpu.CompilerParams(vmem_limit_bytes=VMEM_LIMIT),
        cost_estimate=SMALL,
        name="low_sums",
    )(starts, ends, rows, *packs, *after)


def term_kernel(lows, pieces, peers, start_ref, end_ref, *rest):
    low_refs, rest = rest[:lows], rest[lows:]
    own_refs, rest = rest[:pieces], rest[pieces:]
    up_refs, out_refs = rest[:peers], rest[-pieces:]
    rank, row_total = low_refs[0].shape
    width = out_refs[0].shape[1]
    cols = width * pieces
    low = low_refs[0][...]
    for ref in low_refs[1:]:
        low = low + ref[...]
    low = low.astype(BF16).astype(F32)
    place = lax.broadcasted_iota(jnp.int32, (rank, row_total), 1)
    spread = []
    for q in range(len(up_refs) * CAP):
        member = jnp.logical_and(place >= start_ref[q], place < end_ref[q])
        spread.append(jnp.where(member, low, 0.0))
    spread = jnp.concatenate(spread, axis=0).astype(BF16)
    ups = jnp.concatenate([ref[...].reshape(CAP * rank, cols) for ref in up_refs], axis=0)
    for piece in range(pieces):
        columns = slice(piece * width, (piece + 1) * width)
        term = lax.dot_general(
            spread, ups[:, columns], (((0,), (0,)), ((), ())), preferred_element_type=F32
        )
        out_refs[piece][...] = own_refs[piece][...].astype(F32) + term


def adapter_term(starts, ends, lows, owns, packs, after):
    row_total, width = owns[0].shape
    cols = width * len(owns)
    smem = pl.BlockSpec(memory_space=pltpu.SMEM)
    vmem = pl.BlockSpec(memory_space=pltpu.VMEM)
    depth = packs[0].shape[2] - cols
    return pl.pallas_call(
        functools.partial(term_kernel, len(lows), len(owns), len(packs)),
        grid=(1,),
        in_specs=[smem, smem]
        + [vmem] * (len(lows) + len(owns))
        + [pack_spec(p, depth, cols) for p in packs]
        + [pl.BlockSpec(memory_space=pl.ANY)] * len(after),
        out_specs=[vmem] * len(owns),
        out_shape=[jax.ShapeDtypeStruct((row_total, width), F32)] * len(owns),
        compiler_params=pltpu.CompilerParams(vmem_limit_bytes=VMEM_LIMIT),
        cost_estimate=SMALL,
        name="adapter_term",
    )(starts, ends, *lows, *owns, *packs, *after)


def finish_kernel(addends, term_ref, *rest):
    total = term_ref[...]
    for ref in rest[:addends]:
        total = total + ref[...].astype(F32)
    rest[-1][...] = total.astype(rest[-1].dtype)


def finish(term, arrivals, piece, pieces, result):
    row_total, width = term.shape
    height = min(row_total, 128)
    block = pl.BlockSpec((height, width), lambda i: (i, 0))
    held = [] if result is None else [result]
    return pl.pallas_call(
        functools.partial(finish_kernel, len(arrivals)),
        grid=(row_total // height,),
        in_specs=[block] * (1 + len(arrivals)) + [pl.BlockSpec(memory_space=pl.ANY)] * len(held),
        out_specs=pl.BlockSpec((height, width), lambda i: (i, piece)),
        out_shape=jax.ShapeDtypeStruct((row_total, width * pieces), BF16),
        input_output_aliases={1 + len(arrivals): 0} if held else {},
        compiler_params=pltpu.CompilerParams(vmem_limit_bytes=VMEM_LIMIT),
        cost_estimate=SMALL,
        name="finish",
    )(term, *arrivals, *held)


def local(req_total, tp_total, rows, weight, down, up, table, ids, lens):
    rank = down.shape[1]
    cols = up.shape[2]
    width = cols // PIECES
    me_req = lax.axis_index("req").astype(jnp.int32)
    me = lax.axis_index("tp").astype(jnp.int32)
    right = [(i, (i + 1) % tp_total) for i in range(tp_total)]
    steps = tp_total - 1

    def partial(back, piece, **options):
        block = lax.rem(me + (tp_total - back), tp_total)
        return block_product(rows, weight, block * cols + piece * width, width, **options)

    moving, owns = [None] * PIECES, [None] * PIECES
    last, ids = partial(1, 0, ids=ids)
    moving[0] = lax.ppermute(last, "tp", right)

    all_ids = [ids]
    for x in range(1, req_total):
        all_ids.append(lax.ppermute(ids, "req", [(i, i ^ x) for i in range(req_total)]))
    for piece in range(1, PIECES):
        last = partial(1, piece, after=[last])
        moving[piece] = lax.ppermute(last, "tp", right)
    packs, starts, ends = pick_adapters(me_req, table, all_ids, lens, down, up, [last])
    for x in range(1, req_total):
        packs[x] = lax.ppermute(packs[x], "req", [(i, i ^ x) for i in range(req_total)])

    last = starts
    for step in range(1, steps):
        for piece in range(PIECES):
            if step == steps - 1 and piece == PIECES - 1:
                low = low_sums(starts, ends, rows, packs, rank, [last])
                lows = [low]
                for x in range(1, tp_total):
                    pairs = [(i, i ^ x) for i in range(tp_total)]
                    lows.append(lax.ppermute(low, "tp", pairs))
                last = low
            last = partial(1 + step, piece, addends=[moving[piece]], after=[last])
            moving[piece] = lax.ppermute(last, "tp", right)
            if step == 1:
                last = owns[piece] = partial(0, piece, after=[last])

    terms = adapter_term(starts, ends, lows, owns, packs, [last])
    result = None
    for piece in range(PIECES):
        result = finish(terms[piece], [moving[piece]], piece, PIECES, result)
    return result


def solution(mesh):
    return jax.shard_map(
        functools.partial(local, mesh.shape["req"], mesh.shape["tp"]),
        mesh=mesh,
        in_specs=(
            P(("groups", "req"), "tp"),
            P("tp", None),
            P(("groups", "req"), None, "tp"),
            P(("groups", "req"), None, "tp"),
            P("groups"),
            P(("groups", "req"), None),
            P(("groups", "req"), None),
        ),
        out_specs=P(("groups", "req"), "tp"),
        check_vma=False,
    )
```

```python
import functools

import jax
import jax.numpy as jnp
from jax import lax
from jax.experimental import pallas as pl
from jax.experimental.pallas import tpu as pltpu
from jax.sharding import PartitionSpec as P

CAP = 6
PIECES = 2
VMEM_LIMIT = 48 * 1024 * 1024
F32 = jnp.float32
BF16 = jnp.bfloat16
SMALL = pl.CostEstimate(flops=1000, bytes_accessed=1000, transcendentals=0)


def product_kernel(addends, with_ids, first_ref, rows_ref, weight_ref, *rest):
    out_ref = rest[-1 - with_ids]
    total = jnp.dot(rows_ref[...], weight_ref[...], preferred_element_type=F32)
    for ref in rest[:addends]:
        total = total + ref[...].astype(F32)
    out_ref[...] = total.astype(out_ref.dtype)
    if with_ids:
        ids_ref, ids_out_ref = rest[addends], rest[-1]
        for s in range(ids_ref.shape[1]):
            ids_out_ref[0, s] = ids_ref[0, s]


def block_product(rows, weight, first, width, addends=(), after=(), ids=None):
    row_total, depth = rows.shape
    tile = min(256, width)
    with_ids = ids is not None
    smem = pl.BlockSpec(memory_space=pltpu.SMEM)
    hbm = pl.BlockSpec(memory_space=pl.ANY)
    columns = pl.BlockSpec((row_total, tile), lambda j, t: (0, j))
    out_specs, out_shape = [columns], [jax.ShapeDtypeStruct((row_total, width), BF16)]
    if with_ids:
        out_specs.append(smem)
        out_shape.append(jax.ShapeDtypeStruct(ids.shape, ids.dtype))
    out = pl.pallas_call(
        functools.partial(product_kernel, len(addends), with_ids),
        grid_spec=pltpu.PrefetchScalarGridSpec(
            num_scalar_prefetch=1,
            grid=(width // tile,),
            in_specs=[
                pl.BlockSpec((row_total, depth), lambda j, t: (0, 0)),
                pl.BlockSpec((depth, tile), lambda j, t: (0, t[0] + j)),
            ]
            + [columns] * len(addends)
            + [smem] * with_ids
            + [hbm] * len(after),
            out_specs=out_specs,
        ),
        out_shape=out_shape,
        compiler_params=pltpu.CompilerParams(vmem_limit_bytes=VMEM_LIMIT),
        cost_estimate=SMALL,
        name="block_product",
    )((first // tile).reshape(1), rows, weight, *addends, *([ids] if with_ids else []), *after)
    return out if with_ids else out[0]


def pick_kernel(peers, afters, me_ref, table_ref, lens_ref, *rest):
    ids_refs = rest[:peers]
    down_ref, up_ref = rest[peers : peers + 2]
    rest = rest[peers + 2 + afters :]
    packs, (start_ref, end_ref, pick_ref, sem) = rest[:peers], rest[peers:]
    segs = lens_ref.shape[1]
    share, _, depth = down_ref.shape
    cols = up_ref.shape[2]
    me = me_ref[0]

    def clear(q, carry):
        pick_ref[q] = 0
        start_ref[q] = 0
        end_ref[q] = 0
        return carry

    lax.fori_loop(0, peers * CAP, clear, 0)

    def copies(x, c, source):
        pack = packs[x].at[c]
        return (
            pltpu.make_async_copy(down_ref.at[source], pack.at[:, pl.ds(0, depth)], sem),
            pltpu.make_async_copy(up_ref.at[source], pack.at[:, pl.ds(depth, cols)], sem),
        )

    for x in reversed(range(peers)):

        def choose(s, count):
            local = table_ref[ids_refs[x][0, s]] - me * share
            mine = jnp.logical_and(local >= 0, local < share)

            @pl.when(jnp.logical_and(mine, count < CAP))
            def _():
                pick_ref[x * CAP + count] = local

            return count + mine.astype(jnp.int32)

        lax.fori_loop(0, segs, choose, 0)
        for c in range(CAP):
            for copy in copies(x, c, pick_ref[x * CAP + c]):
                copy.start()

    for x in range(peers):
        owner = lax.bitwise_xor(me, jnp.int32(x))

        def place(s, carry):
            count, first = carry
            local = table_ref[ids_refs[0][0, s]] - owner * share
            theirs = jnp.logical_and(local >= 0, local < share)
            last = first + lens_ref[0, s]

            @pl.when(jnp.logical_and(theirs, count < CAP))
            def _():
                start_ref[x * CAP + count] = first
                end_ref[x * CAP + count] = last

            return count + theirs.astype(jnp.int32), last

        lax.fori_loop(0, segs, place, (0, 0))

    for x in range(peers):
        for c in range(CAP):
            for copy in copies(x, c, 0):
                copy.wait()


def pick_adapters(me, table, all_ids, lens, down, up, after):
    peers = len(all_ids)
    _, rank, depth = down.shape
    cols = up.shape[2]
    smem = pl.BlockSpec(memory_space=pltpu.SMEM)
    vmem = pl.BlockSpec(memory_space=pltpu.VMEM)
    hbm = pl.BlockSpec(memory_space=pl.ANY)
    out = pl.pallas_call(
        functools.partial(pick_kernel, peers, len(after)),
        in_specs=[smem] * (3 + peers) + [hbm] * (2 + len(after)),
        out_specs=[vmem] * peers + [smem, smem],
        out_shape=[jax.ShapeDtypeStruct((CAP, rank, depth + cols), BF16)] * peers
        + [jax.ShapeDtypeStruct((peers * CAP,), jnp.int32)] * 2,
        scratch_shapes=[pltpu.SMEM((peers * CAP,), jnp.int32), pltpu.SemaphoreType.DMA],
        compiler_params=pltpu.CompilerParams(vmem_limit_bytes=VMEM_LIMIT),
        cost_estimate=SMALL,
        name="pick_adapters",
    )(me.reshape(1), table, lens, *all_ids, down, up, *after)
    return list(out[:-2]), out[-2], out[-1]


def pack_spec(pack, first, width):
    return pl.BlockSpec(pack.shape[:2] + (width,), lambda i: (0, 0, first // width))


def low_kernel(peers, start_ref, end_ref, rows_ref, *rest):
    down_refs, out_ref = rest[:peers], rest[-1]
    row_total, depth = rows_ref.shape
    rank = out_ref.shape[0]
    place = lax.broadcasted_iota(jnp.int32, (rank, row_total), 1)
    total = jnp.zeros((rank, row_total), F32)
    for x, down_ref in enumerate(down_refs):
        part = lax.dot_general(
            down_ref[...].reshape(CAP * rank, depth),
            rows_ref[...],
            (((1,), (1,)), ((), ())),
            preferred_element_type=F32,
        )
        for c in range(CAP):
            q = x * CAP + c
            member = jnp.logical_and(place >= start_ref[q], place < end_ref[q])
            total = jnp.where(member, part[c * rank : (c + 1) * rank], total)
    out_ref[...] = total


def low_sums(starts, ends, rows, packs, rank, after):
    row_total, depth = rows.shape
    smem = pl.BlockSpec(memory_space=pltpu.SMEM)
    vmem = pl.BlockSpec(memory_space=pltpu.VMEM)
    return pl.pallas_call(
        functools.partial(low_kernel, len(packs)),
        grid=(1,),
        in_specs=[smem, smem, vmem]
        + [pack_spec(p, 0, depth) for p in packs]
        + [pl.BlockSpec(memory_space=pl.ANY)] * len(after),
        out_specs=vmem,
        out_shape=jax.ShapeDtypeStruct((rank, row_total), F32),
        compiler_params=pltpu.CompilerParams(vmem_limit_bytes=VMEM_LIMIT),
        cost_estimate=SMALL,
        name="low_sums",
    )(starts, ends, rows, *packs, *after)


def finish_kernel(lows, peers, pieces, parts, start_ref, end_ref, *rest):
    low_refs, rest = rest[:lows], rest[lows:]
    up_refs, base_refs, out_ref, spread_ref = rest[:peers], rest[peers:-2], rest[-2], rest[-1]
    rank, row_total = low_refs[0].shape
    tile = out_ref.shape[1]
    step = pl.program_id(0)

    @pl.when(step == 0)
    def _():
        low = low_refs[0][...]
        for ref in low_refs[1:]:
            low = low + ref[...]
        low = low.astype(BF16).astype(F32)
        place = lax.broadcasted_iota(jnp.int32, (rank, row_total), 1)
        spread = []
        for q in range(peers * CAP):
            member = jnp.logical_and(place >= start_ref[q], place < end_ref[q])
            spread.append(jnp.where(member, low, 0.0))
        spread_ref[...] = jnp.concatenate(spread, axis=0).astype(BF16)

    ups = jnp.concatenate([ref[...].reshape(CAP * rank, tile) for ref in up_refs], axis=0)
    total = lax.dot_general(
        spread_ref[...], ups, (((0,), (0,)), ((), ())), preferred_element_type=F32
    )
    steps = pl.num_programs(0) // pieces
    for piece in range(pieces):

        @pl.when(step // steps == piece)
        def _():
            base = base_refs[piece * parts][...].astype(F32)
            for ref in base_refs[piece * parts + 1 : (piece + 1) * parts]:
                base = base + ref[...].astype(F32)
            out_ref[...] = (base + total).astype(out_ref.dtype)


def finish(starts, ends, lows, packs, bases):
    rank, row_total = lows[0].shape
    pieces, parts = len(bases), len(bases[0])
    width = bases[0][0].shape[1]
    cols = width * pieces
    tile = min(256, width)
    steps = width // tile
    skip = (packs[0].shape[2] - cols) // tile
    smem = pl.BlockSpec(memory_space=pltpu.SMEM)
    in_specs = [smem, smem]
    in_specs += [pl.BlockSpec((rank, row_total), lambda j: (0, 0))] * len(lows)
    in_specs += [pl.BlockSpec((CAP, rank, tile), lambda j: (0, 0, skip + j))] * len(packs)
    for piece in range(pieces):

        def place(j, piece=piece):
            return 0, jnp.clip(j - piece * steps, 0, steps - 1)

        in_specs += [pl.BlockSpec((row_total, tile), place)] * parts
    return pl.pallas_call(
        functools.partial(finish_kernel, len(lows), len(packs), pieces, parts),
        grid=(cols // tile,),
        in_specs=in_specs,
        out_specs=pl.BlockSpec((row_total, tile), lambda j: (0, j)),
        out_shape=jax.ShapeDtypeStruct((row_total, cols), BF16),
        scratch_shapes=[pltpu.VMEM((len(packs) * CAP * rank, row_total), BF16)],
        compiler_params=pltpu.CompilerParams(vmem_limit_bytes=VMEM_LIMIT),
        cost_estimate=SMALL,
        name="finish",
    )(starts, ends, *lows, *packs, *[b for piece in bases for b in piece])


def local(req_total, tp_total, rows, weight, down, up, table, ids, lens):
    rank = down.shape[1]
    cols = up.shape[2]
    width = cols // PIECES
    me_req = lax.axis_index("req").astype(jnp.int32)
    me = lax.axis_index("tp").astype(jnp.int32)
    steps = tp_total - 1

    def move(value, piece):
        way = 1 if piece % 2 == 0 else tp_total - 1
        return lax.ppermute(value, "tp", [(i, (i + way) % tp_total) for i in range(tp_total)])

    def partial(back, piece, **options):
        behind = tp_total - back if piece % 2 == 0 else back
        block = lax.rem(me + behind, tp_total)
        return block_product(rows, weight, block * cols + piece * width, width, **options)

    last = partial(1, 0)
    moving, owns = [move(last, 0)], []
    for piece in range(1, PIECES):
        last, ids = partial(1, piece, after=[last], ids=ids)
        moving.append(move(last, piece))

    all_ids = [ids]
    for x in range(1, req_total):
        all_ids.append(lax.ppermute(ids, "req", [(i, i ^ x) for i in range(req_total)]))
    packs, starts, ends = pick_adapters(me_req, table, all_ids, lens, down, up, [last])
    for x in range(1, req_total):
        packs[x] = lax.ppermute(packs[x], "req", [(i, i ^ x) for i in range(req_total)])

    last = starts
    for step in range(1, steps):
        for piece in range(PIECES):
            if step == steps - 1 and piece == PIECES - 1:
                low = low_sums(starts, ends, rows, packs, rank, [last])
                lows = [low]
                for x in range(1, tp_total):
                    pairs = [(i, i ^ x) for i in range(tp_total)]
                    lows.append(lax.ppermute(low, "tp", pairs))
                last = low
            last = partial(1 + step, piece, addends=[moving[piece]], after=[last])
            moving[piece] = move(last, piece)
            if step == 1:
                last = partial(0, piece, after=[last])
                owns.append(last)

    bases = [[owns[piece], moving[piece]] for piece in range(PIECES)]
    return finish(starts, ends, lows, packs, bases)


def solution(mesh):
    return jax.shard_map(
        functools.partial(local, mesh.shape["req"], mesh.shape["tp"]),
        mesh=mesh,
        in_specs=(
            P(("groups", "req"), "tp"),
            P("tp", None),
            P(("groups", "req"), None, "tp"),
            P(("groups", "req"), None, "tp"),
            P("groups"),
            P(("groups", "req"), None),
            P(("groups", "req"), None),
        ),
        out_specs=P(("groups", "req"), "tp"),
        check_vma=False,
    )
```

```python
import functools

import jax
import jax.numpy as jnp
from jax import lax
from jax.experimental import pallas as pl
from jax.experimental.pallas import tpu as pltpu
from jax.sharding import PartitionSpec as P

CAP = 6
PIECES = 2
VMEM_LIMIT = 48 * 1024 * 1024
F32 = jnp.float32
BF16 = jnp.bfloat16
SMALL = pl.CostEstimate(flops=1000, bytes_accessed=1000, transcendentals=0)


def product_kernel(addends, with_ids, first_ref, rows_ref, weight_ref, *rest):
    out_ref = rest[-1 - with_ids]
    total = jnp.dot(rows_ref[...], weight_ref[...], preferred_element_type=F32)
    for ref in rest[:addends]:
        total = total + ref[...].astype(F32)
    out_ref[...] = total.astype(out_ref.dtype)
    if with_ids:
        ids_ref, ids_out_ref = rest[addends], rest[-1]
        for s in range(ids_ref.shape[1]):
            ids_out_ref[0, s] = ids_ref[0, s]


def block_product(rows, weight, first, width, addends=(), after=(), ids=None):
    row_total, depth = rows.shape
    tile = min(256, width)
    with_ids = ids is not None
    smem = pl.BlockSpec(memory_space=pltpu.SMEM)
    hbm = pl.BlockSpec(memory_space=pl.ANY)
    columns = pl.BlockSpec((row_total, tile), lambda j, t: (0, j))
    out_specs, out_shape = [columns], [jax.ShapeDtypeStruct((row_total, width), BF16)]
    if with_ids:
        out_specs.append(smem)
        out_shape.append(jax.ShapeDtypeStruct(ids.shape, ids.dtype))
    out = pl.pallas_call(
        functools.partial(product_kernel, len(addends), with_ids),
        grid_spec=pltpu.PrefetchScalarGridSpec(
            num_scalar_prefetch=1,
            grid=(width // tile,),
            in_specs=[
                pl.BlockSpec((row_total, depth), lambda j, t: (0, 0)),
                pl.BlockSpec((depth, tile), lambda j, t: (0, t[0] + j)),
            ]
            + [columns] * len(addends)
            + [smem] * with_ids
            + [hbm] * len(after),
            out_specs=out_specs,
        ),
        out_shape=out_shape,
        compiler_params=pltpu.CompilerParams(vmem_limit_bytes=VMEM_LIMIT),
        cost_estimate=SMALL,
        name="block_product",
    )((first // tile).reshape(1), rows, weight, *addends, *([ids] if with_ids else []), *after)
    return out if with_ids else out[0]


def pick_kernel(peers, afters, me_ref, table_ref, lens_ref, *rest):
    ids_refs = rest[:peers]
    down_ref, up_ref = rest[peers : peers + 2]
    rest = rest[peers + 2 + afters :]
    packs, (start_ref, end_ref, pick_ref, sem) = rest[:peers], rest[peers:]
    segs = lens_ref.shape[1]
    share, _, depth = down_ref.shape
    cols = up_ref.shape[2]
    me = me_ref[0]

    def clear(q, carry):
        pick_ref[q] = 0
        start_ref[q] = 0
        end_ref[q] = 0
        return carry

    lax.fori_loop(0, peers * CAP, clear, 0)

    def copies(x, c, source):
        pack = packs[x].at[c]
        return (
            pltpu.make_async_copy(down_ref.at[source], pack.at[:, pl.ds(0, depth)], sem),
            pltpu.make_async_copy(up_ref.at[source], pack.at[:, pl.ds(depth, cols)], sem),
        )

    for x in reversed(range(peers)):

        def choose(s, count):
            local = table_ref[ids_refs[x][0, s]] - me * share
            mine = jnp.logical_and(local >= 0, local < share)

            @pl.when(jnp.logical_and(mine, count < CAP))
            def _():
                pick_ref[x * CAP + count] = local

            return count + mine.astype(jnp.int32)

        lax.fori_loop(0, segs, choose, 0)
        for c in range(CAP):
            for copy in copies(x, c, pick_ref[x * CAP + c]):
                copy.start()

    for x in range(peers):
        owner = lax.bitwise_xor(me, jnp.int32(x))

        def place(s, carry):
            count, first = carry
            local = table_ref[ids_refs[0][0, s]] - owner * share
            theirs = jnp.logical_and(local >= 0, local < share)
            last = first + lens_ref[0, s]

            @pl.when(jnp.logical_and(theirs, count < CAP))
            def _():
                start_ref[x * CAP + count] = first
                end_ref[x * CAP + count] = last

            return count + theirs.astype(jnp.int32), last

        lax.fori_loop(0, segs, place, (0, 0))

    for x in range(peers):
        for c in range(CAP):
            for copy in copies(x, c, 0):
                copy.wait()


def pick_adapters(me, table, all_ids, lens, down, up, after):
    peers = len(all_ids)
    _, rank, depth = down.shape
    cols = up.shape[2]
    smem = pl.BlockSpec(memory_space=pltpu.SMEM)
    vmem = pl.BlockSpec(memory_space=pltpu.VMEM)
    hbm = pl.BlockSpec(memory_space=pl.ANY)
    out = pl.pallas_call(
        functools.partial(pick_kernel, peers, len(after)),
        in_specs=[smem] * (3 + peers) + [hbm] * (2 + len(after)),
        out_specs=[vmem] * peers + [smem, smem],
        out_shape=[jax.ShapeDtypeStruct((CAP, rank, depth + cols), BF16)] * peers
        + [jax.ShapeDtypeStruct((peers * CAP,), jnp.int32)] * 2,
        scratch_shapes=[pltpu.SMEM((peers * CAP,), jnp.int32), pltpu.SemaphoreType.DMA],
        compiler_params=pltpu.CompilerParams(vmem_limit_bytes=VMEM_LIMIT),
        cost_estimate=SMALL,
        name="pick_adapters",
    )(me.reshape(1), table, lens, *all_ids, down, up, *after)
    return list(out[:-2]), out[-2], out[-1]


def pack_spec(pack, first, width):
    return pl.BlockSpec(pack.shape[:2] + (width,), lambda i: (0, 0, first // width))


def low_kernel(peers, start_ref, end_ref, rows_ref, *rest):
    down_refs, out_ref = rest[:peers], rest[-1]
    row_total, depth = rows_ref.shape
    rank = out_ref.shape[0]
    place = lax.broadcasted_iota(jnp.int32, (rank, row_total), 1)
    total = jnp.zeros((rank, row_total), F32)
    for x, down_ref in enumerate(down_refs):
        part = lax.dot_general(
            down_ref[...].reshape(CAP * rank, depth),
            rows_ref[...],
            (((1,), (1,)), ((), ())),
            preferred_element_type=F32,
        )
        for c in range(CAP):
            q = x * CAP + c
            member = jnp.logical_and(place >= start_ref[q], place < end_ref[q])
            total = jnp.where(member, part[c * rank : (c + 1) * rank], total)
    out_ref[...] = total


def low_sums(starts, ends, rows, packs, rank, after):
    row_total, depth = rows.shape
    smem = pl.BlockSpec(memory_space=pltpu.SMEM)
    vmem = pl.BlockSpec(memory_space=pltpu.VMEM)
    return pl.pallas_call(
        functools.partial(low_kernel, len(packs)),
        grid=(1,),
        in_specs=[smem, smem, vmem]
        + [pack_spec(p, 0, depth) for p in packs]
        + [pl.BlockSpec(memory_space=pl.ANY)] * len(after),
        out_specs=vmem,
        out_shape=jax.ShapeDtypeStruct((rank, row_total), F32),
        compiler_params=pltpu.CompilerParams(vmem_limit_bytes=VMEM_LIMIT),
        cost_estimate=SMALL,
        name="low_sums",
    )(starts, ends, rows, *packs, *after)


def finish_kernel(lows, peers, pieces, parts, start_ref, end_ref, *rest):
    low_refs, rest = rest[:lows], rest[lows:]
    up_refs, base_refs, out_ref, spread_ref = rest[:peers], rest[peers:-2], rest[-2], rest[-1]
    rank, row_total = low_refs[0].shape
    tile = out_ref.shape[1]
    step = pl.program_id(0)

    @pl.when(step == 0)
    def _():
        low = low_refs[0][...]
        for ref in low_refs[1:]:
            low = low + ref[...]
        low = low.astype(BF16).astype(F32)
        place = lax.broadcasted_iota(jnp.int32, (rank, row_total), 1)
        spread = []
        for q in range(peers * CAP):
            member = jnp.logical_and(place >= start_ref[q], place < end_ref[q])
            spread.append(jnp.where(member, low, 0.0))
        spread_ref[...] = jnp.concatenate(spread, axis=0).astype(BF16)

    ups = jnp.concatenate([ref[...].reshape(CAP * rank, tile) for ref in up_refs], axis=0)
    total = lax.dot_general(
        spread_ref[...], ups, (((0,), (0,)), ((), ())), preferred_element_type=F32
    )
    steps = pl.num_programs(0) // pieces
    for piece in range(pieces):

        @pl.when(step // steps == piece)
        def _():
            base = base_refs[piece * parts][...].astype(F32)
            for ref in base_refs[piece * parts + 1 : (piece + 1) * parts]:
                base = base + ref[...].astype(F32)
            out_ref[...] = (base + total).astype(out_ref.dtype)


def finish(starts, ends, lows, packs, bases):
    rank, row_total = lows[0].shape
    pieces, parts = len(bases), len(bases[0])
    width = bases[0][0].shape[1]
    cols = width * pieces
    tile = min(256, width)
    steps = width // tile
    skip = (packs[0].shape[2] - cols) // tile
    smem = pl.BlockSpec(memory_space=pltpu.SMEM)
    in_specs = [smem, smem]
    in_specs += [pl.BlockSpec((rank, row_total), lambda j: (0, 0))] * len(lows)
    in_specs += [pl.BlockSpec((CAP, rank, tile), lambda j: (0, 0, skip + j))] * len(packs)
    for piece in range(pieces):

        def place(j, piece=piece):
            return 0, jnp.clip(j - piece * steps, 0, steps - 1)

        in_specs += [pl.BlockSpec((row_total, tile), place)] * parts
    return pl.pallas_call(
        functools.partial(finish_kernel, len(lows), len(packs), pieces, parts),
        grid=(cols // tile,),
        in_specs=in_specs,
        out_specs=pl.BlockSpec((row_total, tile), lambda j: (0, j)),
        out_shape=jax.ShapeDtypeStruct((row_total, cols), BF16),
        scratch_shapes=[pltpu.VMEM((len(packs) * CAP * rank, row_total), BF16)],
        compiler_params=pltpu.CompilerParams(vmem_limit_bytes=VMEM_LIMIT),
        cost_estimate=SMALL,
        name="finish",
    )(starts, ends, *lows, *packs, *[b for piece in bases for b in piece])


def local(req_total, tp_total, rows, weight, down, up, table, ids, lens):
    rank = down.shape[1]
    cols = up.shape[2]
    width = cols // PIECES
    me_req = lax.axis_index("req").astype(jnp.int32)
    me = lax.axis_index("tp").astype(jnp.int32)
    steps = tp_total - 1

    def move(value, piece):
        pairs = []
        for r in range(req_total):
            way = 1 if (r + piece) % 2 == 0 else tp_total - 1
            for i in range(tp_total):
                pairs.append((r * tp_total + i, r * tp_total + (i + way) % tp_total))
        return lax.ppermute(value, ("req", "tp"), pairs)

    def partial(back, piece, **options):
        behind = jnp.where(lax.rem(me_req + piece, 2) == 0, tp_total - back, back)
        block = lax.rem(me + behind, tp_total)
        return block_product(rows, weight, block * cols + piece * width, width, **options)

    last = partial(1, 0)
    moving, owns = [move(last, 0)], []
    for piece in range(1, PIECES):
        last, ids = partial(1, piece, after=[last], ids=ids)
        moving.append(move(last, piece))

    all_ids = [ids]
    for x in range(1, req_total):
        all_ids.append(lax.ppermute(ids, "req", [(i, i ^ x) for i in range(req_total)]))
    packs, starts, ends = pick_adapters(me_req, table, all_ids, lens, down, up, [last])
    for x in range(1, req_total):
        packs[x] = lax.ppermute(packs[x], "req", [(i, i ^ x) for i in range(req_total)])

    last = starts
    for step in range(1, steps):
        for piece in range(PIECES):
            if step == steps - 1 and piece == PIECES - 1:
                low = low_sums(starts, ends, rows, packs, rank, [last])
                lows = [low]
                for x in range(1, tp_total):
                    pairs = [(i, i ^ x) for i in range(tp_total)]
                    lows.append(lax.ppermute(low, "tp", pairs))
                last = low
            last = partial(1 + step, piece, addends=[moving[piece]], after=[last])
            moving[piece] = move(last, piece)
            if step == 1:
                last = partial(0, piece, after=[last])
                owns.append(last)

    bases = [[owns[piece], moving[piece]] for piece in range(PIECES)]
    return finish(starts, ends, lows, packs, bases)


def solution(mesh):
    return jax.shard_map(
        functools.partial(local, mesh.shape["req"], mesh.shape["tp"]),
        mesh=mesh,
        in_specs=(
            P(("groups", "req"), "tp"),
            P("tp", None),
            P(("groups", "req"), None, "tp"),
            P(("groups", "req"), None, "tp"),
            P("groups"),
            P(("groups", "req"), None),
            P(("groups", "req"), None),
        ),
        out_specs=P(("groups", "req"), "tp"),
        check_vma=False,
    )
```

```python
import functools

import jax
import jax.numpy as jnp
from jax import lax
from jax.experimental import pallas as pl
from jax.experimental.pallas import tpu as pltpu
from jax.sharding import PartitionSpec as P

CAP = 6
PIECES = 2
VMEM_LIMIT = 48 * 1024 * 1024
F32 = jnp.float32
BF16 = jnp.bfloat16
SMALL = pl.CostEstimate(flops=1000, bytes_accessed=1000, transcendentals=0)
LARGE = pl.CostEstimate(flops=10**11, bytes_accessed=4 * 10**8, transcendentals=0)


def product_kernel(addends, with_ids, first_ref, rows_ref, weight_ref, *rest):
    out_ref = rest[-1 - with_ids]
    total = jnp.dot(rows_ref[...], weight_ref[...], preferred_element_type=F32)
    for ref in rest[:addends]:
        total = total + ref[...].astype(F32)
    out_ref[...] = total.astype(out_ref.dtype)
    if with_ids:
        ids_ref, ids_out_ref = rest[addends], rest[-1]
        for s in range(ids_ref.shape[1]):
            ids_out_ref[0, s] = ids_ref[0, s]


def block_product(rows, weight, first, width, addends=(), after=(), ids=None):
    row_total, depth = rows.shape
    tile = min(256, width)
    with_ids = ids is not None
    smem = pl.BlockSpec(memory_space=pltpu.SMEM)
    hbm = pl.BlockSpec(memory_space=pl.ANY)
    columns = pl.BlockSpec((row_total, tile), lambda j, t: (0, j))
    out_specs, out_shape = [columns], [jax.ShapeDtypeStruct((row_total, width), BF16)]
    if with_ids:
        out_specs.append(smem)
        out_shape.append(jax.ShapeDtypeStruct(ids.shape, ids.dtype))
    out = pl.pallas_call(
        functools.partial(product_kernel, len(addends), with_ids),
        grid_spec=pltpu.PrefetchScalarGridSpec(
            num_scalar_prefetch=1,
            grid=(width // tile,),
            in_specs=[
                pl.BlockSpec((row_total, depth), lambda j, t: (0, 0)),
                pl.BlockSpec((depth, tile), lambda j, t: (0, t[0] + j)),
            ]
            + [columns] * len(addends)
            + [smem] * with_ids
            + [hbm] * len(after),
            out_specs=out_specs,
        ),
        out_shape=out_shape,
        compiler_params=pltpu.CompilerParams(vmem_limit_bytes=VMEM_LIMIT),
        cost_estimate=SMALL,
        name="block_product",
    )((first // tile).reshape(1), rows, weight, *addends, *([ids] if with_ids else []), *after)
    return out if with_ids else out[0]


def first_kernel(chunk, first_ref, rows_ref, weight_ref, out_ref, lhs_ref, rhs_ref, acc_ref, sems):
    columns = pl.ds(pl.multiple_of(first_ref[0], 128), out_ref.shape[1])
    chunks = lhs_ref.shape[0]

    def copies(k):
        part = pl.ds(k * chunk, chunk)
        return (
            pltpu.make_async_copy(rows_ref.at[:, part], lhs_ref.at[k], sems.at[0, k]),
            pltpu.make_async_copy(weight_ref.at[part, columns], rhs_ref.at[k], sems.at[1, k]),
        )

    for k in range(chunks):
        for copy in copies(k):
            copy.start()
    for k in range(chunks):
        for copy in copies(k):
            copy.wait()
        part = jnp.dot(lhs_ref[k], rhs_ref[k], preferred_element_type=F32)
        if k == 0:
            acc_ref[...] = part
        elif k < chunks - 1:
            acc_ref[...] += part
        else:
            out_ref[...] = (acc_ref[...] + part).astype(out_ref.dtype)


def first_product(rows, weight, first, width):
    row_total, depth = rows.shape
    chunk = min(512, depth // 2)
    chunks = depth // chunk
    hbm = pl.BlockSpec(memory_space=pltpu.HBM)
    return pl.pallas_call(
        functools.partial(first_kernel, chunk),
        in_specs=[pl.BlockSpec(memory_space=pltpu.SMEM), hbm, hbm],
        out_specs=pl.BlockSpec(memory_space=pltpu.VMEM),
        out_shape=jax.ShapeDtypeStruct((row_total, width), BF16),
        scratch_shapes=[
            pltpu.VMEM((chunks, row_total, chunk), BF16),
            pltpu.VMEM((chunks, chunk, width), BF16),
            pltpu.VMEM((row_total, width), F32),
            pltpu.SemaphoreType.DMA((2, chunks)),
        ],
        compiler_params=pltpu.CompilerParams(vmem_limit_bytes=VMEM_LIMIT),
        cost_estimate=SMALL,
        name="first_product",
    )(first.reshape(1), rows, weight)


def pick_kernel(peers, afters, me_ref, table_ref, lens_ref, *rest):
    ids_refs = rest[:peers]
    down_ref, up_ref = rest[peers : peers + 2]
    rest = rest[peers + 2 + afters :]
    packs, (start_ref, end_ref, pick_ref, count_ref, sem) = rest[:peers], rest[peers:]
    segs = lens_ref.shape[1]
    share, _, depth = down_ref.shape
    cols = up_ref.shape[2]
    me = me_ref[0]

    def clear(q, carry):
        pick_ref[q] = 0
        start_ref[q] = 0
        end_ref[q] = 0
        return carry

    lax.fori_loop(0, peers * CAP, clear, 0, unroll=8)
    for x in range(peers):
        count_ref[x] = 0

    def copies(x, c, source):
        pack = packs[x].at[c]
        return (
            pltpu.make_async_copy(down_ref.at[source], pack.at[:, pl.ds(0, depth)], sem),
            pltpu.make_async_copy(up_ref.at[source], pack.at[:, pl.ds(depth, cols)], sem),
        )

    for x in reversed(range(peers)):

        def choose(s, count):
            local = table_ref[ids_refs[x][0, s]] - me * share
            mine = jnp.logical_and(local >= 0, local < share)

            @pl.when(jnp.logical_and(mine, count < CAP))
            def _():
                pick_ref[x * CAP + count] = local

            return count + mine.astype(jnp.int32)

        lax.fori_loop(0, segs, choose, 0, unroll=4)
        for c in range(CAP):
            for copy in copies(x, c, pick_ref[x * CAP + c]):
                copy.start()

    def place(s, first):
        x = lax.bitwise_xor(table_ref[ids_refs[0][0, s]] // share, me)
        count = count_ref[x]
        last = first + lens_ref[0, s]

        @pl.when(count < CAP)
        def _():
            start_ref[x * CAP + count] = first
            end_ref[x * CAP + count] = last

        count_ref[x] = count + 1
        return last

    lax.fori_loop(0, segs, place, 0, unroll=4)

    for x in range(peers):
        for c in range(CAP):
            for copy in copies(x, c, 0):
                copy.wait()


def pick_adapters(me, table, all_ids, lens, down, up, after):
    peers = len(all_ids)
    _, rank, depth = down.shape
    cols = up.shape[2]
    smem = pl.BlockSpec(memory_space=pltpu.SMEM)
    vmem = pl.BlockSpec(memory_space=pltpu.VMEM)
    hbm = pl.BlockSpec(memory_space=pl.ANY)
    out = pl.pallas_call(
        functools.partial(pick_kernel, peers, len(after)),
        in_specs=[smem] * (3 + peers) + [hbm] * (2 + len(after)),
        out_specs=[vmem] * peers + [smem, smem],
        out_shape=[jax.ShapeDtypeStruct((CAP, rank, depth + cols), BF16)] * peers
        + [jax.ShapeDtypeStruct((peers * CAP,), jnp.int32)] * 2,
        scratch_shapes=[
            pltpu.SMEM((peers * CAP,), jnp.int32),
            pltpu.SMEM((peers,), jnp.int32),
            pltpu.SemaphoreType.DMA,
        ],
        compiler_params=pltpu.CompilerParams(vmem_limit_bytes=VMEM_LIMIT),
        cost_estimate=SMALL,
        name="pick_adapters",
    )(me.reshape(1), table, lens, *all_ids, down, up, *after)
    return list(out[:-2]), out[-2], out[-1]


def pack_spec(pack, first, width):
    return pl.BlockSpec(pack.shape[:2] + (width,), lambda i: (0, 0, first // width))


def low_kernel(peers, start_ref, end_ref, rows_ref, *rest):
    down_refs, out_ref = rest[:peers], rest[-1]
    row_total, depth = rows_ref.shape
    rank = out_ref.shape[0]
    place = lax.broadcasted_iota(jnp.int32, (rank, row_total), 1)
    downs = jnp.concatenate([ref[...].reshape(CAP * rank, depth) for ref in down_refs], axis=0)
    part = lax.dot_general(
        downs, rows_ref[...], (((1,), (1,)), ((), ())), preferred_element_type=F32
    )
    total = jnp.zeros((rank, row_total), F32)
    for q in range(peers * CAP):
        member = jnp.logical_and(place >= start_ref[q], place < end_ref[q])
        total = jnp.where(member, part[q * rank : (q + 1) * rank], total)
    out_ref[...] = total


def low_sums(starts, ends, rows, packs, rank, after):
    row_total, depth = rows.shape
    smem = pl.BlockSpec(memory_space=pltpu.SMEM)
    vmem = pl.BlockSpec(memory_space=pltpu.VMEM)
    return pl.pallas_call(
        functools.partial(low_kernel, len(packs)),
        grid=(1,),
        in_specs=[smem, smem, vmem]
        + [pack_spec(p, 0, depth) for p in packs]
        + [pl.BlockSpec(memory_space=pl.ANY)] * len(after),
        out_specs=vmem,
        out_shape=jax.ShapeDtypeStruct((rank, row_total), F32),
        compiler_params=pltpu.CompilerParams(vmem_limit_bytes=VMEM_LIMIT),
        cost_estimate=SMALL,
        name="low_sums",
    )(starts, ends, rows, *packs, *after)


def term_kernel(lows, pieces, peers, start_ref, end_ref, *rest):
    low_refs, rest = rest[:lows], rest[lows:]
    own_refs, rest = rest[:pieces], rest[pieces:]
    up_refs, out_refs = rest[:peers], rest[-pieces:]
    rank, row_total = low_refs[0].shape
    width = out_refs[0].shape[1]
    cols = width * pieces
    low = low_refs[0][...]
    for ref in low_refs[1:]:
        low = low + ref[...]
    low = low.astype(BF16).astype(F32)
    place = lax.broadcasted_iota(jnp.int32, (rank, row_total), 1)
    spread = []
    for q in range(len(up_refs) * CAP):
        member = jnp.logical_and(place >= start_ref[q], place < end_ref[q])
        spread.append(jnp.where(member, low, 0.0))
    spread = jnp.concatenate(spread, axis=0).astype(BF16)
    ups = jnp.concatenate([ref[...].reshape(CAP * rank, cols) for ref in up_refs], axis=0)
    for piece in range(pieces):
        columns = slice(piece * width, (piece + 1) * width)
        term = lax.dot_general(
            spread, ups[:, columns], (((0,), (0,)), ((), ())), preferred_element_type=F32
        )
        out_refs[piece][...] = own_refs[piece][...].astype(F32) + term


def adapter_term(starts, ends, lows, owns, packs, after):
    row_total, width = owns[0].shape
    cols = width * len(owns)
    smem = pl.BlockSpec(memory_space=pltpu.SMEM)
    vmem = pl.BlockSpec(memory_space=pltpu.VMEM)
    depth = packs[0].shape[2] - cols
    return pl.pallas_call(
        functools.partial(term_kernel, len(lows), len(owns), len(packs)),
        grid=(1,),
        in_specs=[smem, smem]
        + [vmem] * (len(lows) + len(owns))
        + [pack_spec(p, depth, cols) for p in packs]
        + [pl.BlockSpec(memory_space=pl.ANY)] * len(after),
        out_specs=[vmem] * len(owns),
        out_shape=[jax.ShapeDtypeStruct((row_total, width), F32)] * len(owns),
        compiler_params=pltpu.CompilerParams(vmem_limit_bytes=VMEM_LIMIT),
        cost_estimate=SMALL,
        name="adapter_term",
    )(starts, ends, *lows, *owns, *packs, *after)


def finish_kernel(addends, term_ref, *rest):
    total = term_ref[...]
    for ref in rest[:addends]:
        total = total + ref[...].astype(F32)
    rest[-1][...] = total.astype(rest[-1].dtype)


def finish(term, arrivals, piece, pieces, result, cost):
    row_total, width = term.shape
    height = min(row_total, 128)
    block = pl.BlockSpec((height, width), lambda i: (i, 0))
    held = [] if result is None else [result]
    return pl.pallas_call(
        functools.partial(finish_kernel, len(arrivals)),
        grid=(row_total // height,),
        in_specs=[block] * (1 + len(arrivals)) + [pl.BlockSpec(memory_space=pl.ANY)] * len(held),
        out_specs=pl.BlockSpec((height, width), lambda i: (i, piece)),
        out_shape=jax.ShapeDtypeStruct((row_total, width * pieces), BF16),
        input_output_aliases={1 + len(arrivals): 0} if held else {},
        compiler_params=pltpu.CompilerParams(vmem_limit_bytes=VMEM_LIMIT),
        cost_estimate=cost,
        name="finish",
    )(term, *arrivals, *held)


def local(req_total, tp_total, rows, weight, down, up, table, ids, lens):
    rank = down.shape[1]
    cols = up.shape[2]
    width = cols // PIECES
    me_req = lax.axis_index("req").astype(jnp.int32)
    me = lax.axis_index("tp").astype(jnp.int32)
    steps = tp_total - 1

    def move(value, piece):
        pairs = []
        for r in range(req_total):
            way = 1 if (r + piece) % 2 == 0 else tp_total - 1
            for i in range(tp_total):
                pairs.append((r * tp_total + i, r * tp_total + (i + way) % tp_total))
        return lax.ppermute(value, ("req", "tp"), pairs)

    def start_of(back, piece):
        behind = jnp.where(lax.rem(me_req + piece, 2) == 0, tp_total - back, back)
        block = lax.rem(me + behind, tp_total)
        return block * cols + piece * width

    def partial(back, piece, **options):
        return block_product(rows, weight, start_of(back, piece), width, **options)

    last = first_product(rows, weight, start_of(1, 0), width)
    moving, owns = [move(last, 0)], []
    for piece in range(1, PIECES):
        last, ids = partial(1, piece, after=[last], ids=ids)
        moving.append(move(last, piece))

    all_ids = [ids]
    for x in range(1, req_total):
        all_ids.append(lax.ppermute(ids, "req", [(i, i ^ x) for i in range(req_total)]))
    packs, starts, ends = pick_adapters(me_req, table, all_ids, lens, down, up, [last])
    for x in range(1, req_total):
        packs[x] = lax.ppermute(packs[x], "req", [(i, i ^ x) for i in range(req_total)])

    last = starts
    for step in range(1, steps):
        for piece in range(PIECES):
            if step == steps - 1 and piece == PIECES - 1:
                low = low_sums(starts, ends, rows, packs, rank, [last])
                lows = [low]
                for x in range(1, tp_total):
                    pairs = [(i, i ^ x) for i in range(tp_total)]
                    lows.append(lax.ppermute(low, "tp", pairs))
                last = low
            last = partial(1 + step, piece, addends=[moving[piece]], after=[last])
            moving[piece] = move(last, piece)
            if step == 1:
                last = partial(0, piece, after=[last])
                owns.append(last)

    terms = adapter_term(starts, ends, lows, owns, packs, [last])
    result = None
    for piece in range(PIECES):
        cost = SMALL if piece == PIECES - 1 else LARGE
        result = finish(terms[piece], [moving[piece]], piece, PIECES, result, cost)
    return result


def solution(mesh):
    return jax.shard_map(
        functools.partial(local, mesh.shape["req"], mesh.shape["tp"]),
        mesh=mesh,
        in_specs=(
            P(("groups", "req"), "tp"),
            P("tp", None),
            P(("groups", "req"), None, "tp"),
            P(("groups", "req"), None, "tp"),
            P("groups"),
            P(("groups", "req"), None),
            P(("groups", "req"), None),
        ),
        out_specs=P(("groups", "req"), "tp"),
        check_vma=False,
    )
```

```python
import functools

import jax
import jax.numpy as jnp
from jax import lax
from jax.experimental import pallas as pl
from jax.experimental.pallas import tpu as pltpu
from jax.sharding import PartitionSpec as P

CAP = 6
PIECES = 2
VMEM_LIMIT = 48 * 1024 * 1024
F32 = jnp.float32
BF16 = jnp.bfloat16
SMALL = pl.CostEstimate(flops=1000, bytes_accessed=1000, transcendentals=0)
LARGE = pl.CostEstimate(flops=2 * 10**10, bytes_accessed=6 * 10**7, transcendentals=0)


def product_kernel(addends, with_ids, first_ref, rows_ref, weight_ref, *rest):
    out_ref = rest[-1 - with_ids]
    total = jnp.dot(rows_ref[...], weight_ref[...], preferred_element_type=F32)
    for ref in rest[:addends]:
        total = total + ref[...].astype(F32)
    out_ref[...] = total.astype(out_ref.dtype)
    if with_ids:
        ids_ref, ids_out_ref = rest[addends], rest[-1]
        for s in range(ids_ref.shape[1]):
            ids_out_ref[0, s] = ids_ref[0, s]


def block_product(rows, weight, first, width, addends=(), after=(), ids=None, cost=SMALL):
    row_total, depth = rows.shape
    tile = min(256, width)
    with_ids = ids is not None
    smem = pl.BlockSpec(memory_space=pltpu.SMEM)
    hbm = pl.BlockSpec(memory_space=pl.ANY)
    columns = pl.BlockSpec((row_total, tile), lambda j, t: (0, j))
    out_specs, out_shape = [columns], [jax.ShapeDtypeStruct((row_total, width), BF16)]
    if with_ids:
        out_specs.append(smem)
        out_shape.append(jax.ShapeDtypeStruct(ids.shape, ids.dtype))
    out = pl.pallas_call(
        functools.partial(product_kernel, len(addends), with_ids),
        grid_spec=pltpu.PrefetchScalarGridSpec(
            num_scalar_prefetch=1,
            grid=(width // tile,),
            in_specs=[
                pl.BlockSpec((row_total, depth), lambda j, t: (0, 0)),
                pl.BlockSpec((depth, tile), lambda j, t: (0, t[0] + j)),
            ]
            + [columns] * len(addends)
            + [smem] * with_ids
            + [hbm] * len(after),
            out_specs=out_specs,
        ),
        out_shape=out_shape,
        compiler_params=pltpu.CompilerParams(vmem_limit_bytes=VMEM_LIMIT),
        cost_estimate=cost,
        name="block_product",
    )((first // tile).reshape(1), rows, weight, *addends, *([ids] if with_ids else []), *after)
    return out if with_ids else out[0]


def first_kernel(chunk, first_ref, rows_ref, weight_ref, out_ref, lhs_ref, rhs_ref, acc_ref, sems):
    columns = pl.ds(pl.multiple_of(first_ref[0], 128), out_ref.shape[1])
    chunks = lhs_ref.shape[0]

    def copies(k):
        part = pl.ds(k * chunk, chunk)
        return (
            pltpu.make_async_copy(rows_ref.at[:, part], lhs_ref.at[k], sems.at[0, k]),
            pltpu.make_async_copy(weight_ref.at[part, columns], rhs_ref.at[k], sems.at[1, k]),
        )

    for k in range(chunks):
        for copy in copies(k):
            copy.start()
    for k in range(chunks):
        for copy in copies(k):
            copy.wait()
        part = jnp.dot(lhs_ref[k], rhs_ref[k], preferred_element_type=F32)
        if k == 0:
            acc_ref[...] = part
        elif k < chunks - 1:
            acc_ref[...] += part
        else:
            out_ref[...] = (acc_ref[...] + part).astype(out_ref.dtype)


def first_product(rows, weight, first, width):
    row_total, depth = rows.shape
    chunk = min(512, depth // 2)
    chunks = depth // chunk
    hbm = pl.BlockSpec(memory_space=pltpu.HBM)
    return pl.pallas_call(
        functools.partial(first_kernel, chunk),
        in_specs=[pl.BlockSpec(memory_space=pltpu.SMEM), hbm, hbm],
        out_specs=pl.BlockSpec(memory_space=pltpu.VMEM),
        out_shape=jax.ShapeDtypeStruct((row_total, width), BF16),
        scratch_shapes=[
            pltpu.VMEM((chunks, row_total, chunk), BF16),
            pltpu.VMEM((chunks, chunk, width), BF16),
            pltpu.VMEM((row_total, width), F32),
            pltpu.SemaphoreType.DMA((2, chunks)),
        ],
        compiler_params=pltpu.CompilerParams(vmem_limit_bytes=VMEM_LIMIT),
        cost_estimate=SMALL,
        name="first_product",
    )(first.reshape(1), rows, weight)


def pick_kernel(peers, afters, me_ref, table_ref, lens_ref, *rest):
    ids_refs = rest[:peers]
    down_ref, up_ref = rest[peers : peers + 2]
    rest = rest[peers + 2 + afters :]
    packs, (start_ref, end_ref, pick_ref, count_ref, sem) = rest[:peers], rest[peers:]
    segs = lens_ref.shape[1]
    share, _, depth = down_ref.shape
    cols = up_ref.shape[2]
    me = me_ref[0]

    def clear(q, carry):
        pick_ref[q] = 0
        start_ref[q] = 0
        end_ref[q] = 0
        return carry

    lax.fori_loop(0, peers * CAP, clear, 0, unroll=8)
    for x in range(peers):
        count_ref[x] = 0

    def copies(x, c, source):
        pack = packs[x].at[c]
        return (
            pltpu.make_async_copy(down_ref.at[source], pack.at[:, pl.ds(0, depth)], sem),
            pltpu.make_async_copy(up_ref.at[source], pack.at[:, pl.ds(depth, cols)], sem),
        )

    for x in reversed(range(peers)):

        def choose(s, count):
            local = table_ref[ids_refs[x][0, s]] - me * share
            mine = jnp.logical_and(local >= 0, local < share)

            @pl.when(jnp.logical_and(mine, count < CAP))
            def _():
                pick_ref[x * CAP + count] = local

            return count + mine.astype(jnp.int32)

        lax.fori_loop(0, segs, choose, 0, unroll=4)
        for c in range(CAP):
            for copy in copies(x, c, pick_ref[x * CAP + c]):
                copy.start()

    def place(s, first):
        x = lax.bitwise_xor(table_ref[ids_refs[0][0, s]] // share, me)
        count = count_ref[x]
        last = first + lens_ref[0, s]

        @pl.when(count < CAP)
        def _():
            start_ref[x * CAP + count] = first
            end_ref[x * CAP + count] = last

        count_ref[x] = count + 1
        return last

    lax.fori_loop(0, segs, place, 0, unroll=4)

    for x in range(peers):
        for c in range(CAP):
            for copy in copies(x, c, 0):
                copy.wait()


def pick_adapters(me, table, all_ids, lens, down, up, after):
    peers = len(all_ids)
    _, rank, depth = down.shape
    cols = up.shape[2]
    smem = pl.BlockSpec(memory_space=pltpu.SMEM)
    vmem = pl.BlockSpec(memory_space=pltpu.VMEM)
    hbm = pl.BlockSpec(memory_space=pl.ANY)
    out = pl.pallas_call(
        functools.partial(pick_kernel, peers, len(after)),
        in_specs=[smem] * (3 + peers) + [hbm] * (2 + len(after)),
        out_specs=[vmem] * peers + [smem, smem],
        out_shape=[jax.ShapeDtypeStruct((CAP, rank, depth + cols), BF16)] * peers
        + [jax.ShapeDtypeStruct((peers * CAP,), jnp.int32)] * 2,
        scratch_shapes=[
            pltpu.SMEM((peers * CAP,), jnp.int32),
            pltpu.SMEM((peers,), jnp.int32),
            pltpu.SemaphoreType.DMA,
        ],
        compiler_params=pltpu.CompilerParams(vmem_limit_bytes=VMEM_LIMIT),
        cost_estimate=SMALL,
        name="pick_adapters",
    )(me.reshape(1), table, lens, *all_ids, down, up, *after)
    return list(out[:-2]), out[-2], out[-1]


def pack_spec(pack, first, width):
    return pl.BlockSpec(pack.shape[:2] + (width,), lambda i: (0, 0, first // width))


def low_kernel(peers, start_ref, end_ref, rows_ref, *rest):
    down_refs, out_ref = rest[:peers], rest[-1]
    row_total, depth = rows_ref.shape
    rank = out_ref.shape[0]
    place = lax.broadcasted_iota(jnp.int32, (rank, row_total), 1)
    downs = jnp.concatenate([ref[...].reshape(CAP * rank, depth) for ref in down_refs], axis=0)
    part = lax.dot_general(
        downs, rows_ref[...], (((1,), (1,)), ((), ())), preferred_element_type=F32
    )
    total = jnp.zeros((rank, row_total), F32)
    for q in range(peers * CAP):
        member = jnp.logical_and(place >= start_ref[q], place < end_ref[q])
        total = jnp.where(member, part[q * rank : (q + 1) * rank], total)
    out_ref[...] = total


def low_sums(starts, ends, rows, packs, rank, after):
    row_total, depth = rows.shape
    smem = pl.BlockSpec(memory_space=pltpu.SMEM)
    vmem = pl.BlockSpec(memory_space=pltpu.VMEM)
    return pl.pallas_call(
        functools.partial(low_kernel, len(packs)),
        grid=(1,),
        in_specs=[smem, smem, vmem]
        + [pack_spec(p, 0, depth) for p in packs]
        + [pl.BlockSpec(memory_space=pl.ANY)] * len(after),
        out_specs=vmem,
        out_shape=jax.ShapeDtypeStruct((rank, row_total), F32),
        compiler_params=pltpu.CompilerParams(vmem_limit_bytes=VMEM_LIMIT),
        cost_estimate=SMALL,
        name="low_sums",
    )(starts, ends, rows, *packs, *after)


def term_kernel(lows, pieces, peers, start_ref, end_ref, *rest):
    low_refs, rest = rest[:lows], rest[lows:]
    own_refs, rest = rest[:pieces], rest[pieces:]
    up_refs, out_refs = rest[:peers], rest[-pieces:]
    rank, row_total = low_refs[0].shape
    width = out_refs[0].shape[1]
    cols = width * pieces
    low = low_refs[0][...]
    for ref in low_refs[1:]:
        low = low + ref[...]
    low = low.astype(BF16).astype(F32)
    place = lax.broadcasted_iota(jnp.int32, (rank, row_total), 1)
    spread = []
    for q in range(len(up_refs) * CAP):
        member = jnp.logical_and(place >= start_ref[q], place < end_ref[q])
        spread.append(jnp.where(member, low, 0.0))
    spread = jnp.concatenate(spread, axis=0).astype(BF16)
    ups = jnp.concatenate([ref[...].reshape(CAP * rank, cols) for ref in up_refs], axis=0)
    for piece in range(pieces):
        columns = slice(piece * width, (piece + 1) * width)
        term = lax.dot_general(
            spread, ups[:, columns], (((0,), (0,)), ((), ())), preferred_element_type=F32
        )
        out_refs[piece][...] = own_refs[piece][...].astype(F32) + term


def adapter_term(starts, ends, lows, owns, packs, after):
    row_total, width = owns[0].shape
    cols = width * len(owns)
    smem = pl.BlockSpec(memory_space=pltpu.SMEM)
    vmem = pl.BlockSpec(memory_space=pltpu.VMEM)
    depth = packs[0].shape[2] - cols
    return pl.pallas_call(
        functools.partial(term_kernel, len(lows), len(owns), len(packs)),
        grid=(1,),
        in_specs=[smem, smem]
        + [vmem] * (len(lows) + len(owns))
        + [pack_spec(p, depth, cols) for p in packs]
        + [pl.BlockSpec(memory_space=pl.ANY)] * len(after),
        out_specs=[vmem] * len(owns),
        out_shape=[jax.ShapeDtypeStruct((row_total, width), F32)] * len(owns),
        compiler_params=pltpu.CompilerParams(vmem_limit_bytes=VMEM_LIMIT),
        cost_estimate=SMALL,
        name="adapter_term",
    )(starts, ends, *lows, *owns, *packs, *after)


def finish_kernel(addends, term_ref, *rest):
    total = term_ref[...]
    for ref in rest[:addends]:
        total = total + ref[...].astype(F32)
    rest[-1][...] = total.astype(rest[-1].dtype)


def finish(term, arrivals, piece, pieces, result, cost):
    row_total, width = term.shape
    height = min(row_total, 128)
    block = pl.BlockSpec((height, width), lambda i: (i, 0))
    held = [] if result is None else [result]
    return pl.pallas_call(
        functools.partial(finish_kernel, len(arrivals)),
        grid=(row_total // height,),
        in_specs=[block] * (1 + len(arrivals)) + [pl.BlockSpec(memory_space=pl.ANY)] * len(held),
        out_specs=pl.BlockSpec((height, width), lambda i: (i, piece)),
        out_shape=jax.ShapeDtypeStruct((row_total, width * pieces), BF16),
        input_output_aliases={1 + len(arrivals): 0} if held else {},
        compiler_params=pltpu.CompilerParams(vmem_limit_bytes=VMEM_LIMIT),
        cost_estimate=cost,
        name="finish",
    )(term, *arrivals, *held)


def local(req_total, tp_total, rows, weight, down, up, table, ids, lens):
    rank = down.shape[1]
    cols = up.shape[2]
    width = cols // PIECES
    me_req = lax.axis_index("req").astype(jnp.int32)
    me = lax.axis_index("tp").astype(jnp.int32)
    steps = tp_total - 1

    def move(value, piece):
        pairs = []
        for r in range(req_total):
            way = 1 if (r + piece) % 2 == 0 else tp_total - 1
            for i in range(tp_total):
                pairs.append((r * tp_total + i, r * tp_total + (i + way) % tp_total))
        return lax.ppermute(value, ("req", "tp"), pairs)

    def start_of(back, piece):
        behind = jnp.where(lax.rem(me_req + piece, 2) == 0, tp_total - back, back)
        block = lax.rem(me + behind, tp_total)
        return block * cols + piece * width

    def partial(back, piece, **options):
        return block_product(rows, weight, start_of(back, piece), width, **options)

    last = first_product(rows, weight, start_of(1, 0), width)
    moving, owns = [move(last, 0)], []
    for piece in range(1, PIECES):
        last, ids = partial(1, piece, after=[last], ids=ids)
        moving.append(move(last, piece))

    all_ids = [ids]
    for x in range(1, req_total):
        all_ids.append(lax.ppermute(ids, "req", [(i, i ^ x) for i in range(req_total)]))
    packs, starts, ends = pick_adapters(me_req, table, all_ids, lens, down, up, [last])
    for x in range(1, req_total):
        packs[x] = lax.ppermute(packs[x], "req", [(i, i ^ x) for i in range(req_total)])

    last = starts
    for step in range(1, steps):
        for piece in range(PIECES):
            if step == steps - 1 and piece == PIECES - 1:
                low = low_sums(starts, ends, rows, packs, rank, [last])
                lows = [low]
                for x in range(1, tp_total):
                    pairs = [(i, i ^ x) for i in range(tp_total)]
                    lows.append(lax.ppermute(low, "tp", pairs))
                last = low
            last = partial(1 + step, piece, addends=[moving[piece]], after=[last])
            moving[piece] = move(last, piece)
            if step == 1:
                last = partial(0, piece, after=[last], cost=LARGE)
                owns.append(last)

    terms = adapter_term(starts, ends, lows, owns, packs, [last])
    result = None
    for piece in range(PIECES):
        cost = SMALL if piece == PIECES - 1 else LARGE
        result = finish(terms[piece], [moving[piece]], piece, PIECES, result, cost)
    return result


def solution(mesh):
    return jax.shard_map(
        functools.partial(local, mesh.shape["req"], mesh.shape["tp"]),
        mesh=mesh,
        in_specs=(
            P(("groups", "req"), "tp"),
            P("tp", None),
            P(("groups", "req"), None, "tp"),
            P(("groups", "req"), None, "tp"),
            P("groups"),
            P(("groups", "req"), None),
            P(("groups", "req"), None),
        ),
        out_specs=P(("groups", "req"), "tp"),
        check_vma=False,
    )
```

```python
import functools

import jax
import jax.numpy as jnp
from jax import lax
from jax.experimental import pallas as pl
from jax.experimental.pallas import tpu as pltpu
from jax.sharding import PartitionSpec as P

CAP = 6
PIECES = 2
VMEM_LIMIT = 20 * 1024 * 1024
F32 = jnp.float32
BF16 = jnp.bfloat16
SMALL = pl.CostEstimate(flops=1000, bytes_accessed=1000, transcendentals=0)
LARGE = pl.CostEstimate(flops=2 * 10**10, bytes_accessed=1000, transcendentals=0)


def product_kernel(addends, with_ids, first_ref, rows_ref, weight_ref, *rest):
    out_ref = rest[-1 - with_ids]
    total = jnp.dot(rows_ref[...], weight_ref[...], preferred_element_type=F32)
    for ref in rest[:addends]:
        total = total + ref[...].astype(F32)
    out_ref[...] = total.astype(out_ref.dtype)
    if with_ids:
        ids_ref, ids_out_ref = rest[addends], rest[-1]
        for s in range(ids_ref.shape[1]):
            ids_out_ref[0, s] = ids_ref[0, s]


def block_product(rows, weight, first, width, addends=(), after=(), ids=None, cost=SMALL):
    row_total, depth = rows.shape
    tile = min(256, width)
    with_ids = ids is not None
    smem = pl.BlockSpec(memory_space=pltpu.SMEM)
    hbm = pl.BlockSpec(memory_space=pl.ANY)
    columns = pl.BlockSpec((row_total, tile), lambda j, t: (0, j))
    out_specs, out_shape = [columns], [jax.ShapeDtypeStruct((row_total, width), BF16)]
    if with_ids:
        out_specs.append(smem)
        out_shape.append(jax.ShapeDtypeStruct(ids.shape, ids.dtype))
    out = pl.pallas_call(
        functools.partial(product_kernel, len(addends), with_ids),
        grid_spec=pltpu.PrefetchScalarGridSpec(
            num_scalar_prefetch=1,
            grid=(width // tile,),
            in_specs=[
                pl.BlockSpec((row_total, depth), lambda j, t: (0, 0)),
                pl.BlockSpec((depth, tile), lambda j, t: (0, t[0] + j)),
            ]
            + [columns] * len(addends)
            + [smem] * with_ids
            + [hbm] * len(after),
            out_specs=out_specs,
        ),
        out_shape=out_shape,
        compiler_params=pltpu.CompilerParams(vmem_limit_bytes=VMEM_LIMIT),
        cost_estimate=cost,
        name="block_product",
    )((first // tile).reshape(1), rows, weight, *addends, *([ids] if with_ids else []), *after)
    return out if with_ids else out[0]


def first_kernel(chunk, first_ref, rows_ref, weight_ref, out_ref, lhs_ref, rhs_ref, acc_ref, sems):
    columns = pl.ds(pl.multiple_of(first_ref[0], 128), out_ref.shape[1])
    chunks = lhs_ref.shape[0]

    def copies(k):
        part = pl.ds(k * chunk, chunk)
        return (
            pltpu.make_async_copy(rows_ref.at[:, part], lhs_ref.at[k], sems.at[0, k]),
            pltpu.make_async_copy(weight_ref.at[part, columns], rhs_ref.at[k], sems.at[1, k]),
        )

    for k in range(chunks):
        for copy in copies(k):
            copy.start()
    for k in range(chunks):
        for copy in copies(k):
            copy.wait()
        part = jnp.dot(lhs_ref[k], rhs_ref[k], preferred_element_type=F32)
        if k == 0:
            acc_ref[...] = part
        elif k < chunks - 1:
            acc_ref[...] += part
        else:
            out_ref[...] = (acc_ref[...] + part).astype(out_ref.dtype)


def first_product(rows, weight, first, width):
    row_total, depth = rows.shape
    chunk = min(512, depth // 2)
    chunks = depth // chunk
    hbm = pl.BlockSpec(memory_space=pltpu.HBM)
    return pl.pallas_call(
        functools.partial(first_kernel, chunk),
        in_specs=[pl.BlockSpec(memory_space=pltpu.SMEM), hbm, hbm],
        out_specs=pl.BlockSpec(memory_space=pltpu.VMEM),
        out_shape=jax.ShapeDtypeStruct((row_total, width), BF16),
        scratch_shapes=[
            pltpu.VMEM((chunks, row_total, chunk), BF16),
            pltpu.VMEM((chunks, chunk, width), BF16),
            pltpu.VMEM((row_total, width), F32),
            pltpu.SemaphoreType.DMA((2, chunks)),
        ],
        compiler_params=pltpu.CompilerParams(vmem_limit_bytes=VMEM_LIMIT),
        cost_estimate=SMALL,
        name="first_product",
    )(first.reshape(1), pltpu.with_memory_space_constraint(rows, pltpu.HBM), weight)


def pick_kernel(peers, afters, me_ref, table_ref, lens_ref, *rest):
    ids_refs = rest[:peers]
    down_ref, up_ref = rest[peers : peers + 2]
    rest = rest[peers + 2 + afters :]
    packs, (start_ref, end_ref, pick_ref, count_ref, sem) = rest[:peers], rest[peers:]
    segs = lens_ref.shape[1]
    share, _, depth = down_ref.shape
    cols = up_ref.shape[2]
    me = me_ref[0]

    def clear(q, carry):
        pick_ref[q] = 0
        start_ref[q] = 0
        end_ref[q] = 0
        return carry

    lax.fori_loop(0, peers * CAP, clear, 0, unroll=8)
    for x in range(peers):
        count_ref[x] = 0

    def copies(x, c, source):
        pack = packs[x].at[c]
        return (
            pltpu.make_async_copy(down_ref.at[source], pack.at[:, pl.ds(0, depth)], sem),
            pltpu.make_async_copy(up_ref.at[source], pack.at[:, pl.ds(depth, cols)], sem),
        )

    for x in reversed(range(peers)):

        def choose(s, count):
            local = table_ref[ids_refs[x][0, s]] - me * share
            mine = jnp.logical_and(local >= 0, local < share)

            @pl.when(jnp.logical_and(mine, count < CAP))
            def _():
                pick_ref[x * CAP + count] = local

            return count + mine.astype(jnp.int32)

        lax.fori_loop(0, segs, choose, 0, unroll=4)
        for c in range(CAP):
            for copy in copies(x, c, pick_ref[x * CAP + c]):
                copy.start()

    def place(s, first):
        x = lax.bitwise_xor(table_ref[ids_refs[0][0, s]] // share, me)
        count = count_ref[x]
        last = first + lens_ref[0, s]

        @pl.when(count < CAP)
        def _():
            start_ref[x * CAP + count] = first
            end_ref[x * CAP + count] = last

        count_ref[x] = count + 1
        return last

    lax.fori_loop(0, segs, place, 0, unroll=4)

    for x in range(peers):
        for c in range(CAP):
            for copy in copies(x, c, 0):
                copy.wait()


def pick_adapters(me, table, all_ids, lens, down, up, after):
    peers = len(all_ids)
    _, rank, depth = down.shape
    cols = up.shape[2]
    smem = pl.BlockSpec(memory_space=pltpu.SMEM)
    vmem = pl.BlockSpec(memory_space=pltpu.VMEM)
    hbm = pl.BlockSpec(memory_space=pl.ANY)
    out = pl.pallas_call(
        functools.partial(pick_kernel, peers, len(after)),
        in_specs=[smem] * (3 + peers) + [hbm] * (2 + len(after)),
        out_specs=[vmem] * peers + [smem, smem],
        out_shape=[jax.ShapeDtypeStruct((CAP, rank, depth + cols), BF16)] * peers
        + [jax.ShapeDtypeStruct((peers * CAP,), jnp.int32)] * 2,
        scratch_shapes=[
            pltpu.SMEM((peers * CAP,), jnp.int32),
            pltpu.SMEM((peers,), jnp.int32),
            pltpu.SemaphoreType.DMA,
        ],
        compiler_params=pltpu.CompilerParams(vmem_limit_bytes=VMEM_LIMIT),
        cost_estimate=SMALL,
        name="pick_adapters",
    )(me.reshape(1), table, lens, *all_ids, down, up, *after)
    return list(out[:-2]), out[-2], out[-1]


def pack_spec(pack, first, width):
    return pl.BlockSpec(pack.shape[:2] + (width,), lambda i: (0, 0, first // width))


def low_kernel(peers, start_ref, end_ref, rows_ref, *rest):
    down_refs, out_ref = rest[:peers], rest[-1]
    row_total, depth = rows_ref.shape
    rank = out_ref.shape[0]
    place = lax.broadcasted_iota(jnp.int32, (rank, row_total), 1)
    downs = jnp.concatenate([ref[...].reshape(CAP * rank, depth) for ref in down_refs], axis=0)
    part = lax.dot_general(
        downs, rows_ref[...], (((1,), (1,)), ((), ())), preferred_element_type=F32
    )
    total = jnp.zeros((rank, row_total), F32)
    for q in range(peers * CAP):
        member = jnp.logical_and(place >= start_ref[q], place < end_ref[q])
        total = jnp.where(member, part[q * rank : (q + 1) * rank], total)
    out_ref[...] = total


def low_sums(starts, ends, rows, packs, rank, after):
    row_total, depth = rows.shape
    smem = pl.BlockSpec(memory_space=pltpu.SMEM)
    vmem = pl.BlockSpec(memory_space=pltpu.VMEM)
    return pl.pallas_call(
        functools.partial(low_kernel, len(packs)),
        grid=(1,),
        in_specs=[smem, smem, vmem]
        + [pack_spec(p, 0, depth) for p in packs]
        + [pl.BlockSpec(memory_space=pl.ANY)] * len(after),
        out_specs=vmem,
        out_shape=jax.ShapeDtypeStruct((rank, row_total), F32),
        compiler_params=pltpu.CompilerParams(vmem_limit_bytes=VMEM_LIMIT),
        cost_estimate=SMALL,
        name="low_sums",
    )(starts, ends, rows, *packs, *after)


def term_kernel(lows, pieces, peers, start_ref, end_ref, *rest):
    low_refs, rest = rest[:lows], rest[lows:]
    own_refs, rest = rest[:pieces], rest[pieces:]
    up_refs, out_refs = rest[:peers], rest[-pieces:]
    rank, row_total = low_refs[0].shape
    width = out_refs[0].shape[1]
    cols = width * pieces
    low = low_refs[0][...]
    for ref in low_refs[1:]:
        low = low + ref[...]
    low = low.astype(BF16).astype(F32)
    place = lax.broadcasted_iota(jnp.int32, (rank, row_total), 1)
    spread = []
    for q in range(len(up_refs) * CAP):
        member = jnp.logical_and(place >= start_ref[q], place < end_ref[q])
        spread.append(jnp.where(member, low, 0.0))
    spread = jnp.concatenate(spread, axis=0).astype(BF16)
    ups = jnp.concatenate([ref[...].reshape(CAP * rank, cols) for ref in up_refs], axis=0)
    for piece in range(pieces):
        columns = slice(piece * width, (piece + 1) * width)
        term = lax.dot_general(
            spread, ups[:, columns], (((0,), (0,)), ((), ())), preferred_element_type=F32
        )
        out_refs[piece][...] = own_refs[piece][...].astype(F32) + term


def adapter_term(starts, ends, lows, owns, packs, after):
    row_total, width = owns[0].shape
    cols = width * len(owns)
    smem = pl.BlockSpec(memory_space=pltpu.SMEM)
    vmem = pl.BlockSpec(memory_space=pltpu.VMEM)
    depth = packs[0].shape[2] - cols
    return pl.pallas_call(
        functools.partial(term_kernel, len(lows), len(owns), len(packs)),
        grid=(1,),
        in_specs=[smem, smem]
        + [vmem] * (len(lows) + len(owns))
        + [pack_spec(p, depth, cols) for p in packs]
        + [pl.BlockSpec(memory_space=pl.ANY)] * len(after),
        out_specs=[vmem] * len(owns),
        out_shape=[jax.ShapeDtypeStruct((row_total, width), F32)] * len(owns),
        compiler_params=pltpu.CompilerParams(vmem_limit_bytes=VMEM_LIMIT),
        cost_estimate=SMALL,
        name="adapter_term",
    )(starts, ends, *lows, *owns, *packs, *after)


def finish_kernel(addends, term_ref, *rest):
    total = term_ref[...]
    for ref in rest[:addends]:
        total = total + ref[...].astype(F32)
    rest[-1][...] = total.astype(rest[-1].dtype)


def finish(term, arrivals, piece, pieces, result, cost):
    row_total, width = term.shape
    height = min(row_total, 128)
    block = pl.BlockSpec((height, width), lambda i: (i, 0))
    held = [] if result is None else [result]
    return pl.pallas_call(
        functools.partial(finish_kernel, len(arrivals)),
        grid=(row_total // height,),
        in_specs=[block] * (1 + len(arrivals)) + [pl.BlockSpec(memory_space=pl.ANY)] * len(held),
        out_specs=pl.BlockSpec((height, width), lambda i: (i, piece)),
        out_shape=jax.ShapeDtypeStruct((row_total, width * pieces), BF16),
        input_output_aliases={1 + len(arrivals): 0} if held else {},
        compiler_params=pltpu.CompilerParams(vmem_limit_bytes=VMEM_LIMIT),
        cost_estimate=cost,
        name="finish",
    )(term, *arrivals, *held)


def local(req_total, tp_total, rows, weight, down, up, table, ids, lens):
    rank = down.shape[1]
    cols = up.shape[2]
    width = cols // PIECES
    me_req = lax.axis_index("req").astype(jnp.int32)
    me = lax.axis_index("tp").astype(jnp.int32)
    steps = tp_total - 1

    def move(value, piece):
        pairs = []
        for r in range(req_total):
            way = 1 if (r + piece) % 2 == 0 else tp_total - 1
            for i in range(tp_total):
                pairs.append((r * tp_total + i, r * tp_total + (i + way) % tp_total))
        return lax.ppermute(value, ("req", "tp"), pairs)

    def start_of(back, piece):
        behind = jnp.where(lax.rem(me_req + piece, 2) == 0, tp_total - back, back)
        block = lax.rem(me + behind, tp_total)
        return block * cols + piece * width

    def partial(back, piece, **options):
        return block_product(rows, weight, start_of(back, piece), width, **options)

    last = first_product(rows, weight, start_of(1, 0), width)
    moving, owns = [move(last, 0)], []
    for piece in range(1, PIECES):
        last, ids = partial(1, piece, after=[last], ids=ids)
        moving.append(move(last, piece))

    all_ids = [ids]
    for x in range(1, req_total):
        all_ids.append(lax.ppermute(ids, "req", [(i, i ^ x) for i in range(req_total)]))
    packs, starts, ends = pick_adapters(me_req, table, all_ids, lens, down, up, [last])
    for x in range(1, req_total):
        packs[x] = lax.ppermute(packs[x], "req", [(i, i ^ x) for i in range(req_total)])

    last = starts
    for step in range(1, steps):
        for piece in range(PIECES):
            if step == steps - 1 and piece == PIECES - 1:
                low = low_sums(starts, ends, rows, packs, rank, [last])
                lows = [low]
                for x in range(1, tp_total):
                    pairs = [(i, i ^ x) for i in range(tp_total)]
                    lows.append(lax.ppermute(low, "tp", pairs))
                last = low
            last = partial(1 + step, piece, addends=[moving[piece]], after=[last])
            moving[piece] = move(last, piece)
            if step == 1:
                last = partial(0, piece, after=[last], cost=LARGE)
                owns.append(last)

    terms = adapter_term(starts, ends, lows, owns, packs, [last])
    result = None
    for piece in range(PIECES):
        cost = SMALL if piece == PIECES - 1 else LARGE
        result = finish(terms[piece], [moving[piece]], piece, PIECES, result, cost)
    return result


def solution(mesh):
    return jax.shard_map(
        functools.partial(local, mesh.shape["req"], mesh.shape["tp"]),
        mesh=mesh,
        in_specs=(
            P(("groups", "req"), "tp"),
            P("tp", None),
            P(("groups", "req"), None, "tp"),
            P(("groups", "req"), None, "tp"),
            P("groups"),
            P(("groups", "req"), None),
            P(("groups", "req"), None),
        ),
        out_specs=P(("groups", "req"), "tp"),
        check_vma=False,
    )
```

```python
import functools

import jax
import jax.numpy as jnp
from jax import lax
from jax.experimental import pallas as pl
from jax.experimental.pallas import tpu as pltpu
from jax.sharding import PartitionSpec as P

CAP = 6
PIECES = 2
VMEM_LIMIT = 20 * 1024 * 1024
F32 = jnp.float32
BF16 = jnp.bfloat16
SMALL = pl.CostEstimate(flops=1000, bytes_accessed=1000, transcendentals=0)
LARGE = pl.CostEstimate(flops=2 * 10**10, bytes_accessed=1000, transcendentals=0)


def product_kernel(addends, with_ids, first_ref, rows_ref, weight_ref, *rest):
    out_ref = rest[-1 - with_ids]
    total = jnp.dot(rows_ref[...], weight_ref[...], preferred_element_type=F32)
    for ref in rest[:addends]:
        total = total + ref[...].astype(F32)
    out_ref[...] = total.astype(out_ref.dtype)
    if with_ids:
        ids_ref, ids_out_ref = rest[addends], rest[-1]
        for s in range(ids_ref.shape[1]):
            ids_out_ref[0, s] = ids_ref[0, s]


def block_product(rows, weight, first, width, addends=(), after=(), ids=None, cost=SMALL):
    row_total, depth = rows.shape
    tile = min(256, width)
    with_ids = ids is not None
    smem = pl.BlockSpec(memory_space=pltpu.SMEM)
    hbm = pl.BlockSpec(memory_space=pl.ANY)
    columns = pl.BlockSpec((row_total, tile), lambda j, t: (0, j))
    out_specs, out_shape = [columns], [jax.ShapeDtypeStruct((row_total, width), BF16)]
    if with_ids:
        out_specs.append(smem)
        out_shape.append(jax.ShapeDtypeStruct(ids.shape, ids.dtype))
    out = pl.pallas_call(
        functools.partial(product_kernel, len(addends), with_ids),
        grid_spec=pltpu.PrefetchScalarGridSpec(
            num_scalar_prefetch=1,
            grid=(width // tile,),
            in_specs=[
                pl.BlockSpec((row_total, depth), lambda j, t: (0, 0)),
                pl.BlockSpec((depth, tile), lambda j, t: (0, t[0] + j)),
            ]
            + [columns] * len(addends)
            + [smem] * with_ids
            + [hbm] * len(after),
            out_specs=out_specs,
        ),
        out_shape=out_shape,
        compiler_params=pltpu.CompilerParams(vmem_limit_bytes=VMEM_LIMIT),
        cost_estimate=cost,
        name="block_product",
    )((first // tile).reshape(1), rows, weight, *addends, *([ids] if with_ids else []), *after)
    return out if with_ids else out[0]


def first_kernel(chunk, first_ref, rows_ref, weight_ref, out_ref, lhs_ref, rhs_ref, acc_ref, sems):
    columns = pl.ds(pl.multiple_of(first_ref[0], 128), out_ref.shape[1])
    chunks = lhs_ref.shape[0]

    def copies(k):
        part = pl.ds(k * chunk, chunk)
        return (
            pltpu.make_async_copy(rows_ref.at[:, part], lhs_ref.at[k], sems.at[0, k]),
            pltpu.make_async_copy(weight_ref.at[part, columns], rhs_ref.at[k], sems.at[1, k]),
        )

    for k in range(chunks):
        for copy in copies(k):
            copy.start()
    for k in range(chunks):
        for copy in copies(k):
            copy.wait()
        part = jnp.dot(lhs_ref[k], rhs_ref[k], preferred_element_type=F32)
        if k == 0:
            acc_ref[...] = part
        elif k < chunks - 1:
            acc_ref[...] += part
        else:
            out_ref[...] = (acc_ref[...] + part).astype(out_ref.dtype)


def first_product(rows, weight, first, width):
    row_total, depth = rows.shape
    chunk = min(512, depth // 2)
    chunks = depth // chunk
    hbm = pl.BlockSpec(memory_space=pltpu.HBM)
    return pl.pallas_call(
        functools.partial(first_kernel, chunk),
        in_specs=[pl.BlockSpec(memory_space=pltpu.SMEM), hbm, hbm],
        out_specs=pl.BlockSpec(memory_space=pltpu.VMEM),
        out_shape=jax.ShapeDtypeStruct((row_total, width), BF16),
        scratch_shapes=[
            pltpu.VMEM((chunks, row_total, chunk), BF16),
            pltpu.VMEM((chunks, chunk, width), BF16),
            pltpu.VMEM((row_total, width), F32),
            pltpu.SemaphoreType.DMA((2, chunks)),
        ],
        compiler_params=pltpu.CompilerParams(vmem_limit_bytes=VMEM_LIMIT),
        cost_estimate=SMALL,
        name="first_product",
    )(first.reshape(1), pltpu.with_memory_space_constraint(rows, pltpu.HBM), weight)


def pick_kernel(peers, afters, me_ref, table_ref, lens_ref, *rest):
    ids_refs = rest[:peers]
    down_ref, up_ref = rest[peers : peers + 2]
    rest = rest[peers + 2 + afters :]
    packs, (start_ref, end_ref, pick_ref, count_ref, sem) = rest[:peers], rest[peers:]
    segs = lens_ref.shape[1]
    share, _, depth = down_ref.shape
    cols = up_ref.shape[2]
    me = me_ref[0]

    def clear(q, carry):
        pick_ref[q] = 0
        start_ref[q] = 0
        end_ref[q] = 0
        return carry

    lax.fori_loop(0, peers * CAP, clear, 0, unroll=8)
    for x in range(peers):
        count_ref[x] = 0

    def copies(x, c, source):
        pack = packs[x].at[c]
        return (
            pltpu.make_async_copy(down_ref.at[source], pack.at[:, pl.ds(0, depth)], sem),
            pltpu.make_async_copy(up_ref.at[source], pack.at[:, pl.ds(depth, cols)], sem),
        )

    for x in reversed(range(peers)):

        def choose(s, count):
            local = table_ref[ids_refs[x][0, s]] - me * share
            mine = jnp.logical_and(local >= 0, local < share)

            @pl.when(jnp.logical_and(mine, count < CAP))
            def _():
                pick_ref[x * CAP + count] = local

            return count + mine.astype(jnp.int32)

        lax.fori_loop(0, segs, choose, 0, unroll=4)
        for c in range(CAP):
            for copy in copies(x, c, pick_ref[x * CAP + c]):
                copy.start()

    def place(s, first):
        x = lax.bitwise_xor(table_ref[ids_refs[0][0, s]] // share, me)
        count = count_ref[x]
        last = first + lens_ref[0, s]

        @pl.when(count < CAP)
        def _():
            start_ref[x * CAP + count] = first
            end_ref[x * CAP + count] = last

        count_ref[x] = count + 1
        return last

    lax.fori_loop(0, segs, place, 0, unroll=4)

    for x in range(peers):
        for c in range(CAP):
            for copy in copies(x, c, 0):
                copy.wait()


def pick_adapters(me, table, all_ids, lens, down, up, after):
    peers = len(all_ids)
    _, rank, depth = down.shape
    cols = up.shape[2]
    smem = pl.BlockSpec(memory_space=pltpu.SMEM)
    vmem = pl.BlockSpec(memory_space=pltpu.VMEM)
    hbm = pl.BlockSpec(memory_space=pl.ANY)
    out = pl.pallas_call(
        functools.partial(pick_kernel, peers, len(after)),
        in_specs=[smem] * (3 + peers) + [hbm] * (2 + len(after)),
        out_specs=[vmem] * peers + [smem, smem],
        out_shape=[jax.ShapeDtypeStruct((CAP, rank, depth + cols), BF16)] * peers
        + [jax.ShapeDtypeStruct((peers * CAP,), jnp.int32)] * 2,
        scratch_shapes=[
            pltpu.SMEM((peers * CAP,), jnp.int32),
            pltpu.SMEM((peers,), jnp.int32),
            pltpu.SemaphoreType.DMA,
        ],
        compiler_params=pltpu.CompilerParams(vmem_limit_bytes=VMEM_LIMIT),
        cost_estimate=SMALL,
        name="pick_adapters",
    )(me.reshape(1), table, lens, *all_ids, down, up, *after)
    return list(out[:-2]), out[-2], out[-1]


def pack_spec(pack, first, width):
    return pl.BlockSpec(pack.shape[:2] + (width,), lambda i: (0, 0, first // width))


def low_kernel(peers, start_ref, end_ref, rows_ref, *rest):
    down_refs, out_ref = rest[:peers], rest[-1]
    row_total, depth = rows_ref.shape
    rank = out_ref.shape[0]
    place = lax.broadcasted_iota(jnp.int32, (rank, row_total), 1)
    downs = jnp.concatenate([ref[...].reshape(CAP * rank, depth) for ref in down_refs], axis=0)
    part = lax.dot_general(
        downs, rows_ref[...], (((1,), (1,)), ((), ())), preferred_element_type=F32
    )
    total = jnp.zeros((rank, row_total), F32)
    for q in range(peers * CAP):
        member = jnp.logical_and(place >= start_ref[q], place < end_ref[q])
        total = jnp.where(member, part[q * rank : (q + 1) * rank], total)
    out_ref[...] = total


def low_sums(starts, ends, rows, packs, rank, after):
    row_total, depth = rows.shape
    smem = pl.BlockSpec(memory_space=pltpu.SMEM)
    vmem = pl.BlockSpec(memory_space=pltpu.VMEM)
    return pl.pallas_call(
        functools.partial(low_kernel, len(packs)),
        grid=(1,),
        in_specs=[smem, smem, vmem]
        + [pack_spec(p, 0, depth) for p in packs]
        + [pl.BlockSpec(memory_space=pl.ANY)] * len(after),
        out_specs=vmem,
        out_shape=jax.ShapeDtypeStruct((rank, row_total), F32),
        compiler_params=pltpu.CompilerParams(vmem_limit_bytes=VMEM_LIMIT),
        cost_estimate=SMALL,
        name="low_sums",
    )(starts, ends, rows, *packs, *after)


def term_kernel(lows, pieces, peers, start_ref, end_ref, *rest):
    low_refs, rest = rest[:lows], rest[lows:]
    own_refs, rest = rest[:pieces], rest[pieces:]
    up_refs, out_refs = rest[:peers], rest[-pieces:]
    rank, row_total = low_refs[0].shape
    width = out_refs[0].shape[1]
    cols = width * pieces
    low = low_refs[0][...]
    for ref in low_refs[1:]:
        low = low + ref[...]
    low = low.astype(BF16).astype(F32)
    place = lax.broadcasted_iota(jnp.int32, (rank, row_total), 1)
    spread = []
    for q in range(len(up_refs) * CAP):
        member = jnp.logical_and(place >= start_ref[q], place < end_ref[q])
        spread.append(jnp.where(member, low, 0.0))
    spread = jnp.concatenate(spread, axis=0).astype(BF16)
    ups = jnp.concatenate([ref[...].reshape(CAP * rank, cols) for ref in up_refs], axis=0)
    for piece in range(pieces):
        columns = slice(piece * width, (piece + 1) * width)
        term = lax.dot_general(
            spread, ups[:, columns], (((0,), (0,)), ((), ())), preferred_element_type=F32
        )
        out_refs[piece][...] = own_refs[piece][...].astype(F32) + term


def adapter_term(starts, ends, lows, owns, packs, after):
    row_total, width = owns[0].shape
    cols = width * len(owns)
    smem = pl.BlockSpec(memory_space=pltpu.SMEM)
    vmem = pl.BlockSpec(memory_space=pltpu.VMEM)
    depth = packs[0].shape[2] - cols
    return pl.pallas_call(
        functools.partial(term_kernel, len(lows), len(owns), len(packs)),
        grid=(1,),
        in_specs=[smem, smem]
        + [vmem] * (len(lows) + len(owns))
        + [pack_spec(p, depth, cols) for p in packs]
        + [pl.BlockSpec(memory_space=pl.ANY)] * len(after),
        out_specs=[vmem] * len(owns),
        out_shape=[jax.ShapeDtypeStruct((row_total, width), F32)] * len(owns),
        compiler_params=pltpu.CompilerParams(vmem_limit_bytes=VMEM_LIMIT),
        cost_estimate=SMALL,
        name="adapter_term",
    )(starts, ends, *lows, *owns, *packs, *after)


def finish_kernel(addends, term_ref, *rest):
    total = term_ref[...]
    for ref in rest[:addends]:
        total = total + ref[...].astype(F32)
    rest[-1][...] = total.astype(rest[-1].dtype)


def finish(term, arrivals, piece, pieces, result, cost):
    row_total, width = term.shape
    height = min(row_total, 128)
    block = pl.BlockSpec((height, width), lambda i: (i, 0))
    held = [] if result is None else [result]
    return pl.pallas_call(
        functools.partial(finish_kernel, len(arrivals)),
        grid=(row_total // height,),
        in_specs=[block] * (1 + len(arrivals)) + [pl.BlockSpec(memory_space=pl.ANY)] * len(held),
        out_specs=pl.BlockSpec((height, width), lambda i: (i, piece)),
        out_shape=jax.ShapeDtypeStruct((row_total, width * pieces), BF16),
        input_output_aliases={1 + len(arrivals): 0} if held else {},
        compiler_params=pltpu.CompilerParams(vmem_limit_bytes=VMEM_LIMIT),
        cost_estimate=cost,
        name="finish",
    )(term, *arrivals, *held)


def local(req_total, tp_total, rows, weight, down, up, table, ids, lens):
    weight = pltpu.with_memory_space_constraint(weight, pltpu.HBM)
    down = pltpu.with_memory_space_constraint(down, pltpu.HBM)
    up = pltpu.with_memory_space_constraint(up, pltpu.HBM)
    rank = down.shape[1]
    cols = up.shape[2]
    width = cols // PIECES
    me_req = lax.axis_index("req").astype(jnp.int32)
    me = lax.axis_index("tp").astype(jnp.int32)
    steps = tp_total - 1

    def move(value, piece):
        pairs = []
        for r in range(req_total):
            way = 1 if (r + piece) % 2 == 0 else tp_total - 1
            for i in range(tp_total):
                pairs.append((r * tp_total + i, r * tp_total + (i + way) % tp_total))
        return lax.ppermute(value, ("req", "tp"), pairs)

    def start_of(back, piece):
        behind = jnp.where(lax.rem(me_req + piece, 2) == 0, tp_total - back, back)
        block = lax.rem(me + behind, tp_total)
        return block * cols + piece * width

    def partial(back, piece, **options):
        return block_product(rows, weight, start_of(back, piece), width, **options)

    last = first_product(rows, weight, start_of(1, 0), width)
    moving, owns = [move(last, 0)], []
    for piece in range(1, PIECES):
        last, ids = partial(1, piece, after=[last], ids=ids)
        moving.append(move(last, piece))

    all_ids = [ids]
    for x in range(1, req_total):
        all_ids.append(lax.ppermute(ids, "req", [(i, i ^ x) for i in range(req_total)]))
    packs, starts, ends = pick_adapters(me_req, table, all_ids, lens, down, up, [last])
    for x in range(1, req_total):
        packs[x] = lax.ppermute(packs[x], "req", [(i, i ^ x) for i in range(req_total)])

    last = starts
    for step in range(1, steps):
        for piece in range(PIECES):
            if step == steps - 1 and piece == PIECES - 1:
                low = low_sums(starts, ends, rows, packs, rank, [last])
                lows = [low]
                for x in range(1, tp_total):
                    pairs = [(i, i ^ x) for i in range(tp_total)]
                    lows.append(lax.ppermute(low, "tp", pairs))
                last = low
            last = partial(1 + step, piece, addends=[moving[piece]], after=[last])
            moving[piece] = move(last, piece)
            if step == 1:
                last = partial(0, piece, after=[last], cost=LARGE)
                owns.append(last)

    terms = adapter_term(starts, ends, lows, owns, packs, [last])
    result = None
    for piece in range(PIECES):
        cost = SMALL if piece == PIECES - 1 else LARGE
        result = finish(terms[piece], [moving[piece]], piece, PIECES, result, cost)
    return result


def solution(mesh):
    return jax.shard_map(
        functools.partial(local, mesh.shape["req"], mesh.shape["tp"]),
        mesh=mesh,
        in_specs=(
            P(("groups", "req"), "tp"),
            P("tp", None),
            P(("groups", "req"), None, "tp"),
            P(("groups", "req"), None, "tp"),
            P("groups"),
            P(("groups", "req"), None),
            P(("groups", "req"), None),
        ),
        out_specs=P(("groups", "req"), "tp"),
        check_vma=False,
    )
```

```python
import functools

import jax
import jax.numpy as jnp
from jax import lax
from jax.experimental import pallas as pl
from jax.experimental.pallas import tpu as pltpu
from jax.sharding import PartitionSpec as P

CAP = 6
PIECES = 2
VMEM_LIMIT = 20 * 1024 * 1024
F32 = jnp.float32
BF16 = jnp.bfloat16
SMALL = pl.CostEstimate(flops=1000, bytes_accessed=1000, transcendentals=0)
LARGE = pl.CostEstimate(flops=2 * 10**10, bytes_accessed=1000, transcendentals=0)


def product_kernel(addends, with_ids, first_ref, rows_ref, weight_ref, *rest):
    out_ref = rest[-1 - with_ids]
    total = jnp.dot(rows_ref[...], weight_ref[...], preferred_element_type=F32)
    for ref in rest[:addends]:
        total = total + ref[...].astype(F32)
    out_ref[...] = total.astype(out_ref.dtype)
    if with_ids:
        ids_ref, ids_out_ref = rest[addends], rest[-1]
        for s in range(ids_ref.shape[1]):
            ids_out_ref[0, s] = ids_ref[0, s]


def block_product(rows, weight, first, width, addends=(), after=(), ids=None, cost=SMALL):
    row_total, depth = rows.shape
    tile = min(256, width)
    with_ids = ids is not None
    smem = pl.BlockSpec(memory_space=pltpu.SMEM)
    hbm = pl.BlockSpec(memory_space=pl.ANY)
    columns = pl.BlockSpec((row_total, tile), lambda j, t: (0, j))
    out_specs, out_shape = [columns], [jax.ShapeDtypeStruct((row_total, width), BF16)]
    if with_ids:
        out_specs.append(smem)
        out_shape.append(jax.ShapeDtypeStruct(ids.shape, ids.dtype))
    out = pl.pallas_call(
        functools.partial(product_kernel, len(addends), with_ids),
        grid_spec=pltpu.PrefetchScalarGridSpec(
            num_scalar_prefetch=1,
            grid=(width // tile,),
            in_specs=[
                pl.BlockSpec((row_total, depth), lambda j, t: (0, 0)),
                pl.BlockSpec((depth, tile), lambda j, t: (0, t[0] + j)),
            ]
            + [columns] * len(addends)
            + [smem] * with_ids
            + [hbm] * len(after),
            out_specs=out_specs,
        ),
        out_shape=out_shape,
        compiler_params=pltpu.CompilerParams(vmem_limit_bytes=VMEM_LIMIT),
        cost_estimate=cost,
        name="block_product",
    )((first // tile).reshape(1), rows, weight, *addends, *([ids] if with_ids else []), *after)
    return out if with_ids else out[0]


def first_kernel(chunk, first_ref, rows_ref, weight_ref, out_ref, lhs_ref, rhs_ref, acc_ref, sems):
    columns = pl.ds(pl.multiple_of(first_ref[0], 128), out_ref.shape[1])
    chunks = lhs_ref.shape[0]

    def copies(k):
        part = pl.ds(k * chunk, chunk)
        return (
            pltpu.make_async_copy(rows_ref.at[:, part], lhs_ref.at[k], sems.at[0, k]),
            pltpu.make_async_copy(weight_ref.at[part, columns], rhs_ref.at[k], sems.at[1, k]),
        )

    for copy in copies(0):
        copy.start()
    for k in range(chunks):
        if k + 1 < chunks:
            for copy in copies(k + 1):
                copy.start()
        for copy in copies(k):
            copy.wait()
        part = jnp.dot(lhs_ref[k], rhs_ref[k], preferred_element_type=F32)
        if k == 0:
            acc_ref[...] = part
        elif k < chunks - 1:
            acc_ref[...] += part
        else:
            out_ref[...] = (acc_ref[...] + part).astype(out_ref.dtype)


def first_product(rows, weight, first, width):
    row_total, depth = rows.shape
    chunk = min(512, depth // 2)
    chunks = depth // chunk
    hbm = pl.BlockSpec(memory_space=pltpu.HBM)
    return pl.pallas_call(
        functools.partial(first_kernel, chunk),
        in_specs=[pl.BlockSpec(memory_space=pltpu.SMEM), hbm, hbm],
        out_specs=pl.BlockSpec(memory_space=pltpu.VMEM),
        out_shape=jax.ShapeDtypeStruct((row_total, width), BF16),
        scratch_shapes=[
            pltpu.VMEM((chunks, row_total, chunk), BF16),
            pltpu.VMEM((chunks, chunk, width), BF16),
            pltpu.VMEM((row_total, width), F32),
            pltpu.SemaphoreType.DMA((2, chunks)),
        ],
        compiler_params=pltpu.CompilerParams(vmem_limit_bytes=VMEM_LIMIT),
        cost_estimate=SMALL,
        name="first_product",
    )(first.reshape(1), pltpu.with_memory_space_constraint(rows, pltpu.HBM), weight)


def pick_kernel(peers, afters, me_ref, table_ref, lens_ref, *rest):
    ids_refs = rest[:peers]
    down_ref, up_ref = rest[peers : peers + 2]
    rest = rest[peers + 2 + afters :]
    packs, (start_ref, end_ref, pick_ref, count_ref, sem) = rest[:peers], rest[peers:]
    segs = lens_ref.shape[1]
    share, _, depth = down_ref.shape
    cols = up_ref.shape[2]
    me = me_ref[0]

    def clear(q, carry):
        pick_ref[q] = 0
        start_ref[q] = 0
        end_ref[q] = 0
        return carry

    lax.fori_loop(0, peers * CAP, clear, 0, unroll=8)
    for x in range(peers):
        count_ref[x] = 0

    def copies(x, c, source):
        pack = packs[x].at[c]
        return (
            pltpu.make_async_copy(down_ref.at[source], pack.at[:, pl.ds(0, depth)], sem),
            pltpu.make_async_copy(up_ref.at[source], pack.at[:, pl.ds(depth, cols)], sem),
        )

    for x in reversed(range(peers)):

        def choose(s, count):
            local = table_ref[ids_refs[x][0, s]] - me * share
            mine = jnp.logical_and(local >= 0, local < share)

            @pl.when(jnp.logical_and(mine, count < CAP))
            def _():
                pick_ref[x * CAP + count] = local

            return count + mine.astype(jnp.int32)

        lax.fori_loop(0, segs, choose, 0, unroll=4)
        for c in range(CAP):
            for copy in copies(x, c, pick_ref[x * CAP + c]):
                copy.start()

    def place(s, first):
        x = lax.bitwise_xor(table_ref[ids_refs[0][0, s]] // share, me)
        count = count_ref[x]
        last = first + lens_ref[0, s]

        @pl.when(count < CAP)
        def _():
            start_ref[x * CAP + count] = first
            end_ref[x * CAP + count] = last

        count_ref[x] = count + 1
        return last

    lax.fori_loop(0, segs, place, 0, unroll=4)

    for x in range(peers):
        for c in range(CAP):
            for copy in copies(x, c, 0):
                copy.wait()


def pick_adapters(me, table, all_ids, lens, down, up, after):
    peers = len(all_ids)
    _, rank, depth = down.shape
    cols = up.shape[2]
    smem = pl.BlockSpec(memory_space=pltpu.SMEM)
    vmem = pl.BlockSpec(memory_space=pltpu.VMEM)
    hbm = pl.BlockSpec(memory_space=pl.ANY)
    out = pl.pallas_call(
        functools.partial(pick_kernel, peers, len(after)),
        in_specs=[smem] * (3 + peers) + [hbm] * (2 + len(after)),
        out_specs=[vmem] * peers + [smem, smem],
        out_shape=[jax.ShapeDtypeStruct((CAP, rank, depth + cols), BF16)] * peers
        + [jax.ShapeDtypeStruct((peers * CAP,), jnp.int32)] * 2,
        scratch_shapes=[
            pltpu.SMEM((peers * CAP,), jnp.int32),
            pltpu.SMEM((peers,), jnp.int32),
            pltpu.SemaphoreType.DMA,
        ],
        compiler_params=pltpu.CompilerParams(vmem_limit_bytes=VMEM_LIMIT),
        cost_estimate=SMALL,
        name="pick_adapters",
    )(me.reshape(1), table, lens, *all_ids, down, up, *after)
    return list(out[:-2]), out[-2], out[-1]


def pack_spec(pack, first, width):
    return pl.BlockSpec(pack.shape[:2] + (width,), lambda i: (0, 0, first // width))


def low_kernel(peers, start_ref, end_ref, rows_ref, *rest):
    down_refs, out_ref = rest[:peers], rest[-1]
    row_total, depth = rows_ref.shape
    rank = out_ref.shape[0]
    place = lax.broadcasted_iota(jnp.int32, (rank, row_total), 1)
    downs = jnp.concatenate([ref[...].reshape(CAP * rank, depth) for ref in down_refs], axis=0)
    part = lax.dot_general(
        downs, rows_ref[...], (((1,), (1,)), ((), ())), preferred_element_type=F32
    )
    total = jnp.zeros((rank, row_total), F32)
    for q in range(peers * CAP):
        member = jnp.logical_and(place >= start_ref[q], place < end_ref[q])
        total = jnp.where(member, part[q * rank : (q + 1) * rank], total)
    out_ref[...] = total


def low_sums(starts, ends, rows, packs, rank, after):
    row_total, depth = rows.shape
    smem = pl.BlockSpec(memory_space=pltpu.SMEM)
    vmem = pl.BlockSpec(memory_space=pltpu.VMEM)
    return pl.pallas_call(
        functools.partial(low_kernel, len(packs)),
        grid=(1,),
        in_specs=[smem, smem, vmem]
        + [pack_spec(p, 0, depth) for p in packs]
        + [pl.BlockSpec(memory_space=pl.ANY)] * len(after),
        out_specs=vmem,
        out_shape=jax.ShapeDtypeStruct((rank, row_total), F32),
        compiler_params=pltpu.CompilerParams(vmem_limit_bytes=VMEM_LIMIT),
        cost_estimate=SMALL,
        name="low_sums",
    )(starts, ends, rows, *packs, *after)


def term_kernel(lows, pieces, peers, start_ref, end_ref, *rest):
    low_refs, rest = rest[:lows], rest[lows:]
    own_refs, rest = rest[:pieces], rest[pieces:]
    up_refs, out_refs = rest[:peers], rest[-pieces:]
    rank, row_total = low_refs[0].shape
    width = out_refs[0].shape[1]
    cols = width * pieces
    low = low_refs[0][...]
    for ref in low_refs[1:]:
        low = low + ref[...]
    low = low.astype(BF16).astype(F32)
    place = lax.broadcasted_iota(jnp.int32, (rank, row_total), 1)
    spread = []
    for q in range(len(up_refs) * CAP):
        member = jnp.logical_and(place >= start_ref[q], place < end_ref[q])
        spread.append(jnp.where(member, low, 0.0))
    spread = jnp.concatenate(spread, axis=0).astype(BF16)
    ups = jnp.concatenate([ref[...].reshape(CAP * rank, cols) for ref in up_refs], axis=0)
    for piece in range(pieces):
        columns = slice(piece * width, (piece + 1) * width)
        term = lax.dot_general(
            spread, ups[:, columns], (((0,), (0,)), ((), ())), preferred_element_type=F32
        )
        out_refs[piece][...] = own_refs[piece][...].astype(F32) + term


def adapter_term(starts, ends, lows, owns, packs, after):
    row_total, width = owns[0].shape
    cols = width * len(owns)
    smem = pl.BlockSpec(memory_space=pltpu.SMEM)
    vmem = pl.BlockSpec(memory_space=pltpu.VMEM)
    depth = packs[0].shape[2] - cols
    return pl.pallas_call(
        functools.partial(term_kernel, len(lows), len(owns), len(packs)),
        grid=(1,),
        in_specs=[smem, smem]
        + [vmem] * (len(lows) + len(owns))
        + [pack_spec(p, depth, cols) for p in packs]
        + [pl.BlockSpec(memory_space=pl.ANY)] * len(after),
        out_specs=[vmem] * len(owns),
        out_shape=[jax.ShapeDtypeStruct((row_total, width), F32)] * len(owns),
        compiler_params=pltpu.CompilerParams(vmem_limit_bytes=VMEM_LIMIT),
        cost_estimate=SMALL,
        name="adapter_term",
    )(starts, ends, *lows, *owns, *packs, *after)


def finish_kernel(addends, term_ref, *rest):
    total = term_ref[...]
    for ref in rest[:addends]:
        total = total + ref[...].astype(F32)
    rest[-1][...] = total.astype(rest[-1].dtype)


def finish(term, arrivals, piece, pieces, result, cost):
    row_total, width = term.shape
    height = min(row_total, 128)
    block = pl.BlockSpec((height, width), lambda i: (i, 0))
    held = [] if result is None else [result]
    return pl.pallas_call(
        functools.partial(finish_kernel, len(arrivals)),
        grid=(row_total // height,),
        in_specs=[block] * (1 + len(arrivals)) + [pl.BlockSpec(memory_space=pl.ANY)] * len(held),
        out_specs=pl.BlockSpec((height, width), lambda i: (i, piece)),
        out_shape=jax.ShapeDtypeStruct((row_total, width * pieces), BF16),
        input_output_aliases={1 + len(arrivals): 0} if held else {},
        compiler_params=pltpu.CompilerParams(vmem_limit_bytes=VMEM_LIMIT),
        cost_estimate=cost,
        name="finish",
    )(term, *arrivals, *held)


def local(req_total, tp_total, rows, weight, down, up, table, ids, lens):
    weight = pltpu.with_memory_space_constraint(weight, pltpu.HBM)
    down = pltpu.with_memory_space_constraint(down, pltpu.HBM)
    up = pltpu.with_memory_space_constraint(up, pltpu.HBM)
    rank = down.shape[1]
    cols = up.shape[2]
    width = cols // PIECES
    me_req = lax.axis_index("req").astype(jnp.int32)
    me = lax.axis_index("tp").astype(jnp.int32)
    steps = tp_total - 1

    def move(value, piece):
        pairs = []
        for r in range(req_total):
            way = 1 if (r + piece) % 2 == 0 else tp_total - 1
            for i in range(tp_total):
                pairs.append((r * tp_total + i, r * tp_total + (i + way) % tp_total))
        return lax.ppermute(value, ("req", "tp"), pairs)

    def start_of(back, piece):
        behind = jnp.where(lax.rem(me_req + piece, 2) == 0, tp_total - back, back)
        block = lax.rem(me + behind, tp_total)
        return block * cols + piece * width

    def partial(back, piece, **options):
        return block_product(rows, weight, start_of(back, piece), width, **options)

    last = first_product(rows, weight, start_of(1, 0), width)
    moving = [move(last, 0)]
    for piece in range(1, PIECES):
        last, ids = partial(1, piece, after=[last], ids=ids)
        moving.append(move(last, piece))

    all_ids = [ids]
    for x in range(1, req_total):
        all_ids.append(lax.ppermute(ids, "req", [(i, i ^ x) for i in range(req_total)]))
    last = partial(0, 0, after=[last])
    owns = [last]
    packs, starts, ends = pick_adapters(me_req, table, all_ids, lens, down, up, [last])
    for x in range(1, req_total):
        packs[x] = lax.ppermute(packs[x], "req", [(i, i ^ x) for i in range(req_total)])

    last = starts
    for step in range(1, steps):
        for piece in range(PIECES):
            if step == steps - 1 and piece == PIECES - 1:
                low = low_sums(starts, ends, rows, packs, rank, [last])
                lows = [low]
                for x in range(1, tp_total):
                    pairs = [(i, i ^ x) for i in range(tp_total)]
                    lows.append(lax.ppermute(low, "tp", pairs))
                last = low
            last = partial(1 + step, piece, addends=[moving[piece]], after=[last])
            moving[piece] = move(last, piece)
            if step == 1 and piece > 0:
                last = partial(0, piece, after=[last], cost=LARGE)
                owns.append(last)

    terms = adapter_term(starts, ends, lows, owns, packs, [last])
    result = None
    for piece in range(PIECES):
        cost = SMALL if piece == PIECES - 1 else LARGE
        result = finish(terms[piece], [moving[piece]], piece, PIECES, result, cost)
    return result


def solution(mesh):
    return jax.shard_map(
        functools.partial(local, mesh.shape["req"], mesh.shape["tp"]),
        mesh=mesh,
        in_specs=(
            P(("groups", "req"), "tp"),
            P("tp", None),
            P(("groups", "req"), None, "tp"),
            P(("groups", "req"), None, "tp"),
            P("groups"),
            P(("groups", "req"), None),
            P(("groups", "req"), None),
        ),
        out_specs=P(("groups", "req"), "tp"),
        check_vma=False,
    )
```

```python
import functools

import jax
import jax.numpy as jnp
from jax import lax
from jax.experimental import pallas as pl
from jax.experimental.pallas import tpu as pltpu
from jax.sharding import PartitionSpec as P

CAP = 6
PIECES = 2
VMEM_LIMIT = 20 * 1024 * 1024
F32 = jnp.float32
BF16 = jnp.bfloat16
SMALL = pl.CostEstimate(flops=1000, bytes_accessed=1000, transcendentals=0)
LARGE = pl.CostEstimate(flops=2 * 10**10, bytes_accessed=1000, transcendentals=0)


def product_kernel(addends, with_ids, first_ref, rows_ref, weight_ref, *rest):
    out_ref = rest[-1 - with_ids]
    total = jnp.dot(rows_ref[...], weight_ref[...], preferred_element_type=F32)
    for ref in rest[:addends]:
        total = total + ref[...].astype(F32)
    out_ref[...] = total.astype(out_ref.dtype)
    if with_ids:
        ids_ref, ids_out_ref = rest[addends], rest[-1]
        for s in range(ids_ref.shape[1]):
            ids_out_ref[0, s] = ids_ref[0, s]


def block_product(rows, weight, first, width, addends=(), after=(), ids=None, cost=SMALL):
    row_total, depth = rows.shape
    tile = min(256, width)
    with_ids = ids is not None
    smem = pl.BlockSpec(memory_space=pltpu.SMEM)
    hbm = pl.BlockSpec(memory_space=pl.ANY)
    columns = pl.BlockSpec((row_total, tile), lambda j, t: (0, j))
    out_specs, out_shape = [columns], [jax.ShapeDtypeStruct((row_total, width), BF16)]
    if with_ids:
        out_specs.append(smem)
        out_shape.append(jax.ShapeDtypeStruct(ids.shape, ids.dtype))
    out = pl.pallas_call(
        functools.partial(product_kernel, len(addends), with_ids),
        grid_spec=pltpu.PrefetchScalarGridSpec(
            num_scalar_prefetch=1,
            grid=(width // tile,),
            in_specs=[
                pl.BlockSpec((row_total, depth), lambda j, t: (0, 0)),
                pl.BlockSpec((depth, tile), lambda j, t: (0, t[0] + j)),
            ]
            + [columns] * len(addends)
            + [smem] * with_ids
            + [hbm] * len(after),
            out_specs=out_specs,
        ),
        out_shape=out_shape,
        compiler_params=pltpu.CompilerParams(vmem_limit_bytes=VMEM_LIMIT),
        cost_estimate=cost,
        name="block_product",
    )((first // tile).reshape(1), rows, weight, *addends, *([ids] if with_ids else []), *after)
    return out if with_ids else out[0]


def first_kernel(chunk, first_ref, rows_ref, weight_ref, out_ref, lhs_ref, rhs_ref, acc_ref, sems):
    columns = pl.ds(pl.multiple_of(first_ref[0], 128), out_ref.shape[1])
    chunks = lhs_ref.shape[0]

    def copies(k):
        part = pl.ds(k * chunk, chunk)
        return (
            pltpu.make_async_copy(rows_ref.at[:, part], lhs_ref.at[k], sems.at[0, k]),
            pltpu.make_async_copy(weight_ref.at[part, columns], rhs_ref.at[k], sems.at[1, k]),
        )

    for k in range(chunks):
        for copy in copies(k):
            copy.start()
    for k in range(chunks):
        for copy in copies(k):
            copy.wait()
        part = jnp.dot(lhs_ref[k], rhs_ref[k], preferred_element_type=F32)
        if k == 0:
            acc_ref[...] = part
        elif k < chunks - 1:
            acc_ref[...] += part
        else:
            out_ref[...] = (acc_ref[...] + part).astype(out_ref.dtype)


def first_product(rows, weight, first, width):
    row_total, depth = rows.shape
    chunk = min(512, depth // 2)
    chunks = depth // chunk
    hbm = pl.BlockSpec(memory_space=pltpu.HBM)
    return pl.pallas_call(
        functools.partial(first_kernel, chunk),
        in_specs=[pl.BlockSpec(memory_space=pltpu.SMEM), hbm, hbm],
        out_specs=pl.BlockSpec(memory_space=pltpu.VMEM),
        out_shape=jax.ShapeDtypeStruct((row_total, width), BF16),
        scratch_shapes=[
            pltpu.VMEM((chunks, row_total, chunk), BF16),
            pltpu.VMEM((chunks, chunk, width), BF16),
            pltpu.VMEM((row_total, width), F32),
            pltpu.SemaphoreType.DMA((2, chunks)),
        ],
        compiler_params=pltpu.CompilerParams(vmem_limit_bytes=VMEM_LIMIT),
        cost_estimate=SMALL,
        name="first_product",
    )(first.reshape(1), pltpu.with_memory_space_constraint(rows, pltpu.HBM), weight)


def pick_kernel(peers, afters, me_ref, table_ref, lens_ref, *rest):
    ids_refs = rest[:peers]
    down_ref, up_ref = rest[peers : peers + 2]
    rest = rest[peers + 2 + afters :]
    packs, (start_ref, end_ref, pick_ref, count_ref, sem) = rest[:peers], rest[peers:]
    segs = lens_ref.shape[1]
    share, _, depth = down_ref.shape
    cols = up_ref.shape[2]
    me = me_ref[0]

    def clear(q, carry):
        pick_ref[q] = 0
        start_ref[q] = 0
        end_ref[q] = 0
        return carry

    lax.fori_loop(0, peers * CAP, clear, 0, unroll=8)
    for x in range(peers):
        count_ref[x] = 0

    def copies(x, c, source):
        pack = packs[x].at[c]
        return (
            pltpu.make_async_copy(down_ref.at[source], pack.at[:, pl.ds(0, depth)], sem),
            pltpu.make_async_copy(up_ref.at[source], pack.at[:, pl.ds(depth, cols)], sem),
        )

    for x in reversed(range(peers)):

        def choose(s, count):
            local = table_ref[ids_refs[x][0, s]] - me * share
            mine = jnp.logical_and(local >= 0, local < share)

            @pl.when(jnp.logical_and(mine, count < CAP))
            def _():
                pick_ref[x * CAP + count] = local

            return count + mine.astype(jnp.int32)

        lax.fori_loop(0, segs, choose, 0, unroll=4)
        for c in range(CAP):
            for copy in copies(x, c, pick_ref[x * CAP + c]):
                copy.start()

    def place(s, first):
        x = lax.bitwise_xor(table_ref[ids_refs[0][0, s]] // share, me)
        count = count_ref[x]
        last = first + lens_ref[0, s]

        @pl.when(count < CAP)
        def _():
            start_ref[x * CAP + count] = first
            end_ref[x * CAP + count] = last

        count_ref[x] = count + 1
        return last

    lax.fori_loop(0, segs, place, 0, unroll=4)

    for x in range(peers):
        for c in range(CAP):
            for copy in copies(x, c, 0):
                copy.wait()


def pick_adapters(me, table, all_ids, lens, down, up, after):
    peers = len(all_ids)
    _, rank, depth = down.shape
    cols = up.shape[2]
    smem = pl.BlockSpec(memory_space=pltpu.SMEM)
    vmem = pl.BlockSpec(memory_space=pltpu.VMEM)
    hbm = pl.BlockSpec(memory_space=pl.ANY)
    out = pl.pallas_call(
        functools.partial(pick_kernel, peers, len(after)),
        in_specs=[smem] * (3 + peers) + [hbm] * (2 + len(after)),
        out_specs=[vmem] * peers + [smem, smem],
        out_shape=[jax.ShapeDtypeStruct((CAP, rank, depth + cols), BF16)] * peers
        + [jax.ShapeDtypeStruct((peers * CAP,), jnp.int32)] * 2,
        scratch_shapes=[
            pltpu.SMEM((peers * CAP,), jnp.int32),
            pltpu.SMEM((peers,), jnp.int32),
            pltpu.SemaphoreType.DMA,
        ],
        compiler_params=pltpu.CompilerParams(vmem_limit_bytes=VMEM_LIMIT),
        cost_estimate=SMALL,
        name="pick_adapters",
    )(me.reshape(1), table, lens, *all_ids, down, up, *after)
    return list(out[:-2]), out[-2], out[-1]


def pack_spec(pack, first, width):
    return pl.BlockSpec(pack.shape[:2] + (width,), lambda i: (0, 0, first // width))


def low_kernel(peers, start_ref, end_ref, rows_ref, *rest):
    down_refs, out_ref = rest[:peers], rest[-1]
    row_total, depth = rows_ref.shape
    rank = out_ref.shape[0]
    place = lax.broadcasted_iota(jnp.int32, (rank, row_total), 1)
    downs = jnp.concatenate([ref[...].reshape(CAP * rank, depth) for ref in down_refs], axis=0)
    part = lax.dot_general(
        downs, rows_ref[...], (((1,), (1,)), ((), ())), preferred_element_type=F32
    )
    total = jnp.zeros((rank, row_total), F32)
    for q in range(peers * CAP):
        member = jnp.logical_and(place >= start_ref[q], place < end_ref[q])
        total = jnp.where(member, part[q * rank : (q + 1) * rank], total)
    out_ref[...] = total


def low_sums(starts, ends, rows, packs, rank, after):
    row_total, depth = rows.shape
    smem = pl.BlockSpec(memory_space=pltpu.SMEM)
    vmem = pl.BlockSpec(memory_space=pltpu.VMEM)
    return pl.pallas_call(
        functools.partial(low_kernel, len(packs)),
        grid=(1,),
        in_specs=[smem, smem, vmem]
        + [pack_spec(p, 0, depth) for p in packs]
        + [pl.BlockSpec(memory_space=pl.ANY)] * len(after),
        out_specs=vmem,
        out_shape=jax.ShapeDtypeStruct((rank, row_total), F32),
        compiler_params=pltpu.CompilerParams(vmem_limit_bytes=VMEM_LIMIT),
        cost_estimate=SMALL,
        name="low_sums",
    )(starts, ends, rows, *packs, *after)


def term_kernel(lows, pieces, peers, start_ref, end_ref, *rest):
    low_refs, rest = rest[:lows], rest[lows:]
    own_refs, rest = rest[:pieces], rest[pieces:]
    up_refs, out_refs = rest[:peers], rest[-pieces:]
    rank, row_total = low_refs[0].shape
    width = out_refs[0].shape[1]
    cols = width * pieces
    low = low_refs[0][...]
    for ref in low_refs[1:]:
        low = low + ref[...]
    low = low.astype(BF16).astype(F32)
    place = lax.broadcasted_iota(jnp.int32, (rank, row_total), 1)
    spread = []
    for q in range(len(up_refs) * CAP):
        member = jnp.logical_and(place >= start_ref[q], place < end_ref[q])
        spread.append(jnp.where(member, low, 0.0))
    spread = jnp.concatenate(spread, axis=0).astype(BF16)
    ups = jnp.concatenate([ref[...].reshape(CAP * rank, cols) for ref in up_refs], axis=0)
    for piece in range(pieces):
        columns = slice(piece * width, (piece + 1) * width)
        term = lax.dot_general(
            spread, ups[:, columns], (((0,), (0,)), ((), ())), preferred_element_type=F32
        )
        out_refs[piece][...] = own_refs[piece][...].astype(F32) + term


def adapter_term(starts, ends, lows, owns, packs, after):
    row_total, width = owns[0].shape
    cols = width * len(owns)
    smem = pl.BlockSpec(memory_space=pltpu.SMEM)
    vmem = pl.BlockSpec(memory_space=pltpu.VMEM)
    depth = packs[0].shape[2] - cols
    return pl.pallas_call(
        functools.partial(term_kernel, len(lows), len(owns), len(packs)),
        grid=(1,),
        in_specs=[smem, smem]
        + [vmem] * (len(lows) + len(owns))
        + [pack_spec(p, depth, cols) for p in packs]
        + [pl.BlockSpec(memory_space=pl.ANY)] * len(after),
        out_specs=[vmem] * len(owns),
        out_shape=[jax.ShapeDtypeStruct((row_total, width), F32)] * len(owns),
        compiler_params=pltpu.CompilerParams(vmem_limit_bytes=VMEM_LIMIT),
        cost_estimate=SMALL,
        name="adapter_term",
    )(starts, ends, *lows, *owns, *packs, *after)


def finish_kernel(addends, term_ref, *rest):
    total = term_ref[...]
    for ref in rest[:addends]:
        total = total + ref[...].astype(F32)
    rest[-1][...] = total.astype(rest[-1].dtype)


def finish(term, arrivals, piece, pieces, result, cost):
    row_total, width = term.shape
    height = min(row_total, 128)
    block = pl.BlockSpec((height, width), lambda i: (i, 0))
    held = [] if result is None else [result]
    return pl.pallas_call(
        functools.partial(finish_kernel, len(arrivals)),
        grid=(row_total // height,),
        in_specs=[block] * (1 + len(arrivals)) + [pl.BlockSpec(memory_space=pl.ANY)] * len(held),
        out_specs=pl.BlockSpec((height, width), lambda i: (i, piece)),
        out_shape=jax.ShapeDtypeStruct((row_total, width * pieces), BF16),
        input_output_aliases={1 + len(arrivals): 0} if held else {},
        compiler_params=pltpu.CompilerParams(vmem_limit_bytes=VMEM_LIMIT),
        cost_estimate=cost,
        name="finish",
    )(term, *arrivals, *held)


def local(req_total, tp_total, rows, weight, down, up, table, ids, lens):
    weight = pltpu.with_memory_space_constraint(weight, pltpu.HBM)
    down = pltpu.with_memory_space_constraint(down, pltpu.HBM)
    up = pltpu.with_memory_space_constraint(up, pltpu.HBM)
    rank = down.shape[1]
    cols = up.shape[2]
    width = cols // PIECES
    me_req = lax.axis_index("req").astype(jnp.int32)
    me = lax.axis_index("tp").astype(jnp.int32)
    steps = tp_total - 1

    ring = list(range(0, tp_total, 2))[:1] + list(range(1, tp_total, 2))
    ring += list(range(2, tp_total, 2))[::-1]

    def move(value, piece):
        pairs = []
        for r in range(req_total):
            way = 1 if (r + piece) % 2 == 0 else tp_total - 1
            for q in range(tp_total):
                target = ring[(q + way) % tp_total]
                pairs.append((r * tp_total + ring[q], r * tp_total + target))
        return lax.ppermute(value, ("req", "tp"), pairs)

    def lookup(table, index):
        result = jnp.int32(table[0])
        for i in range(1, tp_total):
            result = jnp.where(index == i, jnp.int32(table[i]), result)
        return result

    place = lookup([ring.index(i) for i in range(tp_total)], me)

    def start_of(back, piece):
        behind = jnp.where(lax.rem(me_req + piece, 2) == 0, tp_total - back, back)
        block = lookup(ring, lax.rem(place + behind, tp_total))
        return block * cols + piece * width

    def partial(back, piece, **options):
        return block_product(rows, weight, start_of(back, piece), width, **options)

    last = first_product(rows, weight, start_of(1, 0), width)
    moving = [move(last, 0)]
    for piece in range(1, PIECES):
        last, ids = partial(1, piece, after=[last], ids=ids)
        moving.append(move(last, piece))

    all_ids = [ids]
    for x in range(1, req_total):
        all_ids.append(lax.ppermute(ids, "req", [(i, i ^ x) for i in range(req_total)]))
    last = partial(0, 0, after=[last])
    owns = [last]
    packs, starts, ends = pick_adapters(me_req, table, all_ids, lens, down, up, [last])
    for x in range(1, req_total):
        packs[x] = lax.ppermute(packs[x], "req", [(i, i ^ x) for i in range(req_total)])

    last = starts
    for step in range(1, steps):
        for piece in range(PIECES):
            if step == steps - 1 and piece == PIECES - 1:
                low = low_sums(starts, ends, rows, packs, rank, [last])
                lows = [low]
                for x in range(1, tp_total):
                    pairs = [(i, i ^ x) for i in range(tp_total)]
                    lows.append(lax.ppermute(low, "tp", pairs))
                last = low
            last = partial(1 + step, piece, addends=[moving[piece]], after=[last])
            moving[piece] = move(last, piece)
            if step == 1 and piece > 0:
                last = partial(0, piece, after=[last], cost=LARGE)
                owns.append(last)

    terms = adapter_term(starts, ends, lows, owns, packs, [last])
    result = None
    for piece in range(PIECES):
        cost = SMALL if piece == PIECES - 1 else LARGE
        result = finish(terms[piece], [moving[piece]], piece, PIECES, result, cost)
    return result


def solution(mesh):
    return jax.shard_map(
        functools.partial(local, mesh.shape["req"], mesh.shape["tp"]),
        mesh=mesh,
        in_specs=(
            P(("groups", "req"), "tp"),
            P("tp", None),
            P(("groups", "req"), None, "tp"),
            P(("groups", "req"), None, "tp"),
            P("groups"),
            P(("groups", "req"), None),
            P(("groups", "req"), None),
        ),
        out_specs=P(("groups", "req"), "tp"),
        check_vma=False,
    )
```

```python
import functools

import jax
import jax.numpy as jnp
from jax import lax
from jax.experimental import pallas as pl
from jax.experimental.pallas import tpu as pltpu
from jax.sharding import PartitionSpec as P

CAP = 6
PIECES = 2
VMEM_LIMIT = 20 * 1024 * 1024
F32 = jnp.float32
BF16 = jnp.bfloat16
SMALL = pl.CostEstimate(flops=1000, bytes_accessed=1000, transcendentals=0)
LARGE = pl.CostEstimate(flops=2 * 10**10, bytes_accessed=1000, transcendentals=0)


def product_kernel(addends, with_ids, first_ref, rows_ref, weight_ref, *rest):
    out_ref = rest[-1 - with_ids]
    total = jnp.dot(rows_ref[...], weight_ref[...], preferred_element_type=F32)
    for ref in rest[:addends]:
        total = total + ref[...].astype(F32)
    out_ref[...] = total.astype(out_ref.dtype)
    if with_ids:
        ids_ref, ids_out_ref = rest[addends], rest[-1]
        for s in range(ids_ref.shape[1]):
            ids_out_ref[0, s] = ids_ref[0, s]


def block_product(rows, weight, first, width, addends=(), after=(), ids=None, cost=SMALL):
    row_total, depth = rows.shape
    tile = min(256, width)
    with_ids = ids is not None
    smem = pl.BlockSpec(memory_space=pltpu.SMEM)
    hbm = pl.BlockSpec(memory_space=pl.ANY)
    columns = pl.BlockSpec((row_total, tile), lambda j, t: (0, j))
    out_specs, out_shape = [columns], [jax.ShapeDtypeStruct((row_total, width), BF16)]
    if with_ids:
        out_specs.append(smem)
        out_shape.append(jax.ShapeDtypeStruct(ids.shape, ids.dtype))
    out = pl.pallas_call(
        functools.partial(product_kernel, len(addends), with_ids),
        grid_spec=pltpu.PrefetchScalarGridSpec(
            num_scalar_prefetch=1,
            grid=(width // tile,),
            in_specs=[
                pl.BlockSpec((row_total, depth), lambda j, t: (0, 0)),
                pl.BlockSpec((depth, tile), lambda j, t: (0, t[0] + j)),
            ]
            + [columns] * len(addends)
            + [smem] * with_ids
            + [hbm] * len(after),
            out_specs=out_specs,
        ),
        out_shape=out_shape,
        compiler_params=pltpu.CompilerParams(vmem_limit_bytes=VMEM_LIMIT),
        cost_estimate=cost,
        name="block_product",
    )((first // tile).reshape(1), rows, weight, *addends, *([ids] if with_ids else []), *after)
    return out if with_ids else out[0]


def first_kernel(chunk, first_ref, rows_ref, weight_ref, out_ref, lhs_ref, rhs_ref, acc_ref, sems):
    columns = pl.ds(pl.multiple_of(first_ref[0], 128), out_ref.shape[1])
    chunks = lhs_ref.shape[0]

    def copies(k):
        part = pl.ds(k * chunk, chunk)
        return (
            pltpu.make_async_copy(rows_ref.at[:, part], lhs_ref.at[k], sems.at[0, k]),
            pltpu.make_async_copy(weight_ref.at[part, columns], rhs_ref.at[k], sems.at[1, k]),
        )

    for k in range(chunks):
        for copy in copies(k):
            copy.start()
    for k in range(chunks):
        for copy in copies(k):
            copy.wait()
        part = jnp.dot(lhs_ref[k], rhs_ref[k], preferred_element_type=F32)
        if k == 0:
            acc_ref[...] = part
        elif k < chunks - 1:
            acc_ref[...] += part
        else:
            out_ref[...] = (acc_ref[...] + part).astype(out_ref.dtype)


def first_product(rows, weight, first, width):
    row_total, depth = rows.shape
    chunk = min(512, depth // 2)
    chunks = depth // chunk
    hbm = pl.BlockSpec(memory_space=pltpu.HBM)
    return pl.pallas_call(
        functools.partial(first_kernel, chunk),
        in_specs=[pl.BlockSpec(memory_space=pltpu.SMEM), hbm, hbm],
        out_specs=pl.BlockSpec(memory_space=pltpu.VMEM),
        out_shape=jax.ShapeDtypeStruct((row_total, width), BF16),
        scratch_shapes=[
            pltpu.VMEM((chunks, row_total, chunk), BF16),
            pltpu.VMEM((chunks, chunk, width), BF16),
            pltpu.VMEM((row_total, width), F32),
            pltpu.SemaphoreType.DMA((2, chunks)),
        ],
        compiler_params=pltpu.CompilerParams(vmem_limit_bytes=VMEM_LIMIT),
        cost_estimate=SMALL,
        name="first_product",
    )(first.reshape(1), pltpu.with_memory_space_constraint(rows, pltpu.HBM), weight)


def pick_kernel(peers, afters, me_ref, table_ref, lens_ref, *rest):
    ids_refs = rest[:peers]
    down_ref, up_ref = rest[peers : peers + 2]
    rest = rest[peers + 2 + afters :]
    packs, (start_ref, end_ref, pick_ref, count_ref, sem) = rest[:peers], rest[peers:]
    segs = lens_ref.shape[1]
    share, _, depth = down_ref.shape
    cols = up_ref.shape[2]
    me = me_ref[0]

    def clear(q, carry):
        pick_ref[q] = 0
        start_ref[q] = 0
        end_ref[q] = 0
        return carry

    lax.fori_loop(0, peers * CAP, clear, 0, unroll=8)
    for x in range(peers):
        count_ref[x] = 0

    def copies(x, c, source):
        pack = packs[x].at[c]
        return (
            pltpu.make_async_copy(down_ref.at[source], pack.at[:, pl.ds(0, depth)], sem),
            pltpu.make_async_copy(up_ref.at[source], pack.at[:, pl.ds(depth, cols)], sem),
        )

    for x in reversed(range(peers)):

        def choose(s, count):
            local = table_ref[ids_refs[x][0, s]] - me * share
            mine = jnp.logical_and(local >= 0, local < share)

            @pl.when(jnp.logical_and(mine, count < CAP))
            def _():
                pick_ref[x * CAP + count] = local

            return count + mine.astype(jnp.int32)

        lax.fori_loop(0, segs, choose, 0, unroll=4)
        for c in range(CAP):
            for copy in copies(x, c, pick_ref[x * CAP + c]):
                copy.start()

    def place(s, first):
        x = lax.bitwise_xor(table_ref[ids_refs[0][0, s]] // share, me)
        count = count_ref[x]
        last = first + lens_ref[0, s]

        @pl.when(count < CAP)
        def _():
            start_ref[x * CAP + count] = first
            end_ref[x * CAP + count] = last

        count_ref[x] = count + 1
        return last

    lax.fori_loop(0, segs, place, 0, unroll=4)

    for x in range(peers):
        for c in range(CAP):
            for copy in copies(x, c, 0):
                copy.wait()


def pick_adapters(me, table, all_ids, lens, down, up, after):
    peers = len(all_ids)
    _, rank, depth = down.shape
    cols = up.shape[2]
    smem = pl.BlockSpec(memory_space=pltpu.SMEM)
    vmem = pl.BlockSpec(memory_space=pltpu.VMEM)
    hbm = pl.BlockSpec(memory_space=pl.ANY)
    out = pl.pallas_call(
        functools.partial(pick_kernel, peers, len(after)),
        in_specs=[smem] * (3 + peers) + [hbm] * (2 + len(after)),
        out_specs=[vmem] * peers + [smem, smem],
        out_shape=[jax.ShapeDtypeStruct((CAP, rank, depth + cols), BF16)] * peers
        + [jax.ShapeDtypeStruct((peers * CAP,), jnp.int32)] * 2,
        scratch_shapes=[
            pltpu.SMEM((peers * CAP,), jnp.int32),
            pltpu.SMEM((peers,), jnp.int32),
            pltpu.SemaphoreType.DMA,
        ],
        compiler_params=pltpu.CompilerParams(vmem_limit_bytes=VMEM_LIMIT),
        cost_estimate=SMALL,
        name="pick_adapters",
    )(me.reshape(1), table, lens, *all_ids, down, up, *after)
    return list(out[:-2]), out[-2], out[-1]


def pack_spec(pack, first, width):
    return pl.BlockSpec(pack.shape[:2] + (width,), lambda i: (0, 0, first // width))


def low_kernel(peers, start_ref, end_ref, rows_ref, *rest):
    down_refs, out_ref = rest[:peers], rest[-1]
    row_total, depth = rows_ref.shape
    rank = out_ref.shape[0]
    place = lax.broadcasted_iota(jnp.int32, (rank, row_total), 1)
    downs = jnp.concatenate([ref[...].reshape(CAP * rank, depth) for ref in down_refs], axis=0)
    part = lax.dot_general(
        downs, rows_ref[...], (((1,), (1,)), ((), ())), preferred_element_type=F32
    )
    total = jnp.zeros((rank, row_total), F32)
    for q in range(peers * CAP):
        member = jnp.logical_and(place >= start_ref[q], place < end_ref[q])
        total = jnp.where(member, part[q * rank : (q + 1) * rank], total)
    out_ref[...] = total


def low_sums(starts, ends, rows, packs, rank, after):
    row_total, depth = rows.shape
    smem = pl.BlockSpec(memory_space=pltpu.SMEM)
    vmem = pl.BlockSpec(memory_space=pltpu.VMEM)
    return pl.pallas_call(
        functools.partial(low_kernel, len(packs)),
        grid=(1,),
        in_specs=[smem, smem, vmem]
        + [pack_spec(p, 0, depth) for p in packs]
        + [pl.BlockSpec(memory_space=pl.ANY)] * len(after),
        out_specs=vmem,
        out_shape=jax.ShapeDtypeStruct((rank, row_total), F32),
        compiler_params=pltpu.CompilerParams(vmem_limit_bytes=VMEM_LIMIT),
        cost_estimate=SMALL,
        name="low_sums",
    )(starts, ends, rows, *packs, *after)


def term_kernel(lows, pieces, peers, start_ref, end_ref, *rest):
    low_refs, rest = rest[:lows], rest[lows:]
    own_refs, rest = rest[:pieces], rest[pieces:]
    up_refs, out_refs = rest[:peers], rest[-pieces:]
    rank, row_total = low_refs[0].shape
    width = out_refs[0].shape[1]
    cols = width * pieces
    low = low_refs[0][...]
    for ref in low_refs[1:]:
        low = low + ref[...]
    low = low.astype(BF16).astype(F32)
    place = lax.broadcasted_iota(jnp.int32, (rank, row_total), 1)
    spread = []
    for q in range(len(up_refs) * CAP):
        member = jnp.logical_and(place >= start_ref[q], place < end_ref[q])
        spread.append(jnp.where(member, low, 0.0))
    spread = jnp.concatenate(spread, axis=0).astype(BF16)
    ups = jnp.concatenate([ref[...].reshape(CAP * rank, cols) for ref in up_refs], axis=0)
    for piece in range(pieces):
        columns = slice(piece * width, (piece + 1) * width)
        term = lax.dot_general(
            spread, ups[:, columns], (((0,), (0,)), ((), ())), preferred_element_type=F32
        )
        out_refs[piece][...] = own_refs[piece][...].astype(F32) + term


def adapter_term(starts, ends, lows, owns, packs, after):
    row_total, width = owns[0].shape
    cols = width * len(owns)
    smem = pl.BlockSpec(memory_space=pltpu.SMEM)
    vmem = pl.BlockSpec(memory_space=pltpu.VMEM)
    depth = packs[0].shape[2] - cols
    return pl.pallas_call(
        functools.partial(term_kernel, len(lows), len(owns), len(packs)),
        grid=(1,),
        in_specs=[smem, smem]
        + [vmem] * (len(lows) + len(owns))
        + [pack_spec(p, depth, cols) for p in packs]
        + [pl.BlockSpec(memory_space=pl.ANY)] * len(after),
        out_specs=[vmem] * len(owns),
        out_shape=[jax.ShapeDtypeStruct((row_total, width), F32)] * len(owns),
        compiler_params=pltpu.CompilerParams(vmem_limit_bytes=VMEM_LIMIT),
        cost_estimate=SMALL,
        name="adapter_term",
    )(starts, ends, *lows, *owns, *packs, *after)


def finish_kernel(addends, term_ref, *rest):
    total = term_ref[...]
    for ref in rest[:addends]:
        total = total + ref[...].astype(F32)
    rest[-1][...] = total.astype(rest[-1].dtype)


def finish(term, arrivals, piece, pieces, result, cost):
    row_total, width = term.shape
    height = min(row_total, 128)
    block = pl.BlockSpec((height, width), lambda i: (i, 0))
    held = [] if result is None else [result]
    return pl.pallas_call(
        functools.partial(finish_kernel, len(arrivals)),
        grid=(row_total // height,),
        in_specs=[block] * (1 + len(arrivals)) + [pl.BlockSpec(memory_space=pl.ANY)] * len(held),
        out_specs=pl.BlockSpec((height, width), lambda i: (i, piece)),
        out_shape=jax.ShapeDtypeStruct((row_total, width * pieces), BF16),
        input_output_aliases={1 + len(arrivals): 0} if held else {},
        compiler_params=pltpu.CompilerParams(vmem_limit_bytes=VMEM_LIMIT),
        cost_estimate=cost,
        name="finish",
    )(term, *arrivals, *held)


def local(req_total, tp_total, rows, weight, down, up, table, ids, lens):
    weight = pltpu.with_memory_space_constraint(weight, pltpu.HBM)
    down = pltpu.with_memory_space_constraint(down, pltpu.HBM)
    up = pltpu.with_memory_space_constraint(up, pltpu.HBM)
    rank = down.shape[1]
    cols = up.shape[2]
    width = cols // PIECES
    me_req = lax.axis_index("req").astype(jnp.int32)
    me = lax.axis_index("tp").astype(jnp.int32)
    steps = tp_total - 1

    def move(value, piece):
        pairs = []
        for r in range(req_total):
            way = 1 if (r + piece) % 2 == 0 else tp_total - 1
            for i in range(tp_total):
                pairs.append((r * tp_total + i, r * tp_total + (i + way) % tp_total))
        return lax.ppermute(value, ("req", "tp"), pairs)

    def start_of(back, piece):
        behind = jnp.where(lax.rem(me_req + piece, 2) == 0, tp_total - back, back)
        block = lax.rem(me + behind, tp_total)
        return block * cols + piece * width

    def partial(back, piece, **options):
        return block_product(rows, weight, start_of(back, piece), width, **options)

    last = first_product(rows, weight, start_of(1, 0), width)
    moving = [move(last, 0)]
    for piece in range(1, PIECES):
        last, ids = partial(1, piece, after=[last], ids=ids)
        moving.append(move(last, piece))

    all_ids = [ids]
    for x in range(1, req_total):
        all_ids.append(lax.ppermute(ids, "req", [(i, i ^ x) for i in range(req_total)]))
    last = partial(0, 0, after=[last])
    owns = [last]
    packs, starts, ends = pick_adapters(me_req, table, all_ids, lens, down, up, [last])
    for x in range(1, req_total):
        packs[x] = lax.ppermute(packs[x], "req", [(i, i ^ x) for i in range(req_total)])

    last = starts
    for step in range(1, steps):
        for piece in range(PIECES):
            if step == steps - 1 and piece == PIECES - 1:
                low = low_sums(starts, ends, rows, packs, rank, [last])
                lows = [low]
                for x in range(1, tp_total):
                    pairs = [(i, i ^ x) for i in range(tp_total)]
                    lows.append(lax.ppermute(low, "tp", pairs))
                last = low
            last = partial(1 + step, piece, addends=[moving[piece]], after=[last])
            moving[piece] = move(last, piece)
            if step == 1 and piece > 0:
                last = partial(0, piece, after=[last], cost=LARGE)
                owns.append(last)

    terms = adapter_term(starts, ends, lows, owns, packs, [last])
    result = None
    for piece in range(PIECES):
        cost = SMALL if piece == PIECES - 1 else LARGE
        result = finish(terms[piece], [moving[piece]], piece, PIECES, result, cost)
    return result


def solution(mesh):
    return jax.shard_map(
        functools.partial(local, mesh.shape["req"], mesh.shape["tp"]),
        mesh=mesh,
        in_specs=(
            P(("groups", "req"), "tp"),
            P("tp", None),
            P(("groups", "req"), None, "tp"),
            P(("groups", "req"), None, "tp"),
            P("groups"),
            P(("groups", "req"), None),
            P(("groups", "req"), None),
        ),
        out_specs=P(("groups", "req"), "tp"),
        check_vma=False,
    )
```

```python
import functools

import jax
import jax.numpy as jnp
from jax import lax
from jax.experimental import pallas as pl
from jax.experimental.pallas import tpu as pltpu
from jax.sharding import PartitionSpec as P

CAP = 6
PIECES = 2
VMEM_LIMIT = 20 * 1024 * 1024
F32 = jnp.float32
BF16 = jnp.bfloat16
SMALL = pl.CostEstimate(flops=1000, bytes_accessed=1000, transcendentals=0)
LARGE = pl.CostEstimate(flops=2 * 10**10, bytes_accessed=1000, transcendentals=0)


def product_kernel(addends, with_ids, first_ref, rows_ref, weight_ref, *rest):
    out_ref = rest[-1 - with_ids]
    total = jnp.dot(rows_ref[...], weight_ref[...], preferred_element_type=F32)
    for ref in rest[:addends]:
        total = total + ref[...].astype(F32)
    out_ref[...] = total.astype(out_ref.dtype)
    if with_ids:
        ids_ref, ids_out_ref = rest[addends], rest[-1]
        for s in range(ids_ref.shape[1]):
            ids_out_ref[0, s] = ids_ref[0, s]


def block_product(rows, weight, first, width, addends=(), after=(), ids=None, cost=SMALL):
    row_total, depth = rows.shape
    tile = min(256, width)
    with_ids = ids is not None
    smem = pl.BlockSpec(memory_space=pltpu.SMEM)
    hbm = pl.BlockSpec(memory_space=pl.ANY)
    columns = pl.BlockSpec((row_total, tile), lambda j, t: (0, j))
    out_specs, out_shape = [columns], [jax.ShapeDtypeStruct((row_total, width), BF16)]
    if with_ids:
        out_specs.append(smem)
        out_shape.append(jax.ShapeDtypeStruct(ids.shape, ids.dtype))
    out = pl.pallas_call(
        functools.partial(product_kernel, len(addends), with_ids),
        grid_spec=pltpu.PrefetchScalarGridSpec(
            num_scalar_prefetch=1,
            grid=(width // tile,),
            in_specs=[
                pl.BlockSpec((row_total, depth), lambda j, t: (0, 0)),
                pl.BlockSpec((depth, tile), lambda j, t: (0, t[0] + j)),
            ]
            + [columns] * len(addends)
            + [smem] * with_ids
            + [hbm] * len(after),
            out_specs=out_specs,
        ),
        out_shape=out_shape,
        compiler_params=pltpu.CompilerParams(vmem_limit_bytes=VMEM_LIMIT),
        cost_estimate=cost,
        name="block_product",
    )((first // tile).reshape(1), rows, weight, *addends, *([ids] if with_ids else []), *after)
    return out if with_ids else out[0]


def first_kernel(chunk, first_ref, rows_ref, weight_ref, out_ref, lhs_ref, rhs_ref, acc_ref, sems):
    columns = pl.ds(pl.multiple_of(first_ref[0], 128), out_ref.shape[1])
    chunks = lhs_ref.shape[0]

    def copies(k):
        part = pl.ds(k * chunk, chunk)
        return (
            pltpu.make_async_copy(rows_ref.at[:, part], lhs_ref.at[k], sems.at[0, k]),
            pltpu.make_async_copy(weight_ref.at[part, columns], rhs_ref.at[k], sems.at[1, k]),
        )

    for k in range(chunks):
        for copy in copies(k):
            copy.start()
    for k in range(chunks):
        for copy in copies(k):
            copy.wait()
        part = jnp.dot(lhs_ref[k], rhs_ref[k], preferred_element_type=F32)
        if k == 0:
            acc_ref[...] = part
        elif k < chunks - 1:
            acc_ref[...] += part
        else:
            out_ref[...] = (acc_ref[...] + part).astype(out_ref.dtype)


def first_product(rows, weight, first, width):
    row_total, depth = rows.shape
    chunk = min(512, depth // 2)
    chunks = depth // chunk
    hbm = pl.BlockSpec(memory_space=pltpu.HBM)
    return pl.pallas_call(
        functools.partial(first_kernel, chunk),
        in_specs=[pl.BlockSpec(memory_space=pltpu.SMEM), hbm, hbm],
        out_specs=pl.BlockSpec(memory_space=pltpu.VMEM),
        out_shape=jax.ShapeDtypeStruct((row_total, width), BF16),
        scratch_shapes=[
            pltpu.VMEM((chunks, row_total, chunk), BF16),
            pltpu.VMEM((chunks, chunk, width), BF16),
            pltpu.VMEM((row_total, width), F32),
            pltpu.SemaphoreType.DMA((2, chunks)),
        ],
        compiler_params=pltpu.CompilerParams(vmem_limit_bytes=VMEM_LIMIT),
        cost_estimate=SMALL,
        name="first_product",
    )(first.reshape(1), pltpu.with_memory_space_constraint(rows, pltpu.HBM), weight)


def pick_kernel(peers, afters, me_ref, table_ref, lens_ref, *rest):
    ids_refs = rest[:peers]
    down_ref, up_ref = rest[peers : peers + 2]
    rest = rest[peers + 2 + afters :]
    packs, (start_ref, end_ref, pick_ref, count_ref, sem) = rest[:peers], rest[peers:]
    segs = lens_ref.shape[1]
    share, _, depth = down_ref.shape
    cols = up_ref.shape[2]
    me = me_ref[0]

    def clear(q, carry):
        pick_ref[q] = 0
        start_ref[q] = 0
        end_ref[q] = 0
        return carry

    lax.fori_loop(0, peers * CAP, clear, 0, unroll=8)
    for x in range(peers):
        count_ref[x] = 0

    def copies(x, c, source):
        pack = packs[x].at[c]
        return (
            pltpu.make_async_copy(down_ref.at[source], pack.at[:, pl.ds(0, depth)], sem),
            pltpu.make_async_copy(up_ref.at[source], pack.at[:, pl.ds(depth, cols)], sem),
        )

    for x in reversed(range(peers)):

        def choose(s, count):
            local = table_ref[ids_refs[x][0, s]] - me * share
            mine = jnp.logical_and(local >= 0, local < share)

            @pl.when(jnp.logical_and(mine, count < CAP))
            def _():
                pick_ref[x * CAP + count] = local

            return count + mine.astype(jnp.int32)

        lax.fori_loop(0, segs, choose, 0, unroll=4)
        for c in range(CAP):
            for copy in copies(x, c, pick_ref[x * CAP + c]):
                copy.start()

    def place(s, first):
        x = lax.bitwise_xor(table_ref[ids_refs[0][0, s]] // share, me)
        count = count_ref[x]
        last = first + lens_ref[0, s]

        @pl.when(count < CAP)
        def _():
            start_ref[x * CAP + count] = first
            end_ref[x * CAP + count] = last

        count_ref[x] = count + 1
        return last

    lax.fori_loop(0, segs, place, 0, unroll=4)

    for x in range(peers):
        for c in range(CAP):
            for copy in copies(x, c, 0):
                copy.wait()


def pick_adapters(me, table, all_ids, lens, down, up, after):
    peers = len(all_ids)
    _, rank, depth = down.shape
    cols = up.shape[2]
    smem = pl.BlockSpec(memory_space=pltpu.SMEM)
    vmem = pl.BlockSpec(memory_space=pltpu.VMEM)
    hbm = pl.BlockSpec(memory_space=pl.ANY)
    out = pl.pallas_call(
        functools.partial(pick_kernel, peers, len(after)),
        in_specs=[smem] * (3 + peers) + [hbm] * (2 + len(after)),
        out_specs=[vmem] * peers + [smem, smem],
        out_shape=[jax.ShapeDtypeStruct((CAP, rank, depth + cols), BF16)] * peers
        + [jax.ShapeDtypeStruct((peers * CAP,), jnp.int32)] * 2,
        scratch_shapes=[
            pltpu.SMEM((peers * CAP,), jnp.int32),
            pltpu.SMEM((peers,), jnp.int32),
            pltpu.SemaphoreType.DMA,
        ],
        compiler_params=pltpu.CompilerParams(vmem_limit_bytes=VMEM_LIMIT),
        cost_estimate=SMALL,
        name="pick_adapters",
    )(me.reshape(1), table, lens, *all_ids, down, up, *after)
    return list(out[:-2]), out[-2], out[-1]


def pack_spec(pack, first, width):
    return pl.BlockSpec(pack.shape[:2] + (width,), lambda i: (0, 0, first // width))


def low_kernel(peers, start_ref, end_ref, rows_ref, *rest):
    down_refs, out_ref = rest[:peers], rest[-1]
    row_total, depth = rows_ref.shape
    rank = out_ref.shape[0]
    place = lax.broadcasted_iota(jnp.int32, (rank, row_total), 1)
    downs = jnp.concatenate([ref[...].reshape(CAP * rank, depth) for ref in down_refs], axis=0)
    part = lax.dot_general(
        downs, rows_ref[...], (((1,), (1,)), ((), ())), preferred_element_type=F32
    )
    total = jnp.zeros((rank, row_total), F32)
    for q in range(peers * CAP):
        member = jnp.logical_and(place >= start_ref[q], place < end_ref[q])
        total = jnp.where(member, part[q * rank : (q + 1) * rank], total)
    out_ref[...] = total


def low_sums(starts, ends, rows, packs, rank, after):
    row_total, depth = rows.shape
    smem = pl.BlockSpec(memory_space=pltpu.SMEM)
    vmem = pl.BlockSpec(memory_space=pltpu.VMEM)
    return pl.pallas_call(
        functools.partial(low_kernel, len(packs)),
        grid=(1,),
        in_specs=[smem, smem, vmem]
        + [pack_spec(p, 0, depth) for p in packs]
        + [pl.BlockSpec(memory_space=pl.ANY)] * len(after),
        out_specs=vmem,
        out_shape=jax.ShapeDtypeStruct((rank, row_total), F32),
        compiler_params=pltpu.CompilerParams(vmem_limit_bytes=VMEM_LIMIT),
        cost_estimate=SMALL,
        name="low_sums",
    )(starts, ends, rows, *packs, *after)


def term_kernel(lows, pieces, peers, start_ref, end_ref, *rest):
    low_refs, rest = rest[:lows], rest[lows:]
    own_refs, rest = rest[:pieces], rest[pieces:]
    up_refs, out_refs = rest[:peers], rest[-pieces:]
    rank, row_total = low_refs[0].shape
    width = out_refs[0].shape[1]
    cols = width * pieces
    low = low_refs[0][...]
    for ref in low_refs[1:]:
        low = low + ref[...]
    low = low.astype(BF16).astype(F32)
    place = lax.broadcasted_iota(jnp.int32, (rank, row_total), 1)
    spread = []
    for q in range(len(up_refs) * CAP):
        member = jnp.logical_and(place >= start_ref[q], place < end_ref[q])
        spread.append(jnp.where(member, low, 0.0))
    spread = jnp.concatenate(spread, axis=0).astype(BF16)
    ups = jnp.concatenate([ref[...].reshape(CAP * rank, cols) for ref in up_refs], axis=0)
    for piece in range(pieces):
        columns = slice(piece * width, (piece + 1) * width)
        term = lax.dot_general(
            spread, ups[:, columns], (((0,), (0,)), ((), ())), preferred_element_type=F32
        )
        out_refs[piece][...] = own_refs[piece][...].astype(F32) + term


def adapter_term(starts, ends, lows, owns, packs, after):
    row_total, width = owns[0].shape
    cols = width * len(owns)
    smem = pl.BlockSpec(memory_space=pltpu.SMEM)
    vmem = pl.BlockSpec(memory_space=pltpu.VMEM)
    depth = packs[0].shape[2] - cols
    return pl.pallas_call(
        functools.partial(term_kernel, len(lows), len(owns), len(packs)),
        grid=(1,),
        in_specs=[smem, smem]
        + [vmem] * (len(lows) + len(owns))
        + [pack_spec(p, depth, cols) for p in packs]
        + [pl.BlockSpec(memory_space=pl.ANY)] * len(after),
        out_specs=[vmem] * len(owns),
        out_shape=[jax.ShapeDtypeStruct((row_total, width), F32)] * len(owns),
        compiler_params=pltpu.CompilerParams(vmem_limit_bytes=VMEM_LIMIT),
        cost_estimate=SMALL,
        name="adapter_term",
    )(starts, ends, *lows, *owns, *packs, *after)


def finish_kernel(addends, term_ref, *rest):
    total = term_ref[...]
    for ref in rest[:addends]:
        total = total + ref[...].astype(F32)
    rest[-1][...] = total.astype(rest[-1].dtype)


def finish(term, arrivals, piece, pieces, result, cost):
    row_total, width = term.shape
    height = min(row_total, 128)
    block = pl.BlockSpec((height, width), lambda i: (i, 0))
    held = [] if result is None else [result]
    return pl.pallas_call(
        functools.partial(finish_kernel, len(arrivals)),
        grid=(row_total // height,),
        in_specs=[block] * (1 + len(arrivals)) + [pl.BlockSpec(memory_space=pl.ANY)] * len(held),
        out_specs=pl.BlockSpec((height, width), lambda i: (i, piece)),
        out_shape=jax.ShapeDtypeStruct((row_total, width * pieces), BF16),
        input_output_aliases={1 + len(arrivals): 0} if held else {},
        compiler_params=pltpu.CompilerParams(vmem_limit_bytes=VMEM_LIMIT),
        cost_estimate=cost,
        name="finish",
    )(term, *arrivals, *held)


def local(req_total, tp_total, rows, weight, down, up, table, ids, lens):
    weight = pltpu.with_memory_space_constraint(weight, pltpu.HBM)
    down = pltpu.with_memory_space_constraint(down, pltpu.HBM)
    up = pltpu.with_memory_space_constraint(up, pltpu.HBM)
    rank = down.shape[1]
    cols = up.shape[2]
    width = cols // PIECES
    me_req = lax.axis_index("req").astype(jnp.int32)
    me = lax.axis_index("tp").astype(jnp.int32)
    steps = tp_total - 1

    def move(value, piece):
        pairs = []
        for r in range(req_total):
            way = 1 if (r + piece) % 2 == 1 else tp_total - 1
            for i in range(tp_total):
                pairs.append((r * tp_total + i, r * tp_total + (i + way) % tp_total))
        return lax.ppermute(value, ("req", "tp"), pairs)

    def start_of(back, piece):
        behind = jnp.where(lax.rem(me_req + piece, 2) == 1, tp_total - back, back)
        block = lax.rem(me + behind, tp_total)
        return block * cols + piece * width

    def partial(back, piece, **options):
        return block_product(rows, weight, start_of(back, piece), width, **options)

    last = first_product(rows, weight, start_of(1, 0), width)
    moving = [move(last, 0)]
    for piece in range(1, PIECES):
        last, ids = partial(1, piece, after=[last], ids=ids)
        moving.append(move(last, piece))

    all_ids = [ids]
    for x in range(1, req_total):
        all_ids.append(lax.ppermute(ids, "req", [(i, i ^ x) for i in range(req_total)]))
    last = partial(0, 0, after=[last])
    owns = [last]
    packs, starts, ends = pick_adapters(me_req, table, all_ids, lens, down, up, [last])
    for x in range(1, req_total):
        packs[x] = lax.ppermute(packs[x], "req", [(i, i ^ x) for i in range(req_total)])

    last = starts
    for step in range(1, steps):
        for piece in range(PIECES):
            if step == steps - 1 and piece == PIECES - 1:
                low = low_sums(starts, ends, rows, packs, rank, [last])
                lows = [low]
                for x in range(1, tp_total):
                    pairs = [(i, i ^ x) for i in range(tp_total)]
                    lows.append(lax.ppermute(low, "tp", pairs))
                last = low
            last = partial(1 + step, piece, addends=[moving[piece]], after=[last])
            moving[piece] = move(last, piece)
            if step == 1 and piece > 0:
                last = partial(0, piece, after=[last], cost=LARGE)
                owns.append(last)

    terms = adapter_term(starts, ends, lows, owns, packs, [last])
    result = None
    for piece in range(PIECES):
        cost = SMALL if piece == PIECES - 1 else LARGE
        result = finish(terms[piece], [moving[piece]], piece, PIECES, result, cost)
    return result


def solution(mesh):
    return jax.shard_map(
        functools.partial(local, mesh.shape["req"], mesh.shape["tp"]),
        mesh=mesh,
        in_specs=(
            P(("groups", "req"), "tp"),
            P("tp", None),
            P(("groups", "req"), None, "tp"),
            P(("groups", "req"), None, "tp"),
            P("groups"),
            P(("groups", "req"), None),
            P(("groups", "req"), None),
        ),
        out_specs=P(("groups", "req"), "tp"),
        check_vma=False,
    )
```

```python
import functools

import jax
import jax.numpy as jnp
from jax import lax
from jax.experimental import pallas as pl
from jax.experimental.pallas import tpu as pltpu
from jax.sharding import PartitionSpec as P

CAP = 6
PIECES = 2
VMEM_LIMIT = 20 * 1024 * 1024
F32 = jnp.float32
BF16 = jnp.bfloat16
SMALL = pl.CostEstimate(flops=1000, bytes_accessed=1000, transcendentals=0)
LARGE = pl.CostEstimate(flops=2 * 10**10, bytes_accessed=1000, transcendentals=0)


def product_kernel(with_ids, first_ref, rows_ref, weight_ref, *rest):
    out_ref = rest[-1 - with_ids]
    total = jnp.dot(rows_ref[...], weight_ref[...], preferred_element_type=F32)
    out_ref[...] = total.astype(out_ref.dtype)
    if with_ids:
        ids_ref, ids_out_ref = rest[0], rest[-1]
        for s in range(ids_ref.shape[1]):
            ids_out_ref[0, s] = ids_ref[0, s]


def block_product(rows, weight, first, width, after=(), ids=None, cost=SMALL):
    row_total, depth = rows.shape
    tile = min(256, width)
    with_ids = ids is not None
    smem = pl.BlockSpec(memory_space=pltpu.SMEM)
    hbm = pl.BlockSpec(memory_space=pl.ANY)
    columns = pl.BlockSpec((row_total, tile), lambda j, t: (0, j))
    out_specs, out_shape = [columns], [jax.ShapeDtypeStruct((row_total, width), BF16)]
    if with_ids:
        out_specs.append(smem)
        out_shape.append(jax.ShapeDtypeStruct(ids.shape, ids.dtype))
    out = pl.pallas_call(
        functools.partial(product_kernel, with_ids),
        grid_spec=pltpu.PrefetchScalarGridSpec(
            num_scalar_prefetch=1,
            grid=(width // tile,),
            in_specs=[
                pl.BlockSpec((row_total, depth), lambda j, t: (0, 0)),
                pl.BlockSpec((depth, tile), lambda j, t: (0, t[0] + j)),
            ]
            + [smem] * with_ids
            + [hbm] * len(after),
            out_specs=out_specs,
        ),
        out_shape=out_shape,
        compiler_params=pltpu.CompilerParams(vmem_limit_bytes=VMEM_LIMIT),
        cost_estimate=cost,
        name="block_product",
    )((first // tile).reshape(1), rows, weight, *([ids] if with_ids else []), *after)
    return out if with_ids else out[0]


def first_kernel(chunk, first_ref, rows_ref, weight_ref, out_ref, lhs_ref, rhs_ref, acc_ref, sems):
    columns = pl.ds(pl.multiple_of(first_ref[0], 128), out_ref.shape[1])
    chunks = lhs_ref.shape[0]

    def copies(k):
        part = pl.ds(k * chunk, chunk)
        return (
            pltpu.make_async_copy(rows_ref.at[:, part], lhs_ref.at[k], sems.at[0, k]),
            pltpu.make_async_copy(weight_ref.at[part, columns], rhs_ref.at[k], sems.at[1, k]),
        )

    for k in range(chunks):
        for copy in copies(k):
            copy.start()
    for k in range(chunks):
        for copy in copies(k):
            copy.wait()
        part = jnp.dot(lhs_ref[k], rhs_ref[k], preferred_element_type=F32)
        if k == 0:
            acc_ref[...] = part
        elif k < chunks - 1:
            acc_ref[...] += part
        else:
            out_ref[...] = (acc_ref[...] + part).astype(out_ref.dtype)


def first_product(rows, weight, first, width):
    row_total, depth = rows.shape
    chunk = min(512, depth // 2)
    chunks = depth // chunk
    hbm = pl.BlockSpec(memory_space=pltpu.HBM)
    return pl.pallas_call(
        functools.partial(first_kernel, chunk),
        in_specs=[pl.BlockSpec(memory_space=pltpu.SMEM), hbm, hbm],
        out_specs=pl.BlockSpec(memory_space=pltpu.VMEM),
        out_shape=jax.ShapeDtypeStruct((row_total, width), BF16),
        scratch_shapes=[
            pltpu.VMEM((chunks, row_total, chunk), BF16),
            pltpu.VMEM((chunks, chunk, width), BF16),
            pltpu.VMEM((row_total, width), F32),
            pltpu.SemaphoreType.DMA((2, chunks)),
        ],
        compiler_params=pltpu.CompilerParams(vmem_limit_bytes=VMEM_LIMIT),
        cost_estimate=SMALL,
        name="first_product",
    )(first.reshape(1), pltpu.with_memory_space_constraint(rows, pltpu.HBM), weight)


def pick_kernel(peers, afters, me_ref, table_ref, lens_ref, *rest):
    ids_refs = rest[:peers]
    down_ref, up_ref = rest[peers : peers + 2]
    rest = rest[peers + 2 + afters :]
    packs, (start_ref, end_ref, pick_ref, count_ref, sem) = rest[:peers], rest[peers:]
    segs = lens_ref.shape[1]
    share, _, depth = down_ref.shape
    cols = up_ref.shape[2]
    me = me_ref[0]

    def clear(q, carry):
        pick_ref[q] = 0
        start_ref[q] = 0
        end_ref[q] = 0
        return carry

    lax.fori_loop(0, peers * CAP, clear, 0, unroll=8)
    for x in range(peers):
        count_ref[x] = 0

    def copies(x, c, source):
        pack = packs[x].at[c]
        return (
            pltpu.make_async_copy(down_ref.at[source], pack.at[:, pl.ds(0, depth)], sem),
            pltpu.make_async_copy(up_ref.at[source], pack.at[:, pl.ds(depth, cols)], sem),
        )

    for x in reversed(range(peers)):

        def choose(s, count):
            local = table_ref[ids_refs[x][0, s]] - me * share
            mine = jnp.logical_and(local >= 0, local < share)

            @pl.when(jnp.logical_and(mine, count < CAP))
            def _():
                pick_ref[x * CAP + count] = local

            return count + mine.astype(jnp.int32)

        lax.fori_loop(0, segs, choose, 0, unroll=4)
        for c in range(CAP):
            for copy in copies(x, c, pick_ref[x * CAP + c]):
                copy.start()

    def place(s, first):
        x = lax.bitwise_xor(table_ref[ids_refs[0][0, s]] // share, me)
        count = count_ref[x]
        last = first + lens_ref[0, s]

        @pl.when(count < CAP)
        def _():
            start_ref[x * CAP + count] = first
            end_ref[x * CAP + count] = last

        count_ref[x] = count + 1
        return last

    lax.fori_loop(0, segs, place, 0, unroll=4)

    for x in range(peers):
        for c in range(CAP):
            for copy in copies(x, c, 0):
                copy.wait()


def pick_adapters(me, table, all_ids, lens, down, up, after):
    peers = len(all_ids)
    _, rank, depth = down.shape
    cols = up.shape[2]
    smem = pl.BlockSpec(memory_space=pltpu.SMEM)
    vmem = pl.BlockSpec(memory_space=pltpu.VMEM)
    hbm = pl.BlockSpec(memory_space=pl.ANY)
    out = pl.pallas_call(
        functools.partial(pick_kernel, peers, len(after)),
        in_specs=[smem] * (3 + peers) + [hbm] * (2 + len(after)),
        out_specs=[vmem] * peers + [smem, smem],
        out_shape=[jax.ShapeDtypeStruct((CAP, rank, depth + cols), BF16)] * peers
        + [jax.ShapeDtypeStruct((peers * CAP,), jnp.int32)] * 2,
        scratch_shapes=[
            pltpu.SMEM((peers * CAP,), jnp.int32),
            pltpu.SMEM((peers,), jnp.int32),
            pltpu.SemaphoreType.DMA,
        ],
        compiler_params=pltpu.CompilerParams(vmem_limit_bytes=VMEM_LIMIT),
        cost_estimate=SMALL,
        name="pick_adapters",
    )(me.reshape(1), table, lens, *all_ids, down, up, *after)
    return list(out[:-2]), out[-2], out[-1]


def pack_spec(pack, first, width):
    return pl.BlockSpec(pack.shape[:2] + (width,), lambda i: (0, 0, first // width))


def low_kernel(peers, start_ref, end_ref, rows_ref, *rest):
    down_refs, out_ref = rest[:peers], rest[-1]
    row_total, depth = rows_ref.shape
    rank = out_ref.shape[0]
    place = lax.broadcasted_iota(jnp.int32, (rank, row_total), 1)
    downs = jnp.concatenate([ref[...].reshape(CAP * rank, depth) for ref in down_refs], axis=0)
    part = lax.dot_general(
        downs, rows_ref[...], (((1,), (1,)), ((), ())), preferred_element_type=F32
    )
    total = jnp.zeros((rank, row_total), F32)
    for q in range(peers * CAP):
        member = jnp.logical_and(place >= start_ref[q], place < end_ref[q])
        total = jnp.where(member, part[q * rank : (q + 1) * rank], total)
    out_ref[...] = total


def low_sums(starts, ends, rows, packs, rank, after):
    row_total, depth = rows.shape
    smem = pl.BlockSpec(memory_space=pltpu.SMEM)
    vmem = pl.BlockSpec(memory_space=pltpu.VMEM)
    return pl.pallas_call(
        functools.partial(low_kernel, len(packs)),
        grid=(1,),
        in_specs=[smem, smem, vmem]
        + [pack_spec(p, 0, depth) for p in packs]
        + [pl.BlockSpec(memory_space=pl.ANY)] * len(after),
        out_specs=vmem,
        out_shape=jax.ShapeDtypeStruct((rank, row_total), F32),
        compiler_params=pltpu.CompilerParams(vmem_limit_bytes=VMEM_LIMIT),
        cost_estimate=SMALL,
        name="low_sums",
    )(starts, ends, rows, *packs, *after)


def term_kernel(lows, pieces, peers, start_ref, end_ref, *rest):
    low_refs, rest = rest[:lows], rest[lows:]
    own_refs, rest = rest[:pieces], rest[pieces:]
    up_refs, out_refs = rest[:peers], rest[-pieces:]
    rank, row_total = low_refs[0].shape
    width = out_refs[0].shape[1]
    cols = width * pieces
    low = low_refs[0][...]
    for ref in low_refs[1:]:
        low = low + ref[...]
    low = low.astype(BF16).astype(F32)
    place = lax.broadcasted_iota(jnp.int32, (rank, row_total), 1)
    spread = []
    for q in range(len(up_refs) * CAP):
        member = jnp.logical_and(place >= start_ref[q], place < end_ref[q])
        spread.append(jnp.where(member, low, 0.0))
    spread = jnp.concatenate(spread, axis=0).astype(BF16)
    ups = jnp.concatenate([ref[...].reshape(CAP * rank, cols) for ref in up_refs], axis=0)
    for piece in range(pieces):
        columns = slice(piece * width, (piece + 1) * width)
        term = lax.dot_general(
            spread, ups[:, columns], (((0,), (0,)), ((), ())), preferred_element_type=F32
        )
        out_refs[piece][...] = own_refs[piece][...].astype(F32) + term


def adapter_term(starts, ends, lows, owns, packs, after):
    row_total, width = owns[0].shape
    cols = width * len(owns)
    smem = pl.BlockSpec(memory_space=pltpu.SMEM)
    vmem = pl.BlockSpec(memory_space=pltpu.VMEM)
    depth = packs[0].shape[2] - cols
    return pl.pallas_call(
        functools.partial(term_kernel, len(lows), len(owns), len(packs)),
        grid=(1,),
        in_specs=[smem, smem]
        + [vmem] * (len(lows) + len(owns))
        + [pack_spec(p, depth, cols) for p in packs]
        + [pl.BlockSpec(memory_space=pl.ANY)] * len(after),
        out_specs=[vmem] * len(owns),
        out_shape=[jax.ShapeDtypeStruct((row_total, width), F32)] * len(owns),
        compiler_params=pltpu.CompilerParams(vmem_limit_bytes=VMEM_LIMIT),
        cost_estimate=SMALL,
        name="adapter_term",
    )(starts, ends, *lows, *owns, *packs, *after)


def finish_kernel(addends, term_ref, *rest):
    total = term_ref[...]
    for ref in rest[:addends]:
        total = total + ref[...].astype(F32)
    rest[-1][...] = total.astype(rest[-1].dtype)


def finish(term, arrivals, piece, pieces, result, cost):
    row_total, width = term.shape
    height = min(row_total, 128)
    block = pl.BlockSpec((height, width), lambda i: (i, 0))
    held = [] if result is None else [result]
    return pl.pallas_call(
        functools.partial(finish_kernel, len(arrivals)),
        grid=(row_total // height,),
        in_specs=[block] * (1 + len(arrivals)) + [pl.BlockSpec(memory_space=pl.ANY)] * len(held),
        out_specs=pl.BlockSpec((height, width), lambda i: (i, piece)),
        out_shape=jax.ShapeDtypeStruct((row_total, width * pieces), BF16),
        input_output_aliases={1 + len(arrivals): 0} if held else {},
        compiler_params=pltpu.CompilerParams(vmem_limit_bytes=VMEM_LIMIT),
        cost_estimate=cost,
        name="finish",
    )(term, *arrivals, *held)


def local(req_total, tp_total, rows, weight, down, up, table, ids, lens):
    weight = pltpu.with_memory_space_constraint(weight, pltpu.HBM)
    down = pltpu.with_memory_space_constraint(down, pltpu.HBM)
    up = pltpu.with_memory_space_constraint(up, pltpu.HBM)
    rank = down.shape[1]
    cols = up.shape[2]
    width = cols // PIECES
    me_req = lax.axis_index("req").astype(jnp.int32)
    me = lax.axis_index("tp").astype(jnp.int32)
    steps = tp_total - 1

    def move(value, piece):
        pairs = []
        for r in range(req_total):
            way = 1 if (r + piece) % 2 == 0 else tp_total - 1
            for i in range(tp_total):
                pairs.append((r * tp_total + i, r * tp_total + (i + way) % tp_total))
        return lax.ppermute(value, ("req", "tp"), pairs)

    def start_of(back, piece):
        behind = jnp.where(lax.rem(me_req + piece, 2) == 0, tp_total - back, back)
        block = lax.rem(me + behind, tp_total)
        return block * cols + piece * width

    def partial(back, piece, **options):
        return block_product(rows, weight, start_of(back, piece), width, **options)

    last = first_product(rows, weight, start_of(1, 0), width)
    moving = [move(last, 0)]
    for piece in range(1, PIECES):
        last, ids = partial(1, piece, after=[last], ids=ids)
        moving.append(move(last, piece))

    all_ids = [ids]
    for x in range(1, req_total):
        all_ids.append(lax.ppermute(ids, "req", [(i, i ^ x) for i in range(req_total)]))
    last = partial(0, 0, after=[last])
    owns = [last]
    packs, starts, ends = pick_adapters(me_req, table, all_ids, lens, down, up, [last])
    for x in range(1, req_total):
        packs[x] = lax.ppermute(packs[x], "req", [(i, i ^ x) for i in range(req_total)])

    last = starts
    for step in range(1, steps):
        for piece in range(PIECES):
            if step == steps - 1 and piece == PIECES - 1:
                low = low_sums(starts, ends, rows, packs, rank, [last])
                lows = [low]
                for x in range(1, tp_total):
                    pairs = [(i, i ^ x) for i in range(tp_total)]
                    lows.append(lax.ppermute(low, "tp", pairs))
                last = low
            product = partial(1 + step, piece, after=[last])
            last = (product.astype(F32) + moving[piece].astype(F32)).astype(BF16)
            moving[piece] = move(last, piece)
            if step == 1 and piece > 0:
                last = partial(0, piece, after=[last], cost=LARGE)
                owns.append(last)

    terms = adapter_term(starts, ends, lows, owns, packs, [last])
    result = None
    for piece in range(PIECES):
        cost = SMALL if piece == PIECES - 1 else LARGE
        result = finish(terms[piece], [moving[piece]], piece, PIECES, result, cost)
    return result


def solution(mesh):
    return jax.shard_map(
        functools.partial(local, mesh.shape["req"], mesh.shape["tp"]),
        mesh=mesh,
        in_specs=(
            P(("groups", "req"), "tp"),
            P("tp", None),
            P(("groups", "req"), None, "tp"),
            P(("groups", "req"), None, "tp"),
            P("groups"),
            P(("groups", "req"), None),
            P(("groups", "req"), None),
        ),
        out_specs=P(("groups", "req"), "tp"),
        check_vma=False,
    )
```

```python
import functools

import jax
import jax.numpy as jnp
from jax import lax
from jax.experimental import pallas as pl
from jax.experimental.pallas import tpu as pltpu
from jax.sharding import PartitionSpec as P

CAP = 6
PIECES = 2
VMEM_LIMIT = 20 * 1024 * 1024
F32 = jnp.float32
BF16 = jnp.bfloat16
SMALL = pl.CostEstimate(flops=1000, bytes_accessed=1000, transcendentals=0)
LARGE = pl.CostEstimate(flops=2 * 10**10, bytes_accessed=1000, transcendentals=0)


def product_kernel(addends, with_ids, first_ref, rows_ref, weight_ref, *rest):
    out_ref = rest[-1 - with_ids]
    total = jnp.dot(rows_ref[...], weight_ref[...], preferred_element_type=F32)
    for ref in rest[:addends]:
        total = total + ref[...].astype(F32)
    out_ref[...] = total.astype(out_ref.dtype)
    if with_ids:
        ids_ref, ids_out_ref = rest[addends], rest[-1]
        for s in range(ids_ref.shape[1]):
            ids_out_ref[0, s] = ids_ref[0, s]


def block_product(rows, weight, first, width, addends=(), after=(), ids=None, cost=SMALL):
    row_total, depth = rows.shape
    tile = min(256, width)
    with_ids = ids is not None
    smem = pl.BlockSpec(memory_space=pltpu.SMEM)
    hbm = pl.BlockSpec(memory_space=pl.ANY)
    columns = pl.BlockSpec((row_total, tile), lambda j, t: (0, j))
    out_specs, out_shape = [columns], [jax.ShapeDtypeStruct((row_total, width), BF16)]
    if with_ids:
        out_specs.append(smem)
        out_shape.append(jax.ShapeDtypeStruct(ids.shape, ids.dtype))
    out = pl.pallas_call(
        functools.partial(product_kernel, len(addends), with_ids),
        grid_spec=pltpu.PrefetchScalarGridSpec(
            num_scalar_prefetch=1,
            grid=(width // tile,),
            in_specs=[
                pl.BlockSpec((row_total, depth), lambda j, t: (0, 0)),
                pl.BlockSpec((depth, tile), lambda j, t: (0, t[0] + j)),
            ]
            + [columns] * len(addends)
            + [smem] * with_ids
            + [hbm] * len(after),
            out_specs=out_specs,
        ),
        out_shape=out_shape,
        compiler_params=pltpu.CompilerParams(vmem_limit_bytes=VMEM_LIMIT),
        cost_estimate=cost,
        name="block_product",
    )((first // tile).reshape(1), rows, weight, *addends, *([ids] if with_ids else []), *after)
    return out if with_ids else out[0]


def first_kernel(chunk, first_ref, rows_ref, weight_ref, out_ref, lhs_ref, rhs_ref, acc_ref, sems):
    columns = pl.ds(pl.multiple_of(first_ref[0], 128), out_ref.shape[1])
    chunks = rhs_ref.shape[0]

    def copies(k):
        part = pl.ds(k * chunk, chunk)
        return (
            pltpu.make_async_copy(rows_ref.at[:, part], lhs_ref.at[:, part], sems.at[0, k]),
            pltpu.make_async_copy(weight_ref.at[part, columns], rhs_ref.at[k], sems.at[1, k]),
        )

    for k in range(chunks):
        for copy in copies(k):
            copy.start()
    for k in range(chunks):
        for copy in copies(k):
            copy.wait()
        lhs = lhs_ref[:, k * chunk : (k + 1) * chunk]
        part = jnp.dot(lhs, rhs_ref[k], preferred_element_type=F32)
        if k == 0:
            acc_ref[...] = part
        elif k < chunks - 1:
            acc_ref[...] += part
        else:
            out_ref[...] = (acc_ref[...] + part).astype(out_ref.dtype)


def first_product(rows, weight, first, width):
    row_total, depth = rows.shape
    chunk = min(512, depth // 2)
    chunks = depth // chunk
    hbm = pl.BlockSpec(memory_space=pltpu.HBM)
    return pl.pallas_call(
        functools.partial(first_kernel, chunk),
        in_specs=[pl.BlockSpec(memory_space=pltpu.SMEM), hbm, hbm],
        out_specs=[pl.BlockSpec(memory_space=pltpu.VMEM)] * 2,
        out_shape=[
            jax.ShapeDtypeStruct((row_total, width), BF16),
            jax.ShapeDtypeStruct((row_total, depth), BF16),
        ],
        scratch_shapes=[
            pltpu.VMEM((chunks, chunk, width), BF16),
            pltpu.VMEM((row_total, width), F32),
            pltpu.SemaphoreType.DMA((2, chunks)),
        ],
        compiler_params=pltpu.CompilerParams(vmem_limit_bytes=VMEM_LIMIT),
        cost_estimate=SMALL,
        name="first_product",
    )(first.reshape(1), pltpu.with_memory_space_constraint(rows, pltpu.HBM), weight)


def pick_kernel(peers, afters, me_ref, table_ref, lens_ref, *rest):
    ids_refs = rest[:peers]
    down_ref, up_ref = rest[peers : peers + 2]
    rest = rest[peers + 2 + afters :]
    packs, (start_ref, end_ref, pick_ref, count_ref, sem) = rest[:peers], rest[peers:]
    segs = lens_ref.shape[1]
    share, _, depth = down_ref.shape
    cols = up_ref.shape[2]
    me = me_ref[0]

    def clear(q, carry):
        pick_ref[q] = 0
        start_ref[q] = 0
        end_ref[q] = 0
        return carry

    lax.fori_loop(0, peers * CAP, clear, 0, unroll=8)
    for x in range(peers):
        count_ref[x] = 0

    def copies(x, c, source):
        pack = packs[x].at[c]
        return (
            pltpu.make_async_copy(down_ref.at[source], pack.at[:, pl.ds(0, depth)], sem),
            pltpu.make_async_copy(up_ref.at[source], pack.at[:, pl.ds(depth, cols)], sem),
        )

    for x in reversed(range(peers)):

        def choose(s, count):
            local = table_ref[ids_refs[x][0, s]] - me * share
            mine = jnp.logical_and(local >= 0, local < share)

            @pl.when(jnp.logical_and(mine, count < CAP))
            def _():
                pick_ref[x * CAP + count] = local

            return count + mine.astype(jnp.int32)

        lax.fori_loop(0, segs, choose, 0, unroll=4)
        for c in range(CAP):
            for copy in copies(x, c, pick_ref[x * CAP + c]):
                copy.start()

    def place(s, first):
        x = lax.bitwise_xor(table_ref[ids_refs[0][0, s]] // share, me)
        count = count_ref[x]
        last = first + lens_ref[0, s]

        @pl.when(count < CAP)
        def _():
            start_ref[x * CAP + count] = first
            end_ref[x * CAP + count] = last

        count_ref[x] = count + 1
        return last

    lax.fori_loop(0, segs, place, 0, unroll=4)

    for x in range(peers):
        for c in range(CAP):
            for copy in copies(x, c, 0):
                copy.wait()


def pick_adapters(me, table, all_ids, lens, down, up, after):
    peers = len(all_ids)
    _, rank, depth = down.shape
    cols = up.shape[2]
    smem = pl.BlockSpec(memory_space=pltpu.SMEM)
    vmem = pl.BlockSpec(memory_space=pltpu.VMEM)
    hbm = pl.BlockSpec(memory_space=pl.ANY)
    out = pl.pallas_call(
        functools.partial(pick_kernel, peers, len(after)),
        in_specs=[smem] * (3 + peers) + [hbm] * (2 + len(after)),
        out_specs=[vmem] * peers + [smem, smem],
        out_shape=[jax.ShapeDtypeStruct((CAP, rank, depth + cols), BF16)] * peers
        + [jax.ShapeDtypeStruct((peers * CAP,), jnp.int32)] * 2,
        scratch_shapes=[
            pltpu.SMEM((peers * CAP,), jnp.int32),
            pltpu.SMEM((peers,), jnp.int32),
            pltpu.SemaphoreType.DMA,
        ],
        compiler_params=pltpu.CompilerParams(vmem_limit_bytes=VMEM_LIMIT),
        cost_estimate=SMALL,
        name="pick_adapters",
    )(me.reshape(1), table, lens, *all_ids, down, up, *after)
    return list(out[:-2]), out[-2], out[-1]


def pack_spec(pack, first, width):
    return pl.BlockSpec(pack.shape[:2] + (width,), lambda i: (0, 0, first // width))


def low_kernel(peers, start_ref, end_ref, rows_ref, *rest):
    down_refs, out_ref = rest[:peers], rest[-1]
    row_total, depth = rows_ref.shape
    rank = out_ref.shape[0]
    place = lax.broadcasted_iota(jnp.int32, (rank, row_total), 1)
    downs = jnp.concatenate([ref[...].reshape(CAP * rank, depth) for ref in down_refs], axis=0)
    part = lax.dot_general(
        downs, rows_ref[...], (((1,), (1,)), ((), ())), preferred_element_type=F32
    )
    total = jnp.zeros((rank, row_total), F32)
    for q in range(peers * CAP):
        member = jnp.logical_and(place >= start_ref[q], place < end_ref[q])
        total = jnp.where(member, part[q * rank : (q + 1) * rank], total)
    out_ref[...] = total.astype(BF16)


def low_sums(starts, ends, rows, packs, rank, after):
    row_total, depth = rows.shape
    smem = pl.BlockSpec(memory_space=pltpu.SMEM)
    vmem = pl.BlockSpec(memory_space=pltpu.VMEM)
    return pl.pallas_call(
        functools.partial(low_kernel, len(packs)),
        grid=(1,),
        in_specs=[smem, smem, vmem]
        + [pack_spec(p, 0, depth) for p in packs]
        + [pl.BlockSpec(memory_space=pl.ANY)] * len(after),
        out_specs=vmem,
        out_shape=jax.ShapeDtypeStruct((rank, row_total), BF16),
        compiler_params=pltpu.CompilerParams(vmem_limit_bytes=VMEM_LIMIT),
        cost_estimate=SMALL,
        name="low_sums",
    )(starts, ends, rows, *packs, *after)


def term_kernel(lows, pieces, peers, start_ref, end_ref, *rest):
    low_refs, rest = rest[:lows], rest[lows:]
    own_refs, rest = rest[:pieces], rest[pieces:]
    up_refs, out_refs = rest[:peers], rest[-pieces:]
    rank, row_total = low_refs[0].shape
    width = out_refs[0].shape[1]
    cols = width * pieces
    low = low_refs[0][...].astype(F32)
    for ref in low_refs[1:]:
        low = low + ref[...].astype(F32)
    low = low.astype(BF16).astype(F32)
    place = lax.broadcasted_iota(jnp.int32, (rank, row_total), 1)
    spread = []
    for q in range(len(up_refs) * CAP):
        member = jnp.logical_and(place >= start_ref[q], place < end_ref[q])
        spread.append(jnp.where(member, low, 0.0))
    spread = jnp.concatenate(spread, axis=0).astype(BF16)
    ups = jnp.concatenate([ref[...].reshape(CAP * rank, cols) for ref in up_refs], axis=0)
    for piece in range(pieces):
        columns = slice(piece * width, (piece + 1) * width)
        term = lax.dot_general(
            spread, ups[:, columns], (((0,), (0,)), ((), ())), preferred_element_type=F32
        )
        out_refs[piece][...] = own_refs[piece][...].astype(F32) + term


def adapter_term(starts, ends, lows, owns, packs, after):
    row_total, width = owns[0].shape
    cols = width * len(owns)
    smem = pl.BlockSpec(memory_space=pltpu.SMEM)
    vmem = pl.BlockSpec(memory_space=pltpu.VMEM)
    depth = packs[0].shape[2] - cols
    return pl.pallas_call(
        functools.partial(term_kernel, len(lows), len(owns), len(packs)),
        grid=(1,),
        in_specs=[smem, smem]
        + [vmem] * (len(lows) + len(owns))
        + [pack_spec(p, depth, cols) for p in packs]
        + [pl.BlockSpec(memory_space=pl.ANY)] * len(after),
        out_specs=[vmem] * len(owns),
        out_shape=[jax.ShapeDtypeStruct((row_total, width), F32)] * len(owns),
        compiler_params=pltpu.CompilerParams(vmem_limit_bytes=VMEM_LIMIT),
        cost_estimate=SMALL,
        name="adapter_term",
    )(starts, ends, *lows, *owns, *packs, *after)


def finish_kernel(addends, term_ref, *rest):
    total = term_ref[...]
    for ref in rest[:addends]:
        total = total + ref[...].astype(F32)
    rest[-1][...] = total.astype(rest[-1].dtype)


def finish(term, arrivals, piece, pieces, result, cost):
    row_total, width = term.shape
    height = min(row_total, 128)
    block = pl.BlockSpec((height, width), lambda i: (i, 0))
    held = [] if result is None else [result]
    return pl.pallas_call(
        functools.partial(finish_kernel, len(arrivals)),
        grid=(row_total // height,),
        in_specs=[block] * (1 + len(arrivals)) + [pl.BlockSpec(memory_space=pl.ANY)] * len(held),
        out_specs=pl.BlockSpec((height, width), lambda i: (i, piece)),
        out_shape=jax.ShapeDtypeStruct((row_total, width * pieces), BF16),
        input_output_aliases={1 + len(arrivals): 0} if held else {},
        compiler_params=pltpu.CompilerParams(vmem_limit_bytes=VMEM_LIMIT),
        cost_estimate=cost,
        name="finish",
    )(term, *arrivals, *held)


def local(req_total, tp_total, rows, weight, down, up, table, ids, lens):
    weight = pltpu.with_memory_space_constraint(weight, pltpu.HBM)
    down = pltpu.with_memory_space_constraint(down, pltpu.HBM)
    up = pltpu.with_memory_space_constraint(up, pltpu.HBM)
    rank = down.shape[1]
    cols = up.shape[2]
    width = cols // PIECES
    me_req = lax.axis_index("req").astype(jnp.int32)
    me = lax.axis_index("tp").astype(jnp.int32)
    steps = tp_total - 1

    def move(value, piece):
        pairs = []
        for r in range(req_total):
            way = 1 if (r + piece) % 2 == 0 else tp_total - 1
            for i in range(tp_total):
                pairs.append((r * tp_total + i, r * tp_total + (i + way) % tp_total))
        return lax.ppermute(value, ("req", "tp"), pairs)

    def start_of(back, piece):
        behind = jnp.where(lax.rem(me_req + piece, 2) == 0, tp_total - back, back)
        block = lax.rem(me + behind, tp_total)
        return block * cols + piece * width

    def partial(back, piece, **options):
        return block_product(rows, weight, start_of(back, piece), width, **options)

    last, rows = first_product(rows, weight, start_of(1, 0), width)
    rows = pltpu.with_memory_space_constraint(rows, pltpu.VMEM)
    moving = [move(last, 0)]
    for piece in range(1, PIECES):
        last, ids = partial(1, piece, after=[last], ids=ids)
        moving.append(move(last, piece))

    all_ids = [ids]
    for x in range(1, req_total):
        all_ids.append(lax.ppermute(ids, "req", [(i, i ^ x) for i in range(req_total)]))
    last = partial(0, 0, after=[last])
    owns = [last]
    packs, starts, ends = pick_adapters(me_req, table, all_ids, lens, down, up, [last])
    for x in range(1, req_total):
        packs[x] = lax.ppermute(packs[x], "req", [(i, i ^ x) for i in range(req_total)])

    last = starts
    for step in range(1, steps):
        for piece in range(PIECES):
            if step == steps - 1 and piece == PIECES - 1:
                low = low_sums(starts, ends, rows, packs, rank, [last])
                lows = [low]
                for x in range(1, tp_total):
                    pairs = [(i, i ^ x) for i in range(tp_total)]
                    lows.append(lax.ppermute(low, "tp", pairs))
                last = low
            last = partial(1 + step, piece, addends=[moving[piece]], after=[last])
            moving[piece] = move(last, piece)
            if step == 1 and piece > 0:
                last = partial(0, piece, after=[last], cost=LARGE)
                owns.append(last)

    terms = adapter_term(starts, ends, lows, owns, packs, [last])
    result = None
    for piece in range(PIECES):
        cost = SMALL if piece == PIECES - 1 else LARGE
        arrived = pltpu.with_memory_space_constraint(moving[piece], pltpu.VMEM)
        result = finish(terms[piece], [arrived], piece, PIECES, result, cost)
    return result


def solution(mesh):
    return jax.shard_map(
        functools.partial(local, mesh.shape["req"], mesh.shape["tp"]),
        mesh=mesh,
        in_specs=(
            P(("groups", "req"), "tp"),
            P("tp", None),
            P(("groups", "req"), None, "tp"),
            P(("groups", "req"), None, "tp"),
            P("groups"),
            P(("groups", "req"), None),
            P(("groups", "req"), None),
        ),
        out_specs=P(("groups", "req"), "tp"),
        check_vma=False,
    )
```

```python
import functools

import jax
import jax.numpy as jnp
from jax import lax
from jax.experimental import pallas as pl
from jax.experimental.pallas import tpu as pltpu
from jax.sharding import PartitionSpec as P

CAP = 6
VMEM_LIMIT = 20 * 1024 * 1024
F32 = jnp.float32
BF16 = jnp.bfloat16
SMALL = pl.CostEstimate(flops=1000, bytes_accessed=1000, transcendentals=0)
LARGE = pl.CostEstimate(flops=2 * 10**10, bytes_accessed=1000, transcendentals=0)


def product_kernel(addends, with_ids, first_ref, rows_ref, weight_ref, *rest):
    out_ref = rest[-1 - with_ids]
    total = jnp.dot(rows_ref[...], weight_ref[...], preferred_element_type=F32)
    for ref in rest[:addends]:
        total = total + ref[...].astype(F32)
    out_ref[...] = total.astype(out_ref.dtype)
    if with_ids:
        ids_ref, ids_out_ref = rest[addends], rest[-1]
        for s in range(ids_ref.shape[1]):
            ids_out_ref[0, s] = ids_ref[0, s]


def block_product(rows, weight, first, width, addends=(), after=(), ids=None, cost=SMALL):
    row_total, depth = rows.shape
    tile = min(256, width)
    with_ids = ids is not None
    smem = pl.BlockSpec(memory_space=pltpu.SMEM)
    hbm = pl.BlockSpec(memory_space=pl.ANY)
    columns = pl.BlockSpec((row_total, tile), lambda j, t: (0, j))
    out_specs, out_shape = [columns], [jax.ShapeDtypeStruct((row_total, width), BF16)]
    if with_ids:
        out_specs.append(smem)
        out_shape.append(jax.ShapeDtypeStruct(ids.shape, ids.dtype))
    out = pl.pallas_call(
        functools.partial(product_kernel, len(addends), with_ids),
        grid_spec=pltpu.PrefetchScalarGridSpec(
            num_scalar_prefetch=1,
            grid=(width // tile,),
            in_specs=[
                pl.BlockSpec((row_total, depth), lambda j, t: (0, 0)),
                pl.BlockSpec((depth, tile), lambda j, t: (0, t[0] + j)),
            ]
            + [columns] * len(addends)
            + [smem] * with_ids
            + [hbm] * len(after),
            out_specs=out_specs,
        ),
        out_shape=out_shape,
        compiler_params=pltpu.CompilerParams(vmem_limit_bytes=VMEM_LIMIT),
        cost_estimate=cost,
        name="block_product",
    )((first // tile).reshape(1), rows, weight, *addends, *([ids] if with_ids else []), *after)
    return out if with_ids else out[0]


def first_kernel(chunk, first_ref, rows_ref, weight_ref, out_ref, lhs_ref, rhs_ref, acc_ref, sems):
    columns = pl.ds(pl.multiple_of(first_ref[0], 128), out_ref.shape[1])
    chunks = lhs_ref.shape[0]

    def copies(k):
        part = pl.ds(k * chunk, chunk)
        return (
            pltpu.make_async_copy(rows_ref.at[:, part], lhs_ref.at[k], sems.at[0, k]),
            pltpu.make_async_copy(weight_ref.at[part, columns], rhs_ref.at[k], sems.at[1, k]),
        )

    for k in range(chunks):
        for copy in copies(k):
            copy.start()
    for k in range(chunks):
        for copy in copies(k):
            copy.wait()
        part = jnp.dot(lhs_ref[k], rhs_ref[k], preferred_element_type=F32)
        if k == 0:
            acc_ref[...] = part
        elif k < chunks - 1:
            acc_ref[...] += part
        else:
            out_ref[...] = (acc_ref[...] + part).astype(out_ref.dtype)


def first_product(rows, weight, first, width):
    row_total, depth = rows.shape
    chunk = min(512, depth // 2)
    chunks = depth // chunk
    hbm = pl.BlockSpec(memory_space=pltpu.HBM)
    return pl.pallas_call(
        functools.partial(first_kernel, chunk),
        in_specs=[pl.BlockSpec(memory_space=pltpu.SMEM), hbm, hbm],
        out_specs=pl.BlockSpec(memory_space=pltpu.VMEM),
        out_shape=jax.ShapeDtypeStruct((row_total, width), BF16),
        scratch_shapes=[
            pltpu.VMEM((chunks, row_total, chunk), BF16),
            pltpu.VMEM((chunks, chunk, width), BF16),
            pltpu.VMEM((row_total, width), F32),
            pltpu.SemaphoreType.DMA((2, chunks)),
        ],
        compiler_params=pltpu.CompilerParams(vmem_limit_bytes=VMEM_LIMIT),
        cost_estimate=SMALL,
        name="first_product",
    )(first.reshape(1), pltpu.with_memory_space_constraint(rows, pltpu.HBM), weight)


def pick_kernel(peers, afters, me_ref, table_ref, lens_ref, *rest):
    ids_refs = rest[:peers]
    down_ref, up_ref = rest[peers : peers + 2]
    rest = rest[peers + 2 + afters :]
    pairs, (start_ref, end_ref, pick_ref, count_ref, sem) = rest[: peers // 2], rest[peers // 2 :]
    segs = lens_ref.shape[1]
    share, _, depth = down_ref.shape
    cols = up_ref.shape[2]
    me = me_ref[0]

    def clear(q, carry):
        pick_ref[q] = 0
        start_ref[q] = 0
        end_ref[q] = 0
        return carry

    lax.fori_loop(0, peers * CAP, clear, 0, unroll=8)
    for x in range(peers):
        count_ref[x] = 0

    def copies(x, c, source):
        pack = pairs[x // 2].at[x % 2, c]
        return (
            pltpu.make_async_copy(down_ref.at[source], pack.at[:, pl.ds(0, depth)], sem),
            pltpu.make_async_copy(up_ref.at[source], pack.at[:, pl.ds(depth, cols)], sem),
        )

    for x in reversed(range(peers)):

        def choose(s, count):
            local = table_ref[ids_refs[x][0, s]] - me * share
            mine = jnp.logical_and(local >= 0, local < share)

            @pl.when(jnp.logical_and(mine, count < CAP))
            def _():
                pick_ref[x * CAP + count] = local

            return count + mine.astype(jnp.int32)

        lax.fori_loop(0, segs, choose, 0, unroll=4)
        for c in range(CAP):
            for copy in copies(x, c, pick_ref[x * CAP + c]):
                copy.start()

    def place(s, first):
        x = lax.bitwise_xor(table_ref[ids_refs[0][0, s]] // share, me)
        count = count_ref[x]
        last = first + lens_ref[0, s]

        @pl.when(count < CAP)
        def _():
            start_ref[x * CAP + count] = first
            end_ref[x * CAP + count] = last

        count_ref[x] = count + 1
        return last

    lax.fori_loop(0, segs, place, 0, unroll=4)

    for x in range(peers):
        for c in range(CAP):
            for copy in copies(x, c, 0):
                copy.wait()


def pick_adapters(me, table, all_ids, lens, down, up, after):
    peers = len(all_ids)
    _, rank, depth = down.shape
    cols = up.shape[2]
    smem = pl.BlockSpec(memory_space=pltpu.SMEM)
    vmem = pl.BlockSpec(memory_space=pltpu.VMEM)
    hbm = pl.BlockSpec(memory_space=pl.ANY)
    out = pl.pallas_call(
        functools.partial(pick_kernel, peers, len(after)),
        in_specs=[smem] * (3 + peers) + [hbm] * (2 + len(after)),
        out_specs=[vmem] * (peers // 2) + [smem, smem],
        out_shape=[jax.ShapeDtypeStruct((2, CAP, rank, depth + cols), BF16)] * (peers // 2)
        + [jax.ShapeDtypeStruct((peers * CAP,), jnp.int32)] * 2,
        scratch_shapes=[
            pltpu.SMEM((peers * CAP,), jnp.int32),
            pltpu.SMEM((peers,), jnp.int32),
            pltpu.SemaphoreType.DMA,
        ],
        compiler_params=pltpu.CompilerParams(vmem_limit_bytes=VMEM_LIMIT),
        cost_estimate=SMALL,
        name="pick_adapters",
    )(me.reshape(1), table, lens, *all_ids, down, up, *after)
    return list(out[:-2]), out[-2], out[-1]


def exchange(pairs, peers):
    packs = []
    for y, pair in enumerate(pairs):
        if y > 0:
            pair = lax.ppermute(pair, "req", [(i, i ^ (2 * y)) for i in range(peers)])
        other = lax.ppermute(pair, "req", [(i, i ^ 1) for i in range(peers)])
        packs += [(pair, 0), (other, 1)]
    return packs


def pack_spec(pack, first, width):
    array, place = pack
    return pl.BlockSpec((1,) + array.shape[1:3] + (width,), lambda i: (place, 0, 0, first // width))


def low_kernel(peers, start_ref, end_ref, rows_ref, *rest):
    down_refs, out_ref = rest[:peers], rest[-1]
    row_total, depth = rows_ref.shape
    rank = out_ref.shape[0]
    place = lax.broadcasted_iota(jnp.int32, (rank, row_total), 1)
    downs = jnp.concatenate([ref[...].reshape(CAP * rank, depth) for ref in down_refs], axis=0)
    part = lax.dot_general(
        downs, rows_ref[...], (((1,), (1,)), ((), ())), preferred_element_type=F32
    )
    total = jnp.zeros((rank, row_total), F32)
    for q in range(peers * CAP):
        member = jnp.logical_and(place >= start_ref[q], place < end_ref[q])
        total = jnp.where(member, part[q * rank : (q + 1) * rank], total)
    out_ref[...] = total


def low_sums(starts, ends, rows, packs, rank, after):
    row_total, depth = rows.shape
    smem = pl.BlockSpec(memory_space=pltpu.SMEM)
    vmem = pl.BlockSpec(memory_space=pltpu.VMEM)
    return pl.pallas_call(
        functools.partial(low_kernel, len(packs)),
        grid=(1,),
        in_specs=[smem, smem, vmem]
        + [pack_spec(p, 0, depth) for p in packs]
        + [pl.BlockSpec(memory_space=pl.ANY)] * len(after),
        out_specs=vmem,
        out_shape=jax.ShapeDtypeStruct((rank, row_total), F32),
        compiler_params=pltpu.CompilerParams(vmem_limit_bytes=VMEM_LIMIT),
        cost_estimate=SMALL,
        name="low_sums",
    )(starts, ends, rows, *[array for array, _ in packs], *after)


def term_kernel(offsets, peers, start_ref, end_ref, low_ref, came_ref, *rest):
    pieces = len(offsets)
    own_refs, rest = rest[:pieces], rest[pieces:]
    up_refs, out_refs = rest[:peers], rest[-pieces:]
    rank, row_total = low_ref.shape
    cols = sum(ref.shape[1] for ref in out_refs)
    low = low_ref[...] + came_ref[...]
    low = low.astype(BF16).astype(F32)
    place = lax.broadcasted_iota(jnp.int32, (rank, row_total), 1)
    spread = []
    for q in range(len(up_refs) * CAP):
        member = jnp.logical_and(place >= start_ref[q], place < end_ref[q])
        spread.append(jnp.where(member, low, 0.0))
    spread = jnp.concatenate(spread, axis=0).astype(BF16)
    ups = jnp.concatenate([ref[...].reshape(CAP * rank, cols) for ref in up_refs], axis=0)
    for piece in range(pieces):
        columns = slice(offsets[piece], offsets[piece] + out_refs[piece].shape[1])
        term = lax.dot_general(
            spread, ups[:, columns], (((0,), (0,)), ((), ())), preferred_element_type=F32
        )
        out_refs[piece][...] = own_refs[piece][...].astype(F32) + term


def adapter_term(starts, ends, low, came, owns, packs, offsets, after):
    row_total = owns[0].shape[0]
    cols = sum(own.shape[1] for own in owns)
    smem = pl.BlockSpec(memory_space=pltpu.SMEM)
    vmem = pl.BlockSpec(memory_space=pltpu.VMEM)
    depth = packs[0][0].shape[3] - cols
    return pl.pallas_call(
        functools.partial(term_kernel, offsets, len(packs)),
        grid=(1,),
        in_specs=[smem, smem]
        + [vmem] * (2 + len(owns))
        + [pack_spec(p, depth, cols) for p in packs]
        + [pl.BlockSpec(memory_space=pl.ANY)] * len(after),
        out_specs=[vmem] * len(owns),
        out_shape=[jax.ShapeDtypeStruct(own.shape, F32) for own in owns],
        compiler_params=pltpu.CompilerParams(vmem_limit_bytes=VMEM_LIMIT),
        cost_estimate=SMALL,
        name="adapter_term",
    )(starts, ends, low, came, *owns, *[array for array, _ in packs], *after)


def sum_kernel(a_ref, b_ref, *rest):
    rest[-1][...] = a_ref[...] + b_ref[...]


def sum_after(a, b, after):
    vmem = pl.BlockSpec(memory_space=pltpu.VMEM)
    return pl.pallas_call(
        sum_kernel,
        in_specs=[vmem, vmem] + [pl.BlockSpec(memory_space=pl.ANY)] * len(after),
        out_specs=vmem,
        out_shape=jax.ShapeDtypeStruct(a.shape, a.dtype),
        compiler_params=pltpu.CompilerParams(vmem_limit_bytes=VMEM_LIMIT),
        cost_estimate=SMALL,
        name="sum_after",
    )(a, b, *after)


def finish_kernel(addends, term_ref, *rest):
    total = term_ref[...]
    for ref in rest[:addends]:
        total = total + ref[...].astype(F32)
    rest[-1][...] = total.astype(rest[-1].dtype)


def finish(term, arrivals, offset, cols, result, cost):
    row_total, width = term.shape
    height = min(row_total, 128)
    block = pl.BlockSpec((height, width), lambda i: (i, 0))
    held = [] if result is None else [result]
    return pl.pallas_call(
        functools.partial(finish_kernel, len(arrivals)),
        grid=(row_total // height,),
        in_specs=[block] * (1 + len(arrivals)) + [pl.BlockSpec(memory_space=pl.ANY)] * len(held),
        out_specs=pl.BlockSpec((height, width), lambda i: (i, offset // width)),
        out_shape=jax.ShapeDtypeStruct((row_total, cols), BF16),
        input_output_aliases={1 + len(arrivals): 0} if held else {},
        compiler_params=pltpu.CompilerParams(vmem_limit_bytes=VMEM_LIMIT),
        cost_estimate=cost,
        name="finish",
    )(term, *arrivals, *held)


def local(req_total, tp_total, rows, weight, down, up, table, ids, lens):
    weight = pltpu.with_memory_space_constraint(weight, pltpu.HBM)
    down = pltpu.with_memory_space_constraint(down, pltpu.HBM)
    up = pltpu.with_memory_space_constraint(up, pltpu.HBM)
    rank = down.shape[1]
    cols = up.shape[2]
    widths = (cols // 4, cols // 2, cols // 4)
    offsets = (cols // 2, 0, 3 * cols // 4)
    pieces = range(len(widths))
    me_req = lax.axis_index("req").astype(jnp.int32)
    me = lax.axis_index("tp").astype(jnp.int32)
    steps = tp_total - 1

    def move(value, piece):
        pairs = []
        for r in range(req_total):
            way = 1 if (r + piece) % 2 == 0 else tp_total - 1
            for i in range(tp_total):
                pairs.append((r * tp_total + i, r * tp_total + (i + way) % tp_total))
        return lax.ppermute(value, ("req", "tp"), pairs)

    def start_of(back, piece):
        behind = jnp.where(lax.rem(me_req + piece, 2) == 0, tp_total - back, back)
        block = lax.rem(me + behind, tp_total)
        return block * cols + offsets[piece]

    def partial(back, piece, **options):
        return block_product(rows, weight, start_of(back, piece), widths[piece], **options)

    last = first_product(rows, weight, start_of(1, 0), widths[0])
    moving, owns = [move(last, 0)], [None for _ in pieces]
    last, ids = partial(1, 1, after=[last], ids=ids)
    moving.append(move(last, 1))

    all_ids = [ids]
    for x in range(1, req_total):
        all_ids.append(lax.ppermute(ids, "req", [(i, i ^ x) for i in range(req_total)]))
    last = owns[0] = partial(0, 0, after=[last])
    pairs, starts, ends = pick_adapters(me_req, table, all_ids, lens, down, up, [last])
    packs = exchange(pairs, req_total)
    last = partial(1, 2, after=[starts, moving[0]])
    moving.append(move(last, 2))

    for step in range(1, steps):
        for piece in pieces:
            cost = LARGE if step == steps - 1 else SMALL
            last = partial(1 + step, piece, addends=[moving[piece]], after=[last], cost=cost)
            moving[piece] = move(last, piece)
            if step == 1 and piece < 2:
                last = owns[2 - piece] = partial(0, 2 - piece, after=[last], cost=LARGE if piece == 0 else SMALL)
            if step == steps - 1 and piece == 0:
                last = low = low_sums(starts, ends, rows, packs, rank, [last])
                bit = 1
                came = lax.ppermute(low, "tp", [(i, i ^ bit) for i in range(tp_total)])
            if step == steps - 1 and piece == 1:
                while 2 * bit < tp_total:
                    last = low = sum_after(low, came, [last])
                    bit *= 2
                    came = lax.ppermute(low, "tp", [(i, i ^ bit) for i in range(tp_total)])

    terms = adapter_term(starts, ends, low, came, owns, packs, offsets, [last])
    result = None
    for piece in pieces:
        cost = LARGE if piece == 0 else SMALL
        result = finish(terms[piece], [moving[piece]], offsets[piece], cols, result, cost)
    return result


def solution(mesh):
    return jax.shard_map(
        functools.partial(local, mesh.shape["req"], mesh.shape["tp"]),
        mesh=mesh,
        in_specs=(
            P(("groups", "req"), "tp"),
            P("tp", None),
            P(("groups", "req"), None, "tp"),
            P(("groups", "req"), None, "tp"),
            P("groups"),
            P(("groups", "req"), None),
            P(("groups", "req"), None),
        ),
        out_specs=P(("groups", "req"), "tp"),
        check_vma=False,
    )
```

```python
import functools

import jax
import jax.numpy as jnp
from jax import lax
from jax.experimental import pallas as pl
from jax.experimental.pallas import tpu as pltpu
from jax.sharding import PartitionSpec as P

CAP = 6
VMEM_LIMIT = 20 * 1024 * 1024
F32 = jnp.float32
BF16 = jnp.bfloat16
SMALL = pl.CostEstimate(flops=1000, bytes_accessed=1000, transcendentals=0)
LARGE = pl.CostEstimate(flops=2 * 10**10, bytes_accessed=1000, transcendentals=0)


def product_kernel(addends, with_ids, first_ref, rows_ref, weight_ref, *rest):
    out_ref = rest[-1 - with_ids]
    total = jnp.dot(rows_ref[...], weight_ref[...], preferred_element_type=F32)
    for ref in rest[:addends]:
        total = total + ref[...].astype(F32)
    out_ref[...] = total.astype(out_ref.dtype)
    if with_ids:
        ids_ref, ids_out_ref = rest[addends], rest[-1]
        for s in range(ids_ref.shape[1]):
            ids_out_ref[0, s] = ids_ref[0, s]


def block_product(rows, weight, first, width, addends=(), after=(), ids=None, cost=SMALL):
    row_total, depth = rows.shape
    tile = min(256, width)
    with_ids = ids is not None
    smem = pl.BlockSpec(memory_space=pltpu.SMEM)
    hbm = pl.BlockSpec(memory_space=pl.ANY)
    columns = pl.BlockSpec((row_total, tile), lambda j, t: (0, j))
    out_specs, out_shape = [columns], [jax.ShapeDtypeStruct((row_total, width), BF16)]
    if with_ids:
        out_specs.append(smem)
        out_shape.append(jax.ShapeDtypeStruct(ids.shape, ids.dtype))
    out = pl.pallas_call(
        functools.partial(product_kernel, len(addends), with_ids),
        grid_spec=pltpu.PrefetchScalarGridSpec(
            num_scalar_prefetch=1,
            grid=(width // tile,),
            in_specs=[
                pl.BlockSpec((row_total, depth), lambda j, t: (0, 0)),
                pl.BlockSpec((depth, tile), lambda j, t: (0, t[0] + j)),
            ]
            + [columns] * len(addends)
            + [smem] * with_ids
            + [hbm] * len(after),
            out_specs=out_specs,
        ),
        out_shape=out_shape,
        compiler_params=pltpu.CompilerParams(vmem_limit_bytes=VMEM_LIMIT),
        cost_estimate=cost,
        name="block_product",
    )((first // tile).reshape(1), rows, weight, *addends, *([ids] if with_ids else []), *after)
    return out if with_ids else out[0]


def first_kernel(chunk, first_ref, rows_ref, weight_ref, out_ref, lhs_ref, rhs_ref, acc_ref, sems):
    columns = pl.ds(pl.multiple_of(first_ref[0], 128), out_ref.shape[1])
    chunks = lhs_ref.shape[0]

    def copies(k):
        part = pl.ds(k * chunk, chunk)
        return (
            pltpu.make_async_copy(rows_ref.at[:, part], lhs_ref.at[k], sems.at[0, k]),
            pltpu.make_async_copy(weight_ref.at[part, columns], rhs_ref.at[k], sems.at[1, k]),
        )

    for k in range(chunks):
        for copy in copies(k):
            copy.start()
    for k in range(chunks):
        for copy in copies(k):
            copy.wait()
        part = jnp.dot(lhs_ref[k], rhs_ref[k], preferred_element_type=F32)
        if k == 0:
            acc_ref[...] = part
        elif k < chunks - 1:
            acc_ref[...] += part
        else:
            out_ref[...] = (acc_ref[...] + part).astype(out_ref.dtype)


def first_product(rows, weight, first, width):
    row_total, depth = rows.shape
    chunk = min(512, depth // 2)
    chunks = depth // chunk
    hbm = pl.BlockSpec(memory_space=pltpu.HBM)
    return pl.pallas_call(
        functools.partial(first_kernel, chunk),
        in_specs=[pl.BlockSpec(memory_space=pltpu.SMEM), hbm, hbm],
        out_specs=pl.BlockSpec(memory_space=pltpu.VMEM),
        out_shape=jax.ShapeDtypeStruct((row_total, width), BF16),
        scratch_shapes=[
            pltpu.VMEM((chunks, row_total, chunk), BF16),
            pltpu.VMEM((chunks, chunk, width), BF16),
            pltpu.VMEM((row_total, width), F32),
            pltpu.SemaphoreType.DMA((2, chunks)),
        ],
        compiler_params=pltpu.CompilerParams(vmem_limit_bytes=VMEM_LIMIT),
        cost_estimate=SMALL,
        name="first_product",
    )(first.reshape(1), pltpu.with_memory_space_constraint(rows, pltpu.HBM), weight)


def pick_kernel(peers, afters, me_ref, table_ref, lens_ref, *rest):
    ids_refs = rest[:peers]
    down_ref, up_ref = rest[peers : peers + 2]
    rest = rest[peers + 2 + afters :]
    pairs, (start_ref, end_ref, pick_ref, count_ref, sem) = rest[: peers // 2], rest[peers // 2 :]
    segs = lens_ref.shape[1]
    share, _, depth = down_ref.shape
    cols = up_ref.shape[2]
    me = me_ref[0]

    def clear(q, carry):
        pick_ref[q] = 0
        start_ref[q] = 0
        end_ref[q] = 0
        return carry

    lax.fori_loop(0, peers * CAP, clear, 0, unroll=8)
    for x in range(peers):
        count_ref[x] = 0

    def copies(x, c, source):
        pack = pairs[x // 2].at[x % 2, c]
        return (
            pltpu.make_async_copy(down_ref.at[source], pack.at[:, pl.ds(0, depth)], sem),
            pltpu.make_async_copy(up_ref.at[source], pack.at[:, pl.ds(depth, cols)], sem),
        )

    for x in reversed(range(peers)):

        def choose(s, count):
            local = table_ref[ids_refs[x][0, s]] - me * share
            mine = jnp.logical_and(local >= 0, local < share)

            @pl.when(jnp.logical_and(mine, count < CAP))
            def _():
                pick_ref[x * CAP + count] = local

            return count + mine.astype(jnp.int32)

        lax.fori_loop(0, segs, choose, 0, unroll=4)
        for c in range(CAP):
            for copy in copies(x, c, pick_ref[x * CAP + c]):
                copy.start()

    def place(s, first):
        x = lax.bitwise_xor(table_ref[ids_refs[0][0, s]] // share, me)
        count = count_ref[x]
        last = first + lens_ref[0, s]

        @pl.when(count < CAP)
        def _():
            start_ref[x * CAP + count] = first
            end_ref[x * CAP + count] = last

        count_ref[x] = count + 1
        return last

    lax.fori_loop(0, segs, place, 0, unroll=4)

    for x in range(peers):
        for c in range(CAP):
            for copy in copies(x, c, 0):
                copy.wait()


def pick_adapters(me, table, all_ids, lens, down, up, after):
    peers = len(all_ids)
    _, rank, depth = down.shape
    cols = up.shape[2]
    smem = pl.BlockSpec(memory_space=pltpu.SMEM)
    vmem = pl.BlockSpec(memory_space=pltpu.VMEM)
    hbm = pl.BlockSpec(memory_space=pl.ANY)
    out = pl.pallas_call(
        functools.partial(pick_kernel, peers, len(after)),
        in_specs=[smem] * (3 + peers) + [hbm] * (2 + len(after)),
        out_specs=[vmem] * (peers // 2) + [smem, smem],
        out_shape=[jax.ShapeDtypeStruct((2, CAP, rank, depth + cols), BF16)] * (peers // 2)
        + [jax.ShapeDtypeStruct((peers * CAP,), jnp.int32)] * 2,
        scratch_shapes=[
            pltpu.SMEM((peers * CAP,), jnp.int32),
            pltpu.SMEM((peers,), jnp.int32),
            pltpu.SemaphoreType.DMA,
        ],
        compiler_params=pltpu.CompilerParams(vmem_limit_bytes=VMEM_LIMIT),
        cost_estimate=SMALL,
        name="pick_adapters",
    )(me.reshape(1), table, lens, *all_ids, down, up, *after)
    return list(out[:-2]), out[-2], out[-1]


def exchange(pairs, peers):
    packs = []
    for y, pair in enumerate(pairs):
        if y > 0:
            pair = lax.ppermute(pair, "req", [(i, i ^ (2 * y)) for i in range(peers)])
        other = lax.ppermute(pair, "req", [(i, i ^ 1) for i in range(peers)])
        packs += [(pair, 0), (other, 1)]
    return packs


def pack_spec(pack, first, width):
    array, place = pack
    return pl.BlockSpec((1,) + array.shape[1:3] + (width,), lambda i: (place, 0, 0, first // width))


def low_kernel(peers, start_ref, end_ref, rows_ref, *rest):
    down_refs, out_ref = rest[:peers], rest[-1]
    row_total, depth = rows_ref.shape
    rank = out_ref.shape[0]
    place = lax.broadcasted_iota(jnp.int32, (rank, row_total), 1)
    downs = jnp.concatenate([ref[...].reshape(CAP * rank, depth) for ref in down_refs], axis=0)
    part = lax.dot_general(
        downs, rows_ref[...], (((1,), (1,)), ((), ())), preferred_element_type=F32
    )
    total = jnp.zeros((rank, row_total), F32)
    for q in range(peers * CAP):
        member = jnp.logical_and(place >= start_ref[q], place < end_ref[q])
        total = jnp.where(member, part[q * rank : (q + 1) * rank], total)
    out_ref[...] = total.astype(BF16)


def low_sums(starts, ends, rows, packs, rank, after):
    row_total, depth = rows.shape
    smem = pl.BlockSpec(memory_space=pltpu.SMEM)
    vmem = pl.BlockSpec(memory_space=pltpu.VMEM)
    return pl.pallas_call(
        functools.partial(low_kernel, len(packs)),
        grid=(1,),
        in_specs=[smem, smem, vmem]
        + [pack_spec(p, 0, depth) for p in packs]
        + [pl.BlockSpec(memory_space=pl.ANY)] * len(after),
        out_specs=vmem,
        out_shape=jax.ShapeDtypeStruct((rank, row_total), BF16),
        compiler_params=pltpu.CompilerParams(vmem_limit_bytes=VMEM_LIMIT),
        cost_estimate=SMALL,
        name="low_sums",
    )(starts, ends, rows, *[array for array, _ in packs], *after)


def term_kernel(offsets, lows, peers, start_ref, end_ref, *rest):
    pieces = len(offsets)
    low_refs, rest = rest[:lows], rest[lows:]
    own_refs, rest = rest[:pieces], rest[pieces:]
    up_refs, out_refs = rest[:peers], rest[-pieces:]
    rank, row_total = low_refs[0].shape
    cols = sum(ref.shape[1] for ref in out_refs)
    low = low_refs[0][...].astype(F32)
    for ref in low_refs[1:]:
        low = low + ref[...].astype(F32)
    low = low.astype(BF16).astype(F32)
    place = lax.broadcasted_iota(jnp.int32, (rank, row_total), 1)
    spread = []
    for q in range(len(up_refs) * CAP):
        member = jnp.logical_and(place >= start_ref[q], place < end_ref[q])
        spread.append(jnp.where(member, low, 0.0))
    spread = jnp.concatenate(spread, axis=0).astype(BF16)
    ups = jnp.concatenate([ref[...].reshape(CAP * rank, cols) for ref in up_refs], axis=0)
    for piece in range(pieces):
        columns = slice(offsets[piece], offsets[piece] + out_refs[piece].shape[1])
        term = lax.dot_general(
            spread, ups[:, columns], (((0,), (0,)), ((), ())), preferred_element_type=F32
        )
        out_refs[piece][...] = own_refs[piece][...].astype(F32) + term


def adapter_term(starts, ends, lows, owns, packs, offsets, after):
    row_total = owns[0].shape[0]
    cols = sum(own.shape[1] for own in owns)
    smem = pl.BlockSpec(memory_space=pltpu.SMEM)
    vmem = pl.BlockSpec(memory_space=pltpu.VMEM)
    depth = packs[0][0].shape[3] - cols
    return pl.pallas_call(
        functools.partial(term_kernel, offsets, len(lows), len(packs)),
        grid=(1,),
        in_specs=[smem, smem]
        + [vmem] * (len(lows) + len(owns))
        + [pack_spec(p, depth, cols) for p in packs]
        + [pl.BlockSpec(memory_space=pl.ANY)] * len(after),
        out_specs=[vmem] * len(owns),
        out_shape=[jax.ShapeDtypeStruct(own.shape, F32) for own in owns],
        compiler_params=pltpu.CompilerParams(vmem_limit_bytes=VMEM_LIMIT),
        cost_estimate=SMALL,
        name="adapter_term",
    )(starts, ends, *lows, *owns, *[array for array, _ in packs], *after)


def finish_kernel(addends, term_ref, *rest):
    total = term_ref[...]
    for ref in rest[:addends]:
        total = total + ref[...].astype(F32)
    rest[-1][...] = total.astype(rest[-1].dtype)


def finish(term, arrivals, offset, cols, result, cost):
    row_total, width = term.shape
    height = min(row_total, 128)
    block = pl.BlockSpec((height, width), lambda i: (i, 0))
    held = [] if result is None else [result]
    return pl.pallas_call(
        functools.partial(finish_kernel, len(arrivals)),
        grid=(row_total // height,),
        in_specs=[block] * (1 + len(arrivals)) + [pl.BlockSpec(memory_space=pl.ANY)] * len(held),
        out_specs=pl.BlockSpec((height, width), lambda i: (i, offset // width)),
        out_shape=jax.ShapeDtypeStruct((row_total, cols), BF16),
        input_output_aliases={1 + len(arrivals): 0} if held else {},
        compiler_params=pltpu.CompilerParams(vmem_limit_bytes=VMEM_LIMIT),
        cost_estimate=cost,
        name="finish",
    )(term, *arrivals, *held)


def local(req_total, tp_total, rows, weight, down, up, table, ids, lens):
    weight = pltpu.with_memory_space_constraint(weight, pltpu.HBM)
    down = pltpu.with_memory_space_constraint(down, pltpu.HBM)
    up = pltpu.with_memory_space_constraint(up, pltpu.HBM)
    rank = down.shape[1]
    cols = up.shape[2]
    widths = (cols // 4, cols // 2, cols // 4)
    offsets = (cols // 2, 0, 3 * cols // 4)
    pieces = range(len(widths))
    me_req = lax.axis_index("req").astype(jnp.int32)
    me = lax.axis_index("tp").astype(jnp.int32)
    steps = tp_total - 1

    def move(value, piece):
        pairs = []
        for r in range(req_total):
            way = 1 if (r + piece) % 2 == 0 else tp_total - 1
            for i in range(tp_total):
                pairs.append((r * tp_total + i, r * tp_total + (i + way) % tp_total))
        return lax.ppermute(value, ("req", "tp"), pairs)

    def start_of(back, piece):
        behind = jnp.where(lax.rem(me_req + piece, 2) == 0, tp_total - back, back)
        block = lax.rem(me + behind, tp_total)
        return block * cols + offsets[piece]

    def partial(back, piece, **options):
        return block_product(rows, weight, start_of(back, piece), widths[piece], **options)

    last = first_product(rows, weight, start_of(1, 0), widths[0])
    moving, owns = [move(last, 0)], [None for _ in pieces]
    last, ids = partial(1, 1, after=[last], ids=ids)
    moving.append(move(last, 1))

    all_ids = [ids]
    for x in range(1, req_total):
        all_ids.append(lax.ppermute(ids, "req", [(i, i ^ x) for i in range(req_total)]))
    last = owns[0] = partial(0, 0, after=[last])
    pairs, starts, ends = pick_adapters(me_req, table, all_ids, lens, down, up, [last])
    packs = exchange(pairs, req_total)
    last = partial(1, 2, after=[starts, moving[0]])
    moving.append(move(last, 2))

    for step in range(1, steps):
        for piece in pieces:
            cost = LARGE if step == steps - 1 else SMALL
            last = partial(1 + step, piece, addends=[moving[piece]], after=[last], cost=cost)
            moving[piece] = move(last, piece)
            if step == 1 and piece < 2:
                last = owns[2 - piece] = partial(0, 2 - piece, after=[last], cost=LARGE if piece == 0 else SMALL)
            if step == steps - 1 and piece == 0:
                last = low = low_sums(starts, ends, rows, packs, rank, [last])
                lows = [low]
                for x in range(1, tp_total):
                    pairs = [(i, i ^ x) for i in range(tp_total)]
                    lows.append(lax.ppermute(low, "tp", pairs))

    terms = adapter_term(starts, ends, lows, owns, packs, offsets, [last])
    result = None
    for piece in pieces:
        cost = LARGE if piece == 0 else SMALL
        result = finish(terms[piece], [moving[piece]], offsets[piece], cols, result, cost)
    return result


def solution(mesh):
    return jax.shard_map(
        functools.partial(local, mesh.shape["req"], mesh.shape["tp"]),
        mesh=mesh,
        in_specs=(
            P(("groups", "req"), "tp"),
            P("tp", None),
            P(("groups", "req"), None, "tp"),
            P(("groups", "req"), None, "tp"),
            P("groups"),
            P(("groups", "req"), None),
            P(("groups", "req"), None),
        ),
        out_specs=P(("groups", "req"), "tp"),
        check_vma=False,
    )
```

```python
import functools

import jax
import jax.numpy as jnp
from jax import lax
from jax.experimental import pallas as pl
from jax.experimental.pallas import tpu as pltpu
from jax.sharding import PartitionSpec as P

CAP = 6
VMEM_LIMIT = 20 * 1024 * 1024
F32 = jnp.float32
BF16 = jnp.bfloat16
SMALL = pl.CostEstimate(flops=1000, bytes_accessed=1000, transcendentals=0)
LARGE = pl.CostEstimate(flops=2 * 10**10, bytes_accessed=1000, transcendentals=0)


def product_kernel(addends, with_ids, first_ref, rows_ref, weight_ref, *rest):
    out_ref = rest[-1 - with_ids]
    total = jnp.dot(rows_ref[...], weight_ref[...], preferred_element_type=F32)
    for ref in rest[:addends]:
        total = total + ref[...].astype(F32)
    out_ref[...] = total.astype(out_ref.dtype)
    if with_ids:
        ids_ref, ids_out_ref = rest[addends], rest[-1]
        for s in range(ids_ref.shape[1]):
            ids_out_ref[0, s] = ids_ref[0, s]


def block_product(rows, weight, first, width, addends=(), after=(), ids=None, cost=SMALL):
    row_total, depth = rows.shape
    tile = min(256, width)
    with_ids = ids is not None
    smem = pl.BlockSpec(memory_space=pltpu.SMEM)
    hbm = pl.BlockSpec(memory_space=pl.ANY)
    columns = pl.BlockSpec((row_total, tile), lambda j, t: (0, j))
    out_specs, out_shape = [columns], [jax.ShapeDtypeStruct((row_total, width), BF16)]
    if with_ids:
        out_specs.append(smem)
        out_shape.append(jax.ShapeDtypeStruct(ids.shape, ids.dtype))
    out = pl.pallas_call(
        functools.partial(product_kernel, len(addends), with_ids),
        grid_spec=pltpu.PrefetchScalarGridSpec(
            num_scalar_prefetch=1,
            grid=(width // tile,),
            in_specs=[
                pl.BlockSpec((row_total, depth), lambda j, t: (0, 0)),
                pl.BlockSpec((depth, tile), lambda j, t: (0, t[0] + j)),
            ]
            + [columns] * len(addends)
            + [smem] * with_ids
            + [hbm] * len(after),
            out_specs=out_specs,
        ),
        out_shape=out_shape,
        compiler_params=pltpu.CompilerParams(vmem_limit_bytes=VMEM_LIMIT),
        cost_estimate=cost,
        name="block_product",
    )((first // tile).reshape(1), rows, weight, *addends, *([ids] if with_ids else []), *after)
    return out if with_ids else out[0]


def first_kernel(chunk, first_ref, rows_ref, weight_ref, out_ref, lhs_ref, rhs_ref, acc_ref, sems):
    columns = pl.ds(pl.multiple_of(first_ref[0], 128), out_ref.shape[1])
    chunks = lhs_ref.shape[0]

    def copies(k):
        part = pl.ds(k * chunk, chunk)
        return (
            pltpu.make_async_copy(rows_ref.at[:, part], lhs_ref.at[k], sems.at[0, k]),
            pltpu.make_async_copy(weight_ref.at[part, columns], rhs_ref.at[k], sems.at[1, k]),
        )

    for k in range(chunks):
        for copy in copies(k):
            copy.start()
    for k in range(chunks):
        for copy in copies(k):
            copy.wait()
        part = jnp.dot(lhs_ref[k], rhs_ref[k], preferred_element_type=F32)
        if k == 0:
            acc_ref[...] = part
        elif k < chunks - 1:
            acc_ref[...] += part
        else:
            out_ref[...] = (acc_ref[...] + part).astype(out_ref.dtype)


def first_product(rows, weight, first, width):
    row_total, depth = rows.shape
    chunk = min(512, depth // 2)
    chunks = depth // chunk
    hbm = pl.BlockSpec(memory_space=pltpu.HBM)
    return pl.pallas_call(
        functools.partial(first_kernel, chunk),
        in_specs=[pl.BlockSpec(memory_space=pltpu.SMEM), hbm, hbm],
        out_specs=pl.BlockSpec(memory_space=pltpu.VMEM),
        out_shape=jax.ShapeDtypeStruct((row_total, width), BF16),
        scratch_shapes=[
            pltpu.VMEM((chunks, row_total, chunk), BF16),
            pltpu.VMEM((chunks, chunk, width), BF16),
            pltpu.VMEM((row_total, width), F32),
            pltpu.SemaphoreType.DMA((2, chunks)),
        ],
        compiler_params=pltpu.CompilerParams(vmem_limit_bytes=VMEM_LIMIT),
        cost_estimate=SMALL,
        name="first_product",
    )(first.reshape(1), pltpu.with_memory_space_constraint(rows, pltpu.HBM), weight)


def pick_kernel(peers, afters, me_ref, table_ref, lens_ref, *rest):
    ids_refs = rest[:peers]
    down_ref, up_ref = rest[peers : peers + 2]
    rest = rest[peers + 2 + afters :]
    pairs, (start_ref, end_ref, pick_ref, count_ref, sem) = rest[: peers // 2], rest[peers // 2 :]
    segs = lens_ref.shape[1]
    share, _, depth = down_ref.shape
    cols = up_ref.shape[2]
    me = me_ref[0]

    def clear(q, carry):
        pick_ref[q] = 0
        start_ref[q] = 0
        end_ref[q] = 0
        return carry

    lax.fori_loop(0, peers * CAP, clear, 0, unroll=8)
    for x in range(peers):
        count_ref[x] = 0

    def copies(x, c, source):
        pack = pairs[x // 2].at[x % 2, c]
        return (
            pltpu.make_async_copy(down_ref.at[source], pack.at[:, pl.ds(0, depth)], sem),
            pltpu.make_async_copy(up_ref.at[source], pack.at[:, pl.ds(depth, cols)], sem),
        )

    for x in reversed(range(peers)):

        def choose(s, count):
            local = table_ref[ids_refs[x][0, s]] - me * share
            mine = jnp.logical_and(local >= 0, local < share)

            @pl.when(jnp.logical_and(mine, count < CAP))
            def _():
                pick_ref[x * CAP + count] = local

            return count + mine.astype(jnp.int32)

        lax.fori_loop(0, segs, choose, 0, unroll=4)
        for c in range(CAP):
            for copy in copies(x, c, pick_ref[x * CAP + c]):
                copy.start()

    def place(s, first):
        x = lax.bitwise_xor(table_ref[ids_refs[0][0, s]] // share, me)
        count = count_ref[x]
        last = first + lens_ref[0, s]

        @pl.when(count < CAP)
        def _():
            start_ref[x * CAP + count] = first
            end_ref[x * CAP + count] = last

        count_ref[x] = count + 1
        return last

    lax.fori_loop(0, segs, place, 0, unroll=4)

    for x in range(peers):
        for c in range(CAP):
            for copy in copies(x, c, 0):
                copy.wait()


def pick_adapters(me, table, all_ids, lens, down, up, after):
    peers = len(all_ids)
    _, rank, depth = down.shape
    cols = up.shape[2]
    smem = pl.BlockSpec(memory_space=pltpu.SMEM)
    vmem = pl.BlockSpec(memory_space=pltpu.VMEM)
    hbm = pl.BlockSpec(memory_space=pl.ANY)
    out = pl.pallas_call(
        functools.partial(pick_kernel, peers, len(after)),
        in_specs=[smem] * (3 + peers) + [hbm] * (2 + len(after)),
        out_specs=[vmem] * (peers // 2) + [smem, smem],
        out_shape=[jax.ShapeDtypeStruct((2, CAP, rank, depth + cols), BF16)] * (peers // 2)
        + [jax.ShapeDtypeStruct((peers * CAP,), jnp.int32)] * 2,
        scratch_shapes=[
            pltpu.SMEM((peers * CAP,), jnp.int32),
            pltpu.SMEM((peers,), jnp.int32),
            pltpu.SemaphoreType.DMA,
        ],
        compiler_params=pltpu.CompilerParams(vmem_limit_bytes=VMEM_LIMIT),
        cost_estimate=SMALL,
        name="pick_adapters",
    )(me.reshape(1), table, lens, *all_ids, down, up, *after)
    return list(out[:-2]), out[-2], out[-1]


def exchange(pairs, peers):
    packs = []
    for y, pair in enumerate(pairs):
        if y > 0:
            pair = lax.ppermute(pair, "req", [(i, i ^ (2 * y)) for i in range(peers)])
        other = lax.ppermute(pair, "req", [(i, i ^ 1) for i in range(peers)])
        packs += [(pair, 0), (other, 1)]
    return packs


def pack_spec(pack, first, width):
    array, place = pack
    return pl.BlockSpec((1,) + array.shape[1:3] + (width,), lambda i: (place, 0, 0, first // width))


def low_kernel(peers, start_ref, end_ref, rows_ref, *rest):
    down_refs, out_ref = rest[:peers], rest[-1]
    row_total, depth = rows_ref.shape
    rank = out_ref.shape[0]
    place = lax.broadcasted_iota(jnp.int32, (rank, row_total), 1)
    downs = jnp.concatenate([ref[...].reshape(CAP * rank, depth) for ref in down_refs], axis=0)
    part = lax.dot_general(
        downs, rows_ref[...], (((1,), (1,)), ((), ())), preferred_element_type=F32
    )
    total = jnp.zeros((rank, row_total), F32)
    for q in range(peers * CAP):
        member = jnp.logical_and(place >= start_ref[q], place < end_ref[q])
        total = jnp.where(member, part[q * rank : (q + 1) * rank], total)
    out_ref[...] = total.astype(BF16)


def low_sums(starts, ends, rows, packs, rank, after):
    row_total, depth = rows.shape
    smem = pl.BlockSpec(memory_space=pltpu.SMEM)
    vmem = pl.BlockSpec(memory_space=pltpu.VMEM)
    return pl.pallas_call(
        functools.partial(low_kernel, len(packs)),
        grid=(1,),
        in_specs=[smem, smem, vmem]
        + [pack_spec(p, 0, depth) for p in packs]
        + [pl.BlockSpec(memory_space=pl.ANY)] * len(after),
        out_specs=vmem,
        out_shape=jax.ShapeDtypeStruct((rank, row_total), BF16),
        compiler_params=pltpu.CompilerParams(vmem_limit_bytes=VMEM_LIMIT),
        cost_estimate=SMALL,
        name="low_sums",
    )(starts, ends, rows, *[array for array, _ in packs], *after)


def term_kernel(offsets, lows, peers, start_ref, end_ref, *rest):
    pieces = len(offsets)
    low_refs, rest = rest[:lows], rest[lows:]
    own_refs, rest = rest[:pieces], rest[pieces:]
    up_refs, out_refs = rest[:peers], rest[-pieces:]
    rank, row_total = low_refs[0].shape
    cols = sum(ref.shape[1] for ref in out_refs)
    low = low_refs[0][...].astype(F32)
    for ref in low_refs[1:]:
        low = low + ref[...].astype(F32)
    low = low.astype(BF16).astype(F32)
    place = lax.broadcasted_iota(jnp.int32, (rank, row_total), 1)
    spread = []
    for q in range(len(up_refs) * CAP):
        member = jnp.logical_and(place >= start_ref[q], place < end_ref[q])
        spread.append(jnp.where(member, low, 0.0))
    spread = jnp.concatenate(spread, axis=0).astype(BF16)
    ups = jnp.concatenate([ref[...].reshape(CAP * rank, cols) for ref in up_refs], axis=0)
    for piece in range(pieces):
        columns = slice(offsets[piece], offsets[piece] + out_refs[piece].shape[1])
        term = lax.dot_general(
            spread, ups[:, columns], (((0,), (0,)), ((), ())), preferred_element_type=F32
        )
        out_refs[piece][...] = own_refs[piece][...].astype(F32) + term


def adapter_term(starts, ends, lows, owns, packs, offsets, after):
    row_total = owns[0].shape[0]
    cols = sum(own.shape[1] for own in owns)
    smem = pl.BlockSpec(memory_space=pltpu.SMEM)
    vmem = pl.BlockSpec(memory_space=pltpu.VMEM)
    depth = packs[0][0].shape[3] - cols
    return pl.pallas_call(
        functools.partial(term_kernel, offsets, len(lows), len(packs)),
        grid=(1,),
        in_specs=[smem, smem]
        + [vmem] * (len(lows) + len(owns))
        + [pack_spec(p, depth, cols) for p in packs]
        + [pl.BlockSpec(memory_space=pl.ANY)] * len(after),
        out_specs=[vmem] * len(owns),
        out_shape=[jax.ShapeDtypeStruct(own.shape, F32) for own in owns],
        compiler_params=pltpu.CompilerParams(vmem_limit_bytes=VMEM_LIMIT),
        cost_estimate=SMALL,
        name="adapter_term",
    )(starts, ends, *lows, *owns, *[array for array, _ in packs], *after)


def finish_kernel(addends, term_ref, *rest):
    total = term_ref[...]
    for ref in rest[:addends]:
        total = total + ref[...].astype(F32)
    rest[-1][...] = total.astype(rest[-1].dtype)


def finish(term, arrivals, offset, cols, result, cost):
    row_total, width = term.shape
    height = min(row_total, 128)
    block = pl.BlockSpec((height, width), lambda i: (i, 0))
    held = [] if result is None else [result]
    return pl.pallas_call(
        functools.partial(finish_kernel, len(arrivals)),
        grid=(row_total // height,),
        in_specs=[block] * (1 + len(arrivals)) + [pl.BlockSpec(memory_space=pl.ANY)] * len(held),
        out_specs=pl.BlockSpec((height, width), lambda i: (i, offset // width)),
        out_shape=jax.ShapeDtypeStruct((row_total, cols), BF16),
        input_output_aliases={1 + len(arrivals): 0} if held else {},
        compiler_params=pltpu.CompilerParams(vmem_limit_bytes=VMEM_LIMIT),
        cost_estimate=cost,
        name="finish",
    )(term, *arrivals, *held)


def local(req_total, tp_total, rows, weight, down, up, table, ids, lens):
    weight = pltpu.with_memory_space_constraint(weight, pltpu.HBM)
    down = pltpu.with_memory_space_constraint(down, pltpu.HBM)
    up = pltpu.with_memory_space_constraint(up, pltpu.HBM)
    rank = down.shape[1]
    cols = up.shape[2]
    widths = (cols // 4, cols // 2, cols // 4)
    offsets = (cols // 2, 0, 3 * cols // 4)
    pieces = range(len(widths))
    me_req = lax.axis_index("req").astype(jnp.int32)
    me = lax.axis_index("tp").astype(jnp.int32)
    steps = tp_total - 1

    def move(value, piece):
        pairs = []
        for r in range(req_total):
            way = 1 if (r + piece) % 2 == 0 else tp_total - 1
            for i in range(tp_total):
                pairs.append((r * tp_total + i, r * tp_total + (i + way) % tp_total))
        return lax.ppermute(value, ("req", "tp"), pairs)

    def start_of(back, piece):
        behind = jnp.where(lax.rem(me_req + piece, 2) == 0, tp_total - back, back)
        block = lax.rem(me + behind, tp_total)
        return block * cols + offsets[piece]

    def partial(back, piece, **options):
        return block_product(rows, weight, start_of(back, piece), widths[piece], **options)

    last = first_product(rows, weight, start_of(1, 0), widths[0])
    moving, owns = [move(last, 0)], [None for _ in pieces]
    last, ids = partial(1, 1, after=[last], ids=ids)
    moving.append(move(last, 1))

    all_ids = [ids]
    for x in range(1, req_total):
        all_ids.append(lax.ppermute(ids, "req", [(i, i ^ x) for i in range(req_total)]))
    last = owns[0] = partial(0, 0, after=[last])
    pairs, starts, ends = pick_adapters(me_req, table, all_ids, lens, down, up, [last])
    packs = exchange(pairs, req_total)
    last = partial(1, 2, after=[starts, moving[0]])
    moving.append(move(last, 2))

    for step in range(1, steps):
        for piece in pieces:
            last = partial(1 + step, piece, addends=[moving[piece]], after=[last])
            moving[piece] = move(last, piece)
            if step == 1 and piece == 0:
                last = owns[2] = partial(0, 2, after=[last], cost=LARGE)
            if step == steps - 1 and piece == 0:
                last = owns[1] = partial(0, 1, after=[last], cost=LARGE)
            if step == steps - 1 and piece == 0:
                last = low = low_sums(starts, ends, rows, packs, rank, [last])
                lows = [low]
                for x in range(1, tp_total):
                    pairs = [(i, i ^ x) for i in range(tp_total)]
                    lows.append(lax.ppermute(low, "tp", pairs))

    terms = adapter_term(starts, ends, lows, owns, packs, offsets, [last])
    result = None
    for piece in (0, 2, 1):
        cost = LARGE if piece == 0 else SMALL
        result = finish(terms[piece], [moving[piece]], offsets[piece], cols, result, cost)
    return result


def solution(mesh):
    return jax.shard_map(
        functools.partial(local, mesh.shape["req"], mesh.shape["tp"]),
        mesh=mesh,
        in_specs=(
            P(("groups", "req"), "tp"),
            P("tp", None),
            P(("groups", "req"), None, "tp"),
            P(("groups", "req"), None, "tp"),
            P("groups"),
            P(("groups", "req"), None),
            P(("groups", "req"), None),
        ),
        out_specs=P(("groups", "req"), "tp"),
        check_vma=False,
    )
```

```python
import functools

import jax
import jax.numpy as jnp
from jax import lax
from jax.experimental import pallas as pl
from jax.experimental.pallas import tpu as pltpu
from jax.sharding import PartitionSpec as P

CAP = 6
PIECES = 2
VMEM_LIMIT = 20 * 1024 * 1024
F32 = jnp.float32
BF16 = jnp.bfloat16
SMALL = pl.CostEstimate(flops=1000, bytes_accessed=1000, transcendentals=0)
LARGE = pl.CostEstimate(flops=2 * 10**10, bytes_accessed=1000, transcendentals=0)


def product_kernel(addends, with_ids, first_ref, rows_ref, weight_ref, *rest):
    out_ref = rest[-1 - with_ids]
    total = jnp.dot(rows_ref[...], weight_ref[...], preferred_element_type=F32)
    for ref in rest[:addends]:
        total = total + ref[...].astype(F32)
    out_ref[...] = total.astype(out_ref.dtype)
    if with_ids:
        ids_ref, ids_out_ref = rest[addends], rest[-1]
        for s in range(ids_ref.shape[1]):
            ids_out_ref[0, s] = ids_ref[0, s]


def block_product(
    rows, weight, first, width, addends=(), skip=0, after=(), ids=None, cost=SMALL
):
    row_total, depth = rows.shape
    tile = min(256, width)
    with_ids = ids is not None
    smem = pl.BlockSpec(memory_space=pltpu.SMEM)
    hbm = pl.BlockSpec(memory_space=pl.ANY)
    columns = pl.BlockSpec((row_total, tile), lambda j, t: (0, j))
    out_specs, out_shape = [columns], [jax.ShapeDtypeStruct((row_total, width), BF16)]
    if with_ids:
        out_specs.append(smem)
        out_shape.append(jax.ShapeDtypeStruct(ids.shape, ids.dtype))
    out = pl.pallas_call(
        functools.partial(product_kernel, len(addends), with_ids),
        grid_spec=pltpu.PrefetchScalarGridSpec(
            num_scalar_prefetch=1,
            grid=(width // tile,),
            in_specs=[
                pl.BlockSpec((row_total, depth), lambda j, t: (0, 0)),
                pl.BlockSpec((depth, tile), lambda j, t: (0, t[0] + j)),
            ]
            + [pl.BlockSpec((row_total, tile), lambda j, t: (0, skip // tile + j))] * len(addends)
            + [smem] * with_ids
            + [hbm] * len(after),
            out_specs=out_specs,
        ),
        out_shape=out_shape,
        compiler_params=pltpu.CompilerParams(vmem_limit_bytes=VMEM_LIMIT),
        cost_estimate=cost,
        name="block_product",
    )((first // tile).reshape(1), rows, weight, *addends, *([ids] if with_ids else []), *after)
    return out if with_ids else out[0]


def first_kernel(chunk, first_ref, rows_ref, weight_ref, out_ref, lhs_ref, rhs_ref, acc_ref, sems):
    columns = pl.ds(pl.multiple_of(first_ref[0], 128), out_ref.shape[1])
    chunks = rhs_ref.shape[0]

    def copies(k):
        part = pl.ds(k * chunk, chunk)
        return (
            pltpu.make_async_copy(rows_ref.at[:, part], lhs_ref.at[:, part], sems.at[0, k]),
            pltpu.make_async_copy(weight_ref.at[part, columns], rhs_ref.at[k], sems.at[1, k]),
        )

    for k in range(chunks):
        for copy in copies(k):
            copy.start()
    for k in range(chunks):
        for copy in copies(k):
            copy.wait()
        lhs = lhs_ref[:, k * chunk : (k + 1) * chunk]
        part = jnp.dot(lhs, rhs_ref[k], preferred_element_type=F32)
        if k == 0:
            acc_ref[...] = part
        elif k < chunks - 1:
            acc_ref[...] += part
        else:
            out_ref[...] = (acc_ref[...] + part).astype(out_ref.dtype)


def first_product(rows, weight, first, width):
    row_total, depth = rows.shape
    chunk = min(512, depth // 2)
    chunks = depth // chunk
    hbm = pl.BlockSpec(memory_space=pltpu.HBM)
    return pl.pallas_call(
        functools.partial(first_kernel, chunk),
        in_specs=[pl.BlockSpec(memory_space=pltpu.SMEM), hbm, hbm],
        out_specs=[pl.BlockSpec(memory_space=pltpu.VMEM)] * 2,
        out_shape=[
            jax.ShapeDtypeStruct((row_total, width), BF16),
            jax.ShapeDtypeStruct((row_total, depth), BF16),
        ],
        scratch_shapes=[
            pltpu.VMEM((chunks, chunk, width), BF16),
            pltpu.VMEM((row_total, width), F32),
            pltpu.SemaphoreType.DMA((2, chunks)),
        ],
        compiler_params=pltpu.CompilerParams(vmem_limit_bytes=VMEM_LIMIT),
        cost_estimate=SMALL,
        name="first_product",
    )(first.reshape(1), pltpu.with_memory_space_constraint(rows, pltpu.HBM), weight)


def pick_kernel(peers, afters, me_ref, table_ref, lens_ref, *rest):
    ids_refs = rest[:peers]
    down_ref, up_ref = rest[peers : peers + 2]
    rest = rest[peers + 2 + afters :]
    packs, (start_ref, end_ref, pick_ref, count_ref, sem) = rest[:peers], rest[peers:]
    segs = lens_ref.shape[1]
    share, _, depth = down_ref.shape
    cols = up_ref.shape[2]
    me = me_ref[0]

    def clear(q, carry):
        pick_ref[q] = 0
        start_ref[q] = 0
        end_ref[q] = 0
        return carry

    lax.fori_loop(0, peers * CAP, clear, 0, unroll=8)
    for x in range(peers):
        count_ref[x] = 0

    def copies(x, c, source):
        pack = packs[x].at[c]
        return (
            pltpu.make_async_copy(down_ref.at[source], pack.at[:, pl.ds(0, depth)], sem),
            pltpu.make_async_copy(up_ref.at[source], pack.at[:, pl.ds(depth, cols)], sem),
        )

    for x in reversed(range(peers)):

        def choose(s, count):
            local = table_ref[ids_refs[x][0, s]] - me * share
            mine = jnp.logical_and(local >= 0, local < share)

            @pl.when(jnp.logical_and(mine, count < CAP))
            def _():
                pick_ref[x * CAP + count] = local

            return count + mine.astype(jnp.int32)

        lax.fori_loop(0, segs, choose, 0, unroll=4)
        for c in range(CAP):
            for copy in copies(x, c, pick_ref[x * CAP + c]):
                copy.start()

    def place(s, first):
        x = lax.bitwise_xor(table_ref[ids_refs[0][0, s]] // share, me)
        count = count_ref[x]
        last = first + lens_ref[0, s]

        @pl.when(count < CAP)
        def _():
            start_ref[x * CAP + count] = first
            end_ref[x * CAP + count] = last

        count_ref[x] = count + 1
        return last

    lax.fori_loop(0, segs, place, 0, unroll=4)

    for x in range(peers):
        for c in range(CAP):
            for copy in copies(x, c, 0):
                copy.wait()


def pick_adapters(me, table, all_ids, lens, down, up, after):
    peers = len(all_ids)
    _, rank, depth = down.shape
    cols = up.shape[2]
    smem = pl.BlockSpec(memory_space=pltpu.SMEM)
    vmem = pl.BlockSpec(memory_space=pltpu.VMEM)
    hbm = pl.BlockSpec(memory_space=pl.ANY)
    out = pl.pallas_call(
        functools.partial(pick_kernel, peers, len(after)),
        in_specs=[smem] * (3 + peers) + [hbm] * (2 + len(after)),
        out_specs=[vmem] * peers + [smem, smem],
        out_shape=[jax.ShapeDtypeStruct((CAP, rank, depth + cols), BF16)] * peers
        + [jax.ShapeDtypeStruct((peers * CAP,), jnp.int32)] * 2,
        scratch_shapes=[
            pltpu.SMEM((peers * CAP,), jnp.int32),
            pltpu.SMEM((peers,), jnp.int32),
            pltpu.SemaphoreType.DMA,
        ],
        compiler_params=pltpu.CompilerParams(vmem_limit_bytes=VMEM_LIMIT),
        cost_estimate=SMALL,
        name="pick_adapters",
    )(me.reshape(1), table, lens, *all_ids, down, up, *after)
    return list(out[:-2]), out[-2], out[-1]


def pack_spec(pack, first, width):
    return pl.BlockSpec(pack.shape[:2] + (width,), lambda i: (0, 0, first // width))


def low_kernel(peers, start_ref, end_ref, rows_ref, *rest):
    down_refs, out_ref = rest[:peers], rest[-1]
    row_total, depth = rows_ref.shape
    rank = out_ref.shape[0]
    place = lax.broadcasted_iota(jnp.int32, (rank, row_total), 1)
    downs = jnp.concatenate([ref[...].reshape(CAP * rank, depth) for ref in down_refs], axis=0)
    part = lax.dot_general(
        downs, rows_ref[...], (((1,), (1,)), ((), ())), preferred_element_type=F32
    )
    total = jnp.zeros((rank, row_total), F32)
    for q in range(peers * CAP):
        member = jnp.logical_and(place >= start_ref[q], place < end_ref[q])
        total = jnp.where(member, part[q * rank : (q + 1) * rank], total)
    out_ref[...] = total.astype(BF16)


def low_sums(starts, ends, rows, packs, rank, after):
    row_total, depth = rows.shape
    smem = pl.BlockSpec(memory_space=pltpu.SMEM)
    vmem = pl.BlockSpec(memory_space=pltpu.VMEM)
    return pl.pallas_call(
        functools.partial(low_kernel, len(packs)),
        grid=(1,),
        in_specs=[smem, smem, vmem]
        + [pack_spec(p, 0, depth) for p in packs]
        + [pl.BlockSpec(memory_space=pl.ANY)] * len(after),
        out_specs=vmem,
        out_shape=jax.ShapeDtypeStruct((rank, row_total), BF16),
        compiler_params=pltpu.CompilerParams(vmem_limit_bytes=VMEM_LIMIT),
        cost_estimate=SMALL,
        name="low_sums",
    )(starts, ends, rows, *packs, *after)


def term_kernel(lows, pieces, peers, start_ref, end_ref, *rest):
    low_refs, rest = rest[:lows], rest[lows:]
    own_refs, rest = rest[:pieces], rest[pieces:]
    up_refs, out_refs = rest[:peers], rest[-pieces:]
    rank, row_total = low_refs[0].shape
    width = out_refs[0].shape[1]
    cols = width * pieces
    low = low_refs[0][...].astype(F32)
    for ref in low_refs[1:]:
        low = low + ref[...].astype(F32)
    low = low.astype(BF16).astype(F32)
    place = lax.broadcasted_iota(jnp.int32, (rank, row_total), 1)
    spread = []
    for q in range(len(up_refs) * CAP):
        member = jnp.logical_and(place >= start_ref[q], place < end_ref[q])
        spread.append(jnp.where(member, low, 0.0))
    spread = jnp.concatenate(spread, axis=0).astype(BF16)
    ups = jnp.concatenate([ref[...].reshape(CAP * rank, cols) for ref in up_refs], axis=0)
    for piece in range(pieces):
        columns = slice(piece * width, (piece + 1) * width)
        term = lax.dot_general(
            spread, ups[:, columns], (((0,), (0,)), ((), ())), preferred_element_type=F32
        )
        out_refs[piece][...] = own_refs[piece][...].astype(F32) + term


def adapter_term(starts, ends, lows, owns, packs, after):
    row_total, width = owns[0].shape
    cols = width * len(owns)
    smem = pl.BlockSpec(memory_space=pltpu.SMEM)
    vmem = pl.BlockSpec(memory_space=pltpu.VMEM)
    depth = packs[0].shape[2] - cols
    return pl.pallas_call(
        functools.partial(term_kernel, len(lows), len(owns), len(packs)),
        grid=(1,),
        in_specs=[smem, smem]
        + [vmem] * (len(lows) + len(owns))
        + [pack_spec(p, depth, cols) for p in packs]
        + [pl.BlockSpec(memory_space=pl.ANY)] * len(after),
        out_specs=[vmem] * len(owns),
        out_shape=[jax.ShapeDtypeStruct((row_total, width), F32)] * len(owns),
        compiler_params=pltpu.CompilerParams(vmem_limit_bytes=VMEM_LIMIT),
        cost_estimate=SMALL,
        name="adapter_term",
    )(starts, ends, *lows, *owns, *packs, *after)


def finish_kernel(addends, term_ref, *rest):
    total = term_ref[...]
    for ref in rest[:addends]:
        total = total + ref[...].astype(F32)
    rest[-1][...] = total.astype(rest[-1].dtype)


def finish(term, skip, arrived, offset, cols, result, cost):
    row_total, width = arrived.shape
    height = min(row_total, 128)
    block = pl.BlockSpec((height, width), lambda i: (i, 0))
    held = [] if result is None else [result]
    return pl.pallas_call(
        functools.partial(finish_kernel, 1),
        grid=(row_total // height,),
        in_specs=[pl.BlockSpec((height, width), lambda i: (i, skip // width)), block]
        + [pl.BlockSpec(memory_space=pl.ANY)] * len(held),
        out_specs=pl.BlockSpec((height, width), lambda i: (i, offset // width)),
        out_shape=jax.ShapeDtypeStruct((row_total, cols), BF16),
        input_output_aliases={2: 0} if held else {},
        compiler_params=pltpu.CompilerParams(vmem_limit_bytes=VMEM_LIMIT),
        cost_estimate=cost,
        name="finish",
    )(term, arrived, *held)


def local(req_total, tp_total, rows, weight, down, up, table, ids, lens):
    weight = pltpu.with_memory_space_constraint(weight, pltpu.HBM)
    down = pltpu.with_memory_space_constraint(down, pltpu.HBM)
    up = pltpu.with_memory_space_constraint(up, pltpu.HBM)
    rank = down.shape[1]
    cols = up.shape[2]
    width = cols // PIECES
    me_req = lax.axis_index("req").astype(jnp.int32)
    me = lax.axis_index("tp").astype(jnp.int32)
    steps = tp_total - 1

    def move(value, piece):
        pairs = []
        for r in range(req_total):
            way = 1 if (r + piece) % 2 == 0 else tp_total - 1
            for i in range(tp_total):
                pairs.append((r * tp_total + i, r * tp_total + (i + way) % tp_total))
        return lax.ppermute(value, ("req", "tp"), pairs)

    def start_of(back, piece):
        behind = jnp.where(lax.rem(me_req + piece, 2) == 0, tp_total - back, back)
        block = lax.rem(me + behind, tp_total)
        return block * cols + piece * width

    def partial(back, piece, **options):
        return block_product(rows, weight, start_of(back, piece), width, **options)

    def half_partial(back, piece, skip, **options):
        first = start_of(back, piece) + skip
        return block_product(rows, weight, first, width // 2, skip=skip, **options)

    last, rows = first_product(rows, weight, start_of(1, 0), width)
    rows = pltpu.with_memory_space_constraint(rows, pltpu.VMEM)
    moving = [move(last, 0)]
    for piece in range(1, PIECES):
        last, ids = partial(1, piece, after=[last], ids=ids)
        moving.append(move(last, piece))

    all_ids = [ids]
    for x in range(1, req_total):
        all_ids.append(lax.ppermute(ids, "req", [(i, i ^ x) for i in range(req_total)]))
    last = partial(0, 0, after=[last])
    owns = [last]
    packs, starts, ends = pick_adapters(me_req, table, all_ids, lens, down, up, [last])
    for x in range(1, req_total):
        packs[x] = lax.ppermute(packs[x], "req", [(i, i ^ x) for i in range(req_total)])

    last = starts
    for step in range(1, steps):
        for piece in range(PIECES):
            if step == steps - 1 and piece == PIECES - 1:
                low = low_sums(starts, ends, rows, packs, rank, [last])
                lows = [low]
                for x in range(1, tp_total):
                    pairs = [(i, i ^ x) for i in range(tp_total)]
                    lows.append(lax.ppermute(low, "tp", pairs))
                last = low
            if step == steps - 1 and piece == PIECES - 1:
                halves = []
                for skip in (0, width // 2):
                    last = half_partial(
                        1 + step, piece, skip, addends=[moving[piece]], after=[last]
                    )
                    halves.append(move(last, piece))
                break
            last = partial(1 + step, piece, addends=[moving[piece]], after=[last])
            moving[piece] = move(last, piece)
            if step == 1 and piece > 0:
                last = partial(0, piece, after=[last], cost=LARGE)
                owns.append(last)

    terms = adapter_term(starts, ends, lows, owns, packs, [last])
    parts = [(piece, 0, moving[piece]) for piece in range(PIECES - 1)]
    parts += [(PIECES - 1, skip, half) for skip, half in zip((0, width // 2), halves)]
    result = None
    for piece, skip, arrived in parts:
        arrived = pltpu.with_memory_space_constraint(arrived, pltpu.VMEM)
        cost = LARGE if piece == 0 else SMALL
        offset = piece * width + skip
        result = finish(terms[piece], skip, arrived, offset, cols, result, cost)
    return result


def solution(mesh):
    return jax.shard_map(
        functools.partial(local, mesh.shape["req"], mesh.shape["tp"]),
        mesh=mesh,
        in_specs=(
            P(("groups", "req"), "tp"),
            P("tp", None),
            P(("groups", "req"), None, "tp"),
            P(("groups", "req"), None, "tp"),
            P("groups"),
            P(("groups", "req"), None),
            P(("groups", "req"), None),
        ),
        out_specs=P(("groups", "req"), "tp"),
        check_vma=False,
    )
```

```python
import functools

import jax
import jax.numpy as jnp
from jax import lax
from jax.experimental import pallas as pl
from jax.experimental.pallas import tpu as pltpu
from jax.sharding import PartitionSpec as P

CAP = 6
PIECES = 2
VMEM_LIMIT = 20 * 1024 * 1024
F32 = jnp.float32
BF16 = jnp.bfloat16
SMALL = pl.CostEstimate(flops=1000, bytes_accessed=1000, transcendentals=0)
LARGE = pl.CostEstimate(flops=2 * 10**10, bytes_accessed=1000, transcendentals=0)


def product_kernel(addends, with_ids, first_ref, rows_ref, weight_ref, *rest):
    if with_ids:
        out_ref, ids_out_ref, sem = rest[-3:]
        ids_copy = pltpu.make_async_copy(rest[addends], ids_out_ref, sem)

        @pl.when(pl.program_id(0) == 0)
        def _():
            ids_copy.start()
    else:
        out_ref = rest[-1]
    total = jnp.dot(rows_ref[...], weight_ref[...], preferred_element_type=F32)
    for ref in rest[:addends]:
        total = total + ref[...].astype(F32)
    out_ref[...] = total.astype(out_ref.dtype)
    if with_ids:

        @pl.when(pl.program_id(0) == pl.num_programs(0) - 1)
        def _():
            ids_copy.wait()


def block_product(
    rows, weight, first, width, addends=(), skip=0, after=(), ids=None, cost=SMALL
):
    row_total, depth = rows.shape
    tile = min(256, width)
    with_ids = ids is not None
    smem = pl.BlockSpec(memory_space=pltpu.SMEM)
    hbm = pl.BlockSpec(memory_space=pl.ANY)
    columns = pl.BlockSpec((row_total, tile), lambda j, t: (0, j))
    out_specs, out_shape = [columns], [jax.ShapeDtypeStruct((row_total, width), BF16)]
    if with_ids:
        out_specs.append(hbm)
        out_shape.append(jax.ShapeDtypeStruct(ids.shape, ids.dtype))
    out = pl.pallas_call(
        functools.partial(product_kernel, len(addends), with_ids),
        grid_spec=pltpu.PrefetchScalarGridSpec(
            num_scalar_prefetch=1,
            grid=(width // tile,),
            in_specs=[
                pl.BlockSpec((row_total, depth), lambda j, t: (0, 0)),
                pl.BlockSpec((depth, tile), lambda j, t: (0, t[0] + j)),
            ]
            + [pl.BlockSpec((row_total, tile), lambda j, t: (0, skip // tile + j))] * len(addends)
            + [hbm] * with_ids
            + [hbm] * len(after),
            out_specs=out_specs,
            scratch_shapes=[pltpu.SemaphoreType.DMA] if with_ids else [],
        ),
        out_shape=out_shape,
        compiler_params=pltpu.CompilerParams(vmem_limit_bytes=VMEM_LIMIT),
        cost_estimate=cost,
        name="block_product",
    )((first // tile).reshape(1), rows, weight, *addends, *([ids] if with_ids else []), *after)
    return out if with_ids else out[0]


def first_kernel(chunk, first_ref, rows_ref, weight_ref, out_ref, lhs_ref, rhs_ref, acc_ref, sems):
    columns = pl.ds(pl.multiple_of(first_ref[0], 128), out_ref.shape[1])
    chunks = rhs_ref.shape[0]

    def copies(k):
        part = pl.ds(k * chunk, chunk)
        return (
            pltpu.make_async_copy(rows_ref.at[:, part], lhs_ref.at[:, part], sems.at[0, k]),
            pltpu.make_async_copy(weight_ref.at[part, columns], rhs_ref.at[k], sems.at[1, k]),
        )

    for k in range(chunks):
        for copy in copies(k):
            copy.start()
    for k in range(chunks):
        for copy in copies(k):
            copy.wait()
        lhs = lhs_ref[:, k * chunk : (k + 1) * chunk]
        part = jnp.dot(lhs, rhs_ref[k], preferred_element_type=F32)
        if k == 0:
            acc_ref[...] = part
        elif k < chunks - 1:
            acc_ref[...] += part
        else:
            out_ref[...] = (acc_ref[...] + part).astype(out_ref.dtype)


def first_product(rows, weight, first, width):
    row_total, depth = rows.shape
    chunk = min(512, depth // 2)
    chunks = depth // chunk
    hbm = pl.BlockSpec(memory_space=pltpu.HBM)
    return pl.pallas_call(
        functools.partial(first_kernel, chunk),
        in_specs=[pl.BlockSpec(memory_space=pltpu.SMEM), hbm, hbm],
        out_specs=[pl.BlockSpec(memory_space=pltpu.VMEM)] * 2,
        out_shape=[
            jax.ShapeDtypeStruct((row_total, width), BF16),
            jax.ShapeDtypeStruct((row_total, depth), BF16),
        ],
        scratch_shapes=[
            pltpu.VMEM((chunks, chunk, width), BF16),
            pltpu.VMEM((row_total, width), F32),
            pltpu.SemaphoreType.DMA((2, chunks)),
        ],
        compiler_params=pltpu.CompilerParams(vmem_limit_bytes=VMEM_LIMIT),
        cost_estimate=SMALL,
        name="first_product",
    )(first.reshape(1), pltpu.with_memory_space_constraint(rows, pltpu.HBM), weight)


def pick_kernel(peers, afters, me_ref, table_ref, lens_ref, *rest):
    ids_refs = rest[:peers]
    down_ref, up_ref = rest[peers : peers + 2]
    rest = rest[peers + 2 + afters :]
    packs, (start_ref, end_ref, pick_ref, count_ref, sem) = rest[:peers], rest[peers:]
    segs = lens_ref.shape[1]
    share, _, depth = down_ref.shape
    cols = up_ref.shape[2]
    me = me_ref[0]

    def clear(q, carry):
        pick_ref[q] = 0
        start_ref[q] = 0
        end_ref[q] = 0
        return carry

    lax.fori_loop(0, peers * CAP, clear, 0, unroll=8)
    for x in range(peers):
        count_ref[x] = 0

    def copies(x, c, source):
        pack = packs[x].at[c]
        return (
            pltpu.make_async_copy(down_ref.at[source], pack.at[:, pl.ds(0, depth)], sem),
            pltpu.make_async_copy(up_ref.at[source], pack.at[:, pl.ds(depth, cols)], sem),
        )

    for x in reversed(range(peers)):

        def choose(s, count):
            local = table_ref[ids_refs[x][0, s]] - me * share
            mine = jnp.logical_and(local >= 0, local < share)

            @pl.when(jnp.logical_and(mine, count < CAP))
            def _():
                pick_ref[x * CAP + count] = local

            return count + mine.astype(jnp.int32)

        lax.fori_loop(0, segs, choose, 0, unroll=4)
        for c in range(CAP):
            for copy in copies(x, c, pick_ref[x * CAP + c]):
                copy.start()

    def place(s, first):
        x = lax.bitwise_xor(table_ref[ids_refs[0][0, s]] // share, me)
        count = count_ref[x]
        last = first + lens_ref[0, s]

        @pl.when(count < CAP)
        def _():
            start_ref[x * CAP + count] = first
            end_ref[x * CAP + count] = last

        count_ref[x] = count + 1
        return last

    lax.fori_loop(0, segs, place, 0, unroll=4)

    for x in range(peers):
        for c in range(CAP):
            for copy in copies(x, c, 0):
                copy.wait()


def pick_adapters(me, table, all_ids, lens, down, up, after):
    peers = len(all_ids)
    _, rank, depth = down.shape
    cols = up.shape[2]
    smem = pl.BlockSpec(memory_space=pltpu.SMEM)
    vmem = pl.BlockSpec(memory_space=pltpu.VMEM)
    hbm = pl.BlockSpec(memory_space=pl.ANY)
    out = pl.pallas_call(
        functools.partial(pick_kernel, peers, len(after)),
        in_specs=[smem] * (3 + peers) + [hbm] * (2 + len(after)),
        out_specs=[vmem] * peers + [smem, smem],
        out_shape=[jax.ShapeDtypeStruct((CAP, rank, depth + cols), BF16)] * peers
        + [jax.ShapeDtypeStruct((peers * CAP,), jnp.int32)] * 2,
        scratch_shapes=[
            pltpu.SMEM((peers * CAP,), jnp.int32),
            pltpu.SMEM((peers,), jnp.int32),
            pltpu.SemaphoreType.DMA,
        ],
        compiler_params=pltpu.CompilerParams(vmem_limit_bytes=VMEM_LIMIT),
        cost_estimate=SMALL,
        name="pick_adapters",
    )(me.reshape(1), table, lens, *all_ids, down, up, *after)
    return list(out[:-2]), out[-2], out[-1]


def pack_spec(pack, first, width):
    return pl.BlockSpec(pack.shape[:2] + (width,), lambda i: (0, 0, first // width))


def low_kernel(peers, start_ref, end_ref, rows_ref, *rest):
    down_refs, out_ref = rest[:peers], rest[-1]
    row_total, depth = rows_ref.shape
    rank = out_ref.shape[0]
    place = lax.broadcasted_iota(jnp.int32, (rank, row_total), 1)
    downs = jnp.concatenate([ref[...].reshape(CAP * rank, depth) for ref in down_refs], axis=0)
    part = lax.dot_general(
        downs, rows_ref[...], (((1,), (1,)), ((), ())), preferred_element_type=F32
    )
    total = jnp.zeros((rank, row_total), F32)
    for q in range(peers * CAP):
        member = jnp.logical_and(place >= start_ref[q], place < end_ref[q])
        total = jnp.where(member, part[q * rank : (q + 1) * rank], total)
    out_ref[...] = total.astype(BF16)


def low_sums(starts, ends, rows, packs, rank, after):
    row_total, depth = rows.shape
    smem = pl.BlockSpec(memory_space=pltpu.SMEM)
    vmem = pl.BlockSpec(memory_space=pltpu.VMEM)
    return pl.pallas_call(
        functools.partial(low_kernel, len(packs)),
        grid=(1,),
        in_specs=[smem, smem, vmem]
        + [pack_spec(p, 0, depth) for p in packs]
        + [pl.BlockSpec(memory_space=pl.ANY)] * len(after),
        out_specs=vmem,
        out_shape=jax.ShapeDtypeStruct((rank, row_total), BF16),
        compiler_params=pltpu.CompilerParams(vmem_limit_bytes=VMEM_LIMIT),
        cost_estimate=SMALL,
        name="low_sums",
    )(starts, ends, rows, *packs, *after)


def term_kernel(lows, pieces, peers, start_ref, end_ref, *rest):
    low_refs, rest = rest[:lows], rest[lows:]
    own_refs, rest = rest[:pieces], rest[pieces:]
    up_refs, out_refs = rest[:peers], rest[-pieces:]
    rank, row_total = low_refs[0].shape
    width = out_refs[0].shape[1]
    cols = width * pieces
    low = low_refs[0][...].astype(F32)
    for ref in low_refs[1:]:
        low = low + ref[...].astype(F32)
    low = low.astype(BF16).astype(F32)
    place = lax.broadcasted_iota(jnp.int32, (rank, row_total), 1)
    spread = []
    for q in range(len(up_refs) * CAP):
        member = jnp.logical_and(place >= start_ref[q], place < end_ref[q])
        spread.append(jnp.where(member, low, 0.0))
    spread = jnp.concatenate(spread, axis=0).astype(BF16)
    ups = jnp.concatenate([ref[...].reshape(CAP * rank, cols) for ref in up_refs], axis=0)
    for piece in range(pieces):
        columns = slice(piece * width, (piece + 1) * width)
        term = lax.dot_general(
            spread, ups[:, columns], (((0,), (0,)), ((), ())), preferred_element_type=F32
        )
        out_refs[piece][...] = own_refs[piece][...].astype(F32) + term


def adapter_term(starts, ends, lows, owns, packs, after):
    row_total, width = owns[0].shape
    cols = width * len(owns)
    smem = pl.BlockSpec(memory_space=pltpu.SMEM)
    vmem = pl.BlockSpec(memory_space=pltpu.VMEM)
    depth = packs[0].shape[2] - cols
    return pl.pallas_call(
        functools.partial(term_kernel, len(lows), len(owns), len(packs)),
        grid=(1,),
        in_specs=[smem, smem]
        + [vmem] * (len(lows) + len(owns))
        + [pack_spec(p, depth, cols) for p in packs]
        + [pl.BlockSpec(memory_space=pl.ANY)] * len(after),
        out_specs=[vmem] * len(owns),
        out_shape=[jax.ShapeDtypeStruct((row_total, width), F32)] * len(owns),
        compiler_params=pltpu.CompilerParams(vmem_limit_bytes=VMEM_LIMIT),
        cost_estimate=SMALL,
        name="adapter_term",
    )(starts, ends, *lows, *owns, *packs, *after)


def finish_kernel(addends, term_ref, *rest):
    total = term_ref[...]
    for ref in rest[:addends]:
        total = total + ref[...].astype(F32)
    rest[-1][...] = total.astype(rest[-1].dtype)


def finish(term, skip, arrived, offset, cols, result, cost):
    row_total, width = arrived.shape
    height = min(row_total, 256)
    block = pl.BlockSpec((height, width), lambda i: (i, 0))
    held = [] if result is None else [result]
    return pl.pallas_call(
        functools.partial(finish_kernel, 1),
        grid=(row_total // height,),
        in_specs=[pl.BlockSpec((height, width), lambda i: (i, skip // width)), block]
        + [pl.BlockSpec(memory_space=pl.ANY)] * len(held),
        out_specs=pl.BlockSpec((height, width), lambda i: (i, offset // width)),
        out_shape=jax.ShapeDtypeStruct((row_total, cols), BF16),
        input_output_aliases={2: 0} if held else {},
        compiler_params=pltpu.CompilerParams(vmem_limit_bytes=VMEM_LIMIT),
        cost_estimate=cost,
        name="finish",
    )(term, arrived, *held)


def local(req_total, tp_total, rows, weight, down, up, table, ids, lens):
    weight = pltpu.with_memory_space_constraint(weight, pltpu.HBM)
    down = pltpu.with_memory_space_constraint(down, pltpu.HBM)
    up = pltpu.with_memory_space_constraint(up, pltpu.HBM)
    rank = down.shape[1]
    cols = up.shape[2]
    width = cols // PIECES
    me_req = lax.axis_index("req").astype(jnp.int32)
    me = lax.axis_index("tp").astype(jnp.int32)
    steps = tp_total - 1

    def move(value, piece):
        pairs = []
        for r in range(req_total):
            way = 1 if (r + piece) % 2 == 0 else tp_total - 1
            for i in range(tp_total):
                pairs.append((r * tp_total + i, r * tp_total + (i + way) % tp_total))
        return lax.ppermute(value, ("req", "tp"), pairs)

    def start_of(back, piece):
        behind = jnp.where(lax.rem(me_req + piece, 2) == 0, tp_total - back, back)
        block = lax.rem(me + behind, tp_total)
        return block * cols + piece * width

    def partial(back, piece, **options):
        return block_product(rows, weight, start_of(back, piece), width, **options)

    def half_partial(back, piece, skip, **options):
        first = start_of(back, piece) + skip
        return block_product(rows, weight, first, width // 2, skip=skip, **options)

    last, rows = first_product(rows, weight, start_of(1, 0), width)
    rows = pltpu.with_memory_space_constraint(rows, pltpu.VMEM)
    moving = [move(last, 0)]
    for piece in range(1, PIECES):
        last, ids = partial(1, piece, after=[last], ids=ids)
        moving.append(move(last, piece))

    all_ids = [ids]
    for x in range(1, req_total):
        all_ids.append(lax.ppermute(ids, "req", [(i, i ^ x) for i in range(req_total)]))
    last = partial(0, 0, after=[last])
    owns = [last]
    packs, starts, ends = pick_adapters(me_req, table, all_ids, lens, down, up, [last])
    for x in range(1, req_total):
        packs[x] = lax.ppermute(packs[x], "req", [(i, i ^ x) for i in range(req_total)])

    last = starts
    for step in range(1, steps):
        for piece in range(PIECES):
            if step == steps - 1 and piece == PIECES - 1:
                low = low_sums(starts, ends, rows, packs, rank, [last])
                lows = [low]
                for x in range(1, tp_total):
                    pairs = [(i, i ^ x) for i in range(tp_total)]
                    lows.append(lax.ppermute(low, "tp", pairs))
                last = low
            if step == steps - 1 and piece == PIECES - 1:
                halves = []
                for skip in (0, width // 2):
                    last = half_partial(
                        1 + step, piece, skip, addends=[moving[piece]], after=[last]
                    )
                    halves.append(move(last, piece))
                break
            last = partial(1 + step, piece, addends=[moving[piece]], after=[last])
            moving[piece] = move(last, piece)
            if step == 1 and piece > 0:
                last = partial(0, piece, after=[last], cost=LARGE)
                owns.append(last)

    terms = adapter_term(starts, ends, lows, owns, packs, [last])
    parts = [(piece, 0, moving[piece]) for piece in range(PIECES - 1)]
    parts += [(PIECES - 1, skip, half) for skip, half in zip((0, width // 2), halves)]
    result = None
    for piece, skip, arrived in parts:
        arrived = pltpu.with_memory_space_constraint(arrived, pltpu.VMEM)
        cost = LARGE if piece == 0 else SMALL
        offset = piece * width + skip
        result = finish(terms[piece], skip, arrived, offset, cols, result, cost)
    return result


def solution(mesh):
    return jax.shard_map(
        functools.partial(local, mesh.shape["req"], mesh.shape["tp"]),
        mesh=mesh,
        in_specs=(
            P(("groups", "req"), "tp"),
            P("tp", None),
            P(("groups", "req"), None, "tp"),
            P(("groups", "req"), None, "tp"),
            P("groups"),
            P(("groups", "req"), None),
            P(("groups", "req"), None),
        ),
        out_specs=P(("groups", "req"), "tp"),
        check_vma=False,
    )
```

```python
import functools

import jax
import jax.numpy as jnp
from jax import lax
from jax.experimental import pallas as pl
from jax.experimental.pallas import tpu as pltpu
from jax.sharding import PartitionSpec as P

CAP = 6
PIECES = 2
VMEM_LIMIT = 20 * 1024 * 1024
F32 = jnp.float32
BF16 = jnp.bfloat16
SMALL = pl.CostEstimate(flops=1000, bytes_accessed=1000, transcendentals=0)
LARGE = pl.CostEstimate(flops=2 * 10**10, bytes_accessed=1000, transcendentals=0)


def product_kernel(addends, with_ids, first_ref, rows_ref, weight_ref, *rest):
    if with_ids:
        out_ref, ids_out_ref, sem = rest[-3:]
        ids_copy = pltpu.make_async_copy(rest[addends], ids_out_ref, sem)

        @pl.when(pl.program_id(0) == 0)
        def _():
            ids_copy.start()
    else:
        out_ref = rest[-1]
    total = jnp.dot(rows_ref[...], weight_ref[...], preferred_element_type=F32)
    for ref in rest[:addends]:
        total = total + ref[...].astype(F32)
    out_ref[...] = total.astype(out_ref.dtype)
    if with_ids:

        @pl.when(pl.program_id(0) == pl.num_programs(0) - 1)
        def _():
            ids_copy.wait()


def block_product(
    rows, weight, first, width, addends=(), skip=0, after=(), ids=None, cost=SMALL
):
    row_total, depth = rows.shape
    tile = 256 if width % 256 == 0 else 128
    with_ids = ids is not None
    smem = pl.BlockSpec(memory_space=pltpu.SMEM)
    hbm = pl.BlockSpec(memory_space=pl.ANY)
    columns = pl.BlockSpec((row_total, tile), lambda j, t: (0, j))
    out_specs, out_shape = [columns], [jax.ShapeDtypeStruct((row_total, width), BF16)]
    if with_ids:
        out_specs.append(hbm)
        out_shape.append(jax.ShapeDtypeStruct(ids.shape, ids.dtype))
    out = pl.pallas_call(
        functools.partial(product_kernel, len(addends), with_ids),
        grid_spec=pltpu.PrefetchScalarGridSpec(
            num_scalar_prefetch=1,
            grid=(width // tile,),
            in_specs=[
                pl.BlockSpec((row_total, depth), lambda j, t: (0, 0)),
                pl.BlockSpec((depth, tile), lambda j, t: (0, t[0] + j)),
            ]
            + [pl.BlockSpec((row_total, tile), lambda j, t: (0, skip // tile + j))] * len(addends)
            + [hbm] * with_ids
            + [hbm] * len(after),
            out_specs=out_specs,
            scratch_shapes=[pltpu.SemaphoreType.DMA] if with_ids else [],
        ),
        out_shape=out_shape,
        compiler_params=pltpu.CompilerParams(vmem_limit_bytes=VMEM_LIMIT),
        cost_estimate=cost,
        name="block_product",
    )((first // tile).reshape(1), rows, weight, *addends, *([ids] if with_ids else []), *after)
    return out if with_ids else out[0]


def first_kernel(chunk, first_ref, rows_ref, weight_ref, out_ref, lhs_ref, rhs_ref, acc_ref, sems):
    columns = pl.ds(pl.multiple_of(first_ref[0], 128), out_ref.shape[1])
    chunks = rhs_ref.shape[0]

    def copies(k):
        part = pl.ds(k * chunk, chunk)
        return (
            pltpu.make_async_copy(rows_ref.at[:, part], lhs_ref.at[:, part], sems.at[0, k]),
            pltpu.make_async_copy(weight_ref.at[part, columns], rhs_ref.at[k], sems.at[1, k]),
        )

    for k in range(chunks):
        for copy in copies(k):
            copy.start()
    for k in range(chunks):
        for copy in copies(k):
            copy.wait()
        lhs = lhs_ref[:, k * chunk : (k + 1) * chunk]
        part = jnp.dot(lhs, rhs_ref[k], preferred_element_type=F32)
        if k == 0:
            acc_ref[...] = part
        elif k < chunks - 1:
            acc_ref[...] += part
        else:
            out_ref[...] = (acc_ref[...] + part).astype(out_ref.dtype)


def first_product(rows, weight, first, width):
    row_total, depth = rows.shape
    chunk = min(512, depth // 2)
    chunks = depth // chunk
    hbm = pl.BlockSpec(memory_space=pltpu.HBM)
    return pl.pallas_call(
        functools.partial(first_kernel, chunk),
        in_specs=[pl.BlockSpec(memory_space=pltpu.SMEM), hbm, hbm],
        out_specs=[pl.BlockSpec(memory_space=pltpu.VMEM)] * 2,
        out_shape=[
            jax.ShapeDtypeStruct((row_total, width), BF16),
            jax.ShapeDtypeStruct((row_total, depth), BF16),
        ],
        scratch_shapes=[
            pltpu.VMEM((chunks, chunk, width), BF16),
            pltpu.VMEM((row_total, width), F32),
            pltpu.SemaphoreType.DMA((2, chunks)),
        ],
        compiler_params=pltpu.CompilerParams(vmem_limit_bytes=VMEM_LIMIT),
        cost_estimate=SMALL,
        name="first_product",
    )(first.reshape(1), pltpu.with_memory_space_constraint(rows, pltpu.HBM), weight)


def pick_kernel(peers, afters, me_ref, table_ref, lens_ref, *rest):
    ids_refs = rest[:peers]
    down_ref, up_ref = rest[peers : peers + 2]
    rest = rest[peers + 2 + afters :]
    packs, (start_ref, end_ref, pick_ref, count_ref, sem) = rest[:peers], rest[peers:]
    segs = lens_ref.shape[1]
    share, _, depth = down_ref.shape
    cols = up_ref.shape[2]
    me = me_ref[0]

    def clear(q, carry):
        pick_ref[q] = 0
        start_ref[q] = 0
        end_ref[q] = 0
        return carry

    lax.fori_loop(0, peers * CAP, clear, 0, unroll=8)
    for x in range(peers):
        count_ref[x] = 0

    def copies(x, c, source):
        pack = packs[x].at[c]
        return (
            pltpu.make_async_copy(down_ref.at[source], pack.at[:, pl.ds(0, depth)], sem),
            pltpu.make_async_copy(up_ref.at[source], pack.at[:, pl.ds(depth, cols)], sem),
        )

    for x in reversed(range(peers)):

        def choose(s, count):
            local = table_ref[ids_refs[x][0, s]] - me * share
            mine = jnp.logical_and(local >= 0, local < share)

            @pl.when(jnp.logical_and(mine, count < CAP))
            def _():
                pick_ref[x * CAP + count] = local

            return count + mine.astype(jnp.int32)

        lax.fori_loop(0, segs, choose, 0, unroll=4)
        for c in range(CAP):
            for copy in copies(x, c, pick_ref[x * CAP + c]):
                copy.start()

    def place(s, first):
        x = lax.bitwise_xor(table_ref[ids_refs[0][0, s]] // share, me)
        count = count_ref[x]
        last = first + lens_ref[0, s]

        @pl.when(count < CAP)
        def _():
            start_ref[x * CAP + count] = first
            end_ref[x * CAP + count] = last

        count_ref[x] = count + 1
        return last

    lax.fori_loop(0, segs, place, 0, unroll=4)

    for x in range(peers):
        for c in range(CAP):
            for copy in copies(x, c, 0):
                copy.wait()


def pick_adapters(me, table, all_ids, lens, down, up, after):
    peers = len(all_ids)
    _, rank, depth = down.shape
    cols = up.shape[2]
    smem = pl.BlockSpec(memory_space=pltpu.SMEM)
    vmem = pl.BlockSpec(memory_space=pltpu.VMEM)
    hbm = pl.BlockSpec(memory_space=pl.ANY)
    out = pl.pallas_call(
        functools.partial(pick_kernel, peers, len(after)),
        in_specs=[smem] * (3 + peers) + [hbm] * (2 + len(after)),
        out_specs=[vmem] * peers + [smem, smem],
        out_shape=[jax.ShapeDtypeStruct((CAP, rank, depth + cols), BF16)] * peers
        + [jax.ShapeDtypeStruct((peers * CAP,), jnp.int32)] * 2,
        scratch_shapes=[
            pltpu.SMEM((peers * CAP,), jnp.int32),
            pltpu.SMEM((peers,), jnp.int32),
            pltpu.SemaphoreType.DMA,
        ],
        compiler_params=pltpu.CompilerParams(vmem_limit_bytes=VMEM_LIMIT),
        cost_estimate=SMALL,
        name="pick_adapters",
    )(me.reshape(1), table, lens, *all_ids, down, up, *after)
    return list(out[:-2]), out[-2], out[-1]


def pack_spec(pack, first, width):
    return pl.BlockSpec(pack.shape[:2] + (width,), lambda i: (0, 0, first // width))


def low_kernel(peers, start_ref, end_ref, rows_ref, *rest):
    down_refs, out_ref = rest[:peers], rest[-1]
    row_total, depth = rows_ref.shape
    rank = out_ref.shape[0]
    place = lax.broadcasted_iota(jnp.int32, (rank, row_total), 1)
    downs = jnp.concatenate([ref[...].reshape(CAP * rank, depth) for ref in down_refs], axis=0)
    part = lax.dot_general(
        downs, rows_ref[...], (((1,), (1,)), ((), ())), preferred_element_type=F32
    )
    total = jnp.zeros((rank, row_total), F32)
    for q in range(peers * CAP):
        member = jnp.logical_and(place >= start_ref[q], place < end_ref[q])
        total = jnp.where(member, part[q * rank : (q + 1) * rank], total)
    out_ref[...] = total.astype(BF16)


def low_sums(starts, ends, rows, packs, rank, after):
    row_total, depth = rows.shape
    smem = pl.BlockSpec(memory_space=pltpu.SMEM)
    vmem = pl.BlockSpec(memory_space=pltpu.VMEM)
    return pl.pallas_call(
        functools.partial(low_kernel, len(packs)),
        grid=(1,),
        in_specs=[smem, smem, vmem]
        + [pack_spec(p, 0, depth) for p in packs]
        + [pl.BlockSpec(memory_space=pl.ANY)] * len(after),
        out_specs=vmem,
        out_shape=jax.ShapeDtypeStruct((rank, row_total), BF16),
        compiler_params=pltpu.CompilerParams(vmem_limit_bytes=VMEM_LIMIT),
        cost_estimate=SMALL,
        name="low_sums",
    )(starts, ends, rows, *packs, *after)


def term_kernel(lows, pieces, peers, start_ref, end_ref, *rest):
    low_refs, rest = rest[:lows], rest[lows:]
    own_refs, rest = rest[:pieces], rest[pieces:]
    up_refs, out_refs = rest[:peers], rest[-pieces:]
    rank, row_total = low_refs[0].shape
    width = out_refs[0].shape[1]
    cols = width * pieces
    low = low_refs[0][...].astype(F32)
    for ref in low_refs[1:]:
        low = low + ref[...].astype(F32)
    low = low.astype(BF16).astype(F32)
    place = lax.broadcasted_iota(jnp.int32, (rank, row_total), 1)
    spread = []
    for q in range(len(up_refs) * CAP):
        member = jnp.logical_and(place >= start_ref[q], place < end_ref[q])
        spread.append(jnp.where(member, low, 0.0))
    spread = jnp.concatenate(spread, axis=0).astype(BF16)
    ups = jnp.concatenate([ref[...].reshape(CAP * rank, cols) for ref in up_refs], axis=0)
    for piece in range(pieces):
        first = (pieces - 1 - piece) * width
        columns = slice(first, first + width)
        term = lax.dot_general(
            spread, ups[:, columns], (((0,), (0,)), ((), ())), preferred_element_type=F32
        )
        out_refs[piece][...] = own_refs[piece][...].astype(F32) + term


def adapter_term(starts, ends, lows, owns, packs, after):
    row_total, width = owns[0].shape
    cols = width * len(owns)
    smem = pl.BlockSpec(memory_space=pltpu.SMEM)
    vmem = pl.BlockSpec(memory_space=pltpu.VMEM)
    depth = packs[0].shape[2] - cols
    return pl.pallas_call(
        functools.partial(term_kernel, len(lows), len(owns), len(packs)),
        grid=(1,),
        in_specs=[smem, smem]
        + [vmem] * (len(lows) + len(owns))
        + [pack_spec(p, depth, cols) for p in packs]
        + [pl.BlockSpec(memory_space=pl.ANY)] * len(after),
        out_specs=[vmem] * len(owns),
        out_shape=[jax.ShapeDtypeStruct((row_total, width), F32)] * len(owns),
        compiler_params=pltpu.CompilerParams(vmem_limit_bytes=VMEM_LIMIT),
        cost_estimate=SMALL,
        name="adapter_term",
    )(starts, ends, *lows, *owns, *packs, *after)


def finish_kernel(addends, term_ref, *rest):
    total = term_ref[...]
    for ref in rest[:addends]:
        total = total + ref[...].astype(F32)
    rest[-1][...] = total.astype(rest[-1].dtype)


def finish(term, skip, arrived, offset, cols, result, cost):
    row_total, width = arrived.shape
    height = min(row_total, 256)
    block = pl.BlockSpec((height, width), lambda i: (i, 0))
    held = [] if result is None else [result]
    return pl.pallas_call(
        functools.partial(finish_kernel, 1),
        grid=(row_total // height,),
        in_specs=[pl.BlockSpec((height, width), lambda i: (i, skip // width)), block]
        + [pl.BlockSpec(memory_space=pl.ANY)] * len(held),
        out_specs=pl.BlockSpec((height, width), lambda i: (i, offset // width)),
        out_shape=jax.ShapeDtypeStruct((row_total, cols), BF16),
        input_output_aliases={2: 0} if held else {},
        compiler_params=pltpu.CompilerParams(vmem_limit_bytes=VMEM_LIMIT),
        cost_estimate=cost,
        name="finish",
    )(term, arrived, *held)


def local(req_total, tp_total, rows, weight, down, up, table, ids, lens):
    weight = pltpu.with_memory_space_constraint(weight, pltpu.HBM)
    down = pltpu.with_memory_space_constraint(down, pltpu.HBM)
    up = pltpu.with_memory_space_constraint(up, pltpu.HBM)
    rank = down.shape[1]
    cols = up.shape[2]
    width = cols // PIECES
    offsets = [(PIECES - 1 - piece) * width for piece in range(PIECES)]
    me_req = lax.axis_index("req").astype(jnp.int32)
    me = lax.axis_index("tp").astype(jnp.int32)
    steps = tp_total - 1

    def move(value, piece):
        pairs = []
        for r in range(req_total):
            way = 1 if (r + piece) % 2 == 0 else tp_total - 1
            for i in range(tp_total):
                pairs.append((r * tp_total + i, r * tp_total + (i + way) % tp_total))
        return lax.ppermute(value, ("req", "tp"), pairs)

    def start_of(back, piece):
        behind = jnp.where(lax.rem(me_req + piece, 2) == 0, tp_total - back, back)
        block = lax.rem(me + behind, tp_total)
        return block * cols + offsets[piece]

    def partial(back, piece, **options):
        return block_product(rows, weight, start_of(back, piece), width, **options)

    cut = 3 * width // 4 // 128 * 128
    last_parts = ((0, cut), (cut, width - cut))

    def part_partial(back, piece, part, **options):
        skip, part_width = part
        first = start_of(back, piece) + skip
        return block_product(rows, weight, first, part_width, skip=skip, **options)

    last, rows = first_product(rows, weight, start_of(1, 0), width)
    rows = pltpu.with_memory_space_constraint(rows, pltpu.VMEM)
    moving = [move(last, 0)]
    for piece in range(1, PIECES):
        last, ids = partial(1, piece, after=[last], ids=ids)
        moving.append(move(last, piece))

    all_ids = [ids]
    for x in range(1, req_total):
        all_ids.append(lax.ppermute(ids, "req", [(i, i ^ x) for i in range(req_total)]))
    last = partial(0, 0, after=[last])
    owns = [last]
    packs, starts, ends = pick_adapters(me_req, table, all_ids, lens, down, up, [last])
    for x in range(1, req_total):
        packs[x] = lax.ppermute(packs[x], "req", [(i, i ^ x) for i in range(req_total)])

    last = starts
    for step in range(1, steps):
        for piece in range(PIECES):
            if step == steps - 1 and piece == PIECES - 1:
                low = low_sums(starts, ends, rows, packs, rank, [last])
                lows = [low]
                for x in range(1, tp_total):
                    pairs = [(i, i ^ x) for i in range(tp_total)]
                    lows.append(lax.ppermute(low, "tp", pairs))
                last = low
            if step == steps - 1 and piece == PIECES - 1:
                last_moving = []
                for part in last_parts:
                    last = part_partial(
                        1 + step, piece, part, addends=[moving[piece]], after=[last]
                    )
                    last_moving.append(move(last, piece))
                break
            last = partial(1 + step, piece, addends=[moving[piece]], after=[last])
            moving[piece] = move(last, piece)
            if step == 1 and piece > 0:
                last = partial(0, piece, after=[last], cost=LARGE)
                owns.append(last)

    terms = adapter_term(starts, ends, lows, owns, packs, [last])
    parts = [(piece, 0, moving[piece]) for piece in range(PIECES - 1)]
    parts += [(PIECES - 1, part[0], came) for part, came in zip(last_parts, last_moving)]
    result = None
    for piece, skip, arrived in parts:
        arrived = pltpu.with_memory_space_constraint(arrived, pltpu.VMEM)
        cost = LARGE if piece == 0 else SMALL
        offset = offsets[piece] + skip
        result = finish(terms[piece], skip, arrived, offset, cols, result, cost)
    return result


def solution(mesh):
    return jax.shard_map(
        functools.partial(local, mesh.shape["req"], mesh.shape["tp"]),
        mesh=mesh,
        in_specs=(
            P(("groups", "req"), "tp"),
            P("tp", None),
            P(("groups", "req"), None, "tp"),
            P(("groups", "req"), None, "tp"),
            P("groups"),
            P(("groups", "req"), None),
            P(("groups", "req"), None),
        ),
        out_specs=P(("groups", "req"), "tp"),
        check_vma=False,
    )
```

```python
import functools

import jax
import jax.numpy as jnp
from jax import lax
from jax.experimental import pallas as pl
from jax.experimental.pallas import tpu as pltpu
from jax.sharding import PartitionSpec as P

CAP = 6
PIECES = 2
VMEM_LIMIT = 12 * 1024 * 1024
F32 = jnp.float32
BF16 = jnp.bfloat16
SMALL = pl.CostEstimate(flops=1000, bytes_accessed=1000, transcendentals=0)
LARGE = pl.CostEstimate(flops=2 * 10**10, bytes_accessed=1000, transcendentals=0)


def product_kernel(addends, with_ids, first_ref, rows_ref, weight_ref, *rest):
    if with_ids:
        out_ref, ids_out_ref, sem = rest[-3:]
        ids_copy = pltpu.make_async_copy(rest[addends], ids_out_ref, sem)

        @pl.when(pl.program_id(0) == 0)
        def _():
            ids_copy.start()
    else:
        out_ref = rest[-1]
    total = jnp.dot(rows_ref[...], weight_ref[...], preferred_element_type=F32)
    for ref in rest[:addends]:
        total = total + ref[...].astype(F32)
    out_ref[...] = total.astype(out_ref.dtype)
    if with_ids:

        @pl.when(pl.program_id(0) == pl.num_programs(0) - 1)
        def _():
            ids_copy.wait()


def block_product(
    rows, weight, first, width, addends=(), skip=0, after=(), ids=None, cost=SMALL
):
    row_total, depth = rows.shape
    tile = min(256, width)
    with_ids = ids is not None
    smem = pl.BlockSpec(memory_space=pltpu.SMEM)
    hbm = pl.BlockSpec(memory_space=pl.ANY)
    columns = pl.BlockSpec((row_total, tile), lambda j, t: (0, j))
    out_specs, out_shape = [columns], [jax.ShapeDtypeStruct((row_total, width), BF16)]
    if with_ids:
        out_specs.append(hbm)
        out_shape.append(jax.ShapeDtypeStruct(ids.shape, ids.dtype))
    out = pl.pallas_call(
        functools.partial(product_kernel, len(addends), with_ids),
        grid_spec=pltpu.PrefetchScalarGridSpec(
            num_scalar_prefetch=1,
            grid=(width // tile,),
            in_specs=[
                pl.BlockSpec((row_total, depth), lambda j, t: (0, 0)),
                pl.BlockSpec((depth, tile), lambda j, t: (0, t[0] + j)),
            ]
            + [pl.BlockSpec((row_total, tile), lambda j, t: (0, skip // tile + j))] * len(addends)
            + [hbm] * with_ids
            + [hbm] * len(after),
            out_specs=out_specs,
            scratch_shapes=[pltpu.SemaphoreType.DMA] if with_ids else [],
        ),
        out_shape=out_shape,
        compiler_params=pltpu.CompilerParams(vmem_limit_bytes=VMEM_LIMIT),
        cost_estimate=cost,
        name="block_product",
    )((first // tile).reshape(1), rows, weight, *addends, *([ids] if with_ids else []), *after)
    return out if with_ids else out[0]


def first_kernel(chunk, first_ref, rows_ref, weight_ref, out_ref, lhs_ref, rhs_ref, acc_ref, sems):
    columns = pl.ds(pl.multiple_of(first_ref[0], 128), out_ref.shape[1])
    chunks = rhs_ref.shape[0]

    def copies(k):
        part = pl.ds(k * chunk, chunk)
        return (
            pltpu.make_async_copy(rows_ref.at[:, part], lhs_ref.at[:, part], sems.at[0, k]),
            pltpu.make_async_copy(weight_ref.at[part, columns], rhs_ref.at[k], sems.at[1, k]),
        )

    for k in range(chunks):
        for copy in copies(k):
            copy.start()
    for k in range(chunks):
        for copy in copies(k):
            copy.wait()
        lhs = lhs_ref[:, k * chunk : (k + 1) * chunk]
        part = jnp.dot(lhs, rhs_ref[k], preferred_element_type=F32)
        if k == 0:
            acc_ref[...] = part
        elif k < chunks - 1:
            acc_ref[...] += part
        else:
            out_ref[...] = (acc_ref[...] + part).astype(out_ref.dtype)


def first_product(rows, weight, first, width):
    row_total, depth = rows.shape
    chunk = min(512, depth // 2)
    chunks = depth // chunk
    hbm = pl.BlockSpec(memory_space=pltpu.HBM)
    return pl.pallas_call(
        functools.partial(first_kernel, chunk),
        in_specs=[pl.BlockSpec(memory_space=pltpu.SMEM), hbm, hbm],
        out_specs=[pl.BlockSpec(memory_space=pltpu.VMEM)] * 2,
        out_shape=[
            jax.ShapeDtypeStruct((row_total, width), BF16),
            jax.ShapeDtypeStruct((row_total, depth), BF16),
        ],
        scratch_shapes=[
            pltpu.VMEM((chunks, chunk, width), BF16),
            pltpu.VMEM((row_total, width), F32),
            pltpu.SemaphoreType.DMA((2, chunks)),
        ],
        compiler_params=pltpu.CompilerParams(vmem_limit_bytes=VMEM_LIMIT),
        cost_estimate=SMALL,
        name="first_product",
    )(first.reshape(1), pltpu.with_memory_space_constraint(rows, pltpu.HBM), weight)


def pick_kernel(peers, afters, me_ref, table_ref, lens_ref, *rest):
    ids_refs = rest[:peers]
    down_ref, up_ref = rest[peers : peers + 2]
    rest = rest[peers + 2 + afters :]
    packs, (start_ref, end_ref, pick_ref, count_ref, sem) = rest[:peers], rest[peers:]
    segs = lens_ref.shape[1]
    share, _, depth = down_ref.shape
    cols = up_ref.shape[2]
    me = me_ref[0]

    def clear(q, carry):
        pick_ref[q] = 0
        start_ref[q] = 0
        end_ref[q] = 0
        return carry

    lax.fori_loop(0, peers * CAP, clear, 0, unroll=8)
    for x in range(peers):
        count_ref[x] = 0

    def copies(x, c, source):
        pack = packs[x].at[c]
        return (
            pltpu.make_async_copy(down_ref.at[source], pack.at[:, pl.ds(0, depth)], sem),
            pltpu.make_async_copy(up_ref.at[source], pack.at[:, pl.ds(depth, cols)], sem),
        )

    for x in reversed(range(peers)):

        def choose(s, count):
            local = table_ref[ids_refs[x][0, s]] - me * share
            mine = jnp.logical_and(local >= 0, local < share)

            @pl.when(jnp.logical_and(mine, count < CAP))
            def _():
                pick_ref[x * CAP + count] = local

            return count + mine.astype(jnp.int32)

        lax.fori_loop(0, segs, choose, 0, unroll=4)
        for c in range(CAP):
            for copy in copies(x, c, pick_ref[x * CAP + c]):
                copy.start()

    def place(s, first):
        x = lax.bitwise_xor(table_ref[ids_refs[0][0, s]] // share, me)
        count = count_ref[x]
        last = first + lens_ref[0, s]

        @pl.when(count < CAP)
        def _():
            start_ref[x * CAP + count] = first
            end_ref[x * CAP + count] = last

        count_ref[x] = count + 1
        return last

    lax.fori_loop(0, segs, place, 0, unroll=4)

    for x in range(peers):
        for c in range(CAP):
            for copy in copies(x, c, 0):
                copy.wait()


def pick_adapters(me, table, all_ids, lens, down, up, after):
    peers = len(all_ids)
    _, rank, depth = down.shape
    cols = up.shape[2]
    smem = pl.BlockSpec(memory_space=pltpu.SMEM)
    vmem = pl.BlockSpec(memory_space=pltpu.VMEM)
    hbm = pl.BlockSpec(memory_space=pl.ANY)
    out = pl.pallas_call(
        functools.partial(pick_kernel, peers, len(after)),
        in_specs=[smem] * (3 + peers) + [hbm] * (2 + len(after)),
        out_specs=[vmem] * peers + [smem, smem],
        out_shape=[jax.ShapeDtypeStruct((CAP, rank, depth + cols), BF16)] * peers
        + [jax.ShapeDtypeStruct((peers * CAP,), jnp.int32)] * 2,
        scratch_shapes=[
            pltpu.SMEM((peers * CAP,), jnp.int32),
            pltpu.SMEM((peers,), jnp.int32),
            pltpu.SemaphoreType.DMA,
        ],
        compiler_params=pltpu.CompilerParams(vmem_limit_bytes=VMEM_LIMIT),
        cost_estimate=SMALL,
        name="pick_adapters",
    )(me.reshape(1), table, lens, *all_ids, down, up, *after)
    return list(out[:-2]), out[-2], out[-1]


def pack_spec(pack, first, width):
    return pl.BlockSpec(pack.shape[:2] + (width,), lambda i: (0, 0, first // width))


def low_kernel(peers, start_ref, end_ref, rows_ref, *rest):
    down_refs, out_ref = rest[:peers], rest[-1]
    row_total, depth = rows_ref.shape
    rank = out_ref.shape[0]
    place = lax.broadcasted_iota(jnp.int32, (rank, row_total), 1)
    downs = jnp.concatenate([ref[...].reshape(CAP * rank, depth) for ref in down_refs], axis=0)
    part = lax.dot_general(
        downs, rows_ref[...], (((1,), (1,)), ((), ())), preferred_element_type=F32
    )
    total = jnp.zeros((rank, row_total), F32)
    for q in range(peers * CAP):
        member = jnp.logical_and(place >= start_ref[q], place < end_ref[q])
        total = jnp.where(member, part[q * rank : (q + 1) * rank], total)
    out_ref[...] = total.astype(BF16)


def low_sums(starts, ends, rows, packs, rank, after):
    row_total, depth = rows.shape
    smem = pl.BlockSpec(memory_space=pltpu.SMEM)
    vmem = pl.BlockSpec(memory_space=pltpu.VMEM)
    return pl.pallas_call(
        functools.partial(low_kernel, len(packs)),
        grid=(1,),
        in_specs=[smem, smem, vmem]
        + [pack_spec(p, 0, depth) for p in packs]
        + [pl.BlockSpec(memory_space=pl.ANY)] * len(after),
        out_specs=vmem,
        out_shape=jax.ShapeDtypeStruct((rank, row_total), BF16),
        compiler_params=pltpu.CompilerParams(vmem_limit_bytes=VMEM_LIMIT),
        cost_estimate=SMALL,
        name="low_sums",
    )(starts, ends, rows, *packs, *after)


def term_kernel(lows, pieces, peers, start_ref, end_ref, *rest):
    low_refs, rest = rest[:lows], rest[lows:]
    own_refs, rest = rest[:pieces], rest[pieces:]
    up_refs, out_refs = rest[:peers], rest[-pieces:]
    rank, row_total = low_refs[0].shape
    width = out_refs[0].shape[1]
    cols = width * pieces
    low = low_refs[0][...].astype(F32)
    for ref in low_refs[1:]:
        low = low + ref[...].astype(F32)
    low = low.astype(BF16).astype(F32)
    place = lax.broadcasted_iota(jnp.int32, (rank, row_total), 1)
    spread = []
    for q in range(len(up_refs) * CAP):
        member = jnp.logical_and(place >= start_ref[q], place < end_ref[q])
        spread.append(jnp.where(member, low, 0.0))
    spread = jnp.concatenate(spread, axis=0).astype(BF16)
    ups = jnp.concatenate([ref[...].reshape(CAP * rank, cols) for ref in up_refs], axis=0)
    for piece in range(pieces):
        columns = slice(piece * width, (piece + 1) * width)
        term = lax.dot_general(
            spread, ups[:, columns], (((0,), (0,)), ((), ())), preferred_element_type=F32
        )
        out_refs[piece][...] = own_refs[piece][...].astype(F32) + term


def adapter_term(starts, ends, lows, owns, packs, after):
    row_total, width = owns[0].shape
    cols = width * len(owns)
    smem = pl.BlockSpec(memory_space=pltpu.SMEM)
    vmem = pl.BlockSpec(memory_space=pltpu.VMEM)
    depth = packs[0].shape[2] - cols
    return pl.pallas_call(
        functools.partial(term_kernel, len(lows), len(owns), len(packs)),
        grid=(1,),
        in_specs=[smem, smem]
        + [vmem] * (len(lows) + len(owns))
        + [pack_spec(p, depth, cols) for p in packs]
        + [pl.BlockSpec(memory_space=pl.ANY)] * len(after),
        out_specs=[vmem] * len(owns),
        out_shape=[jax.ShapeDtypeStruct((row_total, width), F32)] * len(owns),
        compiler_params=pltpu.CompilerParams(vmem_limit_bytes=VMEM_LIMIT),
        cost_estimate=SMALL,
        name="adapter_term",
    )(starts, ends, *lows, *owns, *packs, *after)


def finish_kernel(addends, term_ref, *rest):
    total = term_ref[...]
    for ref in rest[:addends]:
        total = total + ref[...].astype(F32)
    rest[-1][...] = total.astype(rest[-1].dtype)


def finish(term, skip, arrived, offset, cols, result, cost):
    row_total, width = arrived.shape
    height = min(row_total, 256)
    block = pl.BlockSpec((height, width), lambda i: (i, 0))
    held = [] if result is None else [result]
    return pl.pallas_call(
        functools.partial(finish_kernel, 1),
        grid=(row_total // height,),
        in_specs=[pl.BlockSpec((height, width), lambda i: (i, skip // width)), block]
        + [pl.BlockSpec(memory_space=pl.ANY)] * len(held),
        out_specs=pl.BlockSpec((height, width), lambda i: (i, offset // width)),
        out_shape=jax.ShapeDtypeStruct((row_total, cols), BF16),
        input_output_aliases={2: 0} if held else {},
        compiler_params=pltpu.CompilerParams(vmem_limit_bytes=VMEM_LIMIT),
        cost_estimate=cost,
        name="finish",
    )(term, arrived, *held)


def local(req_total, tp_total, rows, weight, down, up, table, ids, lens):
    weight = pltpu.with_memory_space_constraint(weight, pltpu.HBM)
    down = pltpu.with_memory_space_constraint(down, pltpu.HBM)
    up = pltpu.with_memory_space_constraint(up, pltpu.HBM)
    rank = down.shape[1]
    cols = up.shape[2]
    width = cols // PIECES
    me_req = lax.axis_index("req").astype(jnp.int32)
    me = lax.axis_index("tp").astype(jnp.int32)
    steps = tp_total - 1

    def move(value, piece):
        pairs = []
        for r in range(req_total):
            way = 1 if (r + piece) % 2 == 0 else tp_total - 1
            for i in range(tp_total):
                pairs.append((r * tp_total + i, r * tp_total + (i + way) % tp_total))
        return lax.ppermute(value, ("req", "tp"), pairs)

    def start_of(back, piece):
        behind = jnp.where(lax.rem(me_req + piece, 2) == 0, tp_total - back, back)
        block = lax.rem(me + behind, tp_total)
        return block * cols + piece * width

    def partial(back, piece, **options):
        return block_product(rows, weight, start_of(back, piece), width, **options)

    def half_partial(back, piece, skip, **options):
        first = start_of(back, piece) + skip
        return block_product(rows, weight, first, width // 2, skip=skip, **options)

    last, rows = first_product(rows, weight, start_of(1, 0), width)
    rows = pltpu.with_memory_space_constraint(rows, pltpu.VMEM)
    moving = [move(last, 0)]
    for piece in range(1, PIECES):
        last, ids = partial(1, piece, after=[last], ids=ids)
        moving.append(move(last, piece))

    all_ids = [ids]
    for x in range(1, req_total):
        all_ids.append(lax.ppermute(ids, "req", [(i, i ^ x) for i in range(req_total)]))
    last = partial(0, 0, after=[last])
    owns = [last]
    packs, starts, ends = pick_adapters(me_req, table, all_ids, lens, down, up, [last])
    for x in range(1, req_total):
        packs[x] = lax.ppermute(packs[x], "req", [(i, i ^ x) for i in range(req_total)])

    last = starts
    for step in range(1, steps):
        for piece in range(PIECES):
            if step == steps - 1 and piece == PIECES - 1:
                low = low_sums(starts, ends, rows, packs, rank, [last])
                lows = [low]
                for x in range(1, tp_total):
                    pairs = [(i, i ^ x) for i in range(tp_total)]
                    lows.append(lax.ppermute(low, "tp", pairs))
                last = low
            if step == steps - 1 and piece == PIECES - 1:
                halves = []
                for skip in (0, width // 2):
                    last = half_partial(
                        1 + step, piece, skip, addends=[moving[piece]], after=[last]
                    )
                    halves.append(move(last, piece))
                break
            last = partial(1 + step, piece, addends=[moving[piece]], after=[last])
            moving[piece] = move(last, piece)
            if step == 1 and piece > 0:
                last = partial(0, piece, after=[last], cost=LARGE)
                owns.append(last)

    terms = adapter_term(starts, ends, lows, owns, packs, [last])
    parts = [(piece, 0, moving[piece]) for piece in range(PIECES - 1)]
    parts += [(PIECES - 1, skip, half) for skip, half in zip((0, width // 2), halves)]
    result = None
    for piece, skip, arrived in parts:
        arrived = pltpu.with_memory_space_constraint(arrived, pltpu.VMEM)
        cost = LARGE if piece == 0 else SMALL
        offset = piece * width + skip
        result = finish(terms[piece], skip, arrived, offset, cols, result, cost)
    return result


def solution(mesh):
    return jax.shard_map(
        functools.partial(local, mesh.shape["req"], mesh.shape["tp"]),
        mesh=mesh,
        in_specs=(
            P(("groups", "req"), "tp"),
            P("tp", None),
            P(("groups", "req"), None, "tp"),
            P(("groups", "req"), None, "tp"),
            P("groups"),
            P(("groups", "req"), None),
            P(("groups", "req"), None),
        ),
        out_specs=P(("groups", "req"), "tp"),
        check_vma=False,
    )
```

```python
import functools

import jax
import jax.numpy as jnp
from jax import lax
from jax.experimental import pallas as pl
from jax.experimental.pallas import tpu as pltpu
from jax.sharding import PartitionSpec as P

CAP = 6
PIECES = 2
VMEM_LIMIT = 20 * 1024 * 1024
F32 = jnp.float32
BF16 = jnp.bfloat16
SMALL = pl.CostEstimate(flops=1000, bytes_accessed=1000, transcendentals=0)
LARGE = pl.CostEstimate(flops=2 * 10**10, bytes_accessed=1000, transcendentals=0)


def product_kernel(addends, with_ids, first_ref, rows_ref, weight_ref, *rest):
    if with_ids:
        out_ref, ids_out_ref, sem = rest[-3:]
        ids_copy = pltpu.make_async_copy(rest[addends], ids_out_ref, sem)

        @pl.when(pl.program_id(0) == 0)
        def _():
            ids_copy.start()
    else:
        out_ref = rest[-1]
    total = jnp.dot(rows_ref[...], weight_ref[...], preferred_element_type=F32)
    for ref in rest[:addends]:
        total = total + ref[...].astype(F32)
    out_ref[...] = total.astype(out_ref.dtype)
    if with_ids:

        @pl.when(pl.program_id(0) == pl.num_programs(0) - 1)
        def _():
            ids_copy.wait()


def block_product(
    rows, weight, first, width, addends=(), skip=0, after=(), ids=None, cost=SMALL
):
    row_total, depth = rows.shape
    tile = min(256, width)
    with_ids = ids is not None
    smem = pl.BlockSpec(memory_space=pltpu.SMEM)
    hbm = pl.BlockSpec(memory_space=pl.ANY)
    columns = pl.BlockSpec((row_total, tile), lambda j, t: (0, j))
    out_specs, out_shape = [columns], [jax.ShapeDtypeStruct((row_total, width), BF16)]
    if with_ids:
        out_specs.append(hbm)
        out_shape.append(jax.ShapeDtypeStruct(ids.shape, ids.dtype))
    out = pl.pallas_call(
        functools.partial(product_kernel, len(addends), with_ids),
        grid_spec=pltpu.PrefetchScalarGridSpec(
            num_scalar_prefetch=1,
            grid=(width // tile,),
            in_specs=[
                pl.BlockSpec((row_total, depth), lambda j, t: (0, 0)),
                pl.BlockSpec((depth, tile), lambda j, t: (0, t[0] + j)),
            ]
            + [pl.BlockSpec((row_total, tile), lambda j, t: (0, skip // tile + j))] * len(addends)
            + [hbm] * with_ids
            + [hbm] * len(after),
            out_specs=out_specs,
            scratch_shapes=[pltpu.SemaphoreType.DMA] if with_ids else [],
        ),
        out_shape=out_shape,
        compiler_params=pltpu.CompilerParams(vmem_limit_bytes=VMEM_LIMIT),
        cost_estimate=cost,
        name="block_product",
    )((first // tile).reshape(1), rows, weight, *addends, *([ids] if with_ids else []), *after)
    return out if with_ids else out[0]


def first_kernel(chunk, first_ref, rows_ref, weight_ref, out_ref, lhs_ref, rhs_ref, acc_ref, sems):
    columns = pl.ds(pl.multiple_of(first_ref[0], 128), out_ref.shape[1])
    chunks = rhs_ref.shape[0]

    def copies(k):
        part = pl.ds(k * chunk, chunk)
        return (
            pltpu.make_async_copy(rows_ref.at[:, part], lhs_ref.at[:, part], sems.at[0, k]),
            pltpu.make_async_copy(weight_ref.at[part, columns], rhs_ref.at[k], sems.at[1, k]),
        )

    for k in range(chunks):
        for copy in copies(k):
            copy.start()
    for k in range(chunks):
        for copy in copies(k):
            copy.wait()
        lhs = lhs_ref[:, k * chunk : (k + 1) * chunk]
        part = jnp.dot(lhs, rhs_ref[k], preferred_element_type=F32)
        if k == 0:
            acc_ref[...] = part
        elif k < chunks - 1:
            acc_ref[...] += part
        else:
            out_ref[...] = (acc_ref[...] + part).astype(out_ref.dtype)


def first_product(rows, weight, first, width):
    row_total, depth = rows.shape
    chunk = min(512, depth // 2)
    chunks = depth // chunk
    hbm = pl.BlockSpec(memory_space=pltpu.HBM)
    return pl.pallas_call(
        functools.partial(first_kernel, chunk),
        in_specs=[pl.BlockSpec(memory_space=pltpu.SMEM), hbm, hbm],
        out_specs=[pl.BlockSpec(memory_space=pltpu.VMEM)] * 2,
        out_shape=[
            jax.ShapeDtypeStruct((row_total, width), BF16),
            jax.ShapeDtypeStruct((row_total, depth), BF16),
        ],
        scratch_shapes=[
            pltpu.VMEM((chunks, chunk, width), BF16),
            pltpu.VMEM((row_total, width), F32),
            pltpu.SemaphoreType.DMA((2, chunks)),
        ],
        compiler_params=pltpu.CompilerParams(vmem_limit_bytes=VMEM_LIMIT),
        cost_estimate=SMALL,
        name="first_product",
    )(first.reshape(1), pltpu.with_memory_space_constraint(rows, pltpu.HBM), weight)


def pick_kernel(peers, afters, me_ref, table_ref, lens_ref, *rest):
    ids_refs = rest[:peers]
    down_ref, up_ref = rest[peers : peers + 2]
    rest = rest[peers + 2 + afters :]
    packs, (start_ref, end_ref, pick_ref, count_ref, sem) = rest[:peers], rest[peers:]
    segs = lens_ref.shape[1]
    share, _, depth = down_ref.shape
    cols = up_ref.shape[2]
    me = me_ref[0]

    def clear(q, carry):
        pick_ref[q] = 0
        start_ref[q] = 0
        end_ref[q] = 0
        return carry

    lax.fori_loop(0, peers * CAP, clear, 0, unroll=8)
    for x in range(peers):
        count_ref[x] = 0

    def copies(x, c, source):
        pack = packs[x].at[c]
        return (
            pltpu.make_async_copy(down_ref.at[source], pack.at[:, pl.ds(0, depth)], sem),
            pltpu.make_async_copy(up_ref.at[source], pack.at[:, pl.ds(depth, cols)], sem),
        )

    for x in reversed(range(peers)):

        def choose(s, count):
            local = table_ref[ids_refs[x][0, s]] - me * share
            mine = jnp.logical_and(local >= 0, local < share)

            @pl.when(jnp.logical_and(mine, count < CAP))
            def _():
                pick_ref[x * CAP + count] = local

            return count + mine.astype(jnp.int32)

        lax.fori_loop(0, segs, choose, 0, unroll=4)
        for c in range(CAP):
            for copy in copies(x, c, pick_ref[x * CAP + c]):
                copy.start()

    def place(s, first):
        x = lax.bitwise_xor(table_ref[ids_refs[0][0, s]] // share, me)
        count = count_ref[x]
        last = first + lens_ref[0, s]

        @pl.when(count < CAP)
        def _():
            start_ref[x * CAP + count] = first
            end_ref[x * CAP + count] = last

        count_ref[x] = count + 1
        return last

    lax.fori_loop(0, segs, place, 0, unroll=4)

    for x in range(peers):
        for c in range(CAP):
            for copy in copies(x, c, 0):
                copy.wait()


def pick_adapters(me, table, all_ids, lens, down, up, after):
    peers = len(all_ids)
    _, rank, depth = down.shape
    cols = up.shape[2]
    smem = pl.BlockSpec(memory_space=pltpu.SMEM)
    vmem = pl.BlockSpec(memory_space=pltpu.VMEM)
    hbm = pl.BlockSpec(memory_space=pl.ANY)
    out = pl.pallas_call(
        functools.partial(pick_kernel, peers, len(after)),
        in_specs=[smem] * (3 + peers) + [hbm] * (2 + len(after)),
        out_specs=[vmem] * peers + [smem, smem],
        out_shape=[jax.ShapeDtypeStruct((CAP, rank, depth + cols), BF16)] * peers
        + [jax.ShapeDtypeStruct((peers * CAP,), jnp.int32)] * 2,
        scratch_shapes=[
            pltpu.SMEM((peers * CAP,), jnp.int32),
            pltpu.SMEM((peers,), jnp.int32),
            pltpu.SemaphoreType.DMA,
        ],
        compiler_params=pltpu.CompilerParams(vmem_limit_bytes=VMEM_LIMIT),
        cost_estimate=SMALL,
        name="pick_adapters",
    )(me.reshape(1), table, lens, *all_ids, down, up, *after)
    return list(out[:-2]), out[-2], out[-1]


def pack_spec(pack, first, width):
    return pl.BlockSpec(pack.shape[:2] + (width,), lambda i: (0, 0, first // width))


def low_kernel(peers, start_ref, end_ref, rows_ref, *rest):
    down_refs, out_ref = rest[:peers], rest[-1]
    row_total, depth = rows_ref.shape
    rank = out_ref.shape[0]
    place = lax.broadcasted_iota(jnp.int32, (rank, row_total), 1)
    downs = jnp.concatenate([ref[...].reshape(CAP * rank, depth) for ref in down_refs], axis=0)
    part = lax.dot_general(
        downs, rows_ref[...], (((1,), (1,)), ((), ())), preferred_element_type=F32
    )
    total = jnp.zeros((rank, row_total), F32)
    for q in range(peers * CAP):
        member = jnp.logical_and(place >= start_ref[q], place < end_ref[q])
        total = jnp.where(member, part[q * rank : (q + 1) * rank], total)
    out_ref[...] = total.astype(BF16)


def low_sums(starts, ends, rows, packs, rank, after):
    row_total, depth = rows.shape
    smem = pl.BlockSpec(memory_space=pltpu.SMEM)
    vmem = pl.BlockSpec(memory_space=pltpu.VMEM)
    return pl.pallas_call(
        functools.partial(low_kernel, len(packs)),
        grid=(1,),
        in_specs=[smem, smem, vmem]
        + [pack_spec(p, 0, depth) for p in packs]
        + [pl.BlockSpec(memory_space=pl.ANY)] * len(after),
        out_specs=vmem,
        out_shape=jax.ShapeDtypeStruct((rank, row_total), BF16),
        compiler_params=pltpu.CompilerParams(vmem_limit_bytes=VMEM_LIMIT),
        cost_estimate=SMALL,
        name="low_sums",
    )(starts, ends, rows, *packs, *after)


def term_kernel(lows, pieces, peers, start_ref, end_ref, *rest):
    low_refs, rest = rest[:lows], rest[lows:]
    own_refs, rest = rest[:pieces], rest[pieces:]
    up_refs, out_refs = rest[:peers], rest[-pieces:]
    rank, row_total = low_refs[0].shape
    width = out_refs[0].shape[1]
    cols = width * pieces
    low = low_refs[0][...].astype(F32)
    for ref in low_refs[1:]:
        low = low + ref[...].astype(F32)
    low = low.astype(BF16).astype(F32)
    place = lax.broadcasted_iota(jnp.int32, (rank, row_total), 1)
    spread = []
    for q in range(len(up_refs) * CAP):
        member = jnp.logical_and(place >= start_ref[q], place < end_ref[q])
        spread.append(jnp.where(member, low, 0.0))
    spread = jnp.concatenate(spread, axis=0).astype(BF16)
    ups = jnp.concatenate([ref[...].reshape(CAP * rank, cols) for ref in up_refs], axis=0)
    for piece in range(pieces):
        columns = slice(piece * width, (piece + 1) * width)
        term = lax.dot_general(
            spread, ups[:, columns], (((0,), (0,)), ((), ())), preferred_element_type=F32
        )
        out_refs[piece][...] = own_refs[piece][...].astype(F32) + term


def adapter_term(starts, ends, lows, owns, packs, after):
    row_total, width = owns[0].shape
    cols = width * len(owns)
    smem = pl.BlockSpec(memory_space=pltpu.SMEM)
    vmem = pl.BlockSpec(memory_space=pltpu.VMEM)
    depth = packs[0].shape[2] - cols
    return pl.pallas_call(
        functools.partial(term_kernel, len(lows), len(owns), len(packs)),
        grid=(1,),
        in_specs=[smem, smem]
        + [vmem] * (len(lows) + len(owns))
        + [pack_spec(p, depth, cols) for p in packs]
        + [pl.BlockSpec(memory_space=pl.ANY)] * len(after),
        out_specs=[vmem] * len(owns),
        out_shape=[jax.ShapeDtypeStruct((row_total, width), F32)] * len(owns),
        compiler_params=pltpu.CompilerParams(vmem_limit_bytes=VMEM_LIMIT),
        cost_estimate=SMALL,
        name="adapter_term",
    )(starts, ends, *lows, *owns, *packs, *after)


def finish_kernel(addends, term_ref, *rest):
    total = term_ref[...]
    for ref in rest[:addends]:
        total = total + ref[...].astype(F32)
    rest[-1][...] = total.astype(rest[-1].dtype)


def finish(term, skip, arrived, offset, cols, result, cost):
    row_total, width = arrived.shape
    height = min(row_total, 256)
    block = pl.BlockSpec((height, width), lambda i: (i, 0))
    held = [] if result is None else [result]
    return pl.pallas_call(
        functools.partial(finish_kernel, 1),
        grid=(row_total // height,),
        in_specs=[pl.BlockSpec((height, width), lambda i: (i, skip // width)), block]
        + [pl.BlockSpec(memory_space=pl.ANY)] * len(held),
        out_specs=pl.BlockSpec((height, width), lambda i: (i, offset // width)),
        out_shape=jax.ShapeDtypeStruct((row_total, cols), BF16),
        input_output_aliases={2: 0} if held else {},
        compiler_params=pltpu.CompilerParams(vmem_limit_bytes=VMEM_LIMIT),
        cost_estimate=cost,
        name="finish",
    )(term, arrived, *held)


def local(req_total, tp_total, rows, weight, down, up, table, ids, lens):
    weight = pltpu.with_memory_space_constraint(weight, pltpu.HBM)
    down = pltpu.with_memory_space_constraint(down, pltpu.HBM)
    up = pltpu.with_memory_space_constraint(up, pltpu.HBM)
    rank = down.shape[1]
    cols = up.shape[2]
    width = cols // PIECES
    me_req = lax.axis_index("req").astype(jnp.int32)
    me = lax.axis_index("tp").astype(jnp.int32)
    steps = tp_total - 1

    def move(value, piece):
        pairs = []
        for r in range(req_total):
            way = 1 if (r + piece) % 2 == 0 else tp_total - 1
            for i in range(tp_total):
                pairs.append((r * tp_total + i, r * tp_total + (i + way) % tp_total))
        return lax.ppermute(value, ("req", "tp"), pairs)

    def start_of(back, piece):
        behind = jnp.where(lax.rem(me_req + piece, 2) == 0, tp_total - back, back)
        block = lax.rem(me + behind, tp_total)
        return block * cols + piece * width

    def partial(back, piece, **options):
        return block_product(rows, weight, start_of(back, piece), width, **options)

    def half_partial(back, piece, skip, **options):
        first = start_of(back, piece) + skip
        return block_product(rows, weight, first, width // 2, skip=skip, **options)

    last, rows = first_product(rows, weight, start_of(1, 0), width)
    rows = pltpu.with_memory_space_constraint(rows, pltpu.VMEM)
    moving = [move(last, 0)]
    last, ids = partial(0, 0, after=[last], ids=ids)
    owns = [last]

    all_ids = [ids]
    for x in range(1, req_total):
        all_ids.append(lax.ppermute(ids, "req", [(i, i ^ x) for i in range(req_total)]))
    for piece in range(1, PIECES):
        last = partial(1, piece, after=[last])
        moving.append(move(last, piece))
    packs, starts, ends = pick_adapters(me_req, table, all_ids, lens, down, up, [last])
    for x in range(1, req_total):
        packs[x] = lax.ppermute(packs[x], "req", [(i, i ^ x) for i in range(req_total)])

    last = starts
    for step in range(1, steps):
        for piece in range(PIECES):
            if step == steps - 1 and piece == PIECES - 1:
                low = low_sums(starts, ends, rows, packs, rank, [last])
                lows = [low]
                for x in range(1, tp_total):
                    pairs = [(i, i ^ x) for i in range(tp_total)]
                    lows.append(lax.ppermute(low, "tp", pairs))
                last = low
            if step == steps - 1 and piece == PIECES - 1:
                halves = []
                for skip in (0, width // 2):
                    last = half_partial(
                        1 + step, piece, skip, addends=[moving[piece]], after=[last]
                    )
                    halves.append(move(last, piece))
                break
            last = partial(1 + step, piece, addends=[moving[piece]], after=[last])
            moving[piece] = move(last, piece)
            if step == 1 and piece > 0:
                last = partial(0, piece, after=[last], cost=LARGE)
                owns.append(last)

    terms = adapter_term(starts, ends, lows, owns, packs, [last])
    parts = [(piece, 0, moving[piece]) for piece in range(PIECES - 1)]
    parts += [(PIECES - 1, skip, half) for skip, half in zip((0, width // 2), halves)]
    result = None
    for piece, skip, arrived in parts:
        arrived = pltpu.with_memory_space_constraint(arrived, pltpu.VMEM)
        cost = LARGE if piece == 0 else SMALL
        offset = piece * width + skip
        result = finish(terms[piece], skip, arrived, offset, cols, result, cost)
    return result


def solution(mesh):
    return jax.shard_map(
        functools.partial(local, mesh.shape["req"], mesh.shape["tp"]),
        mesh=mesh,
        in_specs=(
            P(("groups", "req"), "tp"),
            P("tp", None),
            P(("groups", "req"), None, "tp"),
            P(("groups", "req"), None, "tp"),
            P("groups"),
            P(("groups", "req"), None),
            P(("groups", "req"), None),
        ),
        out_specs=P(("groups", "req"), "tp"),
        check_vma=False,
    )
```

```python
import functools

import jax
import jax.numpy as jnp
from jax import lax
from jax.experimental import pallas as pl
from jax.experimental.pallas import tpu as pltpu
from jax.sharding import PartitionSpec as P

CAP = 6
PIECES = 2
VMEM_LIMIT = 20 * 1024 * 1024
F32 = jnp.float32
BF16 = jnp.bfloat16
SMALL = pl.CostEstimate(flops=1000, bytes_accessed=1000, transcendentals=0)
LARGE = pl.CostEstimate(flops=8 * 10**9, bytes_accessed=1000, transcendentals=0)


def product_kernel(addends, with_ids, first_ref, rows_ref, weight_ref, *rest):
    if with_ids:
        out_ref, ids_out_ref, sem = rest[-3:]
        ids_copy = pltpu.make_async_copy(rest[addends], ids_out_ref, sem)

        @pl.when(pl.program_id(0) == 0)
        def _():
            ids_copy.start()
    else:
        out_ref = rest[-1]
    total = jnp.dot(rows_ref[...], weight_ref[...], preferred_element_type=F32)
    for ref in rest[:addends]:
        total = total + ref[...].astype(F32)
    out_ref[...] = total.astype(out_ref.dtype)
    if with_ids:

        @pl.when(pl.program_id(0) == pl.num_programs(0) - 1)
        def _():
            ids_copy.wait()


def block_product(
    rows, weight, first, width, addends=(), skip=0, after=(), ids=None, cost=SMALL
):
    row_total, depth = rows.shape
    tile = min(256, width)
    with_ids = ids is not None
    smem = pl.BlockSpec(memory_space=pltpu.SMEM)
    hbm = pl.BlockSpec(memory_space=pl.ANY)
    columns = pl.BlockSpec((row_total, tile), lambda j, t: (0, j))
    out_specs, out_shape = [columns], [jax.ShapeDtypeStruct((row_total, width), BF16)]
    if with_ids:
        out_specs.append(hbm)
        out_shape.append(jax.ShapeDtypeStruct(ids.shape, ids.dtype))
    out = pl.pallas_call(
        functools.partial(product_kernel, len(addends), with_ids),
        grid_spec=pltpu.PrefetchScalarGridSpec(
            num_scalar_prefetch=1,
            grid=(width // tile,),
            in_specs=[
                pl.BlockSpec((row_total, depth), lambda j, t: (0, 0)),
                pl.BlockSpec((depth, tile), lambda j, t: (0, t[0] + j)),
            ]
            + [pl.BlockSpec((row_total, tile), lambda j, t: (0, skip // tile + j))] * len(addends)
            + [hbm] * with_ids
            + [hbm] * len(after),
            out_specs=out_specs,
            scratch_shapes=[pltpu.SemaphoreType.DMA] if with_ids else [],
        ),
        out_shape=out_shape,
        compiler_params=pltpu.CompilerParams(vmem_limit_bytes=VMEM_LIMIT),
        cost_estimate=cost,
        name="block_product",
    )((first // tile).reshape(1), rows, weight, *addends, *([ids] if with_ids else []), *after)
    return out if with_ids else out[0]


def first_kernel(chunk, first_ref, rows_ref, weight_ref, out_ref, lhs_ref, rhs_ref, acc_ref, sems):
    columns = pl.ds(pl.multiple_of(first_ref[0], 128), out_ref.shape[1])
    chunks = rhs_ref.shape[0]

    def copies(k):
        part = pl.ds(k * chunk, chunk)
        return (
            pltpu.make_async_copy(rows_ref.at[:, part], lhs_ref.at[:, part], sems.at[0, k]),
            pltpu.make_async_copy(weight_ref.at[part, columns], rhs_ref.at[k], sems.at[1, k]),
        )

    for k in range(chunks):
        for copy in copies(k):
            copy.start()
    for k in range(chunks):
        for copy in copies(k):
            copy.wait()
        lhs = lhs_ref[:, k * chunk : (k + 1) * chunk]
        part = jnp.dot(lhs, rhs_ref[k], preferred_element_type=F32)
        if k == 0:
            acc_ref[...] = part
        elif k < chunks - 1:
            acc_ref[...] += part
        else:
            out_ref[...] = (acc_ref[...] + part).astype(out_ref.dtype)


def first_product(rows, weight, first, width):
    row_total, depth = rows.shape
    chunk = min(512, depth // 2)
    chunks = depth // chunk
    hbm = pl.BlockSpec(memory_space=pltpu.HBM)
    return pl.pallas_call(
        functools.partial(first_kernel, chunk),
        in_specs=[pl.BlockSpec(memory_space=pltpu.SMEM), hbm, hbm],
        out_specs=[pl.BlockSpec(memory_space=pltpu.VMEM)] * 2,
        out_shape=[
            jax.ShapeDtypeStruct((row_total, width), BF16),
            jax.ShapeDtypeStruct((row_total, depth), BF16),
        ],
        scratch_shapes=[
            pltpu.VMEM((chunks, chunk, width), BF16),
            pltpu.VMEM((row_total, width), F32),
            pltpu.SemaphoreType.DMA((2, chunks)),
        ],
        compiler_params=pltpu.CompilerParams(vmem_limit_bytes=VMEM_LIMIT),
        cost_estimate=SMALL,
        name="first_product",
    )(first.reshape(1), pltpu.with_memory_space_constraint(rows, pltpu.HBM), weight)


def pick_kernel(peers, afters, me_ref, table_ref, lens_ref, *rest):
    ids_refs = rest[:peers]
    down_ref, up_ref = rest[peers : peers + 2]
    rest = rest[peers + 2 + afters :]
    packs, (start_ref, end_ref, pick_ref, count_ref, sem) = rest[:peers], rest[peers:]
    segs = lens_ref.shape[1]
    share, _, depth = down_ref.shape
    cols = up_ref.shape[2]
    me = me_ref[0]

    def clear(q, carry):
        pick_ref[q] = 0
        start_ref[q] = 0
        end_ref[q] = 0
        return carry

    lax.fori_loop(0, peers * CAP, clear, 0, unroll=8)
    for x in range(peers):
        count_ref[x] = 0

    def copies(x, c, source):
        pack = packs[x].at[c]
        return (
            pltpu.make_async_copy(down_ref.at[source], pack.at[:, pl.ds(0, depth)], sem),
            pltpu.make_async_copy(up_ref.at[source], pack.at[:, pl.ds(depth, cols)], sem),
        )

    for x in reversed(range(peers)):

        def choose(s, count):
            local = table_ref[ids_refs[x][0, s]] - me * share
            mine = jnp.logical_and(local >= 0, local < share)

            @pl.when(jnp.logical_and(mine, count < CAP))
            def _():
                pick_ref[x * CAP + count] = local

            return count + mine.astype(jnp.int32)

        lax.fori_loop(0, segs, choose, 0, unroll=4)
        for c in range(CAP):
            for copy in copies(x, c, pick_ref[x * CAP + c]):
                copy.start()

    def place(s, first):
        x = lax.bitwise_xor(table_ref[ids_refs[0][0, s]] // share, me)
        count = count_ref[x]
        last = first + lens_ref[0, s]

        @pl.when(count < CAP)
        def _():
            start_ref[x * CAP + count] = first
            end_ref[x * CAP + count] = last

        count_ref[x] = count + 1
        return last

    lax.fori_loop(0, segs, place, 0, unroll=4)

    for x in range(peers):
        for c in range(CAP):
            for copy in copies(x, c, 0):
                copy.wait()


def pick_adapters(me, table, all_ids, lens, down, up, after):
    peers = len(all_ids)
    _, rank, depth = down.shape
    cols = up.shape[2]
    smem = pl.BlockSpec(memory_space=pltpu.SMEM)
    vmem = pl.BlockSpec(memory_space=pltpu.VMEM)
    hbm = pl.BlockSpec(memory_space=pl.ANY)
    out = pl.pallas_call(
        functools.partial(pick_kernel, peers, len(after)),
        in_specs=[smem] * (3 + peers) + [hbm] * (2 + len(after)),
        out_specs=[vmem] * peers + [smem, smem],
        out_shape=[jax.ShapeDtypeStruct((CAP, rank, depth + cols), BF16)] * peers
        + [jax.ShapeDtypeStruct((peers * CAP,), jnp.int32)] * 2,
        scratch_shapes=[
            pltpu.SMEM((peers * CAP,), jnp.int32),
            pltpu.SMEM((peers,), jnp.int32),
            pltpu.SemaphoreType.DMA,
        ],
        compiler_params=pltpu.CompilerParams(vmem_limit_bytes=VMEM_LIMIT),
        cost_estimate=SMALL,
        name="pick_adapters",
    )(me.reshape(1), table, lens, *all_ids, down, up, *after)
    return list(out[:-2]), out[-2], out[-1]


def pack_spec(pack, first, width):
    return pl.BlockSpec(pack.shape[:2] + (width,), lambda i: (0, 0, first // width))


def low_kernel(peers, start_ref, end_ref, rows_ref, *rest):
    down_refs, out_ref = rest[:peers], rest[-1]
    row_total, depth = rows_ref.shape
    rank = out_ref.shape[0]
    place = lax.broadcasted_iota(jnp.int32, (rank, row_total), 1)
    downs = jnp.concatenate([ref[...].reshape(CAP * rank, depth) for ref in down_refs], axis=0)
    part = lax.dot_general(
        downs, rows_ref[...], (((1,), (1,)), ((), ())), preferred_element_type=F32
    )
    total = jnp.zeros((rank, row_total), F32)
    for q in range(peers * CAP):
        member = jnp.logical_and(place >= start_ref[q], place < end_ref[q])
        total = jnp.where(member, part[q * rank : (q + 1) * rank], total)
    out_ref[...] = total.astype(BF16)


def low_sums(starts, ends, rows, packs, rank, after):
    row_total, depth = rows.shape
    smem = pl.BlockSpec(memory_space=pltpu.SMEM)
    vmem = pl.BlockSpec(memory_space=pltpu.VMEM)
    return pl.pallas_call(
        functools.partial(low_kernel, len(packs)),
        grid=(1,),
        in_specs=[smem, smem, vmem]
        + [pack_spec(p, 0, depth) for p in packs]
        + [pl.BlockSpec(memory_space=pl.ANY)] * len(after),
        out_specs=vmem,
        out_shape=jax.ShapeDtypeStruct((rank, row_total), BF16),
        compiler_params=pltpu.CompilerParams(vmem_limit_bytes=VMEM_LIMIT),
        cost_estimate=SMALL,
        name="low_sums",
    )(starts, ends, rows, *packs, *after)


def term_kernel(lows, pieces, peers, start_ref, end_ref, *rest):
    low_refs, rest = rest[:lows], rest[lows:]
    own_refs, rest = rest[:pieces], rest[pieces:]
    up_refs, out_refs = rest[:peers], rest[-pieces:]
    rank, row_total = low_refs[0].shape
    width = out_refs[0].shape[1]
    cols = width * pieces
    low = low_refs[0][...].astype(F32)
    for ref in low_refs[1:]:
        low = low + ref[...].astype(F32)
    low = low.astype(BF16).astype(F32)
    place = lax.broadcasted_iota(jnp.int32, (rank, row_total), 1)
    spread = []
    for q in range(len(up_refs) * CAP):
        member = jnp.logical_and(place >= start_ref[q], place < end_ref[q])
        spread.append(jnp.where(member, low, 0.0))
    spread = jnp.concatenate(spread, axis=0).astype(BF16)
    ups = jnp.concatenate([ref[...].reshape(CAP * rank, cols) for ref in up_refs], axis=0)
    for piece in range(pieces):
        columns = slice(piece * width, (piece + 1) * width)
        term = lax.dot_general(
            spread, ups[:, columns], (((0,), (0,)), ((), ())), preferred_element_type=F32
        )
        out_refs[piece][...] = own_refs[piece][...].astype(F32) + term


def adapter_term(starts, ends, lows, owns, packs, after):
    row_total, width = owns[0].shape
    cols = width * len(owns)
    smem = pl.BlockSpec(memory_space=pltpu.SMEM)
    vmem = pl.BlockSpec(memory_space=pltpu.VMEM)
    depth = packs[0].shape[2] - cols
    return pl.pallas_call(
        functools.partial(term_kernel, len(lows), len(owns), len(packs)),
        grid=(1,),
        in_specs=[smem, smem]
        + [vmem] * (len(lows) + len(owns))
        + [pack_spec(p, depth, cols) for p in packs]
        + [pl.BlockSpec(memory_space=pl.ANY)] * len(after),
        out_specs=[vmem] * len(owns),
        out_shape=[jax.ShapeDtypeStruct((row_total, width), F32)] * len(owns),
        compiler_params=pltpu.CompilerParams(vmem_limit_bytes=VMEM_LIMIT),
        cost_estimate=SMALL,
        name="adapter_term",
    )(starts, ends, *lows, *owns, *packs, *after)


def finish_kernel(addends, term_ref, *rest):
    total = term_ref[...]
    for ref in rest[:addends]:
        total = total + ref[...].astype(F32)
    rest[-1][...] = total.astype(rest[-1].dtype)


def finish(term, skip, arrived, offset, cols, result, cost):
    row_total, width = arrived.shape
    height = min(row_total, 256)
    block = pl.BlockSpec((height, width), lambda i: (i, 0))
    held = [] if result is None else [result]
    return pl.pallas_call(
        functools.partial(finish_kernel, 1),
        grid=(row_total // height,),
        in_specs=[pl.BlockSpec((height, width), lambda i: (i, skip // width)), block]
        + [pl.BlockSpec(memory_space=pl.ANY)] * len(held),
        out_specs=pl.BlockSpec((height, width), lambda i: (i, offset // width)),
        out_shape=jax.ShapeDtypeStruct((row_total, cols), BF16),
        input_output_aliases={2: 0} if held else {},
        compiler_params=pltpu.CompilerParams(vmem_limit_bytes=VMEM_LIMIT),
        cost_estimate=cost,
        name="finish",
    )(term, arrived, *held)


def local(req_total, tp_total, rows, weight, down, up, table, ids, lens):
    weight = pltpu.with_memory_space_constraint(weight, pltpu.HBM)
    down = pltpu.with_memory_space_constraint(down, pltpu.HBM)
    up = pltpu.with_memory_space_constraint(up, pltpu.HBM)
    rank = down.shape[1]
    cols = up.shape[2]
    width = cols // PIECES
    me_req = lax.axis_index("req").astype(jnp.int32)
    me = lax.axis_index("tp").astype(jnp.int32)
    steps = tp_total - 1

    def move(value, piece):
        pairs = []
        for r in range(req_total):
            way = 1 if (r + piece) % 2 == 0 else tp_total - 1
            for i in range(tp_total):
                pairs.append((r * tp_total + i, r * tp_total + (i + way) % tp_total))
        return lax.ppermute(value, ("req", "tp"), pairs)

    def start_of(back, piece):
        behind = jnp.where(lax.rem(me_req + piece, 2) == 0, tp_total - back, back)
        block = lax.rem(me + behind, tp_total)
        return block * cols + piece * width

    def partial(back, piece, **options):
        return block_product(rows, weight, start_of(back, piece), width, **options)

    def half_partial(back, piece, skip, **options):
        first = start_of(back, piece) + skip
        return block_product(rows, weight, first, width // 2, skip=skip, **options)

    last, rows = first_product(rows, weight, start_of(1, 0), width)
    rows = pltpu.with_memory_space_constraint(rows, pltpu.VMEM)
    moving = [move(last, 0)]
    for piece in range(1, PIECES):
        last, ids = partial(1, piece, after=[last], ids=ids)
        moving.append(move(last, piece))

    all_ids = [ids]
    for x in range(1, req_total):
        all_ids.append(lax.ppermute(ids, "req", [(i, i ^ x) for i in range(req_total)]))
    last = partial(0, 0, after=[last])
    owns = [last]
    packs, starts, ends = pick_adapters(me_req, table, all_ids, lens, down, up, [last])
    for x in range(1, req_total):
        packs[x] = lax.ppermute(packs[x], "req", [(i, i ^ x) for i in range(req_total)])

    last = starts
    for step in range(1, steps):
        for piece in range(PIECES):
            if step == steps - 1 and piece == PIECES - 1:
                low = low_sums(starts, ends, rows, packs, rank, [last])
                lows = [low]
                for x in range(1, tp_total):
                    pairs = [(i, i ^ x) for i in range(tp_total)]
                    lows.append(lax.ppermute(low, "tp", pairs))
                last = low
            if step == steps - 1 and piece == PIECES - 1:
                halves = []
                for skip in (0, width // 2):
                    last = half_partial(
                        1 + step, piece, skip, addends=[moving[piece]], after=[last]
                    )
                    halves.append(move(last, piece))
                break
            last = partial(1 + step, piece, addends=[moving[piece]], after=[last])
            moving[piece] = move(last, piece)
            if step == 1 and piece > 0:
                last = partial(0, piece, after=[last], cost=LARGE)
                owns.append(last)

    terms = adapter_term(starts, ends, lows, owns, packs, [last])
    parts = [(piece, 0, moving[piece]) for piece in range(PIECES - 1)]
    parts += [(PIECES - 1, skip, half) for skip, half in zip((0, width // 2), halves)]
    result = None
    for piece, skip, arrived in parts:
        arrived = pltpu.with_memory_space_constraint(arrived, pltpu.VMEM)
        cost = LARGE if piece == 0 else SMALL
        offset = piece * width + skip
        result = finish(terms[piece], skip, arrived, offset, cols, result, cost)
    return result


def solution(mesh):
    return jax.shard_map(
        functools.partial(local, mesh.shape["req"], mesh.shape["tp"]),
        mesh=mesh,
        in_specs=(
            P(("groups", "req"), "tp"),
            P("tp", None),
            P(("groups", "req"), None, "tp"),
            P(("groups", "req"), None, "tp"),
            P("groups"),
            P(("groups", "req"), None),
            P(("groups", "req"), None),
        ),
        out_specs=P(("groups", "req"), "tp"),
        check_vma=False,
    )
```

```python
import functools

import jax
import jax.numpy as jnp
from jax import lax
from jax.experimental import pallas as pl
from jax.experimental.pallas import tpu as pltpu
from jax.sharding import PartitionSpec as P

CAP = 6
PIECES = 2
VMEM_LIMIT = 20 * 1024 * 1024
F32 = jnp.float32
BF16 = jnp.bfloat16
SMALL = pl.CostEstimate(flops=1000, bytes_accessed=1000, transcendentals=0)
LARGE = pl.CostEstimate(flops=8 * 10**9, bytes_accessed=1000, transcendentals=0)


def product_kernel(addends, with_ids, first_ref, rows_ref, weight_ref, *rest):
    if with_ids:
        out_ref, ids_out_ref, sem = rest[-3:]
        ids_copy = pltpu.make_async_copy(rest[addends], ids_out_ref, sem)

        @pl.when(pl.program_id(0) == 0)
        def _():
            ids_copy.start()
    else:
        out_ref = rest[-1]
    total = jnp.dot(rows_ref[...], weight_ref[...], preferred_element_type=F32)
    for ref in rest[:addends]:
        total = total + ref[...].astype(F32)
    out_ref[...] = total.astype(out_ref.dtype)
    if with_ids:

        @pl.when(pl.program_id(0) == pl.num_programs(0) - 1)
        def _():
            ids_copy.wait()


def block_product(
    rows, weight, first, width, addends=(), skip=0, after=(), ids=None, cost=SMALL
):
    row_total, depth = rows.shape
    tile = min(256, width)
    with_ids = ids is not None
    smem = pl.BlockSpec(memory_space=pltpu.SMEM)
    hbm = pl.BlockSpec(memory_space=pl.ANY)
    columns = pl.BlockSpec((row_total, tile), lambda j, t: (0, j))
    out_specs, out_shape = [columns], [pltpu.VMEM((row_total, width), BF16)]
    if with_ids:
        out_specs.append(hbm)
        out_shape.append(jax.ShapeDtypeStruct(ids.shape, ids.dtype))
    out = pl.pallas_call(
        functools.partial(product_kernel, len(addends), with_ids),
        grid_spec=pltpu.PrefetchScalarGridSpec(
            num_scalar_prefetch=1,
            grid=(width // tile,),
            in_specs=[
                pl.BlockSpec((row_total, depth), lambda j, t: (0, 0)),
                pl.BlockSpec((depth, tile), lambda j, t: (0, t[0] + j)),
            ]
            + [pl.BlockSpec((row_total, tile), lambda j, t: (0, skip // tile + j))] * len(addends)
            + [hbm] * with_ids
            + [hbm] * len(after),
            out_specs=out_specs,
            scratch_shapes=[pltpu.SemaphoreType.DMA] if with_ids else [],
        ),
        out_shape=out_shape,
        compiler_params=pltpu.CompilerParams(vmem_limit_bytes=VMEM_LIMIT),
        cost_estimate=cost,
        name="block_product",
    )((first // tile).reshape(1), rows, weight, *addends, *([ids] if with_ids else []), *after)
    return out if with_ids else out[0]


def first_kernel(chunk, first_ref, rows_ref, weight_ref, out_ref, lhs_ref, rhs_ref, acc_ref, sems):
    columns = pl.ds(pl.multiple_of(first_ref[0], 128), out_ref.shape[1])
    chunks = rhs_ref.shape[0]

    def copies(k):
        part = pl.ds(k * chunk, chunk)
        return (
            pltpu.make_async_copy(rows_ref.at[:, part], lhs_ref.at[:, part], sems.at[0, k]),
            pltpu.make_async_copy(weight_ref.at[part, columns], rhs_ref.at[k], sems.at[1, k]),
        )

    for k in range(chunks):
        for copy in copies(k):
            copy.start()
    for k in range(chunks):
        for copy in copies(k):
            copy.wait()
        lhs = lhs_ref[:, k * chunk : (k + 1) * chunk]
        part = jnp.dot(lhs, rhs_ref[k], preferred_element_type=F32)
        if k == 0:
            acc_ref[...] = part
        elif k < chunks - 1:
            acc_ref[...] += part
        else:
            out_ref[...] = (acc_ref[...] + part).astype(out_ref.dtype)


def first_product(rows, weight, first, width):
    row_total, depth = rows.shape
    chunk = min(512, depth // 2)
    chunks = depth // chunk
    hbm = pl.BlockSpec(memory_space=pltpu.HBM)
    return pl.pallas_call(
        functools.partial(first_kernel, chunk),
        in_specs=[pl.BlockSpec(memory_space=pltpu.SMEM), hbm, hbm],
        out_specs=[pl.BlockSpec(memory_space=pltpu.VMEM)] * 2,
        out_shape=[
            pltpu.VMEM((row_total, width), BF16),
            pltpu.VMEM((row_total, depth), BF16),
        ],
        scratch_shapes=[
            pltpu.VMEM((chunks, chunk, width), BF16),
            pltpu.VMEM((row_total, width), F32),
            pltpu.SemaphoreType.DMA((2, chunks)),
        ],
        compiler_params=pltpu.CompilerParams(vmem_limit_bytes=VMEM_LIMIT),
        cost_estimate=SMALL,
        name="first_product",
    )(first.reshape(1), pltpu.with_memory_space_constraint(rows, pltpu.HBM), weight)


def pick_kernel(peers, afters, me_ref, table_ref, lens_ref, *rest):
    ids_refs = rest[:peers]
    down_ref, up_ref = rest[peers : peers + 2]
    rest = rest[peers + 2 + afters :]
    packs, (start_ref, end_ref, pick_ref, count_ref, sem) = rest[:peers], rest[peers:]
    segs = lens_ref.shape[1]
    share, _, depth = down_ref.shape
    cols = up_ref.shape[2]
    me = me_ref[0]

    def clear(q, carry):
        pick_ref[q] = 0
        start_ref[q] = 0
        end_ref[q] = 0
        return carry

    lax.fori_loop(0, peers * CAP, clear, 0, unroll=8)
    for x in range(peers):
        count_ref[x] = 0

    def copies(x, c, source):
        pack = packs[x].at[c]
        return (
            pltpu.make_async_copy(down_ref.at[source], pack.at[:, pl.ds(0, depth)], sem),
            pltpu.make_async_copy(up_ref.at[source], pack.at[:, pl.ds(depth, cols)], sem),
        )

    for x in reversed(range(peers)):

        def choose(s, count):
            local = table_ref[ids_refs[x][0, s]] - me * share
            mine = jnp.logical_and(local >= 0, local < share)

            @pl.when(jnp.logical_and(mine, count < CAP))
            def _():
                pick_ref[x * CAP + count] = local

            return count + mine.astype(jnp.int32)

        lax.fori_loop(0, segs, choose, 0, unroll=4)
        for c in range(CAP):
            for copy in copies(x, c, pick_ref[x * CAP + c]):
                copy.start()

    def place(s, first):
        x = lax.bitwise_xor(table_ref[ids_refs[0][0, s]] // share, me)
        count = count_ref[x]
        last = first + lens_ref[0, s]

        @pl.when(count < CAP)
        def _():
            start_ref[x * CAP + count] = first
            end_ref[x * CAP + count] = last

        count_ref[x] = count + 1
        return last

    lax.fori_loop(0, segs, place, 0, unroll=4)

    for x in range(peers):
        for c in range(CAP):
            for copy in copies(x, c, 0):
                copy.wait()


def pick_adapters(me, table, all_ids, lens, down, up, after):
    peers = len(all_ids)
    _, rank, depth = down.shape
    cols = up.shape[2]
    smem = pl.BlockSpec(memory_space=pltpu.SMEM)
    vmem = pl.BlockSpec(memory_space=pltpu.VMEM)
    hbm = pl.BlockSpec(memory_space=pl.ANY)
    out = pl.pallas_call(
        functools.partial(pick_kernel, peers, len(after)),
        in_specs=[smem] * (3 + peers) + [hbm] * (2 + len(after)),
        out_specs=[vmem] * peers + [smem, smem],
        out_shape=[jax.ShapeDtypeStruct((CAP, rank, depth + cols), BF16)] * peers
        + [jax.ShapeDtypeStruct((peers * CAP,), jnp.int32)] * 2,
        scratch_shapes=[
            pltpu.SMEM((peers * CAP,), jnp.int32),
            pltpu.SMEM((peers,), jnp.int32),
            pltpu.SemaphoreType.DMA,
        ],
        compiler_params=pltpu.CompilerParams(vmem_limit_bytes=VMEM_LIMIT),
        cost_estimate=SMALL,
        name="pick_adapters",
    )(me.reshape(1), table, lens, *all_ids, down, up, *after)
    return list(out[:-2]), out[-2], out[-1]


def pack_spec(pack, first, width):
    return pl.BlockSpec(pack.shape[:2] + (width,), lambda i: (0, 0, first // width))


def low_kernel(peers, start_ref, end_ref, rows_ref, *rest):
    down_refs, out_ref = rest[:peers], rest[-1]
    row_total, depth = rows_ref.shape
    rank = out_ref.shape[0]
    place = lax.broadcasted_iota(jnp.int32, (rank, row_total), 1)
    downs = jnp.concatenate([ref[...].reshape(CAP * rank, depth) for ref in down_refs], axis=0)
    part = lax.dot_general(
        downs, rows_ref[...], (((1,), (1,)), ((), ())), preferred_element_type=F32
    )
    total = jnp.zeros((rank, row_total), F32)
    for q in range(peers * CAP):
        member = jnp.logical_and(place >= start_ref[q], place < end_ref[q])
        total = jnp.where(member, part[q * rank : (q + 1) * rank], total)
    out_ref[...] = total.astype(BF16)


def low_sums(starts, ends, rows, packs, rank, after):
    row_total, depth = rows.shape
    smem = pl.BlockSpec(memory_space=pltpu.SMEM)
    vmem = pl.BlockSpec(memory_space=pltpu.VMEM)
    return pl.pallas_call(
        functools.partial(low_kernel, len(packs)),
        grid=(1,),
        in_specs=[smem, smem, vmem]
        + [pack_spec(p, 0, depth) for p in packs]
        + [pl.BlockSpec(memory_space=pl.ANY)] * len(after),
        out_specs=vmem,
        out_shape=jax.ShapeDtypeStruct((rank, row_total), BF16),
        compiler_params=pltpu.CompilerParams(vmem_limit_bytes=VMEM_LIMIT),
        cost_estimate=SMALL,
        name="low_sums",
    )(starts, ends, rows, *packs, *after)


def term_kernel(lows, pieces, peers, start_ref, end_ref, *rest):
    low_refs, rest = rest[:lows], rest[lows:]
    own_refs, rest = rest[:pieces], rest[pieces:]
    up_refs, out_refs = rest[:peers], rest[-pieces:]
    rank, row_total = low_refs[0].shape
    width = out_refs[0].shape[1]
    cols = width * pieces
    low = low_refs[0][...].astype(F32)
    for ref in low_refs[1:]:
        low = low + ref[...].astype(F32)
    low = low.astype(BF16).astype(F32)
    place = lax.broadcasted_iota(jnp.int32, (rank, row_total), 1)
    spread = []
    for q in range(len(up_refs) * CAP):
        member = jnp.logical_and(place >= start_ref[q], place < end_ref[q])
        spread.append(jnp.where(member, low, 0.0))
    spread = jnp.concatenate(spread, axis=0).astype(BF16)
    ups = jnp.concatenate([ref[...].reshape(CAP * rank, cols) for ref in up_refs], axis=0)
    for piece in range(pieces):
        columns = slice(piece * width, (piece + 1) * width)
        term = lax.dot_general(
            spread, ups[:, columns], (((0,), (0,)), ((), ())), preferred_element_type=F32
        )
        out_refs[piece][...] = own_refs[piece][...].astype(F32) + term


def adapter_term(starts, ends, lows, owns, packs, after):
    row_total, width = owns[0].shape
    cols = width * len(owns)
    smem = pl.BlockSpec(memory_space=pltpu.SMEM)
    vmem = pl.BlockSpec(memory_space=pltpu.VMEM)
    depth = packs[0].shape[2] - cols
    return pl.pallas_call(
        functools.partial(term_kernel, len(lows), len(owns), len(packs)),
        grid=(1,),
        in_specs=[smem, smem]
        + [vmem] * (len(lows) + len(owns))
        + [pack_spec(p, depth, cols) for p in packs]
        + [pl.BlockSpec(memory_space=pl.ANY)] * len(after),
        out_specs=[vmem] * len(owns),
        out_shape=[jax.ShapeDtypeStruct((row_total, width), F32)] * len(owns),
        compiler_params=pltpu.CompilerParams(vmem_limit_bytes=VMEM_LIMIT),
        cost_estimate=SMALL,
        name="adapter_term",
    )(starts, ends, *lows, *owns, *packs, *after)


def finish_kernel(addends, term_ref, *rest):
    total = term_ref[...]
    for ref in rest[:addends]:
        total = total + ref[...].astype(F32)
    rest[-1][...] = total.astype(rest[-1].dtype)


def finish(term, skip, arrived, offset, cols, result, cost):
    row_total, width = arrived.shape
    height = min(row_total, 256)
    block = pl.BlockSpec((height, width), lambda i: (i, 0))
    held = [] if result is None else [result]
    return pl.pallas_call(
        functools.partial(finish_kernel, 1),
        grid=(row_total // height,),
        in_specs=[pl.BlockSpec((height, width), lambda i: (i, skip // width)), block]
        + [pl.BlockSpec(memory_space=pl.ANY)] * len(held),
        out_specs=pl.BlockSpec((height, width), lambda i: (i, offset // width)),
        out_shape=jax.ShapeDtypeStruct((row_total, cols), BF16),
        input_output_aliases={2: 0} if held else {},
        compiler_params=pltpu.CompilerParams(vmem_limit_bytes=VMEM_LIMIT),
        cost_estimate=cost,
        name="finish",
    )(term, arrived, *held)


def local(req_total, tp_total, rows, weight, down, up, table, ids, lens):
    weight = pltpu.with_memory_space_constraint(weight, pltpu.HBM)
    down = pltpu.with_memory_space_constraint(down, pltpu.HBM)
    up = pltpu.with_memory_space_constraint(up, pltpu.HBM)
    rank = down.shape[1]
    cols = up.shape[2]
    width = cols // PIECES
    me_req = lax.axis_index("req").astype(jnp.int32)
    me = lax.axis_index("tp").astype(jnp.int32)
    steps = tp_total - 1

    def move(value, piece):
        pairs = []
        for r in range(req_total):
            way = 1 if (r + piece) % 2 == 0 else tp_total - 1
            for i in range(tp_total):
                pairs.append((r * tp_total + i, r * tp_total + (i + way) % tp_total))
        return lax.ppermute(value, ("req", "tp"), pairs)

    def start_of(back, piece):
        behind = jnp.where(lax.rem(me_req + piece, 2) == 0, tp_total - back, back)
        block = lax.rem(me + behind, tp_total)
        return block * cols + piece * width

    def partial(back, piece, **options):
        return block_product(rows, weight, start_of(back, piece), width, **options)

    def half_partial(back, piece, skip, **options):
        first = start_of(back, piece) + skip
        return block_product(rows, weight, first, width // 2, skip=skip, **options)

    last, rows = first_product(rows, weight, start_of(1, 0), width)
    rows = pltpu.with_memory_space_constraint(rows, pltpu.VMEM)
    moving = [move(last, 0)]
    for piece in range(1, PIECES):
        last, ids = partial(1, piece, after=[last], ids=ids)
        moving.append(move(last, piece))

    all_ids = [ids]
    for x in range(1, req_total):
        all_ids.append(lax.ppermute(ids, "req", [(i, i ^ x) for i in range(req_total)]))
    last = partial(0, 0, after=[last])
    owns = [last]
    packs, starts, ends = pick_adapters(me_req, table, all_ids, lens, down, up, [last])
    for x in range(1, req_total):
        packs[x] = lax.ppermute(packs[x], "req", [(i, i ^ x) for i in range(req_total)])

    last = starts
    for step in range(1, steps):
        for piece in range(PIECES):
            if step == steps - 1 and piece == PIECES - 1:
                low = low_sums(starts, ends, rows, packs, rank, [last])
                lows = [low]
                for x in range(1, tp_total):
                    pairs = [(i, i ^ x) for i in range(tp_total)]
                    lows.append(lax.ppermute(low, "tp", pairs))
                last = low
            if step == steps - 1 and piece == PIECES - 1:
                halves = []
                for skip in (0, width // 2):
                    last = half_partial(
                        1 + step, piece, skip, addends=[moving[piece]], after=[last]
                    )
                    halves.append(move(last, piece))
                break
            last = partial(1 + step, piece, addends=[moving[piece]], after=[last])
            moving[piece] = move(last, piece)
            if step == 1 and piece > 0:
                last = partial(0, piece, after=[last], cost=LARGE)
                owns.append(last)

    terms = adapter_term(starts, ends, lows, owns, packs, [last])
    parts = [(piece, 0, moving[piece]) for piece in range(PIECES - 1)]
    parts += [(PIECES - 1, skip, half) for skip, half in zip((0, width // 2), halves)]
    result = None
    for piece, skip, arrived in parts:
        arrived = pltpu.with_memory_space_constraint(arrived, pltpu.VMEM)
        cost = LARGE if piece == 0 else SMALL
        offset = piece * width + skip
        result = finish(terms[piece], skip, arrived, offset, cols, result, cost)
    return result


def solution(mesh):
    return jax.shard_map(
        functools.partial(local, mesh.shape["req"], mesh.shape["tp"]),
        mesh=mesh,
        in_specs=(
            P(("groups", "req"), "tp"),
            P("tp", None),
            P(("groups", "req"), None, "tp"),
            P(("groups", "req"), None, "tp"),
            P("groups"),
            P(("groups", "req"), None),
            P(("groups", "req"), None),
        ),
        out_specs=P(("groups", "req"), "tp"),
        check_vma=False,
    )
```

```python
import functools

import jax
import jax.numpy as jnp
from jax import lax
from jax.experimental import pallas as pl
from jax.experimental.pallas import tpu as pltpu
from jax.sharding import PartitionSpec as P

CAP = 6
PIECES = 2
VMEM_LIMIT = 20 * 1024 * 1024
F32 = jnp.float32
BF16 = jnp.bfloat16
SMALL = pl.CostEstimate(flops=1000, bytes_accessed=1000, transcendentals=0)
LARGE = pl.CostEstimate(flops=8 * 10**9, bytes_accessed=1000, transcendentals=0)


def product_kernel(addends, with_ids, first_ref, rows_ref, weight_ref, *rest):
    if with_ids:
        out_ref, ids_out_ref, sem = rest[-3:]
        ids_copy = pltpu.make_async_copy(rest[addends], ids_out_ref, sem)

        @pl.when(pl.program_id(0) == 0)
        def _():
            ids_copy.start()
    else:
        out_ref = rest[-1]
    total = jnp.dot(rows_ref[...], weight_ref[...], preferred_element_type=F32)
    for ref in rest[:addends]:
        total = total + ref[...].astype(F32)
    out_ref[...] = total.astype(out_ref.dtype)
    if with_ids:

        @pl.when(pl.program_id(0) == pl.num_programs(0) - 1)
        def _():
            ids_copy.wait()


def block_product(
    rows, weight, first, width, addends=(), skip=0, after=(), ids=None, cost=SMALL
):
    row_total, depth = rows.shape
    tile = min(256, width)
    with_ids = ids is not None
    smem = pl.BlockSpec(memory_space=pltpu.SMEM)
    hbm = pl.BlockSpec(memory_space=pl.ANY)
    columns = pl.BlockSpec((row_total, tile), lambda j, t: (0, j))
    out_specs, out_shape = [columns], [pltpu.VMEM((row_total, width), BF16)]
    if with_ids:
        out_specs.append(hbm)
        out_shape.append(jax.ShapeDtypeStruct(ids.shape, ids.dtype))
    out = pl.pallas_call(
        functools.partial(product_kernel, len(addends), with_ids),
        grid_spec=pltpu.PrefetchScalarGridSpec(
            num_scalar_prefetch=1,
            grid=(width // tile,),
            in_specs=[
                pl.BlockSpec((row_total, depth), lambda j, t: (0, 0)),
                pl.BlockSpec((depth, tile), lambda j, t: (0, t[0] + j)),
            ]
            + [pl.BlockSpec((row_total, tile), lambda j, t: (0, skip // tile + j))] * len(addends)
            + [hbm] * with_ids
            + [hbm] * len(after),
            out_specs=out_specs,
            scratch_shapes=[pltpu.SemaphoreType.DMA] if with_ids else [],
        ),
        out_shape=out_shape,
        compiler_params=pltpu.CompilerParams(vmem_limit_bytes=VMEM_LIMIT),
        cost_estimate=cost,
        name="block_product",
    )((first // tile).reshape(1), rows, weight, *addends, *([ids] if with_ids else []), *after)
    return out if with_ids else out[0]


def first_kernel(chunk, first_ref, rows_ref, weight_ref, out_ref, lhs_ref, rhs_ref, acc_ref, sems):
    columns = pl.ds(pl.multiple_of(first_ref[0], 128), out_ref.shape[1])
    chunks = rhs_ref.shape[0]

    def copies(k):
        part = pl.ds(k * chunk, chunk)
        return (
            pltpu.make_async_copy(rows_ref.at[:, part], lhs_ref.at[:, part], sems.at[0, k]),
            pltpu.make_async_copy(weight_ref.at[part, columns], rhs_ref.at[k], sems.at[1, k]),
        )

    for k in range(chunks):
        for copy in copies(k):
            copy.start()
    for k in range(chunks):
        for copy in copies(k):
            copy.wait()
        lhs = lhs_ref[:, k * chunk : (k + 1) * chunk]
        part = jnp.dot(lhs, rhs_ref[k], preferred_element_type=F32)
        if k == 0:
            acc_ref[...] = part
        elif k < chunks - 1:
            acc_ref[...] += part
        else:
            out_ref[...] = (acc_ref[...] + part).astype(out_ref.dtype)


def first_product(rows, weight, first, width):
    row_total, depth = rows.shape
    chunk = min(512, depth // 2)
    chunks = depth // chunk
    hbm = pl.BlockSpec(memory_space=pltpu.HBM)
    return pl.pallas_call(
        functools.partial(first_kernel, chunk),
        in_specs=[pl.BlockSpec(memory_space=pltpu.SMEM), hbm, hbm],
        out_specs=[pl.BlockSpec(memory_space=pltpu.VMEM)] * 2,
        out_shape=[
            pltpu.VMEM((row_total, width), BF16),
            pltpu.VMEM((row_total, depth), BF16),
        ],
        scratch_shapes=[
            pltpu.VMEM((chunks, chunk, width), BF16),
            pltpu.VMEM((row_total, width), F32),
            pltpu.SemaphoreType.DMA((2, chunks)),
        ],
        compiler_params=pltpu.CompilerParams(vmem_limit_bytes=VMEM_LIMIT),
        cost_estimate=SMALL,
        name="first_product",
    )(first.reshape(1), pltpu.with_memory_space_constraint(rows, pltpu.HBM), weight)


def pick_kernel(peers, afters, me_ref, table_ref, lens_ref, *rest):
    ids_refs = rest[:peers]
    down_ref, up_ref = rest[peers : peers + 2]
    rest = rest[peers + 2 + afters :]
    packs, (start_ref, end_ref, pick_ref, count_ref, sem) = rest[:peers], rest[peers:]
    segs = lens_ref.shape[1]
    share, _, depth = down_ref.shape
    cols = up_ref.shape[2]
    me = me_ref[0]

    def clear(q, carry):
        pick_ref[q] = 0
        start_ref[q] = 0
        end_ref[q] = 0
        return carry

    lax.fori_loop(0, peers * CAP, clear, 0, unroll=8)
    for x in range(peers):
        count_ref[x] = 0

    def copies(x, c, source):
        pack = packs[x].at[c]
        return (
            pltpu.make_async_copy(down_ref.at[source], pack.at[:, pl.ds(0, depth)], sem),
            pltpu.make_async_copy(up_ref.at[source], pack.at[:, pl.ds(depth, cols)], sem),
        )

    for x in reversed(range(peers)):

        def choose(s, count):
            local = table_ref[ids_refs[x][0, s]] - me * share
            mine = jnp.logical_and(local >= 0, local < share)

            @pl.when(jnp.logical_and(mine, count < CAP))
            def _():
                pick_ref[x * CAP + count] = local

            return count + mine.astype(jnp.int32)

        lax.fori_loop(0, segs, choose, 0, unroll=4)
        for c in range(CAP):
            for copy in copies(x, c, pick_ref[x * CAP + c]):
                copy.start()

    def place(s, first):
        x = lax.bitwise_xor(table_ref[ids_refs[0][0, s]] // share, me)
        count = count_ref[x]
        last = first + lens_ref[0, s]

        @pl.when(count < CAP)
        def _():
            start_ref[x * CAP + count] = first
            end_ref[x * CAP + count] = last

        count_ref[x] = count + 1
        return last

    lax.fori_loop(0, segs, place, 0, unroll=4)

    for x in range(peers):
        for c in range(CAP):
            for copy in copies(x, c, 0):
                copy.wait()


def pick_adapters(me, table, all_ids, lens, down, up, after):
    peers = len(all_ids)
    _, rank, depth = down.shape
    cols = up.shape[2]
    smem = pl.BlockSpec(memory_space=pltpu.SMEM)
    vmem = pl.BlockSpec(memory_space=pltpu.VMEM)
    hbm = pl.BlockSpec(memory_space=pl.ANY)
    out = pl.pallas_call(
        functools.partial(pick_kernel, peers, len(after)),
        in_specs=[smem] * (3 + peers) + [hbm] * (2 + len(after)),
        out_specs=[vmem] * peers + [smem, smem],
        out_shape=[jax.ShapeDtypeStruct((CAP, rank, depth + cols), BF16)] * peers
        + [jax.ShapeDtypeStruct((peers * CAP,), jnp.int32)] * 2,
        scratch_shapes=[
            pltpu.SMEM((peers * CAP,), jnp.int32),
            pltpu.SMEM((peers,), jnp.int32),
            pltpu.SemaphoreType.DMA,
        ],
        compiler_params=pltpu.CompilerParams(vmem_limit_bytes=VMEM_LIMIT),
        cost_estimate=SMALL,
        name="pick_adapters",
    )(me.reshape(1), table, lens, *all_ids, down, up, *after)
    return list(out[:-2]), out[-2], out[-1]


def pack_spec(pack, first, width):
    return pl.BlockSpec(pack.shape[:2] + (width,), lambda i: (0, 0, first // width))


def low_kernel(peers, start_ref, end_ref, rows_ref, *rest):
    down_refs, out_ref = rest[:peers], rest[-1]
    row_total, depth = rows_ref.shape
    rank = out_ref.shape[0]
    place = lax.broadcasted_iota(jnp.int32, (rank, row_total), 1)
    downs = jnp.concatenate([ref[...].reshape(CAP * rank, depth) for ref in down_refs], axis=0)
    part = lax.dot_general(
        downs, rows_ref[...], (((1,), (1,)), ((), ())), preferred_element_type=F32
    )
    total = jnp.zeros((rank, row_total), F32)
    for q in range(peers * CAP):
        member = jnp.logical_and(place >= start_ref[q], place < end_ref[q])
        total = jnp.where(member, part[q * rank : (q + 1) * rank], total)
    out_ref[...] = total.astype(BF16)


def low_sums(starts, ends, rows, packs, rank, after):
    row_total, depth = rows.shape
    smem = pl.BlockSpec(memory_space=pltpu.SMEM)
    vmem = pl.BlockSpec(memory_space=pltpu.VMEM)
    return pl.pallas_call(
        functools.partial(low_kernel, len(packs)),
        grid=(1,),
        in_specs=[smem, smem, vmem]
        + [pack_spec(p, 0, depth) for p in packs]
        + [pl.BlockSpec(memory_space=pl.ANY)] * len(after),
        out_specs=vmem,
        out_shape=jax.ShapeDtypeStruct((rank, row_total), BF16),
        compiler_params=pltpu.CompilerParams(vmem_limit_bytes=VMEM_LIMIT),
        cost_estimate=SMALL,
        name="low_sums",
    )(starts, ends, rows, *packs, *after)


def term_kernel(lows, pieces, peers, start_ref, end_ref, *rest):
    low_refs, rest = rest[:lows], rest[lows:]
    own_refs, rest = rest[:pieces], rest[pieces:]
    up_refs, out_refs = rest[:peers], rest[-pieces:]
    rank, row_total = low_refs[0].shape
    width = out_refs[0].shape[1]
    cols = width * pieces
    low = low_refs[0][...].astype(F32)
    for ref in low_refs[1:]:
        low = low + ref[...].astype(F32)
    low = low.astype(BF16).astype(F32)
    place = lax.broadcasted_iota(jnp.int32, (rank, row_total), 1)
    spread = []
    for q in range(len(up_refs) * CAP):
        member = jnp.logical_and(place >= start_ref[q], place < end_ref[q])
        spread.append(jnp.where(member, low, 0.0))
    spread = jnp.concatenate(spread, axis=0).astype(BF16)
    ups = jnp.concatenate([ref[...].reshape(CAP * rank, cols) for ref in up_refs], axis=0)
    for piece in range(pieces):
        columns = slice(piece * width, (piece + 1) * width)
        term = lax.dot_general(
            spread, ups[:, columns], (((0,), (0,)), ((), ())), preferred_element_type=F32
        )
        out_refs[piece][...] = own_refs[piece][...].astype(F32) + term


def adapter_term(starts, ends, lows, owns, packs, after):
    row_total, width = owns[0].shape
    cols = width * len(owns)
    smem = pl.BlockSpec(memory_space=pltpu.SMEM)
    vmem = pl.BlockSpec(memory_space=pltpu.VMEM)
    depth = packs[0].shape[2] - cols
    return pl.pallas_call(
        functools.partial(term_kernel, len(lows), len(owns), len(packs)),
        grid=(1,),
        in_specs=[smem, smem]
        + [vmem] * (len(lows) + len(owns))
        + [pack_spec(p, depth, cols) for p in packs]
        + [pl.BlockSpec(memory_space=pl.ANY)] * len(after),
        out_specs=[vmem] * len(owns),
        out_shape=[jax.ShapeDtypeStruct((row_total, width), F32)] * len(owns),
        compiler_params=pltpu.CompilerParams(vmem_limit_bytes=VMEM_LIMIT),
        cost_estimate=SMALL,
        name="adapter_term",
    )(starts, ends, *lows, *owns, *packs, *after)


def finish_kernel(addends, term_ref, *rest):
    total = term_ref[...]
    for ref in rest[:addends]:
        total = total + ref[...].astype(F32)
    rest[-1][...] = total.astype(rest[-1].dtype)


def finish(term, skip, arrived, offset, cols, result, cost):
    row_total, width = arrived.shape
    height = min(row_total, 256)
    block = pl.BlockSpec((height, width), lambda i: (i, 0))
    held = [] if result is None else [result]
    return pl.pallas_call(
        functools.partial(finish_kernel, 1),
        grid=(row_total // height,),
        in_specs=[pl.BlockSpec((height, width), lambda i: (i, skip // width)), block]
        + [pl.BlockSpec(memory_space=pl.ANY)] * len(held),
        out_specs=pl.BlockSpec((height, width), lambda i: (i, offset // width)),
        out_shape=jax.ShapeDtypeStruct((row_total, cols), BF16),
        input_output_aliases={2: 0} if held else {},
        compiler_params=pltpu.CompilerParams(vmem_limit_bytes=VMEM_LIMIT),
        cost_estimate=cost,
        name="finish",
    )(term, arrived, *held)


def local(req_total, tp_total, rows, weight, down, up, table, ids, lens):
    weight = pltpu.with_memory_space_constraint(weight, pltpu.HBM)
    down = pltpu.with_memory_space_constraint(down, pltpu.HBM)
    up = pltpu.with_memory_space_constraint(up, pltpu.HBM)
    rank = down.shape[1]
    cols = up.shape[2]
    width = cols // PIECES
    me_req = lax.axis_index("req").astype(jnp.int32)
    me = lax.axis_index("tp").astype(jnp.int32)
    steps = tp_total - 1

    def move(value, piece):
        pairs = []
        for r in range(req_total):
            way = 1 if (r + piece) % 2 == 0 else tp_total - 1
            for i in range(tp_total):
                pairs.append((r * tp_total + i, r * tp_total + (i + way) % tp_total))
        return lax.ppermute(value, ("req", "tp"), pairs)

    def start_of(back, piece):
        behind = jnp.where(lax.rem(me_req + piece, 2) == 0, tp_total - back, back)
        block = lax.rem(me + behind, tp_total)
        return block * cols + piece * width

    def partial(back, piece, **options):
        return block_product(rows, weight, start_of(back, piece), width, **options)

    def half_partial(back, piece, skip, **options):
        first = start_of(back, piece) + skip
        return block_product(rows, weight, first, width // 2, skip=skip, **options)

    last, rows = first_product(rows, weight, start_of(1, 0), width)
    rows = pltpu.with_memory_space_constraint(rows, pltpu.VMEM)
    moving = [move(last, 0)]
    for piece in range(1, PIECES):
        last, ids = partial(1, piece, after=[last], ids=ids)
        moving.append(move(last, piece))

    all_ids = [ids]
    for x in range(1, req_total):
        all_ids.append(lax.ppermute(ids, "req", [(i, i ^ x) for i in range(req_total)]))
    last = partial(0, 0, after=[last])
    owns = [last]
    packs, starts, ends = pick_adapters(me_req, table, all_ids, lens, down, up, [last])
    for x in range(1, req_total):
        packs[x] = lax.ppermute(packs[x], "req", [(i, i ^ x) for i in range(req_total)])

    last = starts
    for step in range(1, steps):
        for piece in range(PIECES):
            if step == steps - 1 and piece == PIECES - 1:
                low = low_sums(starts, ends, rows, packs, rank, [last])
                lows = [low]
                for x in reversed(range(1, tp_total)):
                    pairs = [(i, i ^ x) for i in range(tp_total)]
                    lows.append(lax.ppermute(low, "tp", pairs))
                last = low
            if step == steps - 1 and piece == PIECES - 1:
                halves = []
                for skip in (0, width // 2):
                    last = half_partial(
                        1 + step, piece, skip, addends=[moving[piece]], after=[last]
                    )
                    halves.append(move(last, piece))
                break
            last = partial(1 + step, piece, addends=[moving[piece]], after=[last])
            moving[piece] = move(last, piece)
            if step == 1 and piece > 0:
                last = partial(0, piece, after=[last], cost=LARGE)
                owns.append(last)

    terms = adapter_term(starts, ends, lows, owns, packs, [last])
    parts = [(piece, 0, moving[piece]) for piece in range(PIECES - 1)]
    parts += [(PIECES - 1, skip, half) for skip, half in zip((0, width // 2), halves)]
    result = None
    for piece, skip, arrived in parts:
        arrived = pltpu.with_memory_space_constraint(arrived, pltpu.VMEM)
        cost = LARGE if piece == 0 else SMALL
        offset = piece * width + skip
        result = finish(terms[piece], skip, arrived, offset, cols, result, cost)
    return result


def solution(mesh):
    return jax.shard_map(
        functools.partial(local, mesh.shape["req"], mesh.shape["tp"]),
        mesh=mesh,
        in_specs=(
            P(("groups", "req"), "tp"),
            P("tp", None),
            P(("groups", "req"), None, "tp"),
            P(("groups", "req"), None, "tp"),
            P("groups"),
            P(("groups", "req"), None),
            P(("groups", "req"), None),
        ),
        out_specs=P(("groups", "req"), "tp"),
        check_vma=False,
    )
```

```python
import functools

import jax
import jax.numpy as jnp
from jax import lax
from jax.experimental import pallas as pl
from jax.experimental.pallas import tpu as pltpu
from jax.sharding import PartitionSpec as P

CAP = 6
PIECES = 2
VMEM_LIMIT = 20 * 1024 * 1024
F32 = jnp.float32
BF16 = jnp.bfloat16
SMALL = pl.CostEstimate(flops=1000, bytes_accessed=1000, transcendentals=0)
LARGE = pl.CostEstimate(flops=8 * 10**9, bytes_accessed=1000, transcendentals=0)


def product_kernel(addends, with_ids, first_ref, rows_ref, weight_ref, *rest):
    if with_ids:
        out_ref, ids_out_ref, sem = rest[-3:]
        ids_copy = pltpu.make_async_copy(rest[addends], ids_out_ref, sem)

        @pl.when(pl.program_id(0) == 0)
        def _():
            ids_copy.start()
    else:
        out_ref = rest[-1]
    total = jnp.dot(rows_ref[...], weight_ref[...], preferred_element_type=F32)
    for ref in rest[:addends]:
        total = total + ref[...].astype(F32)
    out_ref[...] = total.astype(out_ref.dtype)
    if with_ids:

        @pl.when(pl.program_id(0) == pl.num_programs(0) - 1)
        def _():
            ids_copy.wait()


def block_product(
    rows, weight, first, width, addends=(), skip=0, after=(), ids=None, cost=SMALL
):
    row_total, depth = rows.shape
    tile = min(256, width)
    with_ids = ids is not None
    smem = pl.BlockSpec(memory_space=pltpu.SMEM)
    hbm = pl.BlockSpec(memory_space=pl.ANY)
    columns = pl.BlockSpec((row_total, tile), lambda j, t: (0, j))
    out_specs, out_shape = [columns], [pltpu.VMEM((row_total, width), BF16)]
    if with_ids:
        out_specs.append(hbm)
        out_shape.append(jax.ShapeDtypeStruct(ids.shape, ids.dtype))
    out = pl.pallas_call(
        functools.partial(product_kernel, len(addends), with_ids),
        grid_spec=pltpu.PrefetchScalarGridSpec(
            num_scalar_prefetch=1,
            grid=(width // tile,),
            in_specs=[
                pl.BlockSpec((row_total, depth), lambda j, t: (0, 0)),
                pl.BlockSpec((depth, tile), lambda j, t: (0, t[0] + j)),
            ]
            + [pl.BlockSpec((row_total, tile), lambda j, t: (0, skip // tile + j))] * len(addends)
            + [hbm] * with_ids
            + [hbm] * len(after),
            out_specs=out_specs,
            scratch_shapes=[pltpu.SemaphoreType.DMA] if with_ids else [],
        ),
        out_shape=out_shape,
        compiler_params=pltpu.CompilerParams(vmem_limit_bytes=VMEM_LIMIT),
        cost_estimate=cost,
        name="block_product",
    )((first // tile).reshape(1), rows, weight, *addends, *([ids] if with_ids else []), *after)
    return out if with_ids else out[0]


def first_kernel(chunk, first_ref, rows_ref, weight_ref, out_ref, lhs_ref, rhs_ref, acc_ref, sems):
    columns = pl.ds(pl.multiple_of(first_ref[0], 128), out_ref.shape[1])
    chunks = rhs_ref.shape[0]

    def copies(k):
        part = pl.ds(k * chunk, chunk)
        return (
            pltpu.make_async_copy(rows_ref.at[:, part], lhs_ref.at[:, part], sems.at[0, k]),
            pltpu.make_async_copy(weight_ref.at[part, columns], rhs_ref.at[k], sems.at[1, k]),
        )

    for k in range(chunks):
        for copy in copies(k):
            copy.start()
    for k in range(chunks):
        for copy in copies(k):
            copy.wait()
        lhs = lhs_ref[:, k * chunk : (k + 1) * chunk]
        part = jnp.dot(lhs, rhs_ref[k], preferred_element_type=F32)
        if k == 0:
            acc_ref[...] = part
        elif k < chunks - 1:
            acc_ref[...] += part
        else:
            out_ref[...] = (acc_ref[...] + part).astype(out_ref.dtype)


def first_product(rows, weight, first, width):
    row_total, depth = rows.shape
    chunk = depth // 2
    chunks = depth // chunk
    hbm = pl.BlockSpec(memory_space=pltpu.HBM)
    return pl.pallas_call(
        functools.partial(first_kernel, chunk),
        in_specs=[pl.BlockSpec(memory_space=pltpu.SMEM), hbm, hbm],
        out_specs=[pl.BlockSpec(memory_space=pltpu.VMEM)] * 2,
        out_shape=[
            pltpu.VMEM((row_total, width), BF16),
            pltpu.VMEM((row_total, depth), BF16),
        ],
        scratch_shapes=[
            pltpu.VMEM((chunks, chunk, width), BF16),
            pltpu.VMEM((row_total, width), F32),
            pltpu.SemaphoreType.DMA((2, chunks)),
        ],
        compiler_params=pltpu.CompilerParams(vmem_limit_bytes=VMEM_LIMIT),
        cost_estimate=SMALL,
        name="first_product",
    )(first.reshape(1), pltpu.with_memory_space_constraint(rows, pltpu.HBM), weight)


def pick_kernel(peers, afters, me_ref, table_ref, lens_ref, *rest):
    ids_refs = rest[:peers]
    down_ref, up_ref = rest[peers : peers + 2]
    rest = rest[peers + 2 + afters :]
    packs, (start_ref, end_ref, pick_ref, count_ref, sem) = rest[:peers], rest[peers:]
    segs = lens_ref.shape[1]
    share, _, depth = down_ref.shape
    cols = up_ref.shape[2]
    me = me_ref[0]

    def clear(q, carry):
        pick_ref[q] = 0
        start_ref[q] = 0
        end_ref[q] = 0
        return carry

    lax.fori_loop(0, peers * CAP, clear, 0, unroll=8)
    for x in range(peers):
        count_ref[x] = 0

    def copies(x, c, source):
        pack = packs[x].at[c]
        return (
            pltpu.make_async_copy(down_ref.at[source], pack.at[:, pl.ds(0, depth)], sem),
            pltpu.make_async_copy(up_ref.at[source], pack.at[:, pl.ds(depth, cols)], sem),
        )

    for x in reversed(range(peers)):

        def choose(s, count):
            local = table_ref[ids_refs[x][0, s]] - me * share
            mine = jnp.logical_and(local >= 0, local < share)

            @pl.when(jnp.logical_and(mine, count < CAP))
            def _():
                pick_ref[x * CAP + count] = local

            return count + mine.astype(jnp.int32)

        lax.fori_loop(0, segs, choose, 0, unroll=4)
        for c in range(CAP):
            for copy in copies(x, c, pick_ref[x * CAP + c]):
                copy.start()

    def place(s, first):
        x = lax.bitwise_xor(table_ref[ids_refs[0][0, s]] // share, me)
        count = count_ref[x]
        last = first + lens_ref[0, s]

        @pl.when(count < CAP)
        def _():
            start_ref[x * CAP + count] = first
            end_ref[x * CAP + count] = last

        count_ref[x] = count + 1
        return last

    lax.fori_loop(0, segs, place, 0, unroll=4)

    for x in range(peers):
        for c in range(CAP):
            for copy in copies(x, c, 0):
                copy.wait()


def pick_adapters(me, table, all_ids, lens, down, up, after):
    peers = len(all_ids)
    _, rank, depth = down.shape
    cols = up.shape[2]
    smem = pl.BlockSpec(memory_space=pltpu.SMEM)
    vmem = pl.BlockSpec(memory_space=pltpu.VMEM)
    hbm = pl.BlockSpec(memory_space=pl.ANY)
    out = pl.pallas_call(
        functools.partial(pick_kernel, peers, len(after)),
        in_specs=[smem] * (3 + peers) + [hbm] * (2 + len(after)),
        out_specs=[vmem] * peers + [smem, smem],
        out_shape=[jax.ShapeDtypeStruct((CAP, rank, depth + cols), BF16)] * peers
        + [jax.ShapeDtypeStruct((peers * CAP,), jnp.int32)] * 2,
        scratch_shapes=[
            pltpu.SMEM((peers * CAP,), jnp.int32),
            pltpu.SMEM((peers,), jnp.int32),
            pltpu.SemaphoreType.DMA,
        ],
        compiler_params=pltpu.CompilerParams(vmem_limit_bytes=VMEM_LIMIT),
        cost_estimate=SMALL,
        name="pick_adapters",
    )(me.reshape(1), table, lens, *all_ids, down, up, *after)
    return list(out[:-2]), out[-2], out[-1]


def pack_spec(pack, first, width):
    return pl.BlockSpec(pack.shape[:2] + (width,), lambda i: (0, 0, first // width))


def low_kernel(peers, start_ref, end_ref, rows_ref, *rest):
    down_refs, out_ref = rest[:peers], rest[-1]
    row_total, depth = rows_ref.shape
    rank = out_ref.shape[0]
    place = lax.broadcasted_iota(jnp.int32, (rank, row_total), 1)
    downs = jnp.concatenate([ref[...].reshape(CAP * rank, depth) for ref in down_refs], axis=0)
    part = lax.dot_general(
        downs, rows_ref[...], (((1,), (1,)), ((), ())), preferred_element_type=F32
    )
    total = jnp.zeros((rank, row_total), F32)
    for q in range(peers * CAP):
        member = jnp.logical_and(place >= start_ref[q], place < end_ref[q])
        total = jnp.where(member, part[q * rank : (q + 1) * rank], total)
    out_ref[...] = total.astype(BF16)


def low_sums(starts, ends, rows, packs, rank, after):
    row_total, depth = rows.shape
    smem = pl.BlockSpec(memory_space=pltpu.SMEM)
    vmem = pl.BlockSpec(memory_space=pltpu.VMEM)
    return pl.pallas_call(
        functools.partial(low_kernel, len(packs)),
        grid=(1,),
        in_specs=[smem, smem, vmem]
        + [pack_spec(p, 0, depth) for p in packs]
        + [pl.BlockSpec(memory_space=pl.ANY)] * len(after),
        out_specs=vmem,
        out_shape=jax.ShapeDtypeStruct((rank, row_total), BF16),
        compiler_params=pltpu.CompilerParams(vmem_limit_bytes=VMEM_LIMIT),
        cost_estimate=SMALL,
        name="low_sums",
    )(starts, ends, rows, *packs, *after)


def term_kernel(lows, pieces, peers, start_ref, end_ref, *rest):
    low_refs, rest = rest[:lows], rest[lows:]
    own_refs, rest = rest[:pieces], rest[pieces:]
    up_refs, out_refs = rest[:peers], rest[-pieces:]
    rank, row_total = low_refs[0].shape
    width = out_refs[0].shape[1]
    cols = width * pieces
    low = low_refs[0][...].astype(F32)
    for ref in low_refs[1:]:
        low = low + ref[...].astype(F32)
    low = low.astype(BF16).astype(F32)
    place = lax.broadcasted_iota(jnp.int32, (rank, row_total), 1)
    spread = []
    for q in range(len(up_refs) * CAP):
        member = jnp.logical_and(place >= start_ref[q], place < end_ref[q])
        spread.append(jnp.where(member, low, 0.0))
    spread = jnp.concatenate(spread, axis=0).astype(BF16)
    ups = jnp.concatenate([ref[...].reshape(CAP * rank, cols) for ref in up_refs], axis=0)
    for piece in range(pieces):
        columns = slice(piece * width, (piece + 1) * width)
        term = lax.dot_general(
            spread, ups[:, columns], (((0,), (0,)), ((), ())), preferred_element_type=F32
        )
        out_refs[piece][...] = own_refs[piece][...].astype(F32) + term


def adapter_term(starts, ends, lows, owns, packs, after):
    row_total, width = owns[0].shape
    cols = width * len(owns)
    smem = pl.BlockSpec(memory_space=pltpu.SMEM)
    vmem = pl.BlockSpec(memory_space=pltpu.VMEM)
    depth = packs[0].shape[2] - cols
    return pl.pallas_call(
        functools.partial(term_kernel, len(lows), len(owns), len(packs)),
        grid=(1,),
        in_specs=[smem, smem]
        + [vmem] * (len(lows) + len(owns))
        + [pack_spec(p, depth, cols) for p in packs]
        + [pl.BlockSpec(memory_space=pl.ANY)] * len(after),
        out_specs=[vmem] * len(owns),
        out_shape=[jax.ShapeDtypeStruct((row_total, width), F32)] * len(owns),
        compiler_params=pltpu.CompilerParams(vmem_limit_bytes=VMEM_LIMIT),
        cost_estimate=SMALL,
        name="adapter_term",
    )(starts, ends, *lows, *owns, *packs, *after)


def finish_kernel(addends, term_ref, *rest):
    total = term_ref[...]
    for ref in rest[:addends]:
        total = total + ref[...].astype(F32)
    rest[-1][...] = total.astype(rest[-1].dtype)


def finish(term, skip, arrived, offset, cols, result, cost):
    row_total, width = arrived.shape
    height = min(row_total, 256)
    block = pl.BlockSpec((height, width), lambda i: (i, 0))
    held = [] if result is None else [result]
    return pl.pallas_call(
        functools.partial(finish_kernel, 1),
        grid=(row_total // height,),
        in_specs=[pl.BlockSpec((height, width), lambda i: (i, skip // width)), block]
        + [pl.BlockSpec(memory_space=pl.ANY)] * len(held),
        out_specs=pl.BlockSpec((height, width), lambda i: (i, offset // width)),
        out_shape=jax.ShapeDtypeStruct((row_total, cols), BF16),
        input_output_aliases={2: 0} if held else {},
        compiler_params=pltpu.CompilerParams(vmem_limit_bytes=VMEM_LIMIT),
        cost_estimate=cost,
        name="finish",
    )(term, arrived, *held)


def local(req_total, tp_total, rows, weight, down, up, table, ids, lens):
    weight = pltpu.with_memory_space_constraint(weight, pltpu.HBM)
    down = pltpu.with_memory_space_constraint(down, pltpu.HBM)
    up = pltpu.with_memory_space_constraint(up, pltpu.HBM)
    rank = down.shape[1]
    cols = up.shape[2]
    width = cols // PIECES
    me_req = lax.axis_index("req").astype(jnp.int32)
    me = lax.axis_index("tp").astype(jnp.int32)
    steps = tp_total - 1

    def move(value, piece):
        pairs = []
        for r in range(req_total):
            way = 1 if (r + piece) % 2 == 0 else tp_total - 1
            for i in range(tp_total):
                pairs.append((r * tp_total + i, r * tp_total + (i + way) % tp_total))
        return lax.ppermute(value, ("req", "tp"), pairs)

    def start_of(back, piece):
        behind = jnp.where(lax.rem(me_req + piece, 2) == 0, tp_total - back, back)
        block = lax.rem(me + behind, tp_total)
        return block * cols + piece * width

    def partial(back, piece, **options):
        return block_product(rows, weight, start_of(back, piece), width, **options)

    def half_partial(back, piece, skip, **options):
        first = start_of(back, piece) + skip
        return block_product(rows, weight, first, width // 2, skip=skip, **options)

    last, rows = first_product(rows, weight, start_of(1, 0), width)
    rows = pltpu.with_memory_space_constraint(rows, pltpu.VMEM)
    moving = [move(last, 0)]
    for piece in range(1, PIECES):
        last, ids = partial(1, piece, after=[last], ids=ids)
        moving.append(move(last, piece))

    all_ids = [ids]
    for x in range(1, req_total):
        all_ids.append(lax.ppermute(ids, "req", [(i, i ^ x) for i in range(req_total)]))
    last = partial(0, 0, after=[last])
    owns = [last]
    packs, starts, ends = pick_adapters(me_req, table, all_ids, lens, down, up, [last])
    for x in reversed(range(1, req_total)):
        packs[x] = lax.ppermute(packs[x], "req", [(i, i ^ x) for i in range(req_total)])

    last = starts
    for step in range(1, steps):
        for piece in range(PIECES):
            if step == steps - 1 and piece == PIECES - 1:
                low = low_sums(starts, ends, rows, packs, rank, [last])
                lows = [low]
                for x in range(1, tp_total):
                    pairs = [(i, i ^ x) for i in range(tp_total)]
                    lows.append(lax.ppermute(low, "tp", pairs))
                last = low
            if step == steps - 1 and piece == PIECES - 1:
                halves = []
                for skip in (0, width // 2):
                    last = half_partial(
                        1 + step, piece, skip, addends=[moving[piece]], after=[last]
                    )
                    halves.append(move(last, piece))
                break
            last = partial(1 + step, piece, addends=[moving[piece]], after=[last])
            moving[piece] = move(last, piece)
            if step == 1 and piece > 0:
                last = partial(0, piece, after=[last], cost=LARGE)
                owns.append(last)

    terms = adapter_term(starts, ends, lows, owns, packs, [last])
    parts = [(piece, 0, moving[piece]) for piece in range(PIECES - 1)]
    parts += [(PIECES - 1, skip, half) for skip, half in zip((0, width // 2), halves)]
    result = None
    for piece, skip, arrived in parts:
        arrived = pltpu.with_memory_space_constraint(arrived, pltpu.VMEM)
        cost = LARGE if piece == 0 else SMALL
        offset = piece * width + skip
        result = finish(terms[piece], skip, arrived, offset, cols, result, cost)
    return result


def solution(mesh):
    return jax.shard_map(
        functools.partial(local, mesh.shape["req"], mesh.shape["tp"]),
        mesh=mesh,
        in_specs=(
            P(("groups", "req"), "tp"),
            P("tp", None),
            P(("groups", "req"), None, "tp"),
            P(("groups", "req"), None, "tp"),
            P("groups"),
            P(("groups", "req"), None),
            P(("groups", "req"), None),
        ),
        out_specs=P(("groups", "req"), "tp"),
        check_vma=False,
    )
```
